32 devices in a mesh: dp: 8 (over y, x, core), fsdp: 4 (over z).
Axes of the slice: x: 2, y: 2, z: 4, core: 2. Of those that a mesh axis runs over, the one named last changes fastest.
Arguments:
- events: bfloat16 [96, 128, 1024], P(('dp', 'fsdp')), may hold values from -6 to 6
- query_weight: bfloat16 [1024, 512], P('fsdp'), may hold values from -0.1875 to 0.1875
- keys: bfloat16 [96, 128, 512], P(('dp', 'fsdp')), may hold values from -6 to 6
- values: bfloat16 [96, 128, 512], P(('dp', 'fsdp')), may hold values from -48 to 48
- gates: bfloat16 [96, 128, 512], P(('dp', 'fsdp')), may hold values from -6 to 6
- cotangent: bfloat16 [96, 128, 512], P(('dp', 'fsdp')), may hold values from -6 to 6
- lengths: int32 [96], replicated, may hold values from 1 to 128, as said below
Outputs:
- grad_keys: bfloat16 [96, 128, 512], P(('dp', 'fsdp'))
- grad_values: bfloat16 [96, 128, 512], P(('dp', 'fsdp'))
- grad_gates: bfloat16 [96, 128, 512], P(('dp', 'fsdp'))
- grad_weight: float32 [1024, 512], P('fsdp')
The draws below stay inside these ranges and needn't reach their ends.
Inputs may be any that keep to these rules, and one draw needn't show every extreme that they name: Each sequence fills the first lengths[b] events of its slot of 128 events; the rest is padding that no output reads.
All inputs are finite; a program needn't handle non-finite values.
Results may differ from the reference program's by a relative error of at most 0.015.
Values may be sent and summed in bfloat16 or wider, within the bound.
No kernel may reach another device: no remote copies, remote signals or barrier semaphores. Data moves between devices by JAX's collectives and lax.ppermute only.
A program may use at most 64 MiB of HBM per device.

```python
import math
import jax
import jax.numpy as jnp
from jax import lax

D = 1024
HEADS = 4
HEAD_DIM = 128
BLK = 64
MAXB = 2
SLOTS = 3
SPAN = 128
HW = 512
SEQS = 96


def draw_lengths(key, part):
    key = jax.random.fold_in(key, 7)
    split_keys = jax.random.split(key, 5)
    device_total = SEQS // SLOTS
    loaded = jax.random.randint(split_keys[0], (device_total, 1), 0, 4) == 0
    long_lengths = jax.random.randint(split_keys[1], (device_total, SLOTS), BLK + 1, MAXB * BLK + 1)
    short_lengths = jax.random.randint(split_keys[2], (device_total, SLOTS), 1, BLK + 1)
    drawn = jnp.where(loaded, long_lengths, short_lengths).reshape(SEQS)
    longest_at = jax.random.randint(split_keys[3], (), 0, SEQS // 2)
    shortest_at = SEQS // 2 + jax.random.randint(split_keys[4], (), 0, SEQS // 2)
    drawn = drawn.at[longest_at].set(MAXB * BLK).at[shortest_at].set(1)
    return drawn.astype(jnp.int32)


def shard_levels(rng, extent, pieces, low, largest):
    def one(dim, parts):
        draws = jax.random.uniform(jax.random.fold_in(jax.random.fold_in(rng, 6), dim), (parts,), jnp.float32, low / len(pieces), largest / len(pieces))
        return jnp.repeat(jnp.exp(draws), extent[dim] // parts).reshape((-1,) + (1,) * (len(extent) - dim - 1))

    gain = one(*pieces[0])
    for cut in pieces[1:]:
        gain = gain * one(*cut)
    return gain


def normal_values(own_key, dims, scale, reach, cuts=(), held_as=jnp.bfloat16):
    entries = jax.random.normal(own_key, dims, jnp.float32) * scale
    if len(cuts) > 0:
        entries = shard_levels(own_key, dims, cuts, -0.22, 0.18) * entries
    return jnp.clip(entries, min=-reach, max=reach).astype(held_as)


def setup_inputs(seed: int = 0) -> dict:
    key_of = jax.random.split(jax.random.key(seed), 8)
    events = normal_values(key_of[0], (SEQS, SPAN, D), 1.0, 6.0, ((0, 32),))
    query_weight = normal_values(key_of[1], (D, HW), D ** -0.5, 0.1875, ((0, 4),))
    keys = normal_values(key_of[2], (SEQS, SPAN, HW), 1.0, 6.0, ((0, 32),))
    values = normal_values(key_of[3], (SEQS, SPAN, HW), 8.0, 48.0, ((0, 32),))
    gates = normal_values(key_of[4], (SEQS, SPAN, HW), 1.0, 6.0, ((0, 32),))
    cotangent = normal_values(key_of[5], (SEQS, SPAN, HW), 1.0, 6.0, ((0, 32),))
    lengths = draw_lengths(jax.random.fold_in(key_of[7], 71), 0)
    return dict(events=events, query_weight=query_weight, keys=keys, values=values, gates=gates, cotangent=cotangent, lengths=lengths)


EPSILON = 1e-06

def rounded(values_in):
    return lax.optimization_barrier(values_in.astype(jnp.bfloat16)).astype(jnp.float32)

def slot_grads(queries, key_rows, value_rows, gate_rows, upstream_rows, length, head_count):
    row_count = queries.shape[0]
    head_width = queries.shape[1]
    head_depth = head_width // head_count
    score_scale = 1.0 / math.sqrt(head_depth)
    query_h = queries.astype(jnp.float32).reshape(row_count, head_count, head_depth)
    keys_h = key_rows.astype(jnp.float32).reshape(row_count, head_count, head_depth)
    values_h = value_rows.astype(jnp.float32).reshape(row_count, head_count, head_depth)
    scores = jnp.einsum('qhd,khd->hqk', query_h, keys_h) * score_scale
    places = lax.iota(jnp.int32, row_count)
    causal = (places[None, :] <= places[:, None]) & (places[:, None] < length)
    weight_mask = causal.astype(jnp.float32)[None]
    inverse = 1.0 / length.astype(jnp.float32)
    sigmoid = jax.nn.sigmoid(scores)
    attention = rounded(scores * sigmoid * weight_mask * inverse)
    mixed_rows = jnp.einsum('hqk,khd->qhd', attention, values_h).reshape(row_count, head_width)
    centred = mixed_rows - lax.optimization_barrier(jnp.mean(mixed_rows, axis=1, keepdims=True))
    inv_std = lax.rsqrt(lax.optimization_barrier(jnp.mean(centred * centred, axis=1, keepdims=True)) + EPSILON)
    normed = centred * inv_std
    upstream = upstream_rows.astype(jnp.float32)
    grad_gates = (upstream * normed).astype(jnp.bfloat16)
    valid_rows = (places < length).astype(jnp.float32)[:, None]
    grad_normed = upstream * gate_rows.astype(jnp.float32) * valid_rows
    grad_mixed = inv_std * (grad_normed - lax.optimization_barrier(jnp.mean(grad_normed, axis=1, keepdims=True)) - normed * lax.optimization_barrier(jnp.mean(grad_normed * normed, axis=1, keepdims=True)))
    grad_mixed = rounded(grad_mixed).reshape(row_count, head_count, head_depth)
    grad_values = jnp.einsum('hqk,qhd->khd', attention, grad_mixed)
    grad_attention = jnp.einsum('qhd,khd->hqk', grad_mixed, values_h)
    grad_scores = rounded(grad_attention * sigmoid * (1.0 + scores * (1.0 - sigmoid)) * weight_mask * inverse)
    grad_query = jnp.einsum('hqk,khd->qhd', grad_scores, keys_h) * score_scale
    grad_keys = jnp.einsum('hqk,qhd->khd', grad_scores, query_h) * score_scale
    return (grad_query.reshape(row_count, head_width).astype(jnp.bfloat16), grad_keys.reshape(row_count, head_width).astype(jnp.bfloat16), grad_values.reshape(row_count, head_width).astype(jnp.bfloat16), grad_gates)

def reference(events, query_weight, keys, values, gates, cotangent, lengths):

    def one_sequence(running, operands):
        tokens, key_rows, value_rows, gate_rows, upstream_rows, length = operands
        queries = lax.optimization_barrier(jnp.dot(tokens, query_weight, preferred_element_type=jnp.float32).astype(jnp.bfloat16))
        grad_query, grad_keys, grad_values, grad_gates = slot_grads(queries, key_rows, value_rows, gate_rows, upstream_rows, length, HEADS)
        running = running + jnp.dot(tokens.T, grad_query, preferred_element_type=jnp.float32)
        return (running, (grad_keys, grad_values, grad_gates))
    initial = jnp.zeros((D, HEADS * HEAD_DIM), jnp.float32)
    running, outputs = lax.scan(one_sequence, initial, (events, keys, values, gates, cotangent, lengths))
    return (outputs[0], outputs[1], outputs[2], running / SEQS)
```

```python
import functools
import math

import jax
import jax.numpy as jnp
from jax import lax
from jax.experimental import pallas as pl
from jax.experimental.pallas import tpu as pltpu
from jax.sharding import PartitionSpec as P

HEADS = 4
EPSILON = 1e-06
CORES = 2
BOTH = ("dp", "fsdp")
VMEM_LIMIT = 24 * 1024 * 1024

LAST = (((1,), (1,)), ((), ()))
FIRST = (((0,), (0,)), ((), ()))


def dot(lhs, rhs, dims=(((1,), (0,)), ((), ()))):
    return lax.dot_general(lhs, rhs, dims, preferred_element_type=jnp.float32)


def vmem():
    return pl.BlockSpec(memory_space=pltpu.VMEM)


def params():
    return pltpu.CompilerParams(vmem_limit_bytes=VMEM_LIMIT)


def cost(flops, bytes_accessed):
    return pl.CostEstimate(flops=flops, bytes_accessed=bytes_accessed, transcendentals=0)


def transpose_kernel(own_ref, sibling_ref, out_ref):
    rows = own_ref.shape[0]
    out_ref[:, :rows] = own_ref[...].T
    out_ref[:, rows:] = sibling_ref[...].T


def attend_slot(slot, span, length, query_ref, key_ref, value_ref, gate_ref, upstream_ref,
                grad_key_ref, grad_value_ref, grad_gate_ref, halves_ref):
    width = key_ref.shape[1]
    depth = width // HEADS
    scale = 1.0 / math.sqrt(depth)
    rows = slice(slot * span, (slot + 1) * span)
    columns = [slice(h * depth, (h + 1) * depth) for h in range(HEADS)]
    row = lax.broadcasted_iota(jnp.int32, (span, span), 0)
    column = lax.broadcasted_iota(jnp.int32, (span, span), 1)
    inverse = 1.0 / jnp.full((span, span), length, jnp.int32).astype(jnp.float32)
    weight = jnp.where((column <= row) & (row < length), inverse, 0.0)
    live = lax.broadcasted_iota(jnp.int32, (span, 1), 0) < length

    attention, slopes, mixed = [], [], []
    for h in range(HEADS):
        scores = dot(query_ref[rows, columns[h]], key_ref[rows, columns[h]], LAST) * scale
        sigmoid = 0.5 * jnp.tanh(0.5 * scores) + 0.5
        silu = scores * sigmoid
        attention.append((silu * weight).astype(jnp.bfloat16))
        slopes.append((sigmoid + silu * (1.0 - sigmoid)) * weight)
        mixed.append(dot(attention[h], value_ref[rows, columns[h]]))

    mean = sum(jnp.sum(m, axis=1, keepdims=True) for m in mixed) / width
    centred = [m - mean for m in mixed]
    var = sum(jnp.sum(c * c, axis=1, keepdims=True) for c in centred) / width
    inv_std = lax.rsqrt(var + EPSILON)
    normed = [c * inv_std for c in centred]
    grad_normed = []
    for h in range(HEADS):
        upstream = upstream_ref[rows, columns[h]].astype(jnp.float32)
        grad_gate_ref[rows, columns[h]] = (upstream * normed[h]).astype(jnp.bfloat16)
        gated = upstream * gate_ref[rows, columns[h]].astype(jnp.float32)
        grad_normed.append(jnp.where(live, gated, 0.0))
    first = sum(jnp.sum(g, axis=1, keepdims=True) for g in grad_normed) / width
    second = sum(
        jnp.sum(g * n, axis=1, keepdims=True) for g, n in zip(grad_normed, normed)
    ) / width

    for h in range(HEADS):
        grad_mixed = (inv_std * (grad_normed[h] - first - normed[h] * second)).astype(jnp.bfloat16)
        grad_value_ref[rows, columns[h]] = dot(attention[h], grad_mixed, FIRST).astype(jnp.bfloat16)
        grad_attention = dot(grad_mixed, value_ref[rows, columns[h]], LAST)
        grad_scores = (grad_attention * slopes[h]).astype(jnp.bfloat16)
        grad_query = dot(grad_scores, key_ref[rows, columns[h]]) * scale
        per_half = HEADS // CORES
        place = slice((h % per_half) * depth, (h % per_half + 1) * depth)
        halves_ref[h // per_half, rows, place] = grad_query.astype(jnp.bfloat16)
        grad_key = dot(grad_scores, query_ref[rows, columns[h]], FIRST) * scale
        grad_key_ref[rows, columns[h]] = grad_key.astype(jnp.bfloat16)


def attention_kernel(slots, piece_count, *refs):
    starts_ref, lengths_ref = refs[:2]
    pieces = refs[2 : 2 + piece_count]
    (events_ref, key_ref, value_ref, gate_ref, upstream_ref, grad_key_ref, grad_value_ref,
     grad_gate_ref, keep_ref, send_ref, weight_ref, query_ref, halves_ref, sems) = refs[2 + piece_count :]
    copies = []
    for p, piece in enumerate(pieces):
        rows = piece.shape[0]
        start = pl.multiple_of(starts_ref[p], 16)
        copy = pltpu.make_async_copy(piece, weight_ref.at[pl.ds(start, rows)], sems.at[p])
        copy.start()
        copies.append(copy)
    for copy in copies:
        copy.wait()
    query_ref[...] = dot(events_ref[...], weight_ref[...]).astype(jnp.bfloat16)
    span = key_ref.shape[0] // slots
    for slot in range(slots):
        attend_slot(slot, span, lengths_ref[slot], query_ref, key_ref, value_ref, gate_ref,
                    upstream_ref, grad_key_ref, grad_value_ref, grad_gate_ref, halves_ref)
    core = starts_ref[piece_count]
    keep_ref[...] = halves_ref[core]
    send_ref[...] = halves_ref[1 - core]


def gradient_kernel(shards, chips, place_ref, events_ref, keep_ref, got_ref, *refs):
    outs, both_ref, total_ref = refs[:chips], refs[chips], refs[chips + 1]
    rows = keep_ref.shape[0]
    both_ref[:rows] = keep_ref[...]
    both_ref[rows:] = got_ref[...]
    total_ref[...] = dot(events_ref[...], both_ref[...]).reshape(total_ref.shape)
    for k, out in enumerate(outs):
        chip = lax.rem(place_ref[0] + k, chips)
        for s in range(shards):
            out[s] = total_ref[s, chip].astype(out.dtype)


def shard_sum_kernel(shards, place_ref, *refs):
    terms, outs = refs[: len(refs) - shards], refs[len(refs) - shards :]
    for k, out in enumerate(outs):
        shard = lax.rem(place_ref[0] + k, shards)
        total = terms[0][shard].astype(jnp.float32)
        for term in terms[1:]:
            total = total + term[shard].astype(jnp.float32)
        out[...] = total.astype(out.dtype)


def mean_kernel(count, *refs):
    total = refs[0][...].astype(jnp.float32)
    for term in refs[1:-1]:
        total = total + term[...].astype(jnp.float32)
    refs[-1][...] = (total / count).astype(refs[-1].dtype)


def place_kernel(dp_count, place_ref, *refs):
    out = refs[-1]
    rows, columns = refs[0].shape
    for k, piece in enumerate(refs[:-1]):
        source = lax.rem(place_ref[0] + dp_count - k, dp_count)
        row = pl.multiple_of((source // CORES) * rows, 16)
        column = pl.multiple_of((source % CORES) * columns, 128)
        out[pl.ds(row, rows), pl.ds(column, columns)] = piece[...].astype(out.dtype)


def gather_weight(weight, dp_count, fsdp_count, sibling):
    core = lax.axis_index("dp") % CORES
    here = lax.axis_index("fsdp")
    rows = weight.shape[0]
    pieces, starts = [weight], [here * rows]

    def move(block, forward, backward):
        perm = []
        for d in range(dp_count):
            step = forward if d % CORES == 0 else backward
            for z in range(fsdp_count):
                perm.append((d * fsdp_count + z, d * fsdp_count + (z + step) % fsdp_count))
        return lax.ppermute(block, BOTH, perm)

    for step in range(1, (fsdp_count + 1) // 2):
        got = move(weight, step, fsdp_count - step)
        source = jnp.where(core == 0, here - step, here + step) % fsdp_count
        other = jnp.where(core == 0, here + step, here - step) % fsdp_count
        pieces += [got, sibling(got)]
        starts += [source * rows, other * rows]
    if fsdp_count % 2 == 0:
        step, half = fsdp_count // 2, rows // CORES
        got = move(lax.dynamic_slice_in_dim(weight, core * half, half), step, step)
        source = (here + step) % fsdp_count * rows
        pieces += [got, sibling(got)]
        starts += [source + core * half, source + (1 - core) * half]
    return pieces, starts


def shards(events, query_weight, keys, values, gates, cotangent, lengths):
    slots, span, model_width = events.shape
    width = query_weight.shape[1]
    half_width = width // CORES
    rows = slots * span
    dp_count, fsdp_count = lax.axis_size("dp"), lax.axis_size("fsdp")
    dp_place, fsdp_place = lax.axis_index("dp"), lax.axis_index("fsdp")
    core, chip, chips = dp_place % CORES, dp_place // CORES, dp_count // CORES
    shard_rows = model_width // fsdp_count
    total_seqs = slots * dp_count * fsdp_count
    bf16, f32 = jnp.bfloat16, jnp.float32
    smem = pl.BlockSpec(memory_space=pltpu.SMEM)

    def sibling(block):
        return lax.ppermute(block, "dp", [(d, d ^ 1) for d in range(dp_count)])

    flat_events = events.reshape(rows, model_width)
    pieces, starts = gather_weight(query_weight, dp_count, fsdp_count, sibling)
    events_t = pl.pallas_call(
        transpose_kernel,
        out_shape=jax.ShapeDtypeStruct((model_width, CORES * rows), bf16),
        in_specs=[vmem(), vmem()],
        out_specs=vmem(),
        compiler_params=params(),
        cost_estimate=cost(0, 8 * rows * model_width),
        name="events_transposed",
    )(flat_events, sibling(flat_events))

    device = dp_place * fsdp_count + fsdp_place
    own_lengths = lax.dynamic_slice_in_dim(lengths, device * slots, slots)
    own = [a.reshape(rows, width) for a in (keys, values, gates, cotangent)]
    wide = jax.ShapeDtypeStruct((rows, width), bf16)
    half = jax.ShapeDtypeStruct((rows, half_width), bf16)
    piece_count = len(pieces)
    grad_keys, grad_values, grad_gates, keep, send = pl.pallas_call(
        functools.partial(attention_kernel, slots, piece_count),
        out_shape=(wide, wide, wide, half, half),
        in_specs=[smem, smem] + [pl.BlockSpec(memory_space=pl.ANY)] * piece_count + [vmem()] * 5,
        out_specs=(vmem(),) * 5,
        scratch_shapes=[
            pltpu.VMEM((model_width, width), bf16),
            pltpu.VMEM((rows, width), bf16),
            pltpu.VMEM((CORES, rows, half_width), bf16),
            pltpu.SemaphoreType.DMA((piece_count,)),
        ],
        compiler_params=params(),
        cost_estimate=cost(2 * rows * width * (model_width + 5 * span), 12 * rows * width * 2),
        name="attention_both_ways",
    )(jnp.stack(starts + [core]).astype(jnp.int32), own_lengths, *pieces, flat_events, *own)
    got = sibling(send)

    piece_rows = shard_rows // chips
    staged = piece_rows % 16 == 0
    parts = chips if staged else 1
    part_rows = shard_rows // parts
    first_type = f32
    terms = pl.pallas_call(
        functools.partial(gradient_kernel, fsdp_count, parts),
        out_shape=tuple(
            jax.ShapeDtypeStruct((fsdp_count, part_rows, half_width), bf16 if k else first_type)
            for k in range(parts)
        ),
        in_specs=[smem] + [vmem()] * 3,
        out_specs=(vmem(),) * parts,
        scratch_shapes=[
            pltpu.VMEM((CORES * rows, half_width), bf16),
            pltpu.VMEM((fsdp_count, parts, part_rows, half_width), f32),
        ],
        compiler_params=params(),
        cost_estimate=cost(
            4 * rows * model_width * half_width, 2 * model_width * (2 * rows + half_width)
        ),
        name="weight_gradient",
    )(jnp.reshape(chip if staged else 0 * chip, (1,)), events_t, keep, got)

    if not staged:
        own_half = terms[0].reshape(model_width, half_width)
        whole = lax.dynamic_update_slice_in_dim(
            jnp.zeros((model_width, width), f32), own_half, core * half_width, axis=1
        )
        mine = lax.psum_scatter(whole, "fsdp", scatter_dimension=0, tiled=True)
        grad_weight = lax.psum(mine, "dp") / total_seqs
    else:
        terms = [terms[0]] + [
            lax.ppermute(
                terms[k],
                "dp",
                [
                    (c * CORES + e, (c + k) % chips * CORES + e)
                    for c in range(chips)
                    for e in range(CORES)
                ],
            )
            for k in range(1, chips)
        ]
        block = (part_rows, half_width)
        sums = pl.pallas_call(
            functools.partial(shard_sum_kernel, fsdp_count),
            out_shape=tuple(
                jax.ShapeDtypeStruct(block, bf16 if k else f32) for k in range(fsdp_count)
            ),
            in_specs=[smem] + [vmem()] * len(terms),
            out_specs=(vmem(),) * fsdp_count,
            compiler_params=params(),
            name="sum_over_chips",
        )(jnp.reshape(fsdp_place, (1,)), *terms)
        sums = [sums[0]] + [
            lax.ppermute(sums[k], "fsdp", [(z, (z + k) % fsdp_count) for z in range(fsdp_count)])
            for k in range(1, fsdp_count)
        ]
        mean = pl.pallas_call(
            functools.partial(mean_kernel, total_seqs),
            out_shape=jax.ShapeDtypeStruct(block, bf16),
            in_specs=[vmem()] * len(sums),
            out_specs=vmem(),
            compiler_params=params(),
            name="mean_over_shards",
        )(*sums)
        blocks = [mean] + [
            lax.ppermute(mean, "dp", [(d, (d + k) % dp_count) for d in range(dp_count)])
            for k in range(1, dp_count)
        ]
        grad_weight = pl.pallas_call(
            functools.partial(place_kernel, dp_count),
            out_shape=jax.ShapeDtypeStruct((shard_rows, width), f32),
            in_specs=[smem] + [vmem()] * len(blocks),
            out_specs=vmem(),
            compiler_params=params(),
            name="blocks_in_place",
        )(jnp.reshape(dp_place, (1,)), *blocks)

    shape = (slots, span, width)
    return (
        grad_keys.reshape(shape),
        grad_values.reshape(shape),
        grad_gates.reshape(shape),
        grad_weight,
    )


def solution(mesh):
    split = P(BOTH, None, None)
    return jax.shard_map(
        shards,
        mesh=mesh,
        in_specs=(split, P("fsdp", None), split, split, split, split, P()),
        out_specs=(split, split, split, P("fsdp", None)),
        check_vma=False,
    )
```

```python
import functools
import math

import jax
import jax.numpy as jnp
from jax import lax
from jax.experimental import pallas as pl
from jax.experimental.pallas import tpu as pltpu
from jax.sharding import PartitionSpec as P

HEADS = 4
EPSILON = 1e-06
CORES = 2
BOTH = ("dp", "fsdp")
VMEM_LIMIT = 24 * 1024 * 1024

LAST = (((1,), (1,)), ((), ()))
FIRST = (((0,), (0,)), ((), ()))


def dot(lhs, rhs, dims=(((1,), (0,)), ((), ()))):
    return lax.dot_general(lhs, rhs, dims, preferred_element_type=jnp.float32)


def call(kernel, name, operands, in_specs, out_shape, scratch=(), flops=0, moved=0,
         out_specs=None):
    vmem = pl.BlockSpec(memory_space=pltpu.VMEM)
    many = isinstance(out_shape, tuple)
    operands = [
        pltpu.with_memory_space_constraint(a, pltpu.HBM) if spec is FAR else a
        for a, spec in zip(operands, in_specs)
    ]
    return pl.pallas_call(
        kernel,
        out_shape=out_shape,
        in_specs=in_specs,
        out_specs=out_specs or ((vmem,) * len(out_shape) if many else vmem),
        scratch_shapes=list(scratch),
        compiler_params=pltpu.CompilerParams(vmem_limit_bytes=VMEM_LIMIT),
        cost_estimate=pl.CostEstimate(flops=flops, bytes_accessed=moved, transcendentals=0),
        name=name,
    )(*operands)


NEAR = pl.BlockSpec(memory_space=pltpu.VMEM)
ANYWHERE = pl.BlockSpec(memory_space=pl.ANY)
FAR = pl.BlockSpec(memory_space=pltpu.HBM)


def head_columns(width):
    depth = width // HEADS
    return [slice(h * depth, (h + 1) * depth) for h in range(HEADS)]


def slot_rows(rows, slots):
    span = rows // slots
    return [slice(s * span, (s + 1) * span) for s in range(slots)]


def row_mean(blocks, width):
    return jnp.sum(sum(blocks[1:], blocks[0]), axis=1, keepdims=True) / width


def slice_kernel(group, block_ref, out_ref, sem):
    rows = out_ref.shape[0]
    start = pl.multiple_of(lax.rem(lax.axis_index("dp"), group) * rows, rows)
    copy = pltpu.make_async_copy(block_ref.at[pl.ds(start, rows)], out_ref, sem)
    copy.start()
    copy.wait()


def prepare_kernel(slots, _, lengths_ref, sibling_ref, *refs):
    inputs, held = refs[:6], refs[6:11]
    (events_t_ref, key_t_ref, value_t_ref, weight_ref, gated_ref, first_ref,
     gate_ref, own_lengths_ref, sems) = refs[11:]
    events_ref, key_ref, value_ref, upstream_ref, _ = held
    copies = [
        pltpu.make_async_copy(source, target, sems.at[i])
        for i, (source, target) in enumerate(zip(inputs, held + (gate_ref,)))
    ]
    copies.append(pltpu.make_async_copy(lengths_ref, own_lengths_ref, sems.at[len(copies)]))
    for copy in copies:
        copy.start()
    rows, width = key_ref.shape
    events_t_ref[:, rows:] = sibling_ref[...].T
    for copy in copies:
        copy.wait()
    events_t_ref[:, :rows] = events_ref[...].T
    key_t_ref[...] = key_ref[...].T
    value_t_ref[...] = value_ref[...].T
    span = rows // slots
    row = lax.broadcasted_iota(jnp.int32, (span, span), 0)
    column = lax.broadcasted_iota(jnp.int32, (span, span), 1)
    first_slot = (lax.axis_index("dp") * lax.axis_size("fsdp") + lax.axis_index("fsdp")) * slots
    for s, place in enumerate(slot_rows(rows, slots)):
        length = own_lengths_ref[first_slot + s]
        inverse = 1.0 / jnp.full((span, span), length, jnp.int32).astype(jnp.float32)
        weight_ref[s] = jnp.where((column <= row) & (row < length), inverse, 0.0)
        live = lax.broadcasted_iota(jnp.int32, (span, width), 0) < length
        gated = upstream_ref[place].astype(jnp.float32) * gate_ref[place].astype(jnp.float32)
        gated = jnp.where(live, gated, 0.0)
        gated_ref[place] = gated
        first = row_mean([gated[:, c] for c in head_columns(width)], width)
        first_ref[place] = jnp.broadcast_to(first, (span, first_ref.shape[1]))


def piece_start(origin, shard_rows, group, part_rows):
    flips, member_flip = origin
    device = lax.axis_index("dp")
    flip = jnp.where(lax.rem(device, CORES) == 0, flips[0], flips[1])
    start = (lax.axis_index("fsdp") ^ flip) * shard_rows
    if member_flip is not None:
        start = start + (lax.rem(device, group) ^ member_flip) * part_rows
    return pl.multiple_of(start, 16)


def attention_kernel(slots, group, origins, *refs):
    piece_count = len(origins)
    pieces = refs[:piece_count]
    (events_ref, key_ref, value_ref, key_t_ref, value_t_ref, weight_ref, gated_ref, first_ref,
     grad_query_ref, query_ref, normed_ref, mixed_grad_ref, attention_ref, scores_grad_ref,
     projection_ref, sems) = refs[piece_count:]
    copies = []
    for p, (piece, origin) in enumerate(zip(pieces, origins)):
        rows = piece.shape[0]
        start = piece_start(origin, pieces[0].shape[0], group, rows)
        copies.append(
            pltpu.make_async_copy(piece, projection_ref.at[pl.ds(start, rows)], sems.at[p])
        )
    for copy in copies:
        copy.start()
    for copy in copies:
        copy.wait()
    query_ref[...] = dot(events_ref[...], projection_ref[...]).astype(jnp.bfloat16)

    rows, width = key_ref.shape
    scale = 1.0 / math.sqrt(width // HEADS)
    columns = head_columns(width)
    places = slot_rows(rows, slots)
    each = [(s, h, s * HEADS + h) for s in range(slots) for h in range(HEADS)]
    slopes, mixed, grad_mixed = [], [], []
    for s, h, i in each:
        scores = dot(query_ref[places[s], columns[h]], key_t_ref[columns[h], places[s]]) * scale
        sigmoid = 0.5 * jnp.tanh(0.5 * scores) + 0.5
        silu = scores * sigmoid
        attention_ref[i] = (silu * weight_ref[s]).astype(jnp.bfloat16)
        slopes.append((sigmoid + silu * (1.0 - sigmoid)) * weight_ref[s])
    for s, h, i in each:
        mixed.append(dot(attention_ref[i], value_ref[places[s], columns[h]]))
    for s in range(slots):
        own = mixed[s * HEADS : (s + 1) * HEADS]
        mean = row_mean(own, width)
        centred = [m - mean for m in own]
        inv_std = lax.rsqrt(row_mean([c * c for c in centred], width) + EPSILON)
        normed = [c * inv_std for c in centred]
        gated = [gated_ref[places[s], c] for c in columns]
        second = row_mean([g * n for g, n in zip(gated, normed)], width)
        first = first_ref[places[s]]
        for h in range(HEADS):
            normed_ref[places[s], columns[h]] = normed[h]
            grad = inv_std * (gated[h] - first - normed[h] * second)
            mixed_grad_ref[places[s], columns[h]] = grad.astype(jnp.bfloat16)
    for s, h, i in each:
        grad_attention = dot(
            mixed_grad_ref[places[s], columns[h]], value_t_ref[columns[h], places[s]]
        )
        scores_grad_ref[i] = (grad_attention * slopes[i]).astype(jnp.bfloat16)
    for s, h, i in each:
        grad_query = dot(scores_grad_ref[i], key_ref[places[s], columns[h]]) * scale
        grad_query_ref[places[s], columns[h]] = grad_query.astype(jnp.bfloat16)


def outputs_kernel(slots, _, query_ref, normed_ref, mixed_grad_ref, attention_ref, scores_grad_ref,
                   upstream_ref, grad_key_ref, grad_value_ref, grad_gate_ref):
    rows, width = query_ref.shape
    scale = 1.0 / math.sqrt(width // HEADS)
    columns = head_columns(width)
    places = slot_rows(rows, slots)
    grad_gate_ref[...] = (upstream_ref[...].astype(jnp.float32) * normed_ref[...]).astype(
        jnp.bfloat16
    )
    for s in range(slots):
        for h in range(HEADS):
            i = s * HEADS + h
            grad_value = dot(attention_ref[i], mixed_grad_ref[places[s], columns[h]], FIRST)
            grad_value_ref[places[s], columns[h]] = grad_value.astype(jnp.bfloat16)
            grad_key = dot(scores_grad_ref[i], query_ref[places[s], columns[h]], FIRST) * scale
            grad_key_ref[places[s], columns[h]] = grad_key.astype(jnp.bfloat16)


def gradient_kernel(pairs, events_ref, own_ref, got_ref, *refs):
    outs, both_ref, total_ref = refs[:-2], refs[-2], refs[-1]
    rows, width = own_ref.shape
    shard_rows = total_ref.shape[0]
    half = width // CORES
    both_ref[:rows] = own_ref[...]
    both_ref[rows:] = got_ref[...]
    core, here = lax.rem(lax.axis_index("dp"), CORES), lax.axis_index("fsdp")

    def term(shard, columns):
        place = pl.ds(pl.multiple_of(shard * shard_rows, shard_rows), shard_rows)
        return dot(events_ref[place], both_ref[:, columns])

    at = 0
    for flips in pairs:
        total_ref[:, at : at + width] = term(
            here ^ jnp.where(core == 0, flips[0], flips[1]), slice(None)
        )
        at += width
    columns = pl.ds(pl.multiple_of(core * half, half), half)
    for shard in (here, here ^ (lax.axis_size("fsdp") // 2)):
        total_ref[:, at : at + half] = term(shard, columns)
        at += half
    part_rows = outs[0].shape[0]
    chip = lax.div(lax.axis_index("dp"), CORES)
    for k, out in enumerate(outs):
        start = pl.multiple_of((chip ^ k) * part_rows, part_rows)
        out[...] = total_ref[pl.ds(start, part_rows)].astype(out.dtype)


def chip_sum_kernel(term_count, _, *refs):
    terms, outs = refs[:term_count], refs[term_count:]
    at = 0
    for out in outs:
        columns = slice(at, at + out.shape[1])
        total = terms[0][:, columns].astype(jnp.float32)
        for term in terms[1:]:
            total = total + term[:, columns].astype(jnp.float32)
        out[...] = total.astype(out.dtype)
        at += out.shape[1]


def shard_sum_kernel(own_ref, middle_ref, *refs):
    wholes, out_ref, total_ref = refs[:-2], refs[-2], refs[-1]
    total = wholes[0][...].astype(jnp.float32)
    for whole in wholes[1:]:
        total = total + whole[...].astype(jnp.float32)
    total_ref[...] = total
    half = own_ref.shape[1]
    core = lax.rem(lax.axis_index("dp"), CORES)
    columns = pl.ds(pl.multiple_of(core * half, half), half)
    total_ref[:, columns] += own_ref[...] + middle_ref[...].astype(jnp.float32)
    out_ref[...] = total_ref[...].astype(out_ref.dtype)


def mean_kernel(count, own_ref, sibling_ref, out_ref, half_ref):
    total = own_ref[...].astype(jnp.float32) + sibling_ref[...].astype(jnp.float32)
    out_ref[...] = (total / count).astype(out_ref.dtype)
    rows = half_ref.shape[0]
    core = lax.rem(lax.axis_index("dp"), CORES)
    half_ref[...] = out_ref[pl.ds(pl.multiple_of(core * rows, rows), rows)]


def place_kernel(own_ref, near_ref, sibling_near_ref, half_ref, sibling_half_ref, out_ref, held_ref,
                 sems):
    rows, half = own_ref.shape[0], half_ref.shape[0]
    core, chip = lax.rem(lax.axis_index("dp"), CORES), lax.div(lax.axis_index("dp"), CORES)
    blocks = (
        (own_ref, chip * rows),
        (near_ref, (chip ^ (1 + core)) * rows),
        (sibling_near_ref, (chip ^ (2 - core)) * rows),
        (half_ref, (chip ^ 3) * rows + core * half),
        (sibling_half_ref, (chip ^ 3) * rows + (1 - core) * half),
    )
    copies = []
    for i, (block_ref, start) in enumerate(blocks):
        place = pl.ds(pl.multiple_of(start, half), block_ref.shape[0])
        held_ref[place] = block_ref[...].astype(held_ref.dtype)
        copies.append(pltpu.make_async_copy(held_ref.at[place], out_ref.at[place], sems.at[i]))
        copies[i].start()
    for copy in copies:
        copy.wait()


def flip(block, axis, count, bits):
    return lax.ppermute(block, axis, [(i, i ^ bits) for i in range(count)])


def far_first(count, send):
    return [send(k) for k in range(count - 1, 0, -1)][::-1]


def shard_pairs(fsdp_count):
    others = [d for d in range(1, fsdp_count) if d != fsdp_count // 2]
    return list(zip(others[::2], others[1::2]))


def flip_by_core(block, flips, dp_count, fsdp_count):
    pairs = [
        (d * fsdp_count + z, d * fsdp_count + (z ^ flips[d % CORES]))
        for d in range(dp_count)
        for z in range(fsdp_count)
    ]
    return lax.ppermute(block, BOTH, pairs)


def across_z(weight, dp_count, fsdp_count):
    rows = weight.shape[0]
    group = 4 if dp_count % 4 == 0 and rows % 64 == 0 else 2
    part = call(
        functools.partial(slice_kernel, group),
        "own_part_of_weight",
        [weight],
        [FAR],
        jax.ShapeDtypeStruct((rows // group, weight.shape[1]), weight.dtype),
        [pltpu.SemaphoreType.DMA],
    )
    middle = fsdp_count // 2
    weight, part = lax.optimization_barrier((weight, part))
    arrived = [(flip(part, "fsdp", fsdp_count, middle), (middle, middle), 0)]
    for flips in shard_pairs(fsdp_count):
        arrived.append((flip_by_core(weight, flips, dp_count, fsdp_count), flips, None))
    return group, arrived


def share(group, arrived, ready, dp_count):
    block, flips, member = arrived[0]
    own = [(block, flips, member)]
    if group == 4:
        own.append((flip(block, "dp", dp_count, 2), flips, member ^ 2))
    for block, flips, member in arrived[1:]:
        own.append((lax.optimization_barrier((block, own[-1][0], ready))[0], flips, member))
    found = []
    for block, source, place in own:
        moved = flip(block, "dp", dp_count, 1)
        found.append((block, (source, place)))
        found.append((moved, (source[::-1], None if place is None else place ^ 1)))
    return found


def shards(events, query_weight, keys, values, gates, cotangent, lengths):
    slots, span, model_width = events.shape
    width = query_weight.shape[1]
    half_width = width // CORES
    rows = slots * span
    dp_count, fsdp_count = lax.axis_size("dp"), lax.axis_size("fsdp")
    chips = dp_count // CORES
    shard_rows = model_width // fsdp_count
    total_seqs = slots * dp_count * fsdp_count
    bf16, f32 = jnp.bfloat16, jnp.float32

    def shape(*dims, dtype=bf16):
        return jax.ShapeDtypeStruct(dims, dtype)

    flat_events = events.reshape(rows, model_width)
    keys, values, gates, cotangent = (
        a.reshape(rows, width) for a in (keys, values, gates, cotangent)
    )
    sibling_events = flip(flat_events, "dp", dp_count, 1)
    group, arrived = across_z(query_weight, dp_count, fsdp_count)
    prepared = call(
        functools.partial(prepare_kernel, slots),
        "prepared_operands",
        [arrived[0][0], lengths, sibling_events]
        + [flat_events, keys, values, cotangent, query_weight, gates],
        [ANYWHERE, FAR, NEAR] + [FAR] * 6,
        (
            shape(rows, model_width),
            shape(rows, width),
            shape(rows, width),
            shape(rows, width),
            shape(shard_rows, width),
            shape(model_width, CORES * rows),
            shape(width, rows),
            shape(width, rows),
            shape(slots, span, span, dtype=f32),
            shape(rows, width, dtype=f32),
            shape(rows, span, dtype=f32),
        ),
        [
            pltpu.VMEM((rows, width), bf16),
            pltpu.SMEM(lengths.shape, jnp.int32),
            pltpu.SemaphoreType.DMA((7,)),
        ],
        flops=10**10,
    )
    near_events, near_keys, near_values, near_cotangent, near_weight = prepared[:5]
    events_t, keys_t, values_t, weight, gated, first = prepared[5:]
    found = [(near_weight, ((0, 0), None))] + share(group, arrived, first, dp_count)
    pieces, origins = zip(*found)
    blocks = shape(slots * HEADS, span, span)
    grad_query, query, normed, grad_mixed, attention, grad_scores = call(
        functools.partial(attention_kernel, slots, group, origins),
        "attention_to_grad_query",
        list(pieces)
        + [near_events, near_keys, near_values, keys_t, values_t, weight, gated, first],
        [ANYWHERE] * len(pieces) + [NEAR] * 8,
        (
            shape(rows, width),
            shape(rows, width),
            shape(rows, width, dtype=f32),
            shape(rows, width),
            blocks,
            blocks,
        ),
        [
            pltpu.VMEM((model_width, width), bf16),
            pltpu.SemaphoreType.DMA((len(pieces),)),
        ],
        flops=2 * rows * width * (model_width + 4 * span),
        moved=24 * rows * width,
    )
    part_rows = shard_rows // chips
    staged = chips == 4 and part_rows % 32 == 0 and fsdp_count % 4 == 0
    terms = [grad_query]
    if staged:
        pairs = shard_pairs(fsdp_count)
        columns = len(pairs) * width + 2 * half_width
        terms = call(
            functools.partial(gradient_kernel, pairs),
            "weight_gradient",
            [events_t, grad_query, flip(grad_query, "dp", dp_count, 1)],
            [NEAR] * 3,
            tuple(shape(part_rows, columns, dtype=bf16 if k else f32) for k in range(chips)),
            [
                pltpu.VMEM((CORES * rows, width), bf16),
                pltpu.VMEM((shard_rows, columns), f32),
            ],
            flops=4 * rows * shard_rows * columns,
            moved=2 * model_width * (2 * rows + half_width),
        )
    grad_keys, grad_values, grad_gates = call(
        functools.partial(outputs_kernel, slots),
        "key_value_gate_gradients",
        [terms[0], query, normed, grad_mixed, attention, grad_scores, near_cotangent],
        [ANYWHERE] + [NEAR] * 6,
        (shape(rows, width),) * 3,
        flops=4 * rows * width * span,
        moved=12 * rows * width,
    )
    if staged:
        terms = [terms[0]] + far_first(chips, lambda k: flip(terms[k], "dp", dp_count, k * CORES))
        sums = call(
            functools.partial(chip_sum_kernel, chips),
            "sum_over_chips",
            [grad_keys] + terms,
            [FAR] + [NEAR] * chips,
            (shape(part_rows, width),) * len(pairs)
            + (shape(part_rows, half_width, dtype=f32), shape(part_rows, half_width)),
        )
        wholes = [flip_by_core(a, p, dp_count, fsdp_count) for a, p in zip(sums, pairs)]
        middle = flip(sums[-1], "fsdp", fsdp_count, fsdp_count // 2)
        total = call(
            shard_sum_kernel,
            "sum_over_shards",
            [sums[-2], middle] + wholes,
            [NEAR] * (2 + len(wholes)),
            shape(part_rows, width),
            [pltpu.VMEM((part_rows, width), f32)],
        )
        mean, half = call(
            functools.partial(mean_kernel, total_seqs),
            "mean_of_both_cores",
            [total, flip(total, "dp", dp_count, 1)],
            [NEAR] * 2,
            (shape(part_rows, width), shape(part_rows // CORES, width)),
        )
        half = flip(half, "dp", dp_count, 3 * CORES)
        near = lax.ppermute(
            mean, "dp", [(d, d ^ (CORES * (1 + d % CORES))) for d in range(dp_count)]
        )
        grad_weight = call(
            place_kernel,
            "blocks_in_place",
            [mean, near, flip(near, "dp", dp_count, 1), half, flip(half, "dp", dp_count, 1)],
            [NEAR] * 5,
            shape(shard_rows, width, dtype=f32),
            [pltpu.VMEM((shard_rows, width), f32), pltpu.SemaphoreType.DMA((5,))],
            out_specs=FAR,
        )
    else:
        whole = lax.dot_general(flat_events, grad_query, FIRST, preferred_element_type=f32)
        mine = lax.psum_scatter(whole, "fsdp", scatter_dimension=0, tiled=True)
        grad_weight = lax.psum(mine, "dp") / total_seqs

    full = (slots, span, width)
    return (
        grad_keys.reshape(full),
        grad_values.reshape(full),
        grad_gates.reshape(full),
        grad_weight,
    )


def solution(mesh):
    split = P(BOTH, None, None)
    return jax.shard_map(
        shards,
        mesh=mesh,
        in_specs=(split, P("fsdp", None), split, split, split, split, P()),
        out_specs=(split, split, split, P("fsdp", None)),
        check_vma=False,
    )
```

```python
import functools
import math

import jax
import jax.numpy as jnp
from jax import lax
from jax.experimental import pallas as pl
from jax.experimental.pallas import tpu as pltpu
from jax.sharding import PartitionSpec as P

HEADS = 4
EPSILON = 1e-06
CORES = 2
BOTH = ("dp", "fsdp")
VMEM_LIMIT = 24 * 1024 * 1024

LAST = (((1,), (1,)), ((), ()))
FIRST = (((0,), (0,)), ((), ()))


def dot(lhs, rhs, dims=(((1,), (0,)), ((), ()))):
    return lax.dot_general(lhs, rhs, dims, preferred_element_type=jnp.float32)


def call(kernel, name, operands, in_specs, out_shape, scratch=(), flops=0, moved=0,
         out_specs=None):
    vmem = pl.BlockSpec(memory_space=pltpu.VMEM)
    many = isinstance(out_shape, tuple)
    operands = [
        pltpu.with_memory_space_constraint(a, pltpu.HBM) if spec is FAR else a
        for a, spec in zip(operands, in_specs)
    ]
    return pl.pallas_call(
        kernel,
        out_shape=out_shape,
        in_specs=in_specs,
        out_specs=out_specs or ((vmem,) * len(out_shape) if many else vmem),
        scratch_shapes=list(scratch),
        compiler_params=pltpu.CompilerParams(vmem_limit_bytes=VMEM_LIMIT),
        cost_estimate=pl.CostEstimate(flops=flops, bytes_accessed=moved, transcendentals=0),
        name=name,
    )(*operands)


NEAR = pl.BlockSpec(memory_space=pltpu.VMEM)
ANYWHERE = pl.BlockSpec(memory_space=pl.ANY)
FAR = pl.BlockSpec(memory_space=pltpu.HBM)


def head_columns(width):
    depth = width // HEADS
    return [slice(h * depth, (h + 1) * depth) for h in range(HEADS)]


def slot_rows(rows, slots):
    span = rows // slots
    return [slice(s * span, (s + 1) * span) for s in range(slots)]


def row_mean(blocks, width):
    return jnp.sum(sum(blocks[1:], blocks[0]), axis=1, keepdims=True) / width


def slice_kernel(group, block_ref, out_ref, sem):
    rows = out_ref.shape[0]
    start = pl.multiple_of(lax.rem(lax.axis_index("dp"), group) * rows, rows)
    copy = pltpu.make_async_copy(block_ref.at[pl.ds(start, rows)], out_ref, sem)
    copy.start()
    copy.wait()


def prepare_kernel(slots, _, lengths_ref, sibling_ref, *refs):
    inputs, held = refs[:6], refs[6:11]
    (events_t_ref, key_t_ref, value_t_ref, weight_ref, gated_ref, first_ref,
     gate_ref, own_lengths_ref, sems) = refs[11:]
    events_ref, key_ref, value_ref, upstream_ref, _ = held
    copies = [
        pltpu.make_async_copy(source, target, sems.at[i])
        for i, (source, target) in enumerate(zip(inputs, held + (gate_ref,)))
    ]
    copies.append(pltpu.make_async_copy(lengths_ref, own_lengths_ref, sems.at[len(copies)]))
    for copy in copies:
        copy.start()
    rows, width = key_ref.shape
    events_t_ref[:, rows:] = sibling_ref[...].T
    for copy in copies:
        copy.wait()
    events_t_ref[:, :rows] = events_ref[...].T
    key_t_ref[...] = key_ref[...].T
    value_t_ref[...] = value_ref[...].T
    span = rows // slots
    row = lax.broadcasted_iota(jnp.int32, (span, span), 0)
    column = lax.broadcasted_iota(jnp.int32, (span, span), 1)
    first_slot = (lax.axis_index("dp") * lax.axis_size("fsdp") + lax.axis_index("fsdp")) * slots
    for s, place in enumerate(slot_rows(rows, slots)):
        length = own_lengths_ref[first_slot + s]
        inverse = 1.0 / jnp.full((span, span), length, jnp.int32).astype(jnp.float32)
        weight_ref[s] = jnp.where((column <= row) & (row < length), inverse, 0.0)
        live = lax.broadcasted_iota(jnp.int32, (span, width), 0) < length
        gated = upstream_ref[place].astype(jnp.float32) * gate_ref[place].astype(jnp.float32)
        gated = jnp.where(live, gated, 0.0)
        gated_ref[place] = gated
        first = row_mean([gated[:, c] for c in head_columns(width)], width)
        first_ref[place] = jnp.broadcast_to(first, (span, first_ref.shape[1]))


def piece_start(origin, shard_rows, group, part_rows):
    flips, member_flip = origin
    device = lax.axis_index("dp")
    flip = jnp.where(lax.rem(device, CORES) == 0, flips[0], flips[1])
    start = (lax.axis_index("fsdp") ^ flip) * shard_rows
    if member_flip is not None:
        start = start + (lax.rem(device, group) ^ member_flip) * part_rows
    return pl.multiple_of(start, 16)


def attention_kernel(slots, group, origins, *refs):
    piece_count = len(origins)
    pieces = refs[:piece_count]
    (events_ref, key_ref, value_ref, key_t_ref, value_t_ref, weight_ref, gated_ref, first_ref,
     grad_query_ref, query_ref, normed_ref, mixed_grad_ref, attention_ref, scores_grad_ref,
     projection_ref, sems) = refs[piece_count:]
    copies = []
    for p, (piece, origin) in enumerate(zip(pieces, origins)):
        rows = piece.shape[0]
        start = piece_start(origin, pieces[0].shape[0], group, rows)
        copies.append(
            pltpu.make_async_copy(piece, projection_ref.at[pl.ds(start, rows)], sems.at[p])
        )
    for copy in copies:
        copy.start()
    for copy in copies:
        copy.wait()
    query_ref[...] = dot(events_ref[...], projection_ref[...]).astype(jnp.bfloat16)

    rows, width = key_ref.shape
    scale = 1.0 / math.sqrt(width // HEADS)
    columns = head_columns(width)
    places = slot_rows(rows, slots)
    each = [(s, h, s * HEADS + h) for s in range(slots) for h in range(HEADS)]
    slopes, mixed, grad_mixed = [], [], []
    for s, h, i in each:
        scores = dot(query_ref[places[s], columns[h]], key_t_ref[columns[h], places[s]]) * scale
        sigmoid = 0.5 * jnp.tanh(0.5 * scores) + 0.5
        silu = scores * sigmoid
        attention_ref[i] = (silu * weight_ref[s]).astype(jnp.bfloat16)
        slopes.append((sigmoid + silu * (1.0 - sigmoid)) * weight_ref[s])
    for s, h, i in each:
        mixed.append(dot(attention_ref[i], value_ref[places[s], columns[h]]))
    for s in range(slots):
        own = mixed[s * HEADS : (s + 1) * HEADS]
        mean = row_mean(own, width)
        centred = [m - mean for m in own]
        inv_std = lax.rsqrt(row_mean([c * c for c in centred], width) + EPSILON)
        normed = [c * inv_std for c in centred]
        gated = [gated_ref[places[s], c] for c in columns]
        second = row_mean([g * n for g, n in zip(gated, normed)], width)
        first = first_ref[places[s]]
        for h in range(HEADS):
            normed_ref[places[s], columns[h]] = normed[h]
            grad = inv_std * (gated[h] - first - normed[h] * second)
            mixed_grad_ref[places[s], columns[h]] = grad.astype(jnp.bfloat16)
    for s, h, i in each:
        grad_attention = dot(
            mixed_grad_ref[places[s], columns[h]], value_t_ref[columns[h], places[s]]
        )
        scores_grad_ref[i] = (grad_attention * slopes[i]).astype(jnp.bfloat16)
    for s, h, i in each:
        grad_query = dot(scores_grad_ref[i], key_ref[places[s], columns[h]]) * scale
        grad_query_ref[places[s], columns[h]] = grad_query.astype(jnp.bfloat16)


def outputs_kernel(slots, _, query_ref, normed_ref, mixed_grad_ref, attention_ref, scores_grad_ref,
                   upstream_ref, grad_key_ref, grad_value_ref, grad_gate_ref):
    rows, width = query_ref.shape
    scale = 1.0 / math.sqrt(width // HEADS)
    columns = head_columns(width)
    places = slot_rows(rows, slots)
    grad_gate_ref[...] = (upstream_ref[...].astype(jnp.float32) * normed_ref[...]).astype(
        jnp.bfloat16
    )
    for s in range(slots):
        for h in range(HEADS):
            i = s * HEADS + h
            grad_value = dot(attention_ref[i], mixed_grad_ref[places[s], columns[h]], FIRST)
            grad_value_ref[places[s], columns[h]] = grad_value.astype(jnp.bfloat16)
            grad_key = dot(scores_grad_ref[i], query_ref[places[s], columns[h]], FIRST) * scale
            grad_key_ref[places[s], columns[h]] = grad_key.astype(jnp.bfloat16)


def gradient_kernel(pairs, events_ref, own_ref, got_ref, *refs):
    outs, both_ref, picked_ref = refs[:-2], refs[-2], refs[-1]
    rows, width = own_ref.shape
    half = width // CORES
    both_ref[:rows] = own_ref[...]
    both_ref[rows:] = got_ref[...]
    device, here = lax.axis_index("dp"), lax.axis_index("fsdp")
    part_rows = outs[0].shape[0]
    shard_rows = events_ref.shape[0] // lax.axis_size("fsdp")

    def core_of(k):
        return lax.rem(device, CORES) ^ (1 if k else 0)

    def add(picks, columns, at, wide):
        for i, (k, shard) in enumerate(picks):
            start = shard * shard_rows + (lax.div(device, CORES) ^ k) * part_rows
            place = pl.ds(pl.multiple_of(start, part_rows), part_rows)
            picked_ref[i * part_rows : (i + 1) * part_rows] = events_ref[place]
        total = dot(picked_ref[: len(picks) * part_rows], both_ref[:, columns])
        for i, (k, _) in enumerate(picks):
            block = total[i * part_rows : (i + 1) * part_rows]
            outs[k][:, at(i) : at(i) + wide] = block.astype(outs[k].dtype)

    chips = range(len(outs))
    for p, flips in enumerate(pairs):
        picks = [(k, here ^ jnp.where(core_of(k) == 0, flips[0], flips[1])) for k in chips]
        add(picks, slice(None), lambda i: p * width, width)
    after = len(pairs) * width
    for group in (chips[:1], chips[1:]):
        columns = pl.ds(pl.multiple_of(core_of(group[0]) * half, half), half)
        shards = (here, here ^ (lax.axis_size("fsdp") // 2))
        picks = [(k, shard) for k in group for shard in shards]
        add(picks, columns, lambda i: after + i % 2 * half, half)


def chip_sum_kernel(term_count, _, *refs):
    terms, outs = refs[:term_count], refs[term_count:]
    at = 0
    for out in outs:
        columns = slice(at, at + out.shape[1])
        total = terms[0][:, columns].astype(jnp.float32)
        for term in terms[1:]:
            total = total + term[:, columns].astype(jnp.float32)
        out[...] = total.astype(out.dtype)
        at += out.shape[1]


def shard_sum_kernel(own_ref, middle_ref, *refs):
    wholes, out_ref, total_ref = refs[:-2], refs[-2], refs[-1]
    total = wholes[0][...].astype(jnp.float32)
    for whole in wholes[1:]:
        total = total + whole[...].astype(jnp.float32)
    total_ref[...] = total
    half = own_ref.shape[1]
    core = lax.rem(lax.axis_index("dp"), CORES)
    columns = pl.ds(pl.multiple_of(core * half, half), half)
    total_ref[:, columns] += own_ref[...]
    columns = pl.ds(pl.multiple_of((1 - core) * half, half), half)
    total_ref[:, columns] += middle_ref[...].astype(jnp.float32)
    out_ref[...] = total_ref[...].astype(out_ref.dtype)


def mean_kernel(count, own_ref, sibling_ref, out_ref):
    total = own_ref[...].astype(jnp.float32) + sibling_ref[...].astype(jnp.float32)
    out_ref[...] = (total / count).astype(out_ref.dtype)


def place_kernel(*refs):
    blocks, (out_ref, held_ref, sems) = refs[:-3], refs[-3:]
    rows = blocks[0].shape[0]
    chip = lax.div(lax.axis_index("dp"), CORES)
    copies = []
    for k, block_ref in enumerate(blocks):
        place = pl.ds(pl.multiple_of((chip ^ k) * rows, rows), rows)
        held_ref[place] = block_ref[...].astype(held_ref.dtype)
        copies.append(pltpu.make_async_copy(held_ref.at[place], out_ref.at[place], sems.at[k]))
        copies[k].start()
    for copy in copies:
        copy.wait()


def flip(block, axis, count, bits):
    return lax.ppermute(block, axis, [(i, i ^ bits) for i in range(count)])


def cross(block, dp_count, fsdp_count, chip_bits, shard_bits):
    pairs = [
        (
            d * fsdp_count + z,
            (d ^ (chip_bits * CORES) ^ 1) * fsdp_count + (z ^ shard_bits[d % CORES]),
        )
        for d in range(dp_count)
        for z in range(fsdp_count)
    ]
    return lax.ppermute(block, BOTH, pairs)


def far_first(count, send):
    return [send(k) for k in range(count - 1, 0, -1)][::-1]


def shard_pairs(fsdp_count):
    others = [d for d in range(1, fsdp_count) if d != fsdp_count // 2]
    return list(zip(others[::2], others[1::2]))


def across_z(weight, dp_count, fsdp_count):
    rows = weight.shape[0]
    group = 4 if dp_count % 4 == 0 and rows % 64 == 0 else 2
    part = call(
        functools.partial(slice_kernel, group),
        "own_part_of_weight",
        [weight],
        [FAR],
        jax.ShapeDtypeStruct((rows // group, weight.shape[1]), weight.dtype),
        [pltpu.SemaphoreType.DMA],
    )
    weight, part = lax.optimization_barrier((weight, part))
    middle = (fsdp_count // 2,) * CORES
    arrived = [(cross(part, dp_count, fsdp_count, 0, middle), middle, 1)]
    for flips in shard_pairs(fsdp_count):
        block = cross(weight, dp_count, fsdp_count, 0, flips)
        arrived.append((block, flips[::-1], None))
    return group, arrived


def share(group, arrived, ready, dp_count, fsdp_count):
    block, flips, member = arrived[0]
    own = [(block, flips, member)]
    if group == 4:
        passed = cross(block, dp_count, fsdp_count, 1, (0,) * CORES)
        own.append((passed, flips, member ^ 3))
    for block, flips, member in arrived[1:]:
        own.append((lax.optimization_barrier((block, own[-1][0], ready))[0], flips, member))
    found = []
    for block, source, place in own:
        moved = flip(block, "dp", dp_count, 1)
        found.append((block, (source, place)))
        found.append((moved, (source[::-1], None if place is None else place ^ 1)))
    return found


def shards(events, query_weight, keys, values, gates, cotangent, lengths):
    slots, span, model_width = events.shape
    width = query_weight.shape[1]
    half_width = width // CORES
    rows = slots * span
    dp_count, fsdp_count = lax.axis_size("dp"), lax.axis_size("fsdp")
    chips = dp_count // CORES
    shard_rows = model_width // fsdp_count
    total_seqs = slots * dp_count * fsdp_count
    bf16, f32 = jnp.bfloat16, jnp.float32

    def shape(*dims, dtype=bf16):
        return jax.ShapeDtypeStruct(dims, dtype)

    flat_events = events.reshape(rows, model_width)
    keys, values, gates, cotangent = (
        a.reshape(rows, width) for a in (keys, values, gates, cotangent)
    )
    sibling_events = flip(flat_events, "dp", dp_count, 1)
    group, arrived = across_z(query_weight, dp_count, fsdp_count)
    prepared = call(
        functools.partial(prepare_kernel, slots),
        "prepared_operands",
        [arrived[0][0], lengths, sibling_events]
        + [flat_events, keys, values, cotangent, query_weight, gates],
        [ANYWHERE, FAR, NEAR] + [FAR] * 6,
        (
            shape(rows, model_width),
            shape(rows, width),
            shape(rows, width),
            shape(rows, width),
            shape(shard_rows, width),
            shape(model_width, CORES * rows),
            shape(width, rows),
            shape(width, rows),
            shape(slots, span, span, dtype=f32),
            shape(rows, width, dtype=f32),
            shape(rows, span, dtype=f32),
        ),
        [
            pltpu.VMEM((rows, width), bf16),
            pltpu.SMEM(lengths.shape, jnp.int32),
            pltpu.SemaphoreType.DMA((7,)),
        ],
        flops=10**10,
    )
    near_events, near_keys, near_values, near_cotangent, near_weight = prepared[:5]
    events_t, keys_t, values_t, weight, gated, first = prepared[5:]
    found = [(near_weight, ((0, 0), None))] + share(group, arrived, first, dp_count, fsdp_count)
    pieces, origins = zip(*found)
    blocks = shape(slots * HEADS, span, span)
    grad_query, query, normed, grad_mixed, attention, grad_scores = call(
        functools.partial(attention_kernel, slots, group, origins),
        "attention_to_grad_query",
        list(pieces)
        + [near_events, near_keys, near_values, keys_t, values_t, weight, gated, first],
        [ANYWHERE] * len(pieces) + [NEAR] * 8,
        (
            shape(rows, width),
            shape(rows, width),
            shape(rows, width, dtype=f32),
            shape(rows, width),
            blocks,
            blocks,
        ),
        [
            pltpu.VMEM((model_width, width), bf16),
            pltpu.SemaphoreType.DMA((len(pieces),)),
        ],
        flops=2 * rows * width * (model_width + 4 * span),
        moved=24 * rows * width,
    )
    part_rows = shard_rows // chips
    staged = part_rows % 16 == 0 and fsdp_count % 4 == 0
    terms = [grad_query]
    if staged:
        pairs = shard_pairs(fsdp_count)
        columns = len(pairs) * width + 2 * half_width
        terms = call(
            functools.partial(gradient_kernel, pairs),
            "weight_gradient",
            [events_t, grad_query, flip(grad_query, "dp", dp_count, 1)],
            [NEAR] * 3,
            tuple(shape(part_rows, columns, dtype=bf16 if k else f32) for k in range(chips)),
            [
                pltpu.VMEM((CORES * rows, width), bf16),
                pltpu.VMEM((2 * chips * part_rows, CORES * rows), bf16),
            ],
            flops=4 * rows * shard_rows * columns,
            moved=2 * model_width * (2 * rows + half_width),
        )
    grad_keys, grad_values, grad_gates = call(
        functools.partial(outputs_kernel, slots),
        "key_value_gate_gradients",
        [terms[0], query, normed, grad_mixed, attention, grad_scores, near_cotangent],
        [ANYWHERE] + [NEAR] * 6,
        (shape(rows, width),) * 3,
        flops=4 * rows * width * span,
        moved=12 * rows * width,
    )
    if staged:
        alike = (0,) * CORES

        def to_chip(block, k):
            return cross(block, dp_count, fsdp_count, k, alike)

        terms = [terms[0]] + far_first(chips, lambda k: to_chip(terms[k], k))
        sums = call(
            functools.partial(chip_sum_kernel, chips),
            "sum_over_chips",
            [grad_keys] + terms,
            [FAR] + [NEAR] * chips,
            (shape(part_rows, width),) * len(pairs)
            + (shape(part_rows, half_width, dtype=f32), shape(part_rows, half_width)),
        )
        wholes = [cross(a, dp_count, fsdp_count, 0, p) for a, p in zip(sums, pairs)]
        middle = cross(sums[-1], dp_count, fsdp_count, 0, (fsdp_count // 2,) * CORES)
        total = call(
            shard_sum_kernel,
            "sum_over_shards",
            [sums[-2], middle] + wholes,
            [NEAR] * (2 + len(wholes)),
            shape(part_rows, width),
            [pltpu.VMEM((part_rows, width), f32)],
        )
        mean = call(
            functools.partial(mean_kernel, total_seqs),
            "mean_of_both_cores",
            [total, flip(total, "dp", dp_count, 1)],
            [NEAR] * 2,
            shape(part_rows, width),
        )
        found = [mean] + far_first(chips, lambda k: to_chip(mean, k))
        grad_weight = call(
            place_kernel,
            "blocks_in_place",
            found,
            [NEAR] * chips,
            shape(shard_rows, width, dtype=f32),
            [pltpu.VMEM((shard_rows, width), f32), pltpu.SemaphoreType.DMA((chips,))],
            out_specs=FAR,
        )
    else:
        whole = lax.dot_general(flat_events, grad_query, FIRST, preferred_element_type=f32)
        mine = lax.psum_scatter(whole, "fsdp", scatter_dimension=0, tiled=True)
        grad_weight = lax.psum(mine, "dp") / total_seqs

    full = (slots, span, width)
    return (
        grad_keys.reshape(full),
        grad_values.reshape(full),
        grad_gates.reshape(full),
        grad_weight,
    )


def solution(mesh):
    split = P(BOTH, None, None)
    return jax.shard_map(
        shards,
        mesh=mesh,
        in_specs=(split, P("fsdp", None), split, split, split, split, P()),
        out_specs=(split, split, split, P("fsdp", None)),
        check_vma=False,
    )
```

```python
import functools
import math

import jax
import jax.numpy as jnp
from jax import lax
from jax.experimental import pallas as pl
from jax.experimental.pallas import tpu as pltpu
from jax.sharding import PartitionSpec as P

HEADS = 4
EPSILON = 1e-06
CORES = 2
BOTH = ("dp", "fsdp")
VMEM_LIMIT = 24 * 1024 * 1024

LAST = (((1,), (1,)), ((), ()))
FIRST = (((0,), (0,)), ((), ()))


def dot(lhs, rhs, dims=(((1,), (0,)), ((), ()))):
    return lax.dot_general(lhs, rhs, dims, preferred_element_type=jnp.float32)


def call(kernel, name, operands, in_specs, out_shape, scratch=(), flops=0, moved=0,
         out_specs=None):
    vmem = pl.BlockSpec(memory_space=pltpu.VMEM)
    many = isinstance(out_shape, tuple)
    operands = [
        pltpu.with_memory_space_constraint(a, pltpu.HBM) if spec is FAR else a
        for a, spec in zip(operands, in_specs)
    ]
    return pl.pallas_call(
        kernel,
        out_shape=out_shape,
        in_specs=in_specs,
        out_specs=out_specs or ((vmem,) * len(out_shape) if many else vmem),
        scratch_shapes=list(scratch),
        compiler_params=pltpu.CompilerParams(vmem_limit_bytes=VMEM_LIMIT),
        cost_estimate=pl.CostEstimate(flops=flops, bytes_accessed=moved, transcendentals=0),
        name=name,
    )(*operands)


NEAR = pl.BlockSpec(memory_space=pltpu.VMEM)
ANYWHERE = pl.BlockSpec(memory_space=pl.ANY)
FAR = pl.BlockSpec(memory_space=pltpu.HBM)


def head_columns(width):
    depth = width // HEADS
    return [slice(h * depth, (h + 1) * depth) for h in range(HEADS)]


def slot_rows(rows, slots):
    span = rows // slots
    return [slice(s * span, (s + 1) * span) for s in range(slots)]


def row_mean(blocks, width):
    return jnp.sum(sum(blocks[1:], blocks[0]), axis=1, keepdims=True) / width


def slice_kernel(group, block_ref, out_ref, sem):
    rows = out_ref.shape[0]
    start = pl.multiple_of(lax.rem(lax.axis_index("dp"), group) * rows, rows)
    copy = pltpu.make_async_copy(block_ref.at[pl.ds(start, rows)], out_ref, sem)
    copy.start()
    copy.wait()


def prepare_kernel(slots, _, lengths_ref, sibling_ref, *refs):
    inputs, held = refs[:6], refs[6:11]
    (events_t_ref, key_t_ref, value_t_ref, weight_ref, gated_ref, first_ref,
     gate_ref, own_lengths_ref, sems) = refs[11:]
    events_ref, key_ref, value_ref, upstream_ref, _ = held
    copies = [
        pltpu.make_async_copy(source, target, sems.at[i])
        for i, (source, target) in enumerate(zip(inputs, held + (gate_ref,)))
    ]
    copies.append(pltpu.make_async_copy(lengths_ref, own_lengths_ref, sems.at[len(copies)]))
    for copy in copies:
        copy.start()
    rows, width = key_ref.shape
    events_t_ref[:, rows:] = sibling_ref[...].T
    for copy in copies:
        copy.wait()
    events_t_ref[:, :rows] = events_ref[...].T
    key_t_ref[...] = key_ref[...].T
    value_t_ref[...] = value_ref[...].T
    span = rows // slots
    row = lax.broadcasted_iota(jnp.int32, (span, span), 0)
    column = lax.broadcasted_iota(jnp.int32, (span, span), 1)
    first_slot = (lax.axis_index("dp") * lax.axis_size("fsdp") + lax.axis_index("fsdp")) * slots
    for s, place in enumerate(slot_rows(rows, slots)):
        length = own_lengths_ref[first_slot + s]
        inverse = 1.0 / jnp.full((span, span), length, jnp.int32).astype(jnp.float32)
        weight_ref[s] = jnp.where((column <= row) & (row < length), inverse, 0.0)
        live = lax.broadcasted_iota(jnp.int32, (span, width), 0) < length
        gated = upstream_ref[place].astype(jnp.float32) * gate_ref[place].astype(jnp.float32)
        gated = jnp.where(live, gated, 0.0)
        gated_ref[place] = gated
        first = row_mean([gated[:, c] for c in head_columns(width)], width)
        first_ref[place] = jnp.broadcast_to(first, (span, first_ref.shape[1]))


def piece_start(shard_rows, group, part_rows, flips, member_flip):
    device = lax.axis_index("dp")
    start = (
        lax.axis_index("fsdp") ^ jnp.where(lax.rem(device, CORES) == 0, flips[0], flips[1])
    ) * shard_rows
    if member_flip is not None:
        start = start + (lax.rem(device, group) ^ member_flip) * part_rows
    return pl.multiple_of(start, 16)


def attention_kernel(slots, group, origins, *refs):
    pieces = refs[: len(origins)]
    (events_ref, key_ref, value_ref, key_t_ref, value_t_ref, weight_ref, gated_ref, first_ref,
     grad_query_ref, query_ref, normed_ref, mixed_grad_ref, attention_ref, scores_grad_ref,
     projection_ref, sems) = refs[len(origins) :]
    copies = []
    for piece, (flips, members) in zip(pieces, origins):
        rows = piece.shape[0] // len(members)
        for i, member in enumerate(members):
            start = piece_start(pieces[0].shape[0], group, rows, flips, member)
            copies.append(
                pltpu.make_async_copy(
                    piece.at[pl.ds(i * rows, rows)],
                    projection_ref.at[pl.ds(start, rows)],
                    sems.at[len(copies)],
                )
            )
    for copy in copies:
        copy.start()
    for copy in copies:
        copy.wait()
    query_ref[...] = dot(events_ref[...], projection_ref[...]).astype(jnp.bfloat16)

    rows, width = key_ref.shape
    scale = 1.0 / math.sqrt(width // HEADS)
    columns = head_columns(width)
    places = slot_rows(rows, slots)
    each = [(s, h, s * HEADS + h) for s in range(slots) for h in range(HEADS)]
    slopes, mixed, grad_mixed = [], [], []
    for s, h, i in each:
        scores = dot(query_ref[places[s], columns[h]], key_t_ref[columns[h], places[s]]) * scale
        sigmoid = 0.5 * jnp.tanh(0.5 * scores) + 0.5
        silu = scores * sigmoid
        attention_ref[i] = (silu * weight_ref[s]).astype(jnp.bfloat16)
        slopes.append((sigmoid + silu * (1.0 - sigmoid)) * weight_ref[s])
    for s, h, i in each:
        mixed.append(dot(attention_ref[i], value_ref[places[s], columns[h]]))
    for s in range(slots):
        own = mixed[s * HEADS : (s + 1) * HEADS]
        mean = row_mean(own, width)
        centred = [m - mean for m in own]
        inv_std = lax.rsqrt(row_mean([c * c for c in centred], width) + EPSILON)
        normed = [c * inv_std for c in centred]
        gated = [gated_ref[places[s], c] for c in columns]
        second = row_mean([g * n for g, n in zip(gated, normed)], width)
        first = first_ref[places[s]]
        for h in range(HEADS):
            normed_ref[places[s], columns[h]] = normed[h]
            grad = inv_std * (gated[h] - first - normed[h] * second)
            mixed_grad_ref[places[s], columns[h]] = grad.astype(jnp.bfloat16)
    for s, h, i in each:
        grad_attention = dot(
            mixed_grad_ref[places[s], columns[h]], value_t_ref[columns[h], places[s]]
        )
        scores_grad_ref[i] = (grad_attention * slopes[i]).astype(jnp.bfloat16)
    for s, h, i in each:
        grad_query = dot(scores_grad_ref[i], key_ref[places[s], columns[h]]) * scale
        grad_query_ref[places[s], columns[h]] = grad_query.astype(jnp.bfloat16)


def outputs_kernel(slots, _, query_ref, normed_ref, mixed_grad_ref, attention_ref, scores_grad_ref,
                   upstream_ref, grad_key_ref, grad_value_ref, grad_gate_ref):
    rows, width = query_ref.shape
    scale = 1.0 / math.sqrt(width // HEADS)
    columns = head_columns(width)
    places = slot_rows(rows, slots)
    grad_gate_ref[...] = (upstream_ref[...].astype(jnp.float32) * normed_ref[...]).astype(
        jnp.bfloat16
    )
    for s in range(slots):
        for h in range(HEADS):
            i = s * HEADS + h
            grad_value = dot(attention_ref[i], mixed_grad_ref[places[s], columns[h]], FIRST)
            grad_value_ref[places[s], columns[h]] = grad_value.astype(jnp.bfloat16)
            grad_key = dot(scores_grad_ref[i], query_ref[places[s], columns[h]], FIRST) * scale
            grad_key_ref[places[s], columns[h]] = grad_key.astype(jnp.bfloat16)


def add_gradient(picks, events_ref, both_ref, columns, picked_ref, outs, at):
    part_rows = outs[0].shape[0]
    shard_rows = events_ref.shape[0] // lax.axis_size("fsdp")
    chip = lax.div(lax.axis_index("dp"), CORES)
    for i, (k, shard) in enumerate(picks):
        start = pl.multiple_of(shard * shard_rows + (chip ^ k) * part_rows, part_rows)
        picked_ref[i * part_rows : (i + 1) * part_rows] = events_ref[pl.ds(start, part_rows)]
    total = dot(picked_ref[: len(picks) * part_rows], both_ref[:, columns])
    for i, (k, _) in enumerate(picks):
        block = total[i * part_rows : (i + 1) * part_rows]
        outs[k][:, at(i) : at(i) + total.shape[1]] = block.astype(outs[k].dtype)


def summing_core(k):
    return lax.rem(lax.axis_index("dp"), CORES) ^ (1 if k else 0)


def whole_gradient_kernel(pairs, events_ref, own_ref, got_ref, both_ref, *refs):
    outs, picked_ref = refs[:-1], refs[-1]
    rows, width = own_ref.shape
    both_ref[:rows] = own_ref[...]
    both_ref[rows:] = got_ref[...]
    here = lax.axis_index("fsdp")
    for p, flips in enumerate(pairs):
        picks = [
            (k, here ^ jnp.where(summing_core(k) == 0, flips[0], flips[1]))
            for k in range(len(outs))
        ]
        add_gradient(picks, events_ref, both_ref, slice(None), picked_ref, outs,
                     lambda i: p * width)


def half_gradient_kernel(events_ref, both_ref, *refs):
    outs, picked_ref = refs[:-1], refs[-1]
    half = both_ref.shape[1] // CORES
    here = lax.axis_index("fsdp")
    chips = range(len(outs))
    for group in (chips[:1], chips[1:]):
        columns = pl.ds(pl.multiple_of(summing_core(group[0]) * half, half), half)
        picks = [(k, here ^ z) for k in group for z in (0, lax.axis_size("fsdp") // 2)]
        add_gradient(picks, events_ref, both_ref, columns, picked_ref, outs,
                     lambda i: i % 2 * half)


def chip_sum_kernel(term_count, _, *refs):
    terms, outs = refs[:term_count], refs[term_count:]
    at = 0
    for out in outs:
        columns = slice(at, at + out.shape[1])
        total = terms[0][:, columns].astype(jnp.float32)
        for term in terms[1:]:
            total = total + term[:, columns].astype(jnp.float32)
        out[...] = total.astype(out.dtype)
        at += out.shape[1]


def shard_sum_kernel(own_ref, middle_ref, *refs):
    wholes, out_ref, total_ref = refs[:-2], refs[-2], refs[-1]
    total = wholes[0][...].astype(jnp.float32)
    for whole in wholes[1:]:
        total = total + whole[...].astype(jnp.float32)
    total_ref[...] = total
    half = own_ref.shape[1]
    core = lax.rem(lax.axis_index("dp"), CORES)
    columns = pl.ds(pl.multiple_of(core * half, half), half)
    total_ref[:, columns] += own_ref[...]
    columns = pl.ds(pl.multiple_of((1 - core) * half, half), half)
    total_ref[:, columns] += middle_ref[...].astype(jnp.float32)
    out_ref[...] = total_ref[...].astype(out_ref.dtype)


def mean_kernel(count, own_ref, sibling_ref, out_ref):
    total = own_ref[...].astype(jnp.float32) + sibling_ref[...].astype(jnp.float32)
    out_ref[...] = (total / count).astype(out_ref.dtype)


def place_kernel(*refs):
    blocks, (out_ref, held_ref, sems) = refs[:-3], refs[-3:]
    rows = blocks[0].shape[0]
    chip = lax.div(lax.axis_index("dp"), CORES)
    copies = []
    for k, block_ref in enumerate(blocks):
        place = pl.ds(pl.multiple_of((chip ^ k) * rows, rows), rows)
        held_ref[place] = block_ref[...].astype(held_ref.dtype)
        copies.append(pltpu.make_async_copy(held_ref.at[place], out_ref.at[place], sems.at[k]))
        copies[k].start()
    for copy in copies:
        copy.wait()


def flip(block, axis, count, bits):
    return lax.ppermute(block, axis, [(i, i ^ bits) for i in range(count)])


def cross(block, dp_count, fsdp_count, chip_bits, shard_bits):
    pairs = [
        (
            d * fsdp_count + z,
            (d ^ (chip_bits * CORES) ^ 1) * fsdp_count + (z ^ shard_bits[d % CORES]),
        )
        for d in range(dp_count)
        for z in range(fsdp_count)
    ]
    return lax.ppermute(block, BOTH, pairs)


def far_first(count, send):
    return [send(k) for k in range(count - 1, 0, -1)][::-1]


def shard_pairs(fsdp_count):
    others = [d for d in range(1, fsdp_count) if d != fsdp_count // 2]
    return list(zip(others[::2], others[1::2]))


def across_z(weight, dp_count, fsdp_count):
    rows = weight.shape[0]
    group = max(g for g in (2, 4, 8) if dp_count % g == 0 and rows % (16 * g) == 0)
    part = call(
        functools.partial(slice_kernel, group),
        "own_part_of_weight",
        [weight],
        [FAR],
        jax.ShapeDtypeStruct((rows // group, weight.shape[1]), weight.dtype),
        [pltpu.SemaphoreType.DMA],
    )
    weight, part = lax.optimization_barrier((weight, part))
    middle = (fsdp_count // 2,) * CORES
    part = cross(part, dp_count, fsdp_count, 0, middle)
    wholes = [
        (cross(weight, dp_count, fsdp_count, 0, flips), flips[::-1])
        for flips in shard_pairs(fsdp_count)
    ]
    return group, part, wholes


def stack_kernel(*refs):
    out_ref = refs[-1]
    rows = refs[0].shape[0]
    for i, block_ref in enumerate(refs[:-1]):
        out_ref[i * rows : (i + 1) * rows] = block_ref[...]


def share(group, part, wholes, ready, dp_count, fsdp_count):
    alike = (0,) * CORES
    parts, members = [part], [1]
    for chip_bits in range(1, group // CORES):
        parts.append(cross(part, dp_count, fsdp_count, chip_bits, alike))
        members.append(CORES * chip_bits)
    if len(parts) > 1:
        rows, columns = part.shape
        part = call(
            stack_kernel,
            "parts_of_weight",
            parts,
            [NEAR] * len(parts),
            jax.ShapeDtypeStruct((len(parts) * rows, columns), part.dtype),
        )
    held = [(part, (fsdp_count // 2,) * CORES, members)]
    for block, flips in wholes:
        held.append((lax.optimization_barrier((block, part, ready))[0], flips, [None]))
    found = []
    for block, flips, members in held:
        moved = [m if m is None else m ^ 1 for m in members]
        found.append((block, (flips, members)))
        found.append((flip(block, "dp", dp_count, 1), (flips[::-1], moved)))
    return found


def shards(events, query_weight, keys, values, gates, cotangent, lengths):
    slots, span, model_width = events.shape
    width = query_weight.shape[1]
    half_width = width // CORES
    rows = slots * span
    dp_count, fsdp_count = lax.axis_size("dp"), lax.axis_size("fsdp")
    chips = dp_count // CORES
    shard_rows = model_width // fsdp_count
    total_seqs = slots * dp_count * fsdp_count
    bf16, f32 = jnp.bfloat16, jnp.float32

    def shape(*dims, dtype=bf16):
        return jax.ShapeDtypeStruct(dims, dtype)

    flat_events = events.reshape(rows, model_width)
    keys, values, gates, cotangent = (
        a.reshape(rows, width) for a in (keys, values, gates, cotangent)
    )
    sibling_events = flip(flat_events, "dp", dp_count, 1)
    group, part, wholes = across_z(query_weight, dp_count, fsdp_count)
    prepared = call(
        functools.partial(prepare_kernel, slots),
        "prepared_operands",
        [part, lengths, sibling_events]
        + [flat_events, keys, values, cotangent, query_weight, gates],
        [ANYWHERE, FAR, NEAR] + [FAR] * 6,
        (
            shape(rows, model_width),
            shape(rows, width),
            shape(rows, width),
            shape(rows, width),
            shape(shard_rows, width),
            shape(model_width, CORES * rows),
            shape(width, rows),
            shape(width, rows),
            shape(slots, span, span, dtype=f32),
            shape(rows, width, dtype=f32),
            shape(rows, span, dtype=f32),
        ),
        [
            pltpu.VMEM((rows, width), bf16),
            pltpu.SMEM(lengths.shape, jnp.int32),
            pltpu.SemaphoreType.DMA((7,)),
        ],
        flops=22 * 10**8,
    )
    near_events, near_keys, near_values, near_cotangent, near_weight = prepared[:5]
    events_t, keys_t, values_t, weight, gated, first = prepared[5:]
    found = [(near_weight, ((0, 0), [None]))]
    found += share(group, part, wholes, first, dp_count, fsdp_count)
    pieces, origins = zip(*found)
    blocks = shape(slots * HEADS, span, span)
    grad_query, query, normed, grad_mixed, attention, grad_scores = call(
        functools.partial(attention_kernel, slots, group, origins),
        "attention_to_grad_query",
        list(pieces)
        + [near_events, near_keys, near_values, keys_t, values_t, weight, gated, first],
        [ANYWHERE] * len(pieces) + [NEAR] * 8,
        (
            shape(rows, width),
            shape(rows, width),
            shape(rows, width, dtype=f32),
            shape(rows, width),
            blocks,
            blocks,
        ),
        [
            pltpu.VMEM((model_width, width), bf16),
            pltpu.SemaphoreType.DMA((sum(len(members) for _, members in origins),)),
        ],
        flops=2 * rows * width * (model_width + 4 * span),
        moved=24 * rows * width,
    )
    part_rows = shard_rows // chips
    staged = part_rows % 16 == 0 and fsdp_count % 4 == 0
    terms = [grad_query]
    if staged:
        pairs = shard_pairs(fsdp_count)
        got = flip(grad_query, "dp", dp_count, 1)
        picked = pltpu.VMEM((2 * chips * part_rows, CORES * rows), bf16)

        def for_chips(columns):
            return tuple(shape(part_rows, columns, dtype=bf16 if k else f32) for k in range(chips))

        both, *whole_terms = call(
            functools.partial(whole_gradient_kernel, pairs),
            "weight_gradient_of_whole_shards",
            [events_t, grad_query, got],
            [NEAR] * 3,
            (shape(CORES * rows, width),) + for_chips(len(pairs) * width),
            [picked],
            flops=4 * rows * shard_rows * len(pairs) * width,
            moved=2 * model_width * (rows + width),
        )
        terms = call(
            half_gradient_kernel,
            "weight_gradient_of_halves",
            [events_t, both],
            [NEAR] * 2,
            for_chips(2 * half_width),
            [picked],
            flops=4 * rows * shard_rows * width,
            moved=2 * model_width * (rows + width),
        )
    grad_keys, grad_values, grad_gates = call(
        functools.partial(outputs_kernel, slots),
        "key_value_gate_gradients",
        [terms[0], query, normed, grad_mixed, attention, grad_scores, near_cotangent],
        [ANYWHERE] + [NEAR] * 6,
        (shape(rows, width),) * 3,
        flops=4 * rows * width * span,
        moved=12 * rows * width,
    )
    if staged:
        alike = (0,) * CORES

        def to_chip(block, k):
            return cross(block, dp_count, fsdp_count, k, alike)

        whole_terms[1:] = far_first(chips, lambda k: to_chip(whole_terms[k], k))
        wholes = call(
            functools.partial(chip_sum_kernel, chips),
            "sum_of_whole_shards_over_chips",
            [both] + whole_terms,
            [ANYWHERE] + [NEAR] * chips,
            (shape(part_rows, width),) * len(pairs),
        )
        wholes = [cross(a, dp_count, fsdp_count, 0, p) for a, p in zip(wholes, pairs)]
        terms = [terms[0]] + far_first(chips, lambda k: to_chip(terms[k], k))
        own_half, middle = call(
            functools.partial(chip_sum_kernel, chips),
            "sum_of_halves_over_chips",
            [grad_keys] + terms,
            [FAR] + [NEAR] * chips,
            (shape(part_rows, half_width, dtype=f32), shape(part_rows, half_width)),
        )
        middle = cross(middle, dp_count, fsdp_count, 0, (fsdp_count // 2,) * CORES)
        total = call(
            shard_sum_kernel,
            "sum_over_shards",
            [own_half, middle] + wholes,
            [NEAR] * (2 + len(wholes)),
            shape(part_rows, width),
            [pltpu.VMEM((part_rows, width), f32)],
        )
        mean = call(
            functools.partial(mean_kernel, total_seqs),
            "mean_of_both_cores",
            [total, flip(total, "dp", dp_count, 1)],
            [NEAR] * 2,
            shape(part_rows, width),
        )
        found = [mean] + far_first(chips, lambda k: to_chip(mean, k))
        grad_weight = call(
            place_kernel,
            "blocks_in_place",
            found,
            [NEAR] * chips,
            shape(shard_rows, width, dtype=f32),
            [pltpu.VMEM((shard_rows, width), f32), pltpu.SemaphoreType.DMA((chips,))],
            out_specs=FAR,
        )
    else:
        whole = lax.dot_general(flat_events, grad_query, FIRST, preferred_element_type=f32)
        mine = lax.psum_scatter(whole, "fsdp", scatter_dimension=0, tiled=True)
        grad_weight = lax.psum(mine, "dp") / total_seqs

    full = (slots, span, width)
    return (
        grad_keys.reshape(full),
        grad_values.reshape(full),
        grad_gates.reshape(full),
        grad_weight,
    )


def solution(mesh):
    split = P(BOTH, None, None)
    return jax.shard_map(
        shards,
        mesh=mesh,
        in_specs=(split, P("fsdp", None), split, split, split, split, P()),
        out_specs=(split, split, split, P("fsdp", None)),
        check_vma=False,
    )
```

```python
import functools
import math

import jax
import jax.numpy as jnp
from jax import lax
from jax.experimental import pallas as pl
from jax.experimental.pallas import tpu as pltpu
from jax.sharding import PartitionSpec as P

HEADS = 4
EPSILON = 1e-06
CORES = 2
BOTH = ("dp", "fsdp")
VMEM_LIMIT = 24 * 1024 * 1024

LAST = (((1,), (1,)), ((), ()))
FIRST = (((0,), (0,)), ((), ()))


def dot(lhs, rhs, dims=(((1,), (0,)), ((), ()))):
    return lax.dot_general(lhs, rhs, dims, preferred_element_type=jnp.float32)


def call(kernel, name, operands, in_specs, out_shape, scratch=(), flops=0, moved=0,
         out_specs=None):
    vmem = pl.BlockSpec(memory_space=pltpu.VMEM)
    many = isinstance(out_shape, tuple)
    operands = [
        pltpu.with_memory_space_constraint(a, pltpu.HBM) if spec is FAR else a
        for a, spec in zip(operands, in_specs)
    ]
    return pl.pallas_call(
        kernel,
        out_shape=out_shape,
        in_specs=in_specs,
        out_specs=out_specs or ((vmem,) * len(out_shape) if many else vmem),
        scratch_shapes=list(scratch),
        compiler_params=pltpu.CompilerParams(vmem_limit_bytes=VMEM_LIMIT),
        cost_estimate=pl.CostEstimate(flops=flops, bytes_accessed=moved, transcendentals=0),
        name=name,
    )(*operands)


NEAR = pl.BlockSpec(memory_space=pltpu.VMEM)
ANYWHERE = pl.BlockSpec(memory_space=pl.ANY)
FAR = pl.BlockSpec(memory_space=pltpu.HBM)


def head_columns(width):
    depth = width // HEADS
    return [slice(h * depth, (h + 1) * depth) for h in range(HEADS)]


def slot_rows(rows, slots):
    span = rows // slots
    return [slice(s * span, (s + 1) * span) for s in range(slots)]


def row_mean(blocks, width):
    return jnp.sum(sum(blocks[1:], blocks[0]), axis=1, keepdims=True) / width


def slice_kernel(group, block_ref, out_ref, sem):
    rows = out_ref.shape[0]
    start = pl.multiple_of(lax.rem(lax.axis_index("dp"), group) * rows, rows)
    copy = pltpu.make_async_copy(block_ref.at[pl.ds(start, rows)], out_ref, sem)
    copy.start()
    copy.wait()


def prepare_kernel(slots, lengths_ref, sibling_ref, *refs):
    inputs, held = refs[:6], refs[6:11]
    (events_t_ref, key_t_ref, value_t_ref, weight_ref, gated_ref, first_ref,
     gate_ref, own_lengths_ref, sems) = refs[11:]
    events_ref, key_ref, value_ref, upstream_ref, _ = held
    copies = [
        pltpu.make_async_copy(source, target, sems.at[i])
        for i, (source, target) in enumerate(zip(inputs, held + (gate_ref,)))
    ]
    copies.append(pltpu.make_async_copy(lengths_ref, own_lengths_ref, sems.at[len(copies)]))
    for copy in copies:
        copy.start()
    rows, width = key_ref.shape
    events_t_ref[:, rows:] = sibling_ref[...].T
    for copy in copies:
        copy.wait()
    events_t_ref[:, :rows] = events_ref[...].T
    key_t_ref[...] = key_ref[...].T
    value_t_ref[...] = value_ref[...].T
    span = rows // slots
    row = lax.broadcasted_iota(jnp.int32, (span, span), 0)
    column = lax.broadcasted_iota(jnp.int32, (span, span), 1)
    first_slot = (lax.axis_index("dp") * lax.axis_size("fsdp") + lax.axis_index("fsdp")) * slots
    for s, place in enumerate(slot_rows(rows, slots)):
        length = own_lengths_ref[first_slot + s]
        inverse = 1.0 / jnp.full((span, span), length, jnp.int32).astype(jnp.float32)
        weight_ref[s] = jnp.where((column <= row) & (row < length), inverse, 0.0)
        live = lax.broadcasted_iota(jnp.int32, (span, width), 0) < length
        gated = upstream_ref[place].astype(jnp.float32) * gate_ref[place].astype(jnp.float32)
        gated = jnp.where(live, gated, 0.0)
        gated_ref[place] = gated
        first = row_mean([gated[:, c] for c in head_columns(width)], width)
        first_ref[place] = jnp.broadcast_to(first, (span, first_ref.shape[1]))


def piece_start(shard_rows, group, part_rows, flips, member_flip):
    device = lax.axis_index("dp")
    start = (
        lax.axis_index("fsdp") ^ jnp.where(lax.rem(device, CORES) == 0, flips[0], flips[1])
    ) * shard_rows
    if member_flip is not None:
        start = start + (lax.rem(device, group) ^ member_flip) * part_rows
    return pl.multiple_of(start, 16)


def attention_kernel(slots, group, origins, *refs):
    pieces = refs[: len(origins)]
    (events_ref, key_ref, value_ref, key_t_ref, value_t_ref, weight_ref, gated_ref, first_ref,
     grad_query_ref, query_ref, normed_ref, mixed_grad_ref, attention_ref, scores_grad_ref,
     projection_ref, sems) = refs[len(origins) :]
    copies = []
    for piece, (flips, members) in zip(pieces, origins):
        rows = piece.shape[0] // len(members)
        for i, member in enumerate(members):
            start = piece_start(pieces[0].shape[0], group, rows, flips, member)
            copies.append(
                pltpu.make_async_copy(
                    piece.at[pl.ds(i * rows, rows)],
                    projection_ref.at[pl.ds(start, rows)],
                    sems.at[len(copies)],
                )
            )
    for copy in copies:
        copy.start()
    for copy in copies:
        copy.wait()
    query_ref[...] = dot(events_ref[...], projection_ref[...]).astype(jnp.bfloat16)

    rows, width = key_ref.shape
    scale = 1.0 / math.sqrt(width // HEADS)
    columns = head_columns(width)
    places = slot_rows(rows, slots)
    each = [(s, h, s * HEADS + h) for s in range(slots) for h in range(HEADS)]
    slopes, mixed, grad_mixed = [], [], []
    for s, h, i in each:
        scores = dot(query_ref[places[s], columns[h]], key_t_ref[columns[h], places[s]]) * scale
        sigmoid = 0.5 * jnp.tanh(0.5 * scores) + 0.5
        silu = scores * sigmoid
        attention_ref[i] = (silu * weight_ref[s]).astype(jnp.bfloat16)
        slopes.append((sigmoid + silu * (1.0 - sigmoid)) * weight_ref[s])
    for s, h, i in each:
        mixed.append(dot(attention_ref[i], value_ref[places[s], columns[h]]))
    for s in range(slots):
        own = mixed[s * HEADS : (s + 1) * HEADS]
        mean = row_mean(own, width)
        centred = [m - mean for m in own]
        inv_std = lax.rsqrt(row_mean([c * c for c in centred], width) + EPSILON)
        normed = [c * inv_std for c in centred]
        gated = [gated_ref[places[s], c] for c in columns]
        second = row_mean([g * n for g, n in zip(gated, normed)], width)
        first = first_ref[places[s]]
        for h in range(HEADS):
            normed_ref[places[s], columns[h]] = normed[h]
            grad = inv_std * (gated[h] - first - normed[h] * second)
            mixed_grad_ref[places[s], columns[h]] = grad.astype(jnp.bfloat16)
    for s, h, i in each:
        grad_attention = dot(
            mixed_grad_ref[places[s], columns[h]], value_t_ref[columns[h], places[s]]
        )
        scores_grad_ref[i] = (grad_attention * slopes[i]).astype(jnp.bfloat16)
    for s, h, i in each:
        grad_query = dot(scores_grad_ref[i], key_ref[places[s], columns[h]]) * scale
        grad_query_ref[places[s], columns[h]] = grad_query.astype(jnp.bfloat16)


def outputs_kernel(slots, _, query_ref, normed_ref, mixed_grad_ref, attention_ref, scores_grad_ref,
                   upstream_ref, grad_key_ref, grad_value_ref, grad_gate_ref):
    rows, width = query_ref.shape
    scale = 1.0 / math.sqrt(width // HEADS)
    columns = head_columns(width)
    places = slot_rows(rows, slots)
    grad_gate_ref[...] = (upstream_ref[...].astype(jnp.float32) * normed_ref[...]).astype(
        jnp.bfloat16
    )
    for s in range(slots):
        for h in range(HEADS):
            i = s * HEADS + h
            grad_value = dot(attention_ref[i], mixed_grad_ref[places[s], columns[h]], FIRST)
            grad_value_ref[places[s], columns[h]] = grad_value.astype(jnp.bfloat16)
            grad_key = dot(scores_grad_ref[i], query_ref[places[s], columns[h]], FIRST) * scale
            grad_key_ref[places[s], columns[h]] = grad_key.astype(jnp.bfloat16)


def gradient_rows(picks, part_rows, events_ref, both_ref, columns, picked_ref):
    shard_rows = events_ref.shape[0] // lax.axis_size("fsdp")
    chip = lax.div(lax.axis_index("dp"), CORES)
    for i, (k, shard) in enumerate(picks):
        start = pl.multiple_of(shard * shard_rows + (chip ^ k) * part_rows, part_rows)
        picked_ref[i * part_rows : (i + 1) * part_rows] = events_ref[pl.ds(start, part_rows)]
    total = dot(picked_ref[: len(picks) * part_rows], both_ref[:, columns])
    return [total[i * part_rows : (i + 1) * part_rows] for i in range(len(picks))]


def summing_core(k):
    return lax.rem(lax.axis_index("dp"), CORES) ^ (1 if k else 0)


def half_gradient(shard, core_flip, events_ref, both_ref, out_ref, picked_ref):
    chips, part_rows, half = out_ref.shape
    for group in (range(1), range(1, chips)):
        core = summing_core(group[0]) ^ core_flip
        columns = pl.ds(pl.multiple_of(core * half, half), half)
        picks = [(k, shard) for k in group]
        blocks = gradient_rows(picks, part_rows, events_ref, both_ref, columns, picked_ref)
        for k, block in zip(group, blocks):
            out_ref[k] = block.astype(out_ref.dtype)


def middle_gradient_kernel(events_ref, own_ref, got_ref, both_ref, out_ref, picked_ref):
    rows = own_ref.shape[0]
    both_ref[:rows] = own_ref[...]
    both_ref[rows:] = got_ref[...]
    shard = lax.axis_index("fsdp") ^ (lax.axis_size("fsdp") // 2)
    half_gradient(shard, 1, events_ref, both_ref, out_ref, picked_ref)


def own_gradient_kernel(events_ref, both_ref, out_ref, picked_ref):
    half_gradient(lax.axis_index("fsdp"), 0, events_ref, both_ref, out_ref, picked_ref)


def whole_gradient_kernel(pairs, events_ref, both_ref, *refs):
    outs, picked_ref = refs[:-1], refs[-1]
    width = both_ref.shape[1]
    here = lax.axis_index("fsdp")
    for p, flips in enumerate(pairs):
        picks = [
            (k, here ^ jnp.where(summing_core(k) == 0, flips[0], flips[1]))
            for k in range(len(outs))
        ]
        part_rows = outs[0].shape[0]
        blocks = gradient_rows(picks, part_rows, events_ref, both_ref, slice(None), picked_ref)
        for out, block in zip(outs, blocks):
            out[:, p * width : (p + 1) * width] = block.astype(out.dtype)


def with_middle_kernel(_, own_ref, middle_ref, *outs):
    for k, out in enumerate(outs):
        total = own_ref[k] + middle_ref[k].astype(jnp.float32)
        out[...] = total.astype(out.dtype)


def chip_sum_kernel(term_count, *refs):
    terms, outs = refs[:term_count], refs[term_count:]
    at = 0
    for out in outs:
        columns = slice(at, at + out.shape[1])
        total = terms[0][:, columns].astype(jnp.float32)
        for term in terms[1:]:
            total = total + term[:, columns].astype(jnp.float32)
        out[...] = total.astype(out.dtype)
        at += out.shape[1]


def shard_sum_kernel(chips, *refs):
    halves, wholes, (out_ref, total_ref) = refs[:chips], refs[chips:-2], refs[-2:]
    total = wholes[0][...].astype(jnp.float32)
    for whole in wholes[1:]:
        total = total + whole[...].astype(jnp.float32)
    total_ref[...] = total
    half = halves[0].shape[1]
    core = lax.rem(lax.axis_index("dp"), CORES)
    columns = pl.ds(pl.multiple_of(core * half, half), half)
    own = halves[0][...]
    for term in halves[1:]:
        own = own + term[...].astype(jnp.float32)
    total_ref[:, columns] += own
    out_ref[...] = total_ref[...].astype(out_ref.dtype)


def mean_kernel(count, own_ref, sibling_ref, out_ref):
    total = own_ref[...].astype(jnp.float32) + sibling_ref[...].astype(jnp.float32)
    out_ref[...] = (total / count).astype(out_ref.dtype)


def place_kernel(*refs):
    blocks, (out_ref, held_ref, sems) = refs[:-3], refs[-3:]
    rows = blocks[0].shape[0]
    chip = lax.div(lax.axis_index("dp"), CORES)
    copies = []
    for k, block_ref in enumerate(blocks):
        place = pl.ds(pl.multiple_of((chip ^ k) * rows, rows), rows)
        held_ref[place] = block_ref[...].astype(held_ref.dtype)
        copies.append(pltpu.make_async_copy(held_ref.at[place], out_ref.at[place], sems.at[k]))
        copies[k].start()
    for copy in copies:
        copy.wait()


def flip(block, axis, count, bits):
    return lax.ppermute(block, axis, [(i, i ^ bits) for i in range(count)])


def cross(block, dp_count, fsdp_count, chip_bits, shard_bits):
    pairs = [
        (
            d * fsdp_count + z,
            (d ^ (chip_bits * CORES) ^ 1) * fsdp_count + (z ^ shard_bits[d % CORES]),
        )
        for d in range(dp_count)
        for z in range(fsdp_count)
    ]
    return lax.ppermute(block, BOTH, pairs)


def far_first(count, send):
    return [send(k) for k in range(count - 1, 0, -1)][::-1]


def shard_pairs(fsdp_count):
    others = [d for d in range(1, fsdp_count) if d != fsdp_count // 2]
    return list(zip(others[::2], others[1::2]))


def across_z(weight, dp_count, fsdp_count):
    rows = weight.shape[0]
    group = max(g for g in (2, 4, 8) if dp_count % g == 0 and rows % (16 * g) == 0)
    part = call(
        functools.partial(slice_kernel, group),
        "own_part_of_weight",
        [weight],
        [FAR],
        jax.ShapeDtypeStruct((rows // group, weight.shape[1]), weight.dtype),
        [pltpu.SemaphoreType.DMA],
    )
    weight, part = lax.optimization_barrier((weight, part))
    middle = (fsdp_count // 2,) * CORES
    part = cross(part, dp_count, fsdp_count, 0, middle)
    wholes = [
        (cross(weight, dp_count, fsdp_count, 0, flips), flips[::-1])
        for flips in shard_pairs(fsdp_count)
    ]
    return group, part, wholes


def stack_kernel(*refs):
    out_ref = refs[-1]
    rows = refs[0].shape[0]
    for i, block_ref in enumerate(refs[:-1]):
        out_ref[i * rows : (i + 1) * rows] = block_ref[...]


def share(group, part, wholes, ready, dp_count, fsdp_count):
    alike = (0,) * CORES
    part, ready = lax.optimization_barrier((part, ready))
    parts, members = [part], [1]
    for chip_bits in range(1, group // CORES):
        parts.append(cross(part, dp_count, fsdp_count, chip_bits, alike))
        members.append(CORES * chip_bits)
    if len(parts) > 1:
        rows, columns = part.shape
        part = call(
            stack_kernel,
            "parts_of_weight",
            parts,
            [NEAR] * len(parts),
            jax.ShapeDtypeStruct((len(parts) * rows, columns), part.dtype),
        )
    held = [(part, (fsdp_count // 2,) * CORES, members)]
    for block, flips in wholes:
        held.append((lax.optimization_barrier((block, part))[0], flips, [None]))
    found = []
    for block, flips, members in held:
        moved = [m if m is None else m ^ 1 for m in members]
        found.append((block, (flips, members)))
        found.append((flip(block, "dp", dp_count, 1), (flips[::-1], moved)))
    return found


def shards(events, query_weight, keys, values, gates, cotangent, lengths):
    slots, span, model_width = events.shape
    width = query_weight.shape[1]
    half_width = width // CORES
    rows = slots * span
    dp_count, fsdp_count = lax.axis_size("dp"), lax.axis_size("fsdp")
    chips = dp_count // CORES
    shard_rows = model_width // fsdp_count
    total_seqs = slots * dp_count * fsdp_count
    bf16, f32 = jnp.bfloat16, jnp.float32

    def shape(*dims, dtype=bf16):
        return jax.ShapeDtypeStruct(dims, dtype)

    flat_events = events.reshape(rows, model_width)
    keys, values, gates, cotangent = (
        a.reshape(rows, width) for a in (keys, values, gates, cotangent)
    )
    sibling_events = flip(flat_events, "dp", dp_count, 1)
    group, part, wholes = across_z(query_weight, dp_count, fsdp_count)
    prepared = call(
        functools.partial(prepare_kernel, slots),
        "prepared_operands",
        [lengths, sibling_events]
        + [flat_events, keys, values, cotangent, query_weight, gates],
        [FAR, NEAR] + [FAR] * 6,
        (
            shape(rows, model_width),
            shape(rows, width),
            shape(rows, width),
            shape(rows, width),
            shape(shard_rows, width),
            shape(model_width, CORES * rows),
            shape(width, rows),
            shape(width, rows),
            shape(slots, span, span, dtype=f32),
            shape(rows, width, dtype=f32),
            shape(rows, span, dtype=f32),
        ),
        [
            pltpu.VMEM((rows, width), bf16),
            pltpu.SMEM(lengths.shape, jnp.int32),
            pltpu.SemaphoreType.DMA((7,)),
        ],
        flops=5 * 10**9,
    )
    near_events, near_keys, near_values, near_cotangent, near_weight = prepared[:5]
    events_t, keys_t, values_t, weight, gated, first = prepared[5:]
    found = [(near_weight, ((0, 0), [None]))]
    found += share(group, part, wholes, first, dp_count, fsdp_count)
    pieces, origins = zip(*found)
    blocks = shape(slots * HEADS, span, span)
    grad_query, query, normed, grad_mixed, attention, grad_scores = call(
        functools.partial(attention_kernel, slots, group, origins),
        "attention_to_grad_query",
        list(pieces)
        + [near_events, near_keys, near_values, keys_t, values_t, weight, gated, first],
        [ANYWHERE] * len(pieces) + [NEAR] * 8,
        (
            shape(rows, width),
            shape(rows, width),
            shape(rows, width, dtype=f32),
            shape(rows, width),
            blocks,
            blocks,
        ),
        [
            pltpu.VMEM((model_width, width), bf16),
            pltpu.SemaphoreType.DMA((sum(len(members) for _, members in origins),)),
        ],
        flops=2 * rows * width * (model_width + 4 * span),
        moved=24 * rows * width,
    )
    part_rows = shard_rows // chips
    staged = part_rows % 16 == 0 and fsdp_count % 4 == 0
    terms = [grad_query]
    if staged:
        pairs = shard_pairs(fsdp_count)
        got = flip(grad_query, "dp", dp_count, 1)
        picked = pltpu.VMEM((chips * part_rows, CORES * rows), bf16)
        halves = (chips, part_rows, half_width)
        work = dict(
            flops=4 * rows * shard_rows * half_width,
            moved=2 * (shard_rows + half_width) * CORES * rows,
        )
        both, middle = call(
            middle_gradient_kernel,
            "weight_gradient_of_middle_shard",
            [events_t, grad_query, got],
            [NEAR] * 3,
            (shape(CORES * rows, width), shape(*halves)),
            [picked],
            **work,
        )
        middle = cross(middle, dp_count, fsdp_count, 0, (fsdp_count // 2,) * CORES)
        whole_terms = call(
            functools.partial(whole_gradient_kernel, pairs),
            "weight_gradient_of_whole_shards",
            [events_t, both],
            [NEAR] * 2,
            tuple(
                shape(part_rows, len(pairs) * width, dtype=bf16 if k else f32)
                for k in range(chips)
            ),
            [picked],
            **work,
        )
        terms = call(
            own_gradient_kernel,
            "weight_gradient_of_own_shard",
            [events_t, both],
            [NEAR] * 2,
            shape(*halves, dtype=f32),
            [picked],
            **work,
        )
        terms = [terms]
    grad_keys, grad_values, grad_gates = call(
        functools.partial(outputs_kernel, slots),
        "key_value_gate_gradients",
        [terms[0], query, normed, grad_mixed, attention, grad_scores, near_cotangent],
        [ANYWHERE] + [NEAR] * 6,
        (shape(rows, width),) * 3,
        flops=4 * rows * width * span,
        moved=12 * rows * width,
    )
    if staged:
        alike = (0,) * CORES

        def to_chip(block, k):
            return cross(block, dp_count, fsdp_count, k, alike)

        whole_terms = [whole_terms[0]] + far_first(chips, lambda k: to_chip(whole_terms[k], k))
        wholes = call(
            functools.partial(chip_sum_kernel, chips),
            "sum_of_whole_shards_over_chips",
            whole_terms,
            [NEAR] * chips,
            (shape(part_rows, width),) * len(pairs),
        )
        wholes = [cross(a, dp_count, fsdp_count, 0, p) for a, p in zip(wholes, pairs)]
        terms = call(
            with_middle_kernel,
            "own_and_middle_shard",
            [grad_keys, terms[0], middle],
            [FAR] + [NEAR] * 2,
            tuple(shape(part_rows, half_width, dtype=bf16 if k else f32) for k in range(chips)),
        )
        terms = [terms[0]] + far_first(chips, lambda k: to_chip(terms[k], k))
        total = call(
            functools.partial(shard_sum_kernel, chips),
            "sum_over_shards",
            terms + wholes,
            [NEAR] * (chips + len(wholes)),
            shape(part_rows, width),
            [pltpu.VMEM((part_rows, width), f32)],
        )
        mean = call(
            functools.partial(mean_kernel, total_seqs),
            "mean_of_both_cores",
            [total, flip(total, "dp", dp_count, 1)],
            [NEAR] * 2,
            shape(part_rows, width),
        )
        found = [mean] + far_first(chips, lambda k: to_chip(mean, k))
        grad_weight = call(
            place_kernel,
            "blocks_in_place",
            found,
            [NEAR] * chips,
            shape(shard_rows, width, dtype=f32),
            [pltpu.VMEM((shard_rows, width), f32), pltpu.SemaphoreType.DMA((chips,))],
            out_specs=FAR,
        )
    else:
        whole = lax.dot_general(flat_events, grad_query, FIRST, preferred_element_type=f32)
        mine = lax.psum_scatter(whole, "fsdp", scatter_dimension=0, tiled=True)
        grad_weight = lax.psum(mine, "dp") / total_seqs

    full = (slots, span, width)
    return (
        grad_keys.reshape(full),
        grad_values.reshape(full),
        grad_gates.reshape(full),
        grad_weight,
    )


def solution(mesh):
    split = P(BOTH, None, None)
    return jax.shard_map(
        shards,
        mesh=mesh,
        in_specs=(split, P("fsdp", None), split, split, split, split, P()),
        out_specs=(split, split, split, P("fsdp", None)),
        check_vma=False,
    )
```

```python
import functools
import math

import jax
import jax.numpy as jnp
from jax import lax
from jax.experimental import pallas as pl
from jax.experimental.pallas import tpu as pltpu
from jax.sharding import PartitionSpec as P

HEADS = 4
EPSILON = 1e-06
CORES = 2
BOTH = ("dp", "fsdp")
VMEM_LIMIT = 24 * 1024 * 1024

LAST = (((1,), (1,)), ((), ()))
FIRST = (((0,), (0,)), ((), ()))


def dot(lhs, rhs, dims=(((1,), (0,)), ((), ()))):
    return lax.dot_general(lhs, rhs, dims, preferred_element_type=jnp.float32)


def call(kernel, name, operands, in_specs, out_shape, scratch=(), flops=0, moved=0,
         out_specs=None):
    vmem = pl.BlockSpec(memory_space=pltpu.VMEM)
    many = isinstance(out_shape, tuple)
    operands = [
        pltpu.with_memory_space_constraint(a, pltpu.HBM) if spec is FAR else a
        for a, spec in zip(operands, in_specs)
    ]
    return pl.pallas_call(
        kernel,
        out_shape=out_shape,
        in_specs=in_specs,
        out_specs=out_specs or ((vmem,) * len(out_shape) if many else vmem),
        scratch_shapes=list(scratch),
        compiler_params=pltpu.CompilerParams(vmem_limit_bytes=VMEM_LIMIT),
        cost_estimate=pl.CostEstimate(flops=flops, bytes_accessed=moved, transcendentals=0),
        name=name,
    )(*operands)


NEAR = pl.BlockSpec(memory_space=pltpu.VMEM)
ANYWHERE = pl.BlockSpec(memory_space=pl.ANY)
FAR = pl.BlockSpec(memory_space=pltpu.HBM)


def head_columns(width):
    depth = width // HEADS
    return [slice(h * depth, (h + 1) * depth) for h in range(HEADS)]


def slot_rows(rows, slots):
    span = rows // slots
    return [slice(s * span, (s + 1) * span) for s in range(slots)]


def row_mean(blocks, width):
    return jnp.sum(sum(blocks[1:], blocks[0]), axis=1, keepdims=True) / width


def slice_kernel(group, block_ref, out_ref, sem):
    rows = out_ref.shape[0]
    start = pl.multiple_of(lax.rem(lax.axis_index("dp"), group) * rows, rows)
    copy = pltpu.make_async_copy(block_ref.at[pl.ds(start, rows)], out_ref, sem)
    copy.start()
    copy.wait()


def prepare_kernel(slots, lengths_ref, sibling_ref, *refs):
    inputs, held = refs[:6], refs[6:11]
    (events_t_ref, key_t_ref, value_t_ref, weight_ref, gated_ref, first_ref,
     gate_ref, own_lengths_ref, sems) = refs[11:]
    events_ref, key_ref, value_ref, upstream_ref, _ = held
    copies = [
        pltpu.make_async_copy(source, target, sems.at[i])
        for i, (source, target) in enumerate(zip(inputs, held + (gate_ref,)))
    ]
    copies.append(pltpu.make_async_copy(lengths_ref, own_lengths_ref, sems.at[len(copies)]))
    for copy in copies:
        copy.start()
    rows, width = key_ref.shape
    events_t_ref[:, rows:] = sibling_ref[...].T
    for copy in copies:
        copy.wait()
    events_t_ref[:, :rows] = events_ref[...].T
    key_t_ref[...] = key_ref[...].T
    value_t_ref[...] = value_ref[...].T
    span = rows // slots
    row = lax.broadcasted_iota(jnp.int32, (span, span), 0)
    column = lax.broadcasted_iota(jnp.int32, (span, span), 1)
    first_slot = (lax.axis_index("dp") * lax.axis_size("fsdp") + lax.axis_index("fsdp")) * slots
    for s, place in enumerate(slot_rows(rows, slots)):
        length = own_lengths_ref[first_slot + s]
        inverse = 1.0 / jnp.full((span, span), length, jnp.int32).astype(jnp.float32)
        weight_ref[s] = jnp.where((column <= row) & (row < length), inverse, 0.0)
        live = lax.broadcasted_iota(jnp.int32, (span, width), 0) < length
        gated = upstream_ref[place].astype(jnp.float32) * gate_ref[place].astype(jnp.float32)
        gated = jnp.where(live, gated, 0.0)
        gated_ref[place] = gated
        first = row_mean([gated[:, c] for c in head_columns(width)], width)
        first_ref[place] = jnp.broadcast_to(first, (span, first_ref.shape[1]))


def piece_start(shard_rows, group, part_rows, flips, member_flip):
    device = lax.axis_index("dp")
    start = (
        lax.axis_index("fsdp") ^ jnp.where(lax.rem(device, CORES) == 0, flips[0], flips[1])
    ) * shard_rows
    if member_flip is not None:
        start = start + (lax.rem(device, group) ^ member_flip) * part_rows
    return pl.multiple_of(start, 16)


def attention_kernel(slots, group, origins, *refs):
    pieces = refs[: len(origins)]
    (events_ref, key_ref, value_ref, key_t_ref, value_t_ref, weight_ref, gated_ref, first_ref,
     grad_query_ref, query_ref, normed_ref, mixed_grad_ref, attention_ref, scores_grad_ref,
     projection_ref, sems) = refs[len(origins) :]
    copies = []
    for piece, (flips, members) in zip(pieces, origins):
        rows = piece.shape[0] // len(members)
        for i, member in enumerate(members):
            start = piece_start(pieces[0].shape[0], group, rows, flips, member)
            copies.append(
                pltpu.make_async_copy(
                    piece.at[pl.ds(i * rows, rows)],
                    projection_ref.at[pl.ds(start, rows)],
                    sems.at[len(copies)],
                )
            )
    for copy in copies:
        copy.start()
    for copy in copies:
        copy.wait()
    query_ref[...] = dot(events_ref[...], projection_ref[...]).astype(jnp.bfloat16)

    rows, width = key_ref.shape
    scale = 1.0 / math.sqrt(width // HEADS)
    columns = head_columns(width)
    places = slot_rows(rows, slots)
    each = [(s, h, s * HEADS + h) for s in range(slots) for h in range(HEADS)]
    slopes, mixed, grad_mixed = [], [], []
    for s, h, i in each:
        scores = dot(query_ref[places[s], columns[h]], key_t_ref[columns[h], places[s]]) * scale
        sigmoid = 0.5 * jnp.tanh(0.5 * scores) + 0.5
        silu = scores * sigmoid
        attention_ref[i] = (silu * weight_ref[s]).astype(jnp.bfloat16)
        slopes.append((sigmoid + silu * (1.0 - sigmoid)) * weight_ref[s])
    for s, h, i in each:
        mixed.append(dot(attention_ref[i], value_ref[places[s], columns[h]]))
    for s in range(slots):
        own = mixed[s * HEADS : (s + 1) * HEADS]
        mean = row_mean(own, width)
        centred = [m - mean for m in own]
        inv_std = lax.rsqrt(row_mean([c * c for c in centred], width) + EPSILON)
        normed = [c * inv_std for c in centred]
        gated = [gated_ref[places[s], c] for c in columns]
        second = row_mean([g * n for g, n in zip(gated, normed)], width)
        first = first_ref[places[s]]
        for h in range(HEADS):
            normed_ref[places[s], columns[h]] = normed[h]
            grad = inv_std * (gated[h] - first - normed[h] * second)
            mixed_grad_ref[places[s], columns[h]] = grad.astype(jnp.bfloat16)
    for s, h, i in each:
        grad_attention = dot(
            mixed_grad_ref[places[s], columns[h]], value_t_ref[columns[h], places[s]]
        )
        scores_grad_ref[i] = (grad_attention * slopes[i]).astype(jnp.bfloat16)
    for s, h, i in each:
        grad_query = dot(scores_grad_ref[i], key_ref[places[s], columns[h]]) * scale
        grad_query_ref[places[s], columns[h]] = grad_query.astype(jnp.bfloat16)


def outputs_kernel(slots, _, query_ref, normed_ref, mixed_grad_ref, attention_ref, scores_grad_ref,
                   upstream_ref, grad_key_ref, grad_value_ref, grad_gate_ref):
    rows, width = query_ref.shape
    scale = 1.0 / math.sqrt(width // HEADS)
    columns = head_columns(width)
    places = slot_rows(rows, slots)
    grad_gate_ref[...] = (upstream_ref[...].astype(jnp.float32) * normed_ref[...]).astype(
        jnp.bfloat16
    )
    for s in range(slots):
        for h in range(HEADS):
            i = s * HEADS + h
            grad_value = dot(attention_ref[i], mixed_grad_ref[places[s], columns[h]], FIRST)
            grad_value_ref[places[s], columns[h]] = grad_value.astype(jnp.bfloat16)
            grad_key = dot(scores_grad_ref[i], query_ref[places[s], columns[h]], FIRST) * scale
            grad_key_ref[places[s], columns[h]] = grad_key.astype(jnp.bfloat16)


def summing_half(k, z):
    return lax.rem(lax.axis_index("dp"), CORES) ^ (1 if k else 0) ^ (1 if z else 0)


def gradient_kernel(shard_flips, events_ref, both_ref, outs, picked_ref):
    part_rows = outs[0].shape[0]
    half = both_ref.shape[1] // CORES
    shard_rows = events_ref.shape[0] // lax.axis_size("fsdp")
    chip, here = lax.div(lax.axis_index("dp"), CORES), lax.axis_index("fsdp")
    for other in range(CORES):
        picks = [
            (k, i, z)
            for k in range(len(outs))
            for i, z in enumerate(shard_flips)
            if (k != 0) ^ (z != 0) == bool(other)
        ]
        for p, (k, _, z) in enumerate(picks):
            start = pl.multiple_of((here ^ z) * shard_rows + (chip ^ k) * part_rows, part_rows)
            picked_ref[p * part_rows : (p + 1) * part_rows] = events_ref[pl.ds(start, part_rows)]
        core = summing_half(other, 0)
        columns = pl.ds(pl.multiple_of(core * half, half), half)
        total = dot(picked_ref[: len(picks) * part_rows], both_ref[:, columns])
        for p, (k, i, _) in enumerate(picks):
            block = total[p * part_rows : (p + 1) * part_rows]
            outs[k][:, i * half : (i + 1) * half] = block.astype(outs[k].dtype)


def far_gradient_kernel(shard_flips, events_ref, own_ref, got_ref, both_ref, *refs):
    rows = own_ref.shape[0]
    both_ref[:rows] = own_ref[...]
    both_ref[rows:] = got_ref[...]
    gradient_kernel(shard_flips, events_ref, both_ref, refs[:-1], refs[-1])


def near_gradient_kernel(shard_flips, events_ref, both_ref, *refs):
    gradient_kernel(shard_flips, events_ref, both_ref, refs[:-1], refs[-1])


def chip_sum_kernel(term_count, _, *refs):
    terms, outs = refs[:term_count], refs[term_count:]
    at = 0
    for out in outs:
        columns = slice(at, at + out.shape[1])
        total = terms[0][:, columns].astype(jnp.float32)
        for term in terms[1:]:
            total = total + term[:, columns].astype(jnp.float32)
        out[...] = total.astype(out.dtype)
        at += out.shape[1]


def mean_kernel(count, _, *refs):
    total = refs[0][...].astype(jnp.float32)
    for term in refs[1:-1]:
        total = total + term[...].astype(jnp.float32)
    refs[-1][...] = (total / count).astype(refs[-1].dtype)


def place_kernel(chips, own_ref, sibling_ref, out_ref, held_ref, sems):
    rows, half = own_ref.shape[0] // chips, own_ref.shape[1]
    core, chip = lax.rem(lax.axis_index("dp"), CORES), lax.div(lax.axis_index("dp"), CORES)
    copies = []
    for k in range(chips):
        place = pl.ds(pl.multiple_of((chip ^ k) * rows, rows), rows)
        for block_ref, side in ((own_ref, core), (sibling_ref, 1 - core)):
            columns = pl.ds(pl.multiple_of((side ^ (1 if k else 0)) * half, half), half)
            block = block_ref[k * rows : (k + 1) * rows]
            held_ref[place, columns] = block.astype(held_ref.dtype)
        copies.append(pltpu.make_async_copy(held_ref.at[place], out_ref.at[place], sems.at[k]))
        copies[k].start()
    for copy in copies:
        copy.wait()


def flip(block, axis, count, bits):
    return lax.ppermute(block, axis, [(i, i ^ bits) for i in range(count)])


def cross(block, dp_count, fsdp_count, chip_bits, shard_bits):
    pairs = [
        (
            d * fsdp_count + z,
            (d ^ (chip_bits * CORES) ^ 1) * fsdp_count + (z ^ shard_bits[d % CORES]),
        )
        for d in range(dp_count)
        for z in range(fsdp_count)
    ]
    return lax.ppermute(block, BOTH, pairs)


def far_first(count, send):
    return [send(k) for k in range(count - 1, 0, -1)][::-1]


def shard_pairs(fsdp_count):
    others = [d for d in range(1, fsdp_count) if d != fsdp_count // 2]
    return list(zip(others[::2], others[1::2]))


def across_z(weight, dp_count, fsdp_count):
    rows = weight.shape[0]
    group = max(g for g in (2, 4, 8) if dp_count % g == 0 and rows % (16 * g) == 0)
    part = call(
        functools.partial(slice_kernel, group),
        "own_part_of_weight",
        [weight],
        [FAR],
        jax.ShapeDtypeStruct((rows // group, weight.shape[1]), weight.dtype),
        [pltpu.SemaphoreType.DMA],
    )
    weight, part = lax.optimization_barrier((weight, part))
    middle = (fsdp_count // 2,) * CORES
    part = cross(part, dp_count, fsdp_count, 0, middle)
    wholes = [
        (cross(weight, dp_count, fsdp_count, 0, flips), flips[::-1])
        for flips in shard_pairs(fsdp_count)
    ]
    return group, part, wholes


def stack_kernel(*refs):
    out_ref = refs[-1]
    rows = refs[0].shape[0]
    for i, block_ref in enumerate(refs[:-1]):
        out_ref[i * rows : (i + 1) * rows] = block_ref[...]


def share(group, part, wholes, ready, dp_count, fsdp_count):
    alike = (0,) * CORES
    part, ready = lax.optimization_barrier((part, ready))
    parts, members = [part], [1]
    for chip_bits in range(1, group // CORES):
        parts.append(cross(part, dp_count, fsdp_count, chip_bits, alike))
        members.append(CORES * chip_bits)
    if len(parts) > 1:
        rows, columns = part.shape
        part = call(
            stack_kernel,
            "parts_of_weight",
            parts,
            [NEAR] * len(parts),
            jax.ShapeDtypeStruct((len(parts) * rows, columns), part.dtype),
        )
    held = [(part, (fsdp_count // 2,) * CORES, members)]
    for block, flips in wholes:
        held.append((lax.optimization_barrier((block, part))[0], flips, [None]))
    found = []
    for block, flips, members in held:
        moved = [m if m is None else m ^ 1 for m in members]
        found.append((block, (flips, members)))
        found.append((flip(block, "dp", dp_count, 1), (flips[::-1], moved)))
    return found


def shards(events, query_weight, keys, values, gates, cotangent, lengths):
    slots, span, model_width = events.shape
    width = query_weight.shape[1]
    half_width = width // CORES
    rows = slots * span
    dp_count, fsdp_count = lax.axis_size("dp"), lax.axis_size("fsdp")
    chips = dp_count // CORES
    shard_rows = model_width // fsdp_count
    total_seqs = slots * dp_count * fsdp_count
    bf16, f32 = jnp.bfloat16, jnp.float32

    def shape(*dims, dtype=bf16):
        return jax.ShapeDtypeStruct(dims, dtype)

    flat_events = events.reshape(rows, model_width)
    keys, values, gates, cotangent = (
        a.reshape(rows, width) for a in (keys, values, gates, cotangent)
    )
    sibling_events = flip(flat_events, "dp", dp_count, 1)
    group, part, wholes = across_z(query_weight, dp_count, fsdp_count)
    prepared = call(
        functools.partial(prepare_kernel, slots),
        "prepared_operands",
        [lengths, sibling_events]
        + [flat_events, keys, values, cotangent, query_weight, gates],
        [FAR, NEAR] + [FAR] * 6,
        (
            shape(rows, model_width),
            shape(rows, width),
            shape(rows, width),
            shape(rows, width),
            shape(shard_rows, width),
            shape(model_width, CORES * rows),
            shape(width, rows),
            shape(width, rows),
            shape(slots, span, span, dtype=f32),
            shape(rows, width, dtype=f32),
            shape(rows, span, dtype=f32),
        ),
        [
            pltpu.VMEM((rows, width), bf16),
            pltpu.SMEM(lengths.shape, jnp.int32),
            pltpu.SemaphoreType.DMA((7,)),
        ],
        flops=5 * 10**9,
    )
    near_events, near_keys, near_values, near_cotangent, near_weight = prepared[:5]
    events_t, keys_t, values_t, weight, gated, first = prepared[5:]
    found = [(near_weight, ((0, 0), [None]))]
    found += share(group, part, wholes, first, dp_count, fsdp_count)
    pieces, origins = zip(*found)
    blocks = shape(slots * HEADS, span, span)
    grad_query, query, normed, grad_mixed, attention, grad_scores = call(
        functools.partial(attention_kernel, slots, group, origins),
        "attention_to_grad_query",
        list(pieces)
        + [near_events, near_keys, near_values, keys_t, values_t, weight, gated, first],
        [ANYWHERE] * len(pieces) + [NEAR] * 8,
        (
            shape(rows, width),
            shape(rows, width),
            shape(rows, width, dtype=f32),
            shape(rows, width),
            blocks,
            blocks,
        ),
        [
            pltpu.VMEM((model_width, width), bf16),
            pltpu.SemaphoreType.DMA((sum(len(members) for _, members in origins),)),
        ],
        flops=2 * rows * width * (model_width + 4 * span),
        moved=24 * rows * width,
    )
    part_rows = shard_rows // chips
    staged = part_rows % 16 == 0 and fsdp_count % 4 == 0
    terms = [grad_query]
    if staged:
        alike = (0,) * CORES

        def to_chip(block, k):
            return cross(block, dp_count, fsdp_count, k, alike)

        def summed_over_chips(terms, name, flips, after):
            terms = [terms[0]] + far_first(chips, lambda k: to_chip(terms[k], k))
            return call(
                functools.partial(chip_sum_kernel, chips),
                name,
                [after] + terms,
                [ANYWHERE] + [NEAR] * chips,
                tuple(shape(part_rows, half_width, dtype=bf16 if z else f32) for z in flips),
            )

        def for_chips(flips):
            columns = len(flips) * half_width
            return tuple(shape(part_rows, columns, dtype=bf16 if k else f32) for k in range(chips))

        def work(flips):
            return dict(
                flops=4 * rows * len(flips) * shard_rows * half_width,
                moved=2 * (len(flips) * shard_rows + width) * CORES * rows,
            )

        far_flips, near_flips = tuple(range(2, fsdp_count)), (0, 1)
        got = flip(grad_query, "dp", dp_count, 1)
        picked_rows = (chips - 1) * part_rows * len(far_flips)
        both, *far_terms = call(
            functools.partial(far_gradient_kernel, far_flips),
            "weight_gradient_of_far_shards",
            [events_t, grad_query, got],
            [NEAR] * 3,
            (shape(CORES * rows, width),) + for_chips(far_flips),
            [pltpu.VMEM((picked_rows, CORES * rows), bf16)],
            **work(far_flips),
        )
        terms = call(
            functools.partial(near_gradient_kernel, near_flips),
            "weight_gradient_of_near_shards",
            [events_t, both],
            [NEAR] * 2,
            for_chips(near_flips),
            [pltpu.VMEM((chips * part_rows, CORES * rows), bf16)],
            **work(near_flips),
        )

        def to_shard(block, z):
            return cross(block, dp_count, fsdp_count, 0, (z,) * CORES)

        far_sums = summed_over_chips(far_terms, "far_shards_over_chips", far_flips, both)
        own_sum, next_sum = summed_over_chips(
            terms, "near_shards_over_chips", near_flips, far_sums[0]
        )
        far_sums = [to_shard(a, z) for a, z in reversed(list(zip(far_sums, far_flips)))]
        terms = [next_sum]
        next_sum = to_shard(next_sum, 1)
    grad_keys, grad_values, grad_gates = call(
        functools.partial(outputs_kernel, slots),
        "key_value_gate_gradients",
        [terms[0], query, normed, grad_mixed, attention, grad_scores, near_cotangent],
        [ANYWHERE] + [NEAR] * 6,
        (shape(rows, width),) * 3,
        flops=4 * rows * width * span,
        moved=12 * rows * width,
    )
    if staged:
        mean = call(
            functools.partial(mean_kernel, total_seqs),
            "mean_over_shards",
            [grad_keys, own_sum, next_sum] + far_sums,
            [FAR] + [NEAR] * fsdp_count,
            shape(part_rows, half_width),
        )
        blocks = call(
            stack_kernel,
            "blocks_of_chips",
            [mean] + far_first(chips, lambda k: to_chip(mean, k)),
            [NEAR] * chips,
            shape(shard_rows, half_width),
        )
        grad_weight = call(
            functools.partial(place_kernel, chips),
            "blocks_in_place",
            [blocks, flip(blocks, "dp", dp_count, 1)],
            [NEAR] * 2,
            shape(shard_rows, width, dtype=f32),
            [pltpu.VMEM((shard_rows, width), f32), pltpu.SemaphoreType.DMA((chips,))],
            out_specs=FAR,
        )
    else:
        whole = lax.dot_general(flat_events, grad_query, FIRST, preferred_element_type=f32)
        mine = lax.psum_scatter(whole, "fsdp", scatter_dimension=0, tiled=True)
        grad_weight = lax.psum(mine, "dp") / total_seqs

    full = (slots, span, width)
    return (
        grad_keys.reshape(full),
        grad_values.reshape(full),
        grad_gates.reshape(full),
        grad_weight,
    )


def solution(mesh):
    split = P(BOTH, None, None)
    return jax.shard_map(
        shards,
        mesh=mesh,
        in_specs=(split, P("fsdp", None), split, split, split, split, P()),
        out_specs=(split, split, split, P("fsdp", None)),
        check_vma=False,
    )
```

```python
import functools
import math

import jax
import jax.numpy as jnp
from jax import lax
from jax.experimental import pallas as pl
from jax.experimental.pallas import tpu as pltpu
from jax.sharding import PartitionSpec as P

HEADS = 4
EPSILON = 1e-06
CORES = 2
BOTH = ("dp", "fsdp")
VMEM_LIMIT = 24 * 1024 * 1024

LAST = (((1,), (1,)), ((), ()))
FIRST = (((0,), (0,)), ((), ()))


def dot(lhs, rhs, dims=(((1,), (0,)), ((), ()))):
    return lax.dot_general(lhs, rhs, dims, preferred_element_type=jnp.float32)


def call(kernel, name, operands, in_specs, out_shape, scratch=(), flops=0, moved=0,
         out_specs=None):
    vmem = pl.BlockSpec(memory_space=pltpu.VMEM)
    many = isinstance(out_shape, tuple)
    operands = [
        pltpu.with_memory_space_constraint(a, pltpu.HBM) if spec is FAR else a
        for a, spec in zip(operands, in_specs)
    ]
    return pl.pallas_call(
        kernel,
        out_shape=out_shape,
        in_specs=in_specs,
        out_specs=out_specs or ((vmem,) * len(out_shape) if many else vmem),
        scratch_shapes=list(scratch),
        compiler_params=pltpu.CompilerParams(vmem_limit_bytes=VMEM_LIMIT),
        cost_estimate=pl.CostEstimate(flops=flops, bytes_accessed=moved, transcendentals=0),
        name=name,
    )(*operands)


NEAR = pl.BlockSpec(memory_space=pltpu.VMEM)
ANYWHERE = pl.BlockSpec(memory_space=pl.ANY)
FAR = pl.BlockSpec(memory_space=pltpu.HBM)


def head_columns(width):
    depth = width // HEADS
    return [slice(h * depth, (h + 1) * depth) for h in range(HEADS)]


def slot_rows(rows, slots):
    span = rows // slots
    return [slice(s * span, (s + 1) * span) for s in range(slots)]


def row_mean(blocks, width):
    return jnp.sum(sum(blocks[1:], blocks[0]), axis=1, keepdims=True) / width


def slice_kernel(group, block_ref, out_ref, sem):
    rows = out_ref.shape[0]
    start = pl.multiple_of(lax.rem(lax.axis_index("dp"), group) * rows, rows)
    copy = pltpu.make_async_copy(block_ref.at[pl.ds(start, rows)], out_ref, sem)
    copy.start()
    copy.wait()


def prepare_kernel(slots, lengths_ref, sibling_ref, *refs):
    inputs, held = refs[:6], refs[6:11]
    (events_t_ref, key_t_ref, value_t_ref, weight_ref, gated_ref, first_ref,
     gate_ref, own_lengths_ref, sems) = refs[11:]
    events_ref, key_ref, value_ref, upstream_ref, _ = held
    copies = [
        pltpu.make_async_copy(source, target, sems.at[i])
        for i, (source, target) in enumerate(zip(inputs, held + (gate_ref,)))
    ]
    copies.append(pltpu.make_async_copy(lengths_ref, own_lengths_ref, sems.at[len(copies)]))
    for copy in copies:
        copy.start()
    rows, width = key_ref.shape
    events_t_ref[:, rows:] = sibling_ref[...].T
    for copy in copies:
        copy.wait()
    events_t_ref[:, :rows] = events_ref[...].T
    key_t_ref[...] = key_ref[...].T
    value_t_ref[...] = value_ref[...].T
    span = rows // slots
    row = lax.broadcasted_iota(jnp.int32, (span, span), 0)
    column = lax.broadcasted_iota(jnp.int32, (span, span), 1)
    first_slot = (lax.axis_index("dp") * lax.axis_size("fsdp") + lax.axis_index("fsdp")) * slots
    for s, place in enumerate(slot_rows(rows, slots)):
        length = own_lengths_ref[first_slot + s]
        inverse = 1.0 / jnp.full((span, span), length, jnp.int32).astype(jnp.float32)
        weight_ref[s] = jnp.where((column <= row) & (row < length), inverse, 0.0)
        live = lax.broadcasted_iota(jnp.int32, (span, width), 0) < length
        gated = upstream_ref[place].astype(jnp.float32) * gate_ref[place].astype(jnp.float32)
        gated = jnp.where(live, gated, 0.0)
        gated_ref[place] = gated
        first = row_mean([gated[:, c] for c in head_columns(width)], width)
        first_ref[place] = jnp.broadcast_to(first, (span, first_ref.shape[1]))


def piece_start(shard_rows, group, part_rows, flips, member_flip):
    device = lax.axis_index("dp")
    start = (
        lax.axis_index("fsdp") ^ jnp.where(lax.rem(device, CORES) == 0, flips[0], flips[1])
    ) * shard_rows
    if member_flip is not None:
        start = start + (lax.rem(device, group) ^ member_flip) * part_rows
    return pl.multiple_of(start, 16)


def attention_kernel(slots, group, origins, *refs):
    pieces = refs[: len(origins)]
    (events_ref, key_ref, value_ref, key_t_ref, value_t_ref, weight_ref, gated_ref, first_ref,
     grad_query_ref, query_ref, normed_ref, mixed_grad_ref, attention_ref, scores_grad_ref,
     projection_ref, sems) = refs[len(origins) :]
    copies = []
    for piece, (flips, members) in zip(pieces, origins):
        rows = piece.shape[0] // len(members)
        for i, member in enumerate(members):
            start = piece_start(pieces[0].shape[0], group, rows, flips, member)
            copies.append(
                pltpu.make_async_copy(
                    piece.at[pl.ds(i * rows, rows)],
                    projection_ref.at[pl.ds(start, rows)],
                    sems.at[len(copies)],
                )
            )
    for copy in copies:
        copy.start()
    for copy in copies:
        copy.wait()
    query_ref[...] = dot(events_ref[...], projection_ref[...]).astype(jnp.bfloat16)

    rows, width = key_ref.shape
    scale = 1.0 / math.sqrt(width // HEADS)
    columns = head_columns(width)
    places = slot_rows(rows, slots)
    each = [(s, h, s * HEADS + h) for s in range(slots) for h in range(HEADS)]
    slopes, mixed, grad_mixed = [], [], []
    for s, h, i in each:
        scores = dot(query_ref[places[s], columns[h]], key_t_ref[columns[h], places[s]]) * scale
        sigmoid = 0.5 * jnp.tanh(0.5 * scores) + 0.5
        silu = scores * sigmoid
        attention_ref[i] = (silu * weight_ref[s]).astype(jnp.bfloat16)
        slopes.append((sigmoid + silu * (1.0 - sigmoid)) * weight_ref[s])
    for s, h, i in each:
        mixed.append(dot(attention_ref[i], value_ref[places[s], columns[h]]))
    for s in range(slots):
        own = mixed[s * HEADS : (s + 1) * HEADS]
        mean = row_mean(own, width)
        centred = [m - mean for m in own]
        inv_std = lax.rsqrt(row_mean([c * c for c in centred], width) + EPSILON)
        normed = [c * inv_std for c in centred]
        gated = [gated_ref[places[s], c] for c in columns]
        second = row_mean([g * n for g, n in zip(gated, normed)], width)
        first = first_ref[places[s]]
        for h in range(HEADS):
            normed_ref[places[s], columns[h]] = normed[h]
            grad = inv_std * (gated[h] - first - normed[h] * second)
            mixed_grad_ref[places[s], columns[h]] = grad.astype(jnp.bfloat16)
    for s, h, i in each:
        grad_attention = dot(
            mixed_grad_ref[places[s], columns[h]], value_t_ref[columns[h], places[s]]
        )
        scores_grad_ref[i] = (grad_attention * slopes[i]).astype(jnp.bfloat16)
    for s, h, i in each:
        grad_query = dot(scores_grad_ref[i], key_ref[places[s], columns[h]]) * scale
        grad_query_ref[places[s], columns[h]] = grad_query.astype(jnp.bfloat16)


def outputs_kernel(slots, _, query_ref, normed_ref, mixed_grad_ref, attention_ref, scores_grad_ref,
                   upstream_ref, grad_key_ref, grad_value_ref, grad_gate_ref):
    rows, width = query_ref.shape
    scale = 1.0 / math.sqrt(width // HEADS)
    columns = head_columns(width)
    places = slot_rows(rows, slots)
    grad_gate_ref[...] = (upstream_ref[...].astype(jnp.float32) * normed_ref[...]).astype(
        jnp.bfloat16
    )
    for s in range(slots):
        for h in range(HEADS):
            i = s * HEADS + h
            grad_value = dot(attention_ref[i], mixed_grad_ref[places[s], columns[h]], FIRST)
            grad_value_ref[places[s], columns[h]] = grad_value.astype(jnp.bfloat16)
            grad_key = dot(scores_grad_ref[i], query_ref[places[s], columns[h]], FIRST) * scale
            grad_key_ref[places[s], columns[h]] = grad_key.astype(jnp.bfloat16)


def summing_half(k, z):
    return lax.rem(lax.axis_index("dp"), CORES) ^ (1 if k else 0) ^ (1 if z else 0)


def chip_flips(chips):
    return (0,) + tuple(range(chips - 1, 0, -1))


def gradient_picks(chips, shard_flips):
    every = [(k, i, z) for k in chip_flips(chips) for i, z in enumerate(shard_flips)]
    return [[p for p in every if (p[0] != 0) ^ (p[2] != 0) == bool(side)] for side in range(CORES)]


def half_columns(side, half):
    return pl.ds(pl.multiple_of(summing_half(side, 0) * half, half), half)


def own_gradient_kernel(chips, sets, events_ref, grad_query_ref, *refs):
    outs, picked_ref = refs[:-1], refs[-1]
    rows, half = grad_query_ref.shape[0], grad_query_ref.shape[1] // CORES
    shard_rows = events_ref.shape[0] // lax.axis_size("fsdp")
    part_rows = shard_rows // chips
    chip, here = lax.div(lax.axis_index("dp"), CORES), lax.axis_index("fsdp")
    for flips, term_ref, other_ref in zip(sets, outs[::2], outs[1::2]):
        at = 0
        for side, picks in enumerate(gradient_picks(chips, flips)):
            first = at
            for k, _, z in picks:
                start = (here ^ z) * shard_rows + (chip ^ k) * part_rows
                source = pl.ds(pl.multiple_of(start, part_rows), part_rows)
                picked_ref[at : at + part_rows] = events_ref[source, :rows]
                other_ref[at : at + part_rows] = events_ref[source, rows:]
                at += part_rows
            columns = half_columns(side, half)
            term_ref[first:at] = dot(picked_ref[first:at], grad_query_ref[:, columns])


def gradient_kernel(chips, flips, _, term_ref, events_ref, grad_query_ref, *outs):
    half = term_ref.shape[1]
    part_rows = outs[0].shape[0]
    out_of = dict(zip(chip_flips(chips), outs))
    at = 0
    for side, picks in enumerate(gradient_picks(chips, flips)):
        rows = slice(at, at + len(picks) * part_rows)
        total = term_ref[rows] + dot(events_ref[rows], grad_query_ref[:, half_columns(side, half)])
        for p, (k, i, _) in enumerate(picks):
            block = total[p * part_rows : (p + 1) * part_rows]
            out_of[k][:, i * half : (i + 1) * half] = block.astype(out_of[k].dtype)
        at = rows.stop


def chip_sum_kernel(term_count, _, *refs):
    terms, outs = refs[:term_count], refs[term_count:]
    at = 0
    for out in outs:
        columns = slice(at, at + out.shape[1])
        total = terms[0][:, columns].astype(jnp.float32)
        for term in terms[1:]:
            total = total + term[:, columns].astype(jnp.float32)
        out[...] = total.astype(out.dtype)
        at += out.shape[1]


def mean_kernel(count, _, *refs):
    total = refs[0][...].astype(jnp.float32)
    for term in refs[1:-1]:
        total = total + term[...].astype(jnp.float32)
    refs[-1][...] = (total / count).astype(refs[-1].dtype)


def place_kernel(chips, own_ref, sibling_ref, out_ref, held_ref, sems):
    rows, half = own_ref.shape[0] // chips, own_ref.shape[1]
    core, chip = lax.rem(lax.axis_index("dp"), CORES), lax.div(lax.axis_index("dp"), CORES)
    copies = []
    for k in range(chips):
        place = pl.ds(pl.multiple_of((chip ^ k) * rows, rows), rows)
        for block_ref, side in ((own_ref, core), (sibling_ref, 1 - core)):
            columns = pl.ds(pl.multiple_of((side ^ (1 if k else 0)) * half, half), half)
            block = block_ref[k * rows : (k + 1) * rows]
            held_ref[place, columns] = block.astype(held_ref.dtype)
        copies.append(pltpu.make_async_copy(held_ref.at[place], out_ref.at[place], sems.at[k]))
        copies[k].start()
    for copy in copies:
        copy.wait()


def flip(block, axis, count, bits):
    return lax.ppermute(block, axis, [(i, i ^ bits) for i in range(count)])


def cross(block, dp_count, fsdp_count, chip_bits, shard_bits):
    pairs = [
        (
            d * fsdp_count + z,
            (d ^ (chip_bits * CORES) ^ 1) * fsdp_count + (z ^ shard_bits[d % CORES]),
        )
        for d in range(dp_count)
        for z in range(fsdp_count)
    ]
    return lax.ppermute(block, BOTH, pairs)


def far_first(count, send):
    return [send(k) for k in range(count - 1, 0, -1)][::-1]


def shard_pairs(fsdp_count):
    others = [d for d in range(1, fsdp_count) if d != fsdp_count // 2]
    return list(zip(others[::2], others[1::2]))


def across_z(weight, dp_count, fsdp_count):
    rows = weight.shape[0]
    group = max(g for g in (2, 4, 8) if dp_count % g == 0 and rows % (16 * g) == 0)
    part = call(
        functools.partial(slice_kernel, group),
        "own_part_of_weight",
        [weight],
        [FAR],
        jax.ShapeDtypeStruct((rows // group, weight.shape[1]), weight.dtype),
        [pltpu.SemaphoreType.DMA],
    )
    weight, part = lax.optimization_barrier((weight, part))
    middle = (fsdp_count // 2,) * CORES
    part = cross(part, dp_count, fsdp_count, 0, middle)
    wholes = [
        (cross(weight, dp_count, fsdp_count, 0, flips), flips[::-1])
        for flips in shard_pairs(fsdp_count)
    ]
    return group, part, wholes


def stack_kernel(*refs):
    out_ref = refs[-1]
    rows = refs[0].shape[0]
    for i, block_ref in enumerate(refs[:-1]):
        out_ref[i * rows : (i + 1) * rows] = block_ref[...]


def share(group, part, wholes, ready, dp_count, fsdp_count):
    alike = (0,) * CORES
    part, ready = lax.optimization_barrier((part, ready))
    parts, members = [part], [1]
    for chip_bits in range(1, group // CORES):
        parts.append(cross(part, dp_count, fsdp_count, chip_bits, alike))
        members.append(CORES * chip_bits)
    if len(parts) > 1:
        rows, columns = part.shape
        part = call(
            stack_kernel,
            "parts_of_weight",
            parts,
            [NEAR] * len(parts),
            jax.ShapeDtypeStruct((len(parts) * rows, columns), part.dtype),
        )
    held = [(part, (fsdp_count // 2,) * CORES, members)]
    for block, flips in wholes:
        held.append((lax.optimization_barrier((block, part))[0], flips, [None]))
    found = []
    for block, flips, members in held:
        moved = [m if m is None else m ^ 1 for m in members]
        found.append((block, (flips, members)))
        found.append((flip(block, "dp", dp_count, 1), (flips[::-1], moved)))
    return found


def shards(events, query_weight, keys, values, gates, cotangent, lengths):
    slots, span, model_width = events.shape
    width = query_weight.shape[1]
    half_width = width // CORES
    rows = slots * span
    dp_count, fsdp_count = lax.axis_size("dp"), lax.axis_size("fsdp")
    chips = dp_count // CORES
    shard_rows = model_width // fsdp_count
    total_seqs = slots * dp_count * fsdp_count
    bf16, f32 = jnp.bfloat16, jnp.float32

    def shape(*dims, dtype=bf16):
        return jax.ShapeDtypeStruct(dims, dtype)

    flat_events = events.reshape(rows, model_width)
    keys, values, gates, cotangent = (
        a.reshape(rows, width) for a in (keys, values, gates, cotangent)
    )
    sibling_events = flip(flat_events, "dp", dp_count, 1)
    group, part, wholes = across_z(query_weight, dp_count, fsdp_count)
    prepared = call(
        functools.partial(prepare_kernel, slots),
        "prepared_operands",
        [lengths, sibling_events]
        + [flat_events, keys, values, cotangent, query_weight, gates],
        [FAR, NEAR] + [FAR] * 6,
        (
            shape(rows, model_width),
            shape(rows, width),
            shape(rows, width),
            shape(rows, width),
            shape(shard_rows, width),
            shape(model_width, CORES * rows),
            shape(width, rows),
            shape(width, rows),
            shape(slots, span, span, dtype=f32),
            shape(rows, width, dtype=f32),
            shape(rows, span, dtype=f32),
        ),
        [
            pltpu.VMEM((rows, width), bf16),
            pltpu.SMEM(lengths.shape, jnp.int32),
            pltpu.SemaphoreType.DMA((7,)),
        ],
        flops=5 * 10**9,
    )
    near_events, near_keys, near_values, near_cotangent, near_weight = prepared[:5]
    events_t, keys_t, values_t, weight, gated, first = prepared[5:]
    found = [(near_weight, ((0, 0), [None]))]
    found += share(group, part, wholes, first, dp_count, fsdp_count)
    pieces, origins = zip(*found)
    blocks = shape(slots * HEADS, span, span)
    grad_query, query, normed, grad_mixed, attention, grad_scores = call(
        functools.partial(attention_kernel, slots, group, origins),
        "attention_to_grad_query",
        list(pieces)
        + [near_events, near_keys, near_values, keys_t, values_t, weight, gated, first],
        [ANYWHERE] * len(pieces) + [NEAR] * 8,
        (
            shape(rows, width),
            shape(rows, width),
            shape(rows, width, dtype=f32),
            shape(rows, width),
            blocks,
            blocks,
        ),
        [
            pltpu.VMEM((model_width, width), bf16),
            pltpu.SemaphoreType.DMA((sum(len(members) for _, members in origins),)),
        ],
        flops=2 * rows * width * (model_width + 4 * span),
        moved=24 * rows * width,
    )
    part_rows = shard_rows // chips
    staged = part_rows % 16 == 0 and fsdp_count % 4 == 0
    terms = [grad_query]
    if staged:
        alike = (0,) * CORES

        def to_chip(block, k):
            return cross(block, dp_count, fsdp_count, k, alike)

        order = chip_flips(chips)

        def summed_over_chips(terms, name, flips, after):
            terms = [terms[0]] + [to_chip(a, k) for a, k in zip(terms[1:], order[1:])]
            return call(
                functools.partial(chip_sum_kernel, chips),
                name,
                [after] + terms,
                [ANYWHERE] + [NEAR] * chips,
                tuple(shape(part_rows, half_width, dtype=bf16 if z else f32) for z in flips),
            )

        sets = (tuple(range(2, fsdp_count)), (0, 1))
        picked_rows = [len(flips) * shard_rows for flips in sets]
        got = flip(grad_query, "dp", dp_count, 1)
        own_terms = call(
            functools.partial(own_gradient_kernel, chips, sets),
            "weight_gradient_of_own_events",
            [events_t, grad_query],
            [NEAR] * 2,
            tuple(
                a
                for n in picked_rows
                for a in (shape(n, half_width, dtype=f32), shape(n, rows))
            ),
            [pltpu.VMEM((max(picked_rows), rows), bf16)],
            flops=2 * rows * model_width * half_width,
            moved=8 * model_width * rows,
        )

        def gradient(which, name, after):
            columns = len(sets[which]) * half_width
            return call(
                functools.partial(gradient_kernel, chips, sets[which]),
                name,
                [after, *own_terms[2 * which : 2 * which + 2], got],
                [ANYWHERE] + [NEAR] * 3,
                tuple(shape(part_rows, columns, dtype=bf16 if k else f32) for k in order),
                flops=2 * rows * picked_rows[which] * half_width,
                moved=2 * picked_rows[which] * (rows + 2 * half_width),
            )

        far_terms = gradient(0, "weight_gradient_of_far_shards", got)
        terms = gradient(1, "weight_gradient_of_near_shards", far_terms[0])

        def to_shard(block, z):
            return cross(block, dp_count, fsdp_count, 0, (z,) * CORES)

        far_sums = summed_over_chips(far_terms, "far_shards_over_chips", sets[0], got)
        own_sum, next_sum = summed_over_chips(
            terms, "near_shards_over_chips", sets[1], far_sums[0]
        )
        far_sums = [to_shard(a, z) for a, z in reversed(list(zip(far_sums, sets[0])))]
        terms = [next_sum]
        next_sum = to_shard(next_sum, 1)
    grad_keys, grad_values, grad_gates = call(
        functools.partial(outputs_kernel, slots),
        "key_value_gate_gradients",
        [terms[0], query, normed, grad_mixed, attention, grad_scores, near_cotangent],
        [ANYWHERE] + [NEAR] * 6,
        (shape(rows, width),) * 3,
        flops=4 * rows * width * span,
        moved=12 * rows * width,
    )
    if staged:
        mean = call(
            functools.partial(mean_kernel, total_seqs),
            "mean_over_shards",
            [grad_keys, own_sum, next_sum] + far_sums,
            [FAR] + [NEAR] * fsdp_count,
            shape(part_rows, half_width),
        )
        blocks = call(
            stack_kernel,
            "blocks_of_chips",
            [mean] + far_first(chips, lambda k: to_chip(mean, k)),
            [NEAR] * chips,
            shape(shard_rows, half_width),
        )
        grad_weight = call(
            functools.partial(place_kernel, chips),
            "blocks_in_place",
            [blocks, flip(blocks, "dp", dp_count, 1)],
            [NEAR] * 2,
            shape(shard_rows, width, dtype=f32),
            [pltpu.VMEM((shard_rows, width), f32), pltpu.SemaphoreType.DMA((chips,))],
            out_specs=FAR,
        )
    else:
        whole = lax.dot_general(flat_events, grad_query, FIRST, preferred_element_type=f32)
        mine = lax.psum_scatter(whole, "fsdp", scatter_dimension=0, tiled=True)
        grad_weight = lax.psum(mine, "dp") / total_seqs

    full = (slots, span, width)
    return (
        grad_keys.reshape(full),
        grad_values.reshape(full),
        grad_gates.reshape(full),
        grad_weight,
    )


def solution(mesh):
    split = P(BOTH, None, None)
    return jax.shard_map(
        shards,
        mesh=mesh,
        in_specs=(split, P("fsdp", None), split, split, split, split, P()),
        out_specs=(split, split, split, P("fsdp", None)),
        check_vma=False,
    )
```

```python
import functools
import math

import jax
import jax.numpy as jnp
from jax import lax
from jax.experimental import pallas as pl
from jax.experimental.pallas import tpu as pltpu
from jax.sharding import PartitionSpec as P

HEADS = 4
EPSILON = 1e-06
CORES = 2
BOTH = ("dp", "fsdp")
VMEM_LIMIT = 24 * 1024 * 1024

LAST = (((1,), (1,)), ((), ()))
FIRST = (((0,), (0,)), ((), ()))


def dot(lhs, rhs, dims=(((1,), (0,)), ((), ()))):
    return lax.dot_general(lhs, rhs, dims, preferred_element_type=jnp.float32)


def call(kernel, name, operands, in_specs, out_shape, scratch=(), flops=0, moved=0,
         out_specs=None):
    vmem = pl.BlockSpec(memory_space=pltpu.VMEM)
    many = isinstance(out_shape, tuple)
    operands = [
        pltpu.with_memory_space_constraint(a, pltpu.HBM) if spec is FAR else a
        for a, spec in zip(operands, in_specs)
    ]
    return pl.pallas_call(
        kernel,
        out_shape=out_shape,
        in_specs=in_specs,
        out_specs=out_specs or ((vmem,) * len(out_shape) if many else vmem),
        scratch_shapes=list(scratch),
        compiler_params=pltpu.CompilerParams(vmem_limit_bytes=VMEM_LIMIT),
        cost_estimate=pl.CostEstimate(flops=flops, bytes_accessed=moved, transcendentals=0),
        name=name,
    )(*operands)


NEAR = pl.BlockSpec(memory_space=pltpu.VMEM)
ANYWHERE = pl.BlockSpec(memory_space=pl.ANY)
FAR = pl.BlockSpec(memory_space=pltpu.HBM)


def head_columns(width):
    depth = width // HEADS
    return [slice(h * depth, (h + 1) * depth) for h in range(HEADS)]


def slot_rows(rows, slots):
    span = rows // slots
    return [slice(s * span, (s + 1) * span) for s in range(slots)]


def row_mean(blocks, width):
    return jnp.sum(sum(blocks[1:], blocks[0]), axis=1, keepdims=True) / width


def slice_kernel(group, block_ref, out_ref, sem):
    rows = out_ref.shape[0]
    start = pl.multiple_of(lax.rem(lax.axis_index("dp"), group) * rows, rows)
    copy = pltpu.make_async_copy(block_ref.at[pl.ds(start, rows)], out_ref, sem)
    copy.start()
    copy.wait()


def prepare_kernel(slots, _, lengths_ref, sibling_ref, *refs):
    inputs, held = refs[:6], refs[6:11]
    (events_t_ref, key_t_ref, value_t_ref, weight_ref, gated_ref, first_ref,
     gate_ref, own_lengths_ref, sems) = refs[11:]
    events_ref, key_ref, value_ref, upstream_ref, _ = held
    copies = [
        pltpu.make_async_copy(source, target, sems.at[i])
        for i, (source, target) in enumerate(zip(inputs, held + (gate_ref,)))
    ]
    copies.append(pltpu.make_async_copy(lengths_ref, own_lengths_ref, sems.at[len(copies)]))
    for copy in copies:
        copy.start()
    rows, width = key_ref.shape
    events_t_ref[:, rows:] = sibling_ref[...].T
    for copy in copies:
        copy.wait()
    events_t_ref[:, :rows] = events_ref[...].T
    key_t_ref[...] = key_ref[...].T
    value_t_ref[...] = value_ref[...].T
    span = rows // slots
    row = lax.broadcasted_iota(jnp.int32, (span, span), 0)
    column = lax.broadcasted_iota(jnp.int32, (span, span), 1)
    first_slot = (lax.axis_index("dp") * lax.axis_size("fsdp") + lax.axis_index("fsdp")) * slots
    for s, place in enumerate(slot_rows(rows, slots)):
        length = own_lengths_ref[first_slot + s]
        inverse = 1.0 / jnp.full((span, span), length, jnp.int32).astype(jnp.float32)
        weight_ref[s] = jnp.where((column <= row) & (row < length), inverse, 0.0)
        live = lax.broadcasted_iota(jnp.int32, (span, width), 0) < length
        gated = upstream_ref[place].astype(jnp.float32) * gate_ref[place].astype(jnp.float32)
        gated = jnp.where(live, gated, 0.0)
        gated_ref[place] = gated
        first = row_mean([gated[:, c] for c in head_columns(width)], width)
        first_ref[place] = jnp.broadcast_to(first, (span, first_ref.shape[1]))


def piece_start(shard_rows, group, part_rows, flips, member_flip):
    device = lax.axis_index("dp")
    start = (
        lax.axis_index("fsdp") ^ jnp.where(lax.rem(device, CORES) == 0, flips[0], flips[1])
    ) * shard_rows
    if member_flip is not None:
        start = start + (lax.rem(device, group) ^ member_flip) * part_rows
    return pl.multiple_of(start, 16)


def aligned(shard_rows):
    return shard_rows % 128 == 0


def project(events_ref, pieces, origins, group, shard_rows, spare_ref, sems):
    copies, total = [], None
    for piece, (flips, members) in zip(pieces, origins):
        rows = piece.shape[0] // len(members)
        starts = [piece_start(shard_rows, group, rows, flips, m) for m in members]
        if not aligned(shard_rows):
            for i, start in enumerate(starts):
                copy = pltpu.make_async_copy(
                    piece.at[pl.ds(i * rows, rows)],
                    spare_ref.at[pl.ds(start, rows)],
                    sems.at[len(copies)],
                )
                copy.start()
                copies.append(copy)
            continue
        first = piece_start(shard_rows, group, rows, flips, None)
        if len(members) > 1:
            spare_ref[...] = jnp.zeros_like(spare_ref)
            for i, start in enumerate(starts):
                place = pl.ds(pl.multiple_of(start - first, 16), rows)
                spare_ref[place] = piece[i * rows : (i + 1) * rows]
            piece = spare_ref
        columns = pl.ds(pl.multiple_of(first, 128), shard_rows)
        term = dot(events_ref[:, columns], piece[...])
        total = term if total is None else total + term
    if copies:
        for copy in copies:
            copy.wait()
        total = dot(events_ref[...], spare_ref[...])
    return total


def projection_scratch(shard_rows, model_width, width, origins):
    count = sum(len(members) for _, members in origins)
    spare_rows = shard_rows if aligned(shard_rows) else model_width
    return [pltpu.VMEM((spare_rows, width), jnp.bfloat16), pltpu.SemaphoreType.DMA((count,))]


def held_projection_kernel(group, shard_rows, origins, *refs):
    pieces, (events_ref, out_ref, spare_ref, sems) = refs[: len(origins)], refs[len(origins) :]
    out_ref[...] = project(events_ref, pieces, origins, group, shard_rows, spare_ref, sems)


def attention_kernel(slots, group, shard_rows, origins, *refs):
    pieces = refs[: len(origins)]
    terms, refs = refs[len(origins) : -16], refs[-16:]
    (events_ref, key_ref, value_ref, key_t_ref, value_t_ref, weight_ref, gated_ref, first_ref,
     grad_query_ref, query_ref, normed_ref, mixed_grad_ref, attention_ref, scores_grad_ref,
     spare_ref, sems) = refs
    query = project(events_ref, pieces, origins, group, shard_rows, spare_ref, sems)
    for term in terms:
        query = query + term[...]
    query_ref[...] = query.astype(jnp.bfloat16)

    rows, width = key_ref.shape
    scale = 1.0 / math.sqrt(width // HEADS)
    columns = head_columns(width)
    places = slot_rows(rows, slots)
    each = [(s, h, s * HEADS + h) for s in range(slots) for h in range(HEADS)]
    slopes, mixed, grad_mixed = [], [], []
    for s, h, i in each:
        scores = dot(query_ref[places[s], columns[h]], key_t_ref[columns[h], places[s]]) * scale
        sigmoid = 0.5 * jnp.tanh(0.5 * scores) + 0.5
        silu = scores * sigmoid
        attention_ref[i] = (silu * weight_ref[s]).astype(jnp.bfloat16)
        slopes.append((sigmoid + silu * (1.0 - sigmoid)) * weight_ref[s])
    for s, h, i in each:
        mixed.append(dot(attention_ref[i], value_ref[places[s], columns[h]]))
    for s in range(slots):
        own = mixed[s * HEADS : (s + 1) * HEADS]
        mean = row_mean(own, width)
        centred = [m - mean for m in own]
        inv_std = lax.rsqrt(row_mean([c * c for c in centred], width) + EPSILON)
        normed = [c * inv_std for c in centred]
        gated = [gated_ref[places[s], c] for c in columns]
        second = row_mean([g * n for g, n in zip(gated, normed)], width)
        first = first_ref[places[s]]
        for h in range(HEADS):
            normed_ref[places[s], columns[h]] = normed[h]
            grad = inv_std * (gated[h] - first - normed[h] * second)
            mixed_grad_ref[places[s], columns[h]] = grad.astype(jnp.bfloat16)
    for s, h, i in each:
        grad_attention = dot(
            mixed_grad_ref[places[s], columns[h]], value_t_ref[columns[h], places[s]]
        )
        scores_grad_ref[i] = (grad_attention * slopes[i]).astype(jnp.bfloat16)
    for s, h, i in each:
        grad_query = dot(scores_grad_ref[i], key_ref[places[s], columns[h]]) * scale
        grad_query_ref[places[s], columns[h]] = grad_query.astype(jnp.bfloat16)


def outputs_kernel(slots, _, query_ref, normed_ref, mixed_grad_ref, attention_ref, scores_grad_ref,
                   upstream_ref, grad_key_ref, grad_value_ref, grad_gate_ref):
    rows, width = query_ref.shape
    scale = 1.0 / math.sqrt(width // HEADS)
    columns = head_columns(width)
    places = slot_rows(rows, slots)
    grad_gate_ref[...] = (upstream_ref[...].astype(jnp.float32) * normed_ref[...]).astype(
        jnp.bfloat16
    )
    for s in range(slots):
        for h in range(HEADS):
            i = s * HEADS + h
            grad_value = dot(attention_ref[i], mixed_grad_ref[places[s], columns[h]], FIRST)
            grad_value_ref[places[s], columns[h]] = grad_value.astype(jnp.bfloat16)
            grad_key = dot(scores_grad_ref[i], query_ref[places[s], columns[h]], FIRST) * scale
            grad_key_ref[places[s], columns[h]] = grad_key.astype(jnp.bfloat16)


def summing_half(k, z):
    return lax.rem(lax.axis_index("dp"), CORES) ^ (1 if k else 0) ^ (1 if z else 0)


def chip_flips(chips):
    return (0,) + tuple(range(chips - 1, 0, -1))


def gradient_picks(chips, shard_flips):
    every = [(k, i, z) for k in chip_flips(chips) for i, z in enumerate(shard_flips)]
    return [[p for p in every if (p[0] != 0) ^ (p[2] != 0) == bool(side)] for side in range(CORES)]


def half_columns(side, half):
    return pl.ds(pl.multiple_of(summing_half(side, 0) * half, half), half)


def own_gradient_kernel(chips, sets, events_ref, grad_query_ref, *refs):
    outs, picked_ref = refs[:-1], refs[-1]
    rows, half = grad_query_ref.shape[0], grad_query_ref.shape[1] // CORES
    shard_rows = events_ref.shape[0] // lax.axis_size("fsdp")
    part_rows = shard_rows // chips
    chip, here = lax.div(lax.axis_index("dp"), CORES), lax.axis_index("fsdp")
    for flips, term_ref, other_ref in zip(sets, outs[::2], outs[1::2]):
        at = 0
        for side, picks in enumerate(gradient_picks(chips, flips)):
            first = at
            for k, _, z in picks:
                start = (here ^ z) * shard_rows + (chip ^ k) * part_rows
                source = pl.ds(pl.multiple_of(start, part_rows), part_rows)
                picked_ref[at : at + part_rows] = events_ref[source, :rows]
                other_ref[at : at + part_rows] = events_ref[source, rows:]
                at += part_rows
            columns = half_columns(side, half)
            term_ref[first:at] = dot(picked_ref[first:at], grad_query_ref[:, columns])


def gradient_kernel(chips, flips, _, term_ref, events_ref, grad_query_ref, *outs):
    half = term_ref.shape[1]
    part_rows = outs[0].shape[0]
    out_of = dict(zip(chip_flips(chips), outs))
    at = 0
    for side, picks in enumerate(gradient_picks(chips, flips)):
        rows = slice(at, at + len(picks) * part_rows)
        total = term_ref[rows] + dot(events_ref[rows], grad_query_ref[:, half_columns(side, half)])
        for p, (k, i, _) in enumerate(picks):
            block = total[p * part_rows : (p + 1) * part_rows]
            out_of[k][:, i * half : (i + 1) * half] = block.astype(out_of[k].dtype)
        at = rows.stop


def chip_sum_kernel(term_count, _, *refs):
    terms, outs = refs[:term_count], refs[term_count:]
    at = 0
    for out in outs:
        columns = slice(at, at + out.shape[1])
        total = terms[0][:, columns].astype(jnp.float32)
        for term in terms[1:]:
            total = total + term[:, columns].astype(jnp.float32)
        out[...] = total.astype(out.dtype)
        at += out.shape[1]


def mean_kernel(count, _, *refs):
    total = refs[0][...].astype(jnp.float32)
    for term in refs[1:-1]:
        total = total + term[...].astype(jnp.float32)
    refs[-1][...] = (total / count).astype(refs[-1].dtype)


def place_kernel(chips, own_ref, sibling_ref, out_ref, held_ref, sems):
    rows, half = own_ref.shape[0] // chips, own_ref.shape[1]
    core, chip = lax.rem(lax.axis_index("dp"), CORES), lax.div(lax.axis_index("dp"), CORES)
    copies = []
    for k in range(chips):
        place = pl.ds(pl.multiple_of((chip ^ k) * rows, rows), rows)
        for block_ref, side in ((own_ref, core), (sibling_ref, 1 - core)):
            columns = pl.ds(pl.multiple_of((side ^ (1 if k else 0)) * half, half), half)
            block = block_ref[k * rows : (k + 1) * rows]
            held_ref[place, columns] = block.astype(held_ref.dtype)
        copies.append(pltpu.make_async_copy(held_ref.at[place], out_ref.at[place], sems.at[k]))
        copies[k].start()
    for copy in copies:
        copy.wait()


def flip(block, axis, count, bits):
    return lax.ppermute(block, axis, [(i, i ^ bits) for i in range(count)])


def cross(block, dp_count, fsdp_count, chip_bits, shard_bits):
    pairs = [
        (
            d * fsdp_count + z,
            (d ^ (chip_bits * CORES) ^ 1) * fsdp_count + (z ^ shard_bits[d % CORES]),
        )
        for d in range(dp_count)
        for z in range(fsdp_count)
    ]
    return lax.ppermute(block, BOTH, pairs)


def far_first(count, send):
    return [send(k) for k in range(count - 1, 0, -1)][::-1]


def shard_pairs(fsdp_count):
    others = [d for d in range(1, fsdp_count) if d != fsdp_count // 2]
    return list(zip(others[::2], others[1::2]))


def across_z(weight, dp_count, fsdp_count):
    rows = weight.shape[0]
    group = max(g for g in (2, 4, 8) if dp_count % g == 0 and rows % (16 * g) == 0)
    part = call(
        functools.partial(slice_kernel, group),
        "own_part_of_weight",
        [weight],
        [FAR],
        jax.ShapeDtypeStruct((rows // group, weight.shape[1]), weight.dtype),
        [pltpu.SemaphoreType.DMA],
    )
    weight, part = lax.optimization_barrier((weight, part))
    middle = (fsdp_count // 2,) * CORES
    part = cross(part, dp_count, fsdp_count, 0, middle)
    wholes = [
        (cross(weight, dp_count, fsdp_count, 0, flips), flips[::-1])
        for flips in shard_pairs(fsdp_count)
    ]
    return group, part, wholes


def stack_kernel(_, *refs):
    out_ref = refs[-1]
    rows = refs[0].shape[0]
    for i, block_ref in enumerate(refs[:-1]):
        out_ref[i * rows : (i + 1) * rows] = block_ref[...]


def share(group, part, wholes, ready, dp_count, fsdp_count):
    alike = (0,) * CORES
    parts, members = [part], [1]
    for chip_bits in range(1, group // CORES):
        parts.append(cross(part, dp_count, fsdp_count, chip_bits, alike))
        members.append(CORES * chip_bits)
    if len(parts) > 1:
        rows, columns = part.shape
        part = call(
            stack_kernel,
            "parts_of_weight",
            [ready] + parts,
            [ANYWHERE] + [NEAR] * len(parts),
            jax.ShapeDtypeStruct((len(parts) * rows, columns), part.dtype),
        )
    held = [(part, (fsdp_count // 2,) * CORES, members)]
    for block, flips in wholes:
        held.append((lax.optimization_barrier((block, part))[0], flips, [None]))
    moved = []
    for block, flips, members in held:
        places = [m if m is None else m ^ 1 for m in members]
        moved.append((flip(block, "dp", dp_count, 1), flips[::-1], places))
    return held, moved


def shards(events, query_weight, keys, values, gates, cotangent, lengths):
    slots, span, model_width = events.shape
    width = query_weight.shape[1]
    half_width = width // CORES
    rows = slots * span
    dp_count, fsdp_count = lax.axis_size("dp"), lax.axis_size("fsdp")
    chips = dp_count // CORES
    shard_rows = model_width // fsdp_count
    total_seqs = slots * dp_count * fsdp_count
    bf16, f32 = jnp.bfloat16, jnp.float32

    def shape(*dims, dtype=bf16):
        return jax.ShapeDtypeStruct(dims, dtype)

    flat_events = events.reshape(rows, model_width)
    keys, values, gates, cotangent = (
        a.reshape(rows, width) for a in (keys, values, gates, cotangent)
    )
    sibling_events = flip(flat_events, "dp", dp_count, 1)
    group, part, wholes = across_z(query_weight, dp_count, fsdp_count)
    prepared = call(
        functools.partial(prepare_kernel, slots),
        "prepared_operands",
        [part, lengths, sibling_events]
        + [flat_events, keys, values, cotangent, query_weight, gates],
        [ANYWHERE, FAR, NEAR] + [FAR] * 6,
        (
            shape(rows, model_width),
            shape(rows, width),
            shape(rows, width),
            shape(rows, width),
            shape(shard_rows, width),
            shape(model_width, CORES * rows),
            shape(width, rows),
            shape(width, rows),
            shape(slots, span, span, dtype=f32),
            shape(rows, width, dtype=f32),
            shape(rows, span, dtype=f32),
        ),
        [
            pltpu.VMEM((rows, width), bf16),
            pltpu.SMEM(lengths.shape, jnp.int32),
            pltpu.SemaphoreType.DMA((7,)),
        ],
        flops=5 * 10**9,
    )
    near_events, near_keys, near_values, near_cotangent, near_weight = prepared[:5]
    events_t, keys_t, values_t, weight, gated, first = prepared[5:]
    held, moved = share(group, part, wholes, first, dp_count, fsdp_count)
    held = [(near_weight, (0, 0), [None])] + held
    if not aligned(shard_rows):
        held, moved = [], held + moved

    def split(found):
        return [f[0] for f in found], [f[1:] for f in found]

    terms = []
    if held:
        pieces, origins = split(held)
        terms = [
            call(
                functools.partial(held_projection_kernel, group, shard_rows, origins),
                "projection_by_held_rows",
                pieces + [near_events],
                [NEAR] * (len(pieces) + 1),
                shape(rows, width, dtype=f32),
                projection_scratch(shard_rows, model_width, width, origins),
                flops=2 * rows * width * shard_rows * len(pieces),
                moved=4 * rows * width,
            )
        ]
    pieces, origins = split(moved)
    blocks = shape(slots * HEADS, span, span)
    grad_query, query, normed, grad_mixed, attention, grad_scores = call(
        functools.partial(attention_kernel, slots, group, shard_rows, origins),
        "attention_to_grad_query",
        pieces
        + terms
        + [near_events, near_keys, near_values, keys_t, values_t, weight, gated, first],
        [NEAR] * (len(pieces) + len(terms) + 8),
        (
            shape(rows, width),
            shape(rows, width),
            shape(rows, width, dtype=f32),
            shape(rows, width),
            blocks,
            blocks,
        ),
        projection_scratch(shard_rows, model_width, width, origins),
        flops=2 * rows * width * (model_width + 4 * span),
        moved=24 * rows * width,
    )
    part_rows = shard_rows // chips
    staged = part_rows % 16 == 0 and fsdp_count % 4 == 0
    terms = [grad_query]
    if staged:
        alike = (0,) * CORES

        def to_chip(block, k):
            return cross(block, dp_count, fsdp_count, k, alike)

        order = chip_flips(chips)

        def summed_over_chips(terms, name, flips, after):
            terms = [terms[0]] + [to_chip(a, k) for a, k in zip(terms[1:], order[1:])]
            return call(
                functools.partial(chip_sum_kernel, chips),
                name,
                [after] + terms,
                [ANYWHERE] + [NEAR] * chips,
                tuple(shape(part_rows, half_width, dtype=bf16 if z else f32) for z in flips),
            )

        sets = (tuple(range(2, fsdp_count)), (0, 1))
        picked_rows = [len(flips) * shard_rows for flips in sets]
        got = flip(grad_query, "dp", dp_count, 1)
        own_terms = call(
            functools.partial(own_gradient_kernel, chips, sets),
            "weight_gradient_of_own_events",
            [events_t, grad_query],
            [NEAR] * 2,
            tuple(
                a
                for n in picked_rows
                for a in (shape(n, half_width, dtype=f32), shape(n, rows))
            ),
            [pltpu.VMEM((max(picked_rows), rows), bf16)],
            flops=2 * rows * model_width * half_width,
            moved=8 * model_width * rows,
        )

        def gradient(which, name, after):
            columns = len(sets[which]) * half_width
            return call(
                functools.partial(gradient_kernel, chips, sets[which]),
                name,
                [after, *own_terms[2 * which : 2 * which + 2], got],
                [ANYWHERE] + [NEAR] * 3,
                tuple(shape(part_rows, columns, dtype=bf16 if k else f32) for k in order),
                flops=2 * rows * picked_rows[which] * half_width,
                moved=2 * picked_rows[which] * (rows + 2 * half_width),
            )

        far_terms = gradient(0, "weight_gradient_of_far_shards", got)
        terms = gradient(1, "weight_gradient_of_near_shards", far_terms[0])

        def to_shard(block, z):
            return cross(block, dp_count, fsdp_count, 0, (z,) * CORES)

        far_sums = summed_over_chips(far_terms, "far_shards_over_chips", sets[0], got)
        own_sum, next_sum = summed_over_chips(
            terms, "near_shards_over_chips", sets[1], far_sums[0]
        )
        far_sums = [to_shard(a, z) for a, z in reversed(list(zip(far_sums, sets[0])))]
        terms = [next_sum]
        next_sum = to_shard(next_sum, 1)
    grad_keys, grad_values, grad_gates = call(
        functools.partial(outputs_kernel, slots),
        "key_value_gate_gradients",
        [terms[0], query, normed, grad_mixed, attention, grad_scores, near_cotangent],
        [ANYWHERE] + [NEAR] * 6,
        (shape(rows, width),) * 3,
        flops=4 * rows * width * span,
        moved=12 * rows * width,
    )
    if staged:
        mean = call(
            functools.partial(mean_kernel, total_seqs),
            "mean_over_shards",
            [grad_keys, own_sum, next_sum] + far_sums,
            [FAR] + [NEAR] * fsdp_count,
            shape(part_rows, half_width),
        )
        blocks = call(
            stack_kernel,
            "blocks_of_chips",
            [mean, mean] + far_first(chips, lambda k: to_chip(mean, k)),
            [ANYWHERE] + [NEAR] * chips,
            shape(shard_rows, half_width),
        )
        grad_weight = call(
            functools.partial(place_kernel, chips),
            "blocks_in_place",
            [blocks, flip(blocks, "dp", dp_count, 1)],
            [NEAR] * 2,
            shape(shard_rows, width, dtype=f32),
            [pltpu.VMEM((shard_rows, width), f32), pltpu.SemaphoreType.DMA((chips,))],
            out_specs=FAR,
        )
    else:
        whole = lax.dot_general(flat_events, grad_query, FIRST, preferred_element_type=f32)
        mine = lax.psum_scatter(whole, "fsdp", scatter_dimension=0, tiled=True)
        grad_weight = lax.psum(mine, "dp") / total_seqs

    full = (slots, span, width)
    return (
        grad_keys.reshape(full),
        grad_values.reshape(full),
        grad_gates.reshape(full),
        grad_weight,
    )


def solution(mesh):
    split = P(BOTH, None, None)
    return jax.shard_map(
        shards,
        mesh=mesh,
        in_specs=(split, P("fsdp", None), split, split, split, split, P()),
        out_specs=(split, split, split, P("fsdp", None)),
        check_vma=False,
    )
```

```python
import functools
import math

import jax
import jax.numpy as jnp
from jax import lax
from jax.experimental import pallas as pl
from jax.experimental.pallas import tpu as pltpu
from jax.sharding import PartitionSpec as P

HEADS = 4
EPSILON = 1e-06
CORES = 2
BOTH = ("dp", "fsdp")
VMEM_LIMIT = 24 * 1024 * 1024

LAST = (((1,), (1,)), ((), ()))
FIRST = (((0,), (0,)), ((), ()))


def dot(lhs, rhs, dims=(((1,), (0,)), ((), ()))):
    return lax.dot_general(lhs, rhs, dims, preferred_element_type=jnp.float32)


def call(kernel, name, operands, in_specs, out_shape, scratch=(), flops=0, moved=0,
         out_specs=None):
    vmem = pl.BlockSpec(memory_space=pltpu.VMEM)
    many = isinstance(out_shape, tuple)
    operands = [
        pltpu.with_memory_space_constraint(a, pltpu.HBM) if spec is FAR else a
        for a, spec in zip(operands, in_specs)
    ]
    return pl.pallas_call(
        kernel,
        out_shape=out_shape,
        in_specs=in_specs,
        out_specs=out_specs or ((vmem,) * len(out_shape) if many else vmem),
        scratch_shapes=list(scratch),
        compiler_params=pltpu.CompilerParams(vmem_limit_bytes=VMEM_LIMIT),
        cost_estimate=pl.CostEstimate(flops=flops, bytes_accessed=moved, transcendentals=0),
        name=name,
    )(*operands)


NEAR = pl.BlockSpec(memory_space=pltpu.VMEM)
ANYWHERE = pl.BlockSpec(memory_space=pl.ANY)
FAR = pl.BlockSpec(memory_space=pltpu.HBM)


def head_columns(width):
    depth = width // HEADS
    return [slice(h * depth, (h + 1) * depth) for h in range(HEADS)]


def slot_rows(rows, slots):
    span = rows // slots
    return [slice(s * span, (s + 1) * span) for s in range(slots)]


def row_mean(blocks, width):
    return jnp.sum(sum(blocks[1:], blocks[0]), axis=1, keepdims=True) / width


def slice_kernel(group, block_ref, out_ref, sem):
    rows = out_ref.shape[0]
    start = pl.multiple_of(lax.rem(lax.axis_index("dp"), group) * rows, rows)
    copy = pltpu.make_async_copy(block_ref.at[pl.ds(start, rows)], out_ref, sem)
    copy.start()
    copy.wait()


def prepare_kernel(slots, _, lengths_ref, sibling_ref, *refs):
    inputs, held = refs[:6], refs[6:11]
    (events_t_ref, key_t_ref, value_t_ref, weight_ref, gated_ref, first_ref,
     gate_ref, own_lengths_ref, sems) = refs[11:]
    events_ref, key_ref, value_ref, upstream_ref, _ = held
    copies = [
        pltpu.make_async_copy(source, target, sems.at[i])
        for i, (source, target) in enumerate(zip(inputs, held + (gate_ref,)))
    ]
    copies.append(pltpu.make_async_copy(lengths_ref, own_lengths_ref, sems.at[len(copies)]))
    for copy in copies:
        copy.start()
    rows, width = key_ref.shape
    events_t_ref[:, rows:] = sibling_ref[...].T
    for copy in copies:
        copy.wait()
    events_t_ref[:, :rows] = events_ref[...].T
    key_t_ref[...] = key_ref[...].T
    value_t_ref[...] = value_ref[...].T
    span = rows // slots
    row = lax.broadcasted_iota(jnp.int32, (span, span), 0)
    column = lax.broadcasted_iota(jnp.int32, (span, span), 1)
    first_slot = (lax.axis_index("dp") * lax.axis_size("fsdp") + lax.axis_index("fsdp")) * slots
    for s, place in enumerate(slot_rows(rows, slots)):
        length = own_lengths_ref[first_slot + s]
        inverse = 1.0 / jnp.full((span, span), length, jnp.int32).astype(jnp.float32)
        weight_ref[s] = jnp.where((column <= row) & (row < length), inverse, 0.0)
        live = lax.broadcasted_iota(jnp.int32, (span, width), 0) < length
        gated = upstream_ref[place].astype(jnp.float32) * gate_ref[place].astype(jnp.float32)
        gated = jnp.where(live, gated, 0.0)
        gated_ref[place] = gated
        first = row_mean([gated[:, c] for c in head_columns(width)], width)
        first_ref[place] = jnp.broadcast_to(first, (span, first_ref.shape[1]))


def piece_start(shard_rows, group, part_rows, flips, member_flip):
    device = lax.axis_index("dp")
    start = (
        lax.axis_index("fsdp") ^ jnp.where(lax.rem(device, CORES) == 0, flips[0], flips[1])
    ) * shard_rows
    if member_flip is not None:
        start = start + (lax.rem(device, group) ^ member_flip) * part_rows
    return pl.multiple_of(start, 16)


def aligned(shard_rows):
    return shard_rows % 128 == 0


def project(events_ref, pieces, origins, group, shard_rows, spare_ref, sems):
    copies, total = [], None
    for piece, (flips, members) in zip(pieces, origins):
        rows = piece.shape[0] // len(members)
        starts = [piece_start(shard_rows, group, rows, flips, m) for m in members]
        if not aligned(shard_rows):
            for i, start in enumerate(starts):
                copy = pltpu.make_async_copy(
                    piece.at[pl.ds(i * rows, rows)],
                    spare_ref.at[pl.ds(start, rows)],
                    sems.at[len(copies)],
                )
                copy.start()
                copies.append(copy)
            continue
        first = piece_start(shard_rows, group, rows, flips, None)
        if len(members) > 1:
            spare_ref[...] = jnp.zeros_like(spare_ref)
            for i, start in enumerate(starts):
                place = pl.ds(pl.multiple_of(start - first, 16), rows)
                spare_ref[place] = piece[i * rows : (i + 1) * rows]
            piece = spare_ref
        columns = pl.ds(pl.multiple_of(first, 128), shard_rows)
        term = dot(events_ref[:, columns], piece[...])
        total = term if total is None else total + term
    if copies:
        for copy in copies:
            copy.wait()
        total = dot(events_ref[...], spare_ref[...])
    return total


def projection_scratch(shard_rows, model_width, width, origins):
    count = sum(len(members) for _, members in origins)
    spare_rows = shard_rows if aligned(shard_rows) else model_width
    return [pltpu.VMEM((spare_rows, width), jnp.bfloat16), pltpu.SemaphoreType.DMA((count,))]


def held_projection_kernel(group, shard_rows, origins, *refs):
    pieces, (events_ref, out_ref, spare_ref, sems) = refs[: len(origins)], refs[len(origins) :]
    out_ref[...] = project(events_ref, pieces, origins, group, shard_rows, spare_ref, sems)


def attention_kernel(slots, group, shard_rows, origins, *refs):
    pieces = refs[: len(origins)]
    terms, refs = refs[len(origins) : -16], refs[-16:]
    (events_ref, key_ref, value_ref, key_t_ref, value_t_ref, weight_ref, gated_ref, first_ref,
     grad_query_ref, query_ref, normed_ref, mixed_grad_ref, attention_ref, scores_grad_ref,
     spare_ref, sems) = refs
    query = project(events_ref, pieces, origins, group, shard_rows, spare_ref, sems)
    for term in terms:
        query = query + term[...]
    query_ref[...] = query.astype(jnp.bfloat16)

    rows, width = key_ref.shape
    scale = 1.0 / math.sqrt(width // HEADS)
    columns = head_columns(width)
    places = slot_rows(rows, slots)
    each = [(s, h, s * HEADS + h) for s in range(slots) for h in range(HEADS)]
    slopes, mixed, grad_mixed = [], [], []
    for s, h, i in each:
        scores = dot(query_ref[places[s], columns[h]], key_t_ref[columns[h], places[s]]) * scale
        sigmoid = 1.0 / (1.0 + jnp.exp(-scores))
        silu = scores * sigmoid
        attention_ref[i] = (silu * weight_ref[s]).astype(jnp.bfloat16)
        slopes.append((sigmoid + silu * (1.0 - sigmoid)) * weight_ref[s])
    for s, h, i in each:
        mixed.append(dot(attention_ref[i], value_ref[places[s], columns[h]]))
    for s in range(slots):
        own = mixed[s * HEADS : (s + 1) * HEADS]
        mean = row_mean(own, width)
        centred = [m - mean for m in own]
        inv_std = lax.rsqrt(row_mean([c * c for c in centred], width) + EPSILON)
        normed = [c * inv_std for c in centred]
        gated = [gated_ref[places[s], c] for c in columns]
        second = row_mean([g * n for g, n in zip(gated, normed)], width)
        first = first_ref[places[s]]
        for h in range(HEADS):
            normed_ref[places[s], columns[h]] = normed[h]
            grad = inv_std * (gated[h] - first - normed[h] * second)
            mixed_grad_ref[places[s], columns[h]] = grad.astype(jnp.bfloat16)
    for s, h, i in each:
        grad_attention = dot(
            mixed_grad_ref[places[s], columns[h]], value_t_ref[columns[h], places[s]]
        )
        scores_grad_ref[i] = (grad_attention * slopes[i]).astype(jnp.bfloat16)
    for s, h, i in each:
        grad_query = dot(scores_grad_ref[i], key_ref[places[s], columns[h]]) * scale
        grad_query_ref[places[s], columns[h]] = grad_query.astype(jnp.bfloat16)


def outputs_kernel(slots, _, query_ref, normed_ref, mixed_grad_ref, attention_ref, scores_grad_ref,
                   upstream_ref, grad_key_ref, grad_value_ref, grad_gate_ref):
    rows, width = query_ref.shape
    scale = 1.0 / math.sqrt(width // HEADS)
    columns = head_columns(width)
    places = slot_rows(rows, slots)
    grad_gate_ref[...] = (upstream_ref[...].astype(jnp.float32) * normed_ref[...]).astype(
        jnp.bfloat16
    )
    for s in range(slots):
        for h in range(HEADS):
            i = s * HEADS + h
            grad_value = dot(attention_ref[i], mixed_grad_ref[places[s], columns[h]], FIRST)
            grad_value_ref[places[s], columns[h]] = grad_value.astype(jnp.bfloat16)
            grad_key = dot(scores_grad_ref[i], query_ref[places[s], columns[h]], FIRST) * scale
            grad_key_ref[places[s], columns[h]] = grad_key.astype(jnp.bfloat16)


def summing_half(k, z):
    return lax.rem(lax.axis_index("dp"), CORES) ^ (1 if k else 0) ^ (1 if z else 0)


def gradient_picks(chips, shard_flips):
    every = [(k, i, z) for k in range(chips) for i, z in enumerate(shard_flips)]
    return [[p for p in every if (p[0] != 0) ^ (p[2] != 0) == bool(side)] for side in range(CORES)]


def half_columns(side, half):
    return pl.ds(pl.multiple_of(summing_half(side, 0) * half, half), half)


def own_gradient_kernel(chips, sets, events_ref, grad_query_ref, *refs):
    outs, picked_ref = refs[:-1], refs[-1]
    rows, half = grad_query_ref.shape[0], grad_query_ref.shape[1] // CORES
    shard_rows = events_ref.shape[0] // lax.axis_size("fsdp")
    part_rows = shard_rows // chips
    chip, here = lax.div(lax.axis_index("dp"), CORES), lax.axis_index("fsdp")
    for flips, term_ref, other_ref in zip(sets, outs[::2], outs[1::2]):
        at = 0
        for side, picks in enumerate(gradient_picks(chips, flips)):
            first = at
            for k, _, z in picks:
                start = (here ^ z) * shard_rows + (chip ^ k) * part_rows
                source = pl.ds(pl.multiple_of(start, part_rows), part_rows)
                picked_ref[at : at + part_rows] = events_ref[source, :rows]
                other_ref[at : at + part_rows] = events_ref[source, rows:]
                at += part_rows
            columns = half_columns(side, half)
            term_ref[first:at] = dot(picked_ref[first:at], grad_query_ref[:, columns])


def gradient_kernel(order, flips, _, term_ref, events_ref, grad_query_ref, *outs):
    half = term_ref.shape[1]
    part_rows = outs[0].shape[0]
    out_of = dict(zip(order, outs))
    at = 0
    for side, picks in enumerate(gradient_picks(len(order), flips)):
        rows = slice(at, at + len(picks) * part_rows)
        total = term_ref[rows] + dot(events_ref[rows], grad_query_ref[:, half_columns(side, half)])
        for p, (k, i, _) in enumerate(picks):
            block = total[p * part_rows : (p + 1) * part_rows]
            out_of[k][:, i * half : (i + 1) * half] = block.astype(out_of[k].dtype)
        at = rows.stop


def chip_sum_kernel(term_count, _, *refs):
    terms, outs = refs[:term_count], refs[term_count:]
    at = 0
    for out in outs:
        columns = slice(at, at + out.shape[1])
        total = terms[0][:, columns].astype(jnp.float32)
        for term in terms[1:]:
            total = total + term[:, columns].astype(jnp.float32)
        out[...] = total.astype(out.dtype)
        at += out.shape[1]


def mean_kernel(count, _, *refs):
    total = refs[0][...].astype(jnp.float32)
    for term in refs[1:-1]:
        total = total + term[...].astype(jnp.float32)
    refs[-1][...] = (total / count).astype(refs[-1].dtype)


def place_kernel(chips, own_ref, sibling_ref, out_ref, held_ref, sems):
    rows, half = own_ref.shape[0] // chips, own_ref.shape[1]
    core, chip = lax.rem(lax.axis_index("dp"), CORES), lax.div(lax.axis_index("dp"), CORES)
    copies = []
    for k in range(chips):
        place = pl.ds(pl.multiple_of((chip ^ k) * rows, rows), rows)
        for block_ref, side in ((own_ref, core), (sibling_ref, 1 - core)):
            columns = pl.ds(pl.multiple_of((side ^ (1 if k else 0)) * half, half), half)
            block = block_ref[k * rows : (k + 1) * rows]
            held_ref[place, columns] = block.astype(held_ref.dtype)
        copies.append(pltpu.make_async_copy(held_ref.at[place], out_ref.at[place], sems.at[k]))
        copies[k].start()
    for copy in copies:
        copy.wait()


def flip(block, axis, count, bits):
    return lax.ppermute(block, axis, [(i, i ^ bits) for i in range(count)])


def cross(block, dp_count, fsdp_count, chip_bits, shard_bits):
    pairs = [
        (
            d * fsdp_count + z,
            (d ^ (chip_bits * CORES) ^ 1) * fsdp_count + (z ^ shard_bits[d % CORES]),
        )
        for d in range(dp_count)
        for z in range(fsdp_count)
    ]
    return lax.ppermute(block, BOTH, pairs)


def far_first(count, send):
    return [send(k) for k in range(count - 1, 0, -1)][::-1]


def shard_pairs(fsdp_count):
    others = [d for d in range(1, fsdp_count) if d != fsdp_count // 2]
    return list(zip(others[::2], others[1::2]))


def across_z(weight, dp_count, fsdp_count):
    rows = weight.shape[0]
    group = max(g for g in (2, 4, 8) if dp_count % g == 0 and rows % (16 * g) == 0)
    part = call(
        functools.partial(slice_kernel, group),
        "own_part_of_weight",
        [weight],
        [FAR],
        jax.ShapeDtypeStruct((rows // group, weight.shape[1]), weight.dtype),
        [pltpu.SemaphoreType.DMA],
    )
    weight, part = lax.optimization_barrier((weight, part))
    middle = (fsdp_count // 2,) * CORES
    part = cross(part, dp_count, fsdp_count, 0, middle)
    wholes = [
        (cross(weight, dp_count, fsdp_count, 0, flips), flips[::-1])
        for flips in shard_pairs(fsdp_count)
    ]
    return group, part, wholes


def stack_kernel(_, *refs):
    out_ref = refs[-1]
    rows = refs[0].shape[0]
    for i, block_ref in enumerate(refs[:-1]):
        out_ref[i * rows : (i + 1) * rows] = block_ref[...]


def share(group, part, wholes, ready, dp_count, fsdp_count):
    alike = (0,) * CORES
    parts, members = [part], [1]
    for chip_bits in range(1, group // CORES):
        parts.append(cross(part, dp_count, fsdp_count, chip_bits, alike))
        members.append(CORES * chip_bits)
    if len(parts) > 1:
        rows, columns = part.shape
        part = call(
            stack_kernel,
            "parts_of_weight",
            [ready] + parts,
            [ANYWHERE] + [NEAR] * len(parts),
            jax.ShapeDtypeStruct((len(parts) * rows, columns), part.dtype),
        )
    held = [(part, (fsdp_count // 2,) * CORES, members)]
    for block, flips in wholes:
        held.append((lax.optimization_barrier((block, part))[0], flips, [None]))
    moved = []
    for block, flips, members in held:
        places = [m if m is None else m ^ 1 for m in members]
        moved.append((flip(block, "dp", dp_count, 1), flips[::-1], places))
    return held, moved


def shards(events, query_weight, keys, values, gates, cotangent, lengths):
    slots, span, model_width = events.shape
    width = query_weight.shape[1]
    half_width = width // CORES
    rows = slots * span
    dp_count, fsdp_count = lax.axis_size("dp"), lax.axis_size("fsdp")
    chips = dp_count // CORES
    shard_rows = model_width // fsdp_count
    total_seqs = slots * dp_count * fsdp_count
    bf16, f32 = jnp.bfloat16, jnp.float32

    def shape(*dims, dtype=bf16):
        return jax.ShapeDtypeStruct(dims, dtype)

    flat_events = events.reshape(rows, model_width)
    keys, values, gates, cotangent = (
        a.reshape(rows, width) for a in (keys, values, gates, cotangent)
    )
    sibling_events = flip(flat_events, "dp", dp_count, 1)
    group, part, wholes = across_z(query_weight, dp_count, fsdp_count)
    prepared = call(
        functools.partial(prepare_kernel, slots),
        "prepared_operands",
        [part, lengths, sibling_events]
        + [flat_events, keys, values, cotangent, query_weight, gates],
        [ANYWHERE, FAR, NEAR] + [FAR] * 6,
        (
            shape(rows, model_width),
            shape(rows, width),
            shape(rows, width),
            shape(rows, width),
            shape(shard_rows, width),
            shape(model_width, CORES * rows),
            shape(width, rows),
            shape(width, rows),
            shape(slots, span, span, dtype=f32),
            shape(rows, width, dtype=f32),
            shape(rows, span, dtype=f32),
        ),
        [
            pltpu.VMEM((rows, width), bf16),
            pltpu.SMEM(lengths.shape, jnp.int32),
            pltpu.SemaphoreType.DMA((7,)),
        ],
        flops=5 * 10**9,
    )
    near_events, near_keys, near_values, near_cotangent, near_weight = prepared[:5]
    events_t, keys_t, values_t, weight, gated, first = prepared[5:]
    held, moved = share(group, part, wholes, first, dp_count, fsdp_count)
    held = [(near_weight, (0, 0), [None])] + held
    if not aligned(shard_rows):
        held, moved = [], held + moved

    def split(found):
        return [f[0] for f in found], [f[1:] for f in found]

    terms = []
    if held:
        pieces, origins = split(held)
        terms = [
            call(
                functools.partial(held_projection_kernel, group, shard_rows, origins),
                "projection_by_held_rows",
                pieces + [near_events],
                [NEAR] * (len(pieces) + 1),
                shape(rows, width, dtype=f32),
                projection_scratch(shard_rows, model_width, width, origins),
                flops=2 * rows * width * shard_rows * len(pieces),
                moved=4 * rows * width,
            )
        ]
    pieces, origins = split(moved)
    blocks = shape(slots * HEADS, span, span)
    grad_query, query, normed, grad_mixed, attention, grad_scores = call(
        functools.partial(attention_kernel, slots, group, shard_rows, origins),
        "attention_to_grad_query",
        pieces
        + terms
        + [near_events, near_keys, near_values, keys_t, values_t, weight, gated, first],
        [NEAR] * (len(pieces) + len(terms) + 8),
        (
            shape(rows, width),
            shape(rows, width),
            shape(rows, width, dtype=f32),
            shape(rows, width),
            blocks,
            blocks,
        ),
        projection_scratch(shard_rows, model_width, width, origins),
        flops=2 * rows * width * (model_width + 4 * span),
        moved=24 * rows * width,
    )
    part_rows = shard_rows // chips
    staged = part_rows % 16 == 0 and fsdp_count % 4 == 0
    terms = [grad_query]
    if staged:
        alike = (0,) * CORES

        def to_chip(block, k):
            return cross(block, dp_count, fsdp_count, k, alike)

        orders = (tuple(range(chips)), (0,) + tuple(range(chips - 1, 0, -1)))

        def summed_over_chips(terms, name, which, after):
            flips = sets[which]
            terms = [terms[0]] + [to_chip(a, k) for a, k in zip(terms[1:], orders[which][1:])]
            return call(
                functools.partial(chip_sum_kernel, chips),
                name,
                [after] + terms,
                [ANYWHERE] + [NEAR] * chips,
                tuple(shape(part_rows, half_width, dtype=bf16 if z else f32) for z in flips),
            )

        sets = (tuple(range(2, fsdp_count)), (0, 1))
        picked_rows = [len(flips) * shard_rows for flips in sets]
        got = flip(grad_query, "dp", dp_count, 1)
        own_terms = call(
            functools.partial(own_gradient_kernel, chips, sets),
            "weight_gradient_of_own_events",
            [events_t, grad_query],
            [NEAR] * 2,
            tuple(
                a
                for n in picked_rows
                for a in (shape(n, half_width, dtype=f32), shape(n, rows))
            ),
            [pltpu.VMEM((max(picked_rows), rows), bf16)],
            flops=2 * rows * model_width * half_width,
            moved=8 * model_width * rows,
        )

        def gradient(which, name, after):
            columns = len(sets[which]) * half_width
            return call(
                functools.partial(gradient_kernel, orders[which], sets[which]),
                name,
                [after, *own_terms[2 * which : 2 * which + 2], got],
                [ANYWHERE] + [NEAR] * 3,
                tuple(shape(part_rows, columns, dtype=bf16 if k else f32) for k in orders[which]),
                flops=2 * rows * picked_rows[which] * half_width,
                moved=2 * picked_rows[which] * (rows + 2 * half_width),
            )

        far_terms = gradient(0, "weight_gradient_of_far_shards", got)
        terms = gradient(1, "weight_gradient_of_near_shards", far_terms[0])

        def to_shard(block, z):
            return cross(block, dp_count, fsdp_count, 0, (z,) * CORES)

        far_sums = summed_over_chips(far_terms, "far_shards_over_chips", 0, got)
        own_sum, next_sum = summed_over_chips(
            terms, "near_shards_over_chips", 1, far_sums[0]
        )
        far_sums = [to_shard(a, z) for a, z in reversed(list(zip(far_sums, sets[0])))]
        terms = [next_sum]
        next_sum = to_shard(next_sum, 1)
    grad_keys, grad_values, grad_gates = call(
        functools.partial(outputs_kernel, slots),
        "key_value_gate_gradients",
        [terms[0], query, normed, grad_mixed, attention, grad_scores, near_cotangent],
        [ANYWHERE] + [NEAR] * 6,
        (shape(rows, width),) * 3,
        flops=4 * rows * width * span,
        moved=12 * rows * width,
    )
    if staged:
        mean = call(
            functools.partial(mean_kernel, total_seqs),
            "mean_over_shards",
            [grad_keys, own_sum, next_sum] + far_sums,
            [FAR] + [NEAR] * fsdp_count,
            shape(part_rows, half_width),
        )
        blocks = call(
            stack_kernel,
            "blocks_of_chips",
            [mean, mean] + far_first(chips, lambda k: to_chip(mean, k)),
            [ANYWHERE] + [NEAR] * chips,
            shape(shard_rows, half_width),
        )
        grad_weight = call(
            functools.partial(place_kernel, chips),
            "blocks_in_place",
            [blocks, flip(blocks, "dp", dp_count, 1)],
            [NEAR] * 2,
            shape(shard_rows, width, dtype=f32),
            [pltpu.VMEM((shard_rows, width), f32), pltpu.SemaphoreType.DMA((chips,))],
            out_specs=FAR,
        )
    else:
        whole = lax.dot_general(flat_events, grad_query, FIRST, preferred_element_type=f32)
        mine = lax.psum_scatter(whole, "fsdp", scatter_dimension=0, tiled=True)
        grad_weight = lax.psum(mine, "dp") / total_seqs

    full = (slots, span, width)
    return (
        grad_keys.reshape(full),
        grad_values.reshape(full),
        grad_gates.reshape(full),
        grad_weight,
    )


def solution(mesh):
    split = P(BOTH, None, None)
    return jax.shard_map(
        shards,
        mesh=mesh,
        in_specs=(split, P("fsdp", None), split, split, split, split, P()),
        out_specs=(split, split, split, P("fsdp", None)),
        check_vma=False,
    )
```

```python
import functools
import math

import jax
import jax.numpy as jnp
from jax import lax
from jax.experimental import pallas as pl
from jax.experimental.pallas import tpu as pltpu
from jax.sharding import PartitionSpec as P

HEADS = 4
EPSILON = 1e-06
CORES = 2
BOTH = ("dp", "fsdp")
VMEM_LIMIT = 24 * 1024 * 1024

LAST = (((1,), (1,)), ((), ()))
FIRST = (((0,), (0,)), ((), ()))


def dot(lhs, rhs, dims=(((1,), (0,)), ((), ()))):
    return lax.dot_general(lhs, rhs, dims, preferred_element_type=jnp.float32)


def call(kernel, name, operands, in_specs, out_shape, scratch=(), flops=0, moved=0,
         out_specs=None, aliases=None):
    vmem = pl.BlockSpec(memory_space=pltpu.VMEM)
    many = isinstance(out_shape, tuple)
    operands = [
        pltpu.with_memory_space_constraint(a, pltpu.HBM) if spec is FAR else a
        for a, spec in zip(operands, in_specs)
    ]
    return pl.pallas_call(
        kernel,
        out_shape=out_shape,
        in_specs=in_specs,
        out_specs=out_specs or ((vmem,) * len(out_shape) if many else vmem),
        scratch_shapes=list(scratch),
        input_output_aliases=aliases or {},
        compiler_params=pltpu.CompilerParams(vmem_limit_bytes=VMEM_LIMIT),
        cost_estimate=pl.CostEstimate(flops=flops, bytes_accessed=moved, transcendentals=0),
        name=name,
    )(*operands)


NEAR = pl.BlockSpec(memory_space=pltpu.VMEM)
ANYWHERE = pl.BlockSpec(memory_space=pl.ANY)
FAR = pl.BlockSpec(memory_space=pltpu.HBM)


def head_columns(width):
    depth = width // HEADS
    return [slice(h * depth, (h + 1) * depth) for h in range(HEADS)]


def slot_rows(rows, slots):
    span = rows // slots
    return [slice(s * span, (s + 1) * span) for s in range(slots)]


def row_mean(blocks, width):
    return jnp.sum(sum(blocks[1:], blocks[0]), axis=1, keepdims=True) / width


def slice_kernel(group, block_ref, out_ref, sem):
    rows = out_ref.shape[0]
    start = pl.multiple_of(lax.rem(lax.axis_index("dp"), group) * rows, rows)
    copy = pltpu.make_async_copy(block_ref.at[pl.ds(start, rows)], out_ref, sem)
    copy.start()
    copy.wait()


def prepare_kernel(slots, _, lengths_ref, sibling_ref, *refs):
    inputs, held = refs[:6], refs[6:11]
    (events_t_ref, key_t_ref, value_t_ref, weight_ref, gated_ref, first_ref,
     gate_ref, own_lengths_ref, sems) = refs[11:]
    events_ref, key_ref, value_ref, upstream_ref, _ = held
    copies = [
        pltpu.make_async_copy(source, target, sems.at[i])
        for i, (source, target) in enumerate(zip(inputs, held + (gate_ref,)))
    ]
    copies.append(pltpu.make_async_copy(lengths_ref, own_lengths_ref, sems.at[len(copies)]))
    for copy in copies:
        copy.start()
    rows, width = key_ref.shape
    events_t_ref[:, rows:] = sibling_ref[...].T
    for copy in copies:
        copy.wait()
    events_t_ref[:, :rows] = events_ref[...].T
    key_t_ref[...] = key_ref[...].T
    value_t_ref[...] = value_ref[...].T
    span = rows // slots
    row = lax.broadcasted_iota(jnp.int32, (span, span), 0)
    column = lax.broadcasted_iota(jnp.int32, (span, span), 1)
    first_slot = (lax.axis_index("dp") * lax.axis_size("fsdp") + lax.axis_index("fsdp")) * slots
    for s, place in enumerate(slot_rows(rows, slots)):
        length = own_lengths_ref[first_slot + s]
        inverse = 1.0 / jnp.full((span, span), length, jnp.int32).astype(jnp.float32)
        weight_ref[s] = jnp.where((column <= row) & (row < length), inverse, 0.0)
        live = lax.broadcasted_iota(jnp.int32, (span, width), 0) < length
        gated = upstream_ref[place].astype(jnp.float32) * gate_ref[place].astype(jnp.float32)
        gated = jnp.where(live, gated, 0.0)
        gated_ref[place] = gated
        first = row_mean([gated[:, c] for c in head_columns(width)], width)
        first_ref[place] = jnp.broadcast_to(first, (span, first_ref.shape[1]))


def piece_start(shard_rows, group, part_rows, flips, member_flip):
    device = lax.axis_index("dp")
    start = (
        lax.axis_index("fsdp") ^ jnp.where(lax.rem(device, CORES) == 0, flips[0], flips[1])
    ) * shard_rows
    if member_flip is not None:
        start = start + (lax.rem(device, group) ^ member_flip) * part_rows
    return pl.multiple_of(start, 16)


def aligned(shard_rows):
    return shard_rows % 128 == 0


def project(events_ref, pieces, origins, group, shard_rows, spare_ref, sems):
    copies, total = [], None
    for piece, (flips, members) in zip(pieces, origins):
        rows = piece.shape[0] // len(members)
        starts = [piece_start(shard_rows, group, rows, flips, m) for m in members]
        if not aligned(shard_rows):
            for i, start in enumerate(starts):
                copy = pltpu.make_async_copy(
                    piece.at[pl.ds(i * rows, rows)],
                    spare_ref.at[pl.ds(start, rows)],
                    sems.at[len(copies)],
                )
                copy.start()
                copies.append(copy)
            continue
        first = piece_start(shard_rows, group, rows, flips, None)
        if len(members) > 1:
            spare_ref[...] = jnp.zeros_like(spare_ref)
            for i, start in enumerate(starts):
                place = pl.ds(pl.multiple_of(start - first, 16), rows)
                spare_ref[place] = piece[i * rows : (i + 1) * rows]
            piece = spare_ref
        columns = pl.ds(pl.multiple_of(first, 128), shard_rows)
        term = dot(events_ref[:, columns], piece[...])
        total = term if total is None else total + term
    if copies:
        for copy in copies:
            copy.wait()
        total = dot(events_ref[...], spare_ref[...])
    return total


def projection_scratch(shard_rows, model_width, width, origins):
    count = sum(len(members) for _, members in origins)
    spare_rows = shard_rows if aligned(shard_rows) else model_width
    return [pltpu.VMEM((spare_rows, width), jnp.bfloat16), pltpu.SemaphoreType.DMA((count,))]


def held_projection_kernel(group, shard_rows, origins, *refs):
    pieces, (events_ref, out_ref, spare_ref, sems) = refs[: len(origins)], refs[len(origins) :]
    out_ref[...] = project(events_ref, pieces, origins, group, shard_rows, spare_ref, sems)


def attention_kernel(slots, group, shard_rows, origins, *refs):
    pieces = refs[: len(origins)]
    terms, refs = refs[len(origins) : -16], refs[-16:]
    (events_ref, key_ref, value_ref, key_t_ref, value_t_ref, weight_ref, gated_ref, first_ref,
     grad_query_ref, query_ref, normed_ref, mixed_grad_ref, attention_ref, scores_grad_ref,
     spare_ref, sems) = refs
    query = project(events_ref, pieces, origins, group, shard_rows, spare_ref, sems)
    for term in terms:
        query = query + term[...]
    query_ref[...] = query.astype(jnp.bfloat16)

    rows, width = key_ref.shape
    scale = 1.0 / math.sqrt(width // HEADS)
    columns = head_columns(width)
    places = slot_rows(rows, slots)
    each = [(s, h, s * HEADS + h) for s in range(slots) for h in range(HEADS)]
    slopes, mixed, grad_mixed = [], [], []
    for s, h, i in each:
        scores = dot(query_ref[places[s], columns[h]], key_t_ref[columns[h], places[s]]) * scale
        sigmoid = 1.0 / (1.0 + jnp.exp(-scores))
        silu = scores * sigmoid
        attention_ref[i] = (silu * weight_ref[s]).astype(jnp.bfloat16)
        slopes.append((sigmoid + silu * (1.0 - sigmoid)) * weight_ref[s])
    for s, h, i in each:
        mixed.append(dot(attention_ref[i], value_ref[places[s], columns[h]]))
    for s in range(slots):
        own = mixed[s * HEADS : (s + 1) * HEADS]
        mean = row_mean(own, width)
        centred = [m - mean for m in own]
        inv_std = lax.rsqrt(row_mean([c * c for c in centred], width) + EPSILON)
        normed = [c * inv_std for c in centred]
        gated = [gated_ref[places[s], c] for c in columns]
        second = row_mean([g * n for g, n in zip(gated, normed)], width)
        first = first_ref[places[s]]
        for h in range(HEADS):
            normed_ref[places[s], columns[h]] = normed[h]
            grad = inv_std * (gated[h] - first - normed[h] * second)
            mixed_grad_ref[places[s], columns[h]] = grad.astype(jnp.bfloat16)
    for s, h, i in each:
        grad_attention = dot(
            mixed_grad_ref[places[s], columns[h]], value_t_ref[columns[h], places[s]]
        )
        scores_grad_ref[i] = (grad_attention * slopes[i]).astype(jnp.bfloat16)
    for s, h, i in each:
        grad_query = dot(scores_grad_ref[i], key_ref[places[s], columns[h]]) * scale
        grad_query_ref[places[s], columns[h]] = grad_query.astype(jnp.bfloat16)


def outputs_kernel(slots, _, query_ref, normed_ref, mixed_grad_ref, attention_ref, scores_grad_ref,
                   upstream_ref, grad_key_ref, grad_value_ref, grad_gate_ref):
    rows, width = query_ref.shape
    scale = 1.0 / math.sqrt(width // HEADS)
    columns = head_columns(width)
    places = slot_rows(rows, slots)
    grad_gate_ref[...] = (upstream_ref[...].astype(jnp.float32) * normed_ref[...]).astype(
        jnp.bfloat16
    )
    for s in range(slots):
        for h in range(HEADS):
            i = s * HEADS + h
            grad_value = dot(attention_ref[i], mixed_grad_ref[places[s], columns[h]], FIRST)
            grad_value_ref[places[s], columns[h]] = grad_value.astype(jnp.bfloat16)
            grad_key = dot(scores_grad_ref[i], query_ref[places[s], columns[h]], FIRST) * scale
            grad_key_ref[places[s], columns[h]] = grad_key.astype(jnp.bfloat16)


def summing_half(k, z):
    return lax.rem(lax.axis_index("dp"), CORES) ^ (1 if k else 0) ^ (1 if z else 0)


def gradient_picks(chips, shard_flips):
    every = [(k, i, z) for k in range(chips) for i, z in enumerate(shard_flips)]
    return [[p for p in every if (p[0] != 0) ^ (p[2] != 0) == bool(side)] for side in range(CORES)]


def half_columns(side, half):
    return pl.ds(pl.multiple_of(summing_half(side, 0) * half, half), half)


def own_gradient_kernel(chips, sets, events_ref, grad_query_ref, *refs):
    outs, picked_ref = refs[:-1], refs[-1]
    rows, half = grad_query_ref.shape[0], grad_query_ref.shape[1] // CORES
    shard_rows = events_ref.shape[0] // lax.axis_size("fsdp")
    part_rows = shard_rows // chips
    chip, here = lax.div(lax.axis_index("dp"), CORES), lax.axis_index("fsdp")
    for flips, term_ref, other_ref in zip(sets, outs[::2], outs[1::2]):
        at = 0
        for side, picks in enumerate(gradient_picks(chips, flips)):
            first = at
            for k, _, z in picks:
                start = (here ^ z) * shard_rows + (chip ^ k) * part_rows
                source = pl.ds(pl.multiple_of(start, part_rows), part_rows)
                picked_ref[at : at + part_rows] = events_ref[source, :rows]
                other_ref[at : at + part_rows] = events_ref[source, rows:]
                at += part_rows
            columns = half_columns(side, half)
            term_ref[first:at] = dot(picked_ref[first:at], grad_query_ref[:, columns])


def gradient_kernel(order, flips, _, term_ref, events_ref, grad_query_ref, *outs):
    half = term_ref.shape[1]
    part_rows = outs[0].shape[0]
    out_of = dict(zip(order, outs))
    at = 0
    for side, picks in enumerate(gradient_picks(len(order), flips)):
        rows = slice(at, at + len(picks) * part_rows)
        total = term_ref[rows] + dot(events_ref[rows], grad_query_ref[:, half_columns(side, half)])
        for p, (k, i, _) in enumerate(picks):
            block = total[p * part_rows : (p + 1) * part_rows]
            out_of[k][:, i * half : (i + 1) * half] = block.astype(out_of[k].dtype)
        at = rows.stop


def chip_sum_kernel(term_count, _, *refs):
    terms, outs = refs[:term_count], refs[term_count:]
    at = 0
    for out in outs:
        columns = slice(at, at + out.shape[1])
        total = terms[0][:, columns].astype(jnp.float32)
        for term in terms[1:]:
            total = total + term[:, columns].astype(jnp.float32)
        out[...] = total.astype(out.dtype)
        at += out.shape[1]


def mean_kernel(count, _, *refs):
    total = refs[0][...].astype(jnp.float32)
    for term in refs[1:-1]:
        total = total + term[...].astype(jnp.float32)
    refs[-1][...] = (total / count).astype(refs[-1].dtype)


def place_kernel(side, chips, blocks_ref, *refs):
    out_ref, held_ref, sems = refs[-3:]
    rows, half = blocks_ref.shape[0] // chips, blocks_ref.shape[1]
    core, chip = lax.rem(lax.axis_index("dp"), CORES) ^ side, lax.div(lax.axis_index("dp"), CORES)
    held_ref[...] = blocks_ref[...].astype(held_ref.dtype)
    copies = []
    for k in range(chips):
        place = pl.ds(pl.multiple_of((chip ^ k) * rows, rows), rows)
        columns = pl.ds(pl.multiple_of((core ^ (1 if k else 0)) * half, half), half)
        block = held_ref.at[pl.ds(k * rows, rows)]
        copies.append(pltpu.make_async_copy(block, out_ref.at[place, columns], sems.at[k]))
        copies[k].start()
    for copy in copies:
        copy.wait()


def flip(block, axis, count, bits):
    return lax.ppermute(block, axis, [(i, i ^ bits) for i in range(count)])


def cross(block, dp_count, fsdp_count, chip_bits, shard_bits):
    pairs = [
        (
            d * fsdp_count + z,
            (d ^ (chip_bits * CORES) ^ 1) * fsdp_count + (z ^ shard_bits[d % CORES]),
        )
        for d in range(dp_count)
        for z in range(fsdp_count)
    ]
    return lax.ppermute(block, BOTH, pairs)


def far_first(count, send):
    return [send(k) for k in range(count - 1, 0, -1)][::-1]


def shard_pairs(fsdp_count):
    others = [d for d in range(1, fsdp_count) if d != fsdp_count // 2]
    return list(zip(others[::2], others[1::2]))


def across_z(weight, dp_count, fsdp_count):
    rows = weight.shape[0]
    group = max(g for g in (2, 4, 8) if dp_count % g == 0 and rows % (16 * g) == 0)
    part = call(
        functools.partial(slice_kernel, group),
        "own_part_of_weight",
        [weight],
        [FAR],
        jax.ShapeDtypeStruct((rows // group, weight.shape[1]), weight.dtype),
        [pltpu.SemaphoreType.DMA],
    )
    weight, part = lax.optimization_barrier((weight, part))
    middle = (fsdp_count // 2,) * CORES
    part = cross(part, dp_count, fsdp_count, 0, middle)
    wholes = [
        (cross(weight, dp_count, fsdp_count, 0, flips), flips[::-1])
        for flips in shard_pairs(fsdp_count)
    ]
    return group, part, wholes


def stack_kernel(_, *refs):
    out_ref = refs[-1]
    rows = refs[0].shape[0]
    for i, block_ref in enumerate(refs[:-1]):
        out_ref[i * rows : (i + 1) * rows] = block_ref[...]


def share(group, part, wholes, ready, dp_count, fsdp_count):
    alike = (0,) * CORES
    parts, members = [part], [1]
    for chip_bits in range(1, group // CORES):
        parts.append(cross(part, dp_count, fsdp_count, chip_bits, alike))
        members.append(CORES * chip_bits)
    if len(parts) > 1:
        rows, columns = part.shape
        part = call(
            stack_kernel,
            "parts_of_weight",
            [ready] + parts,
            [ANYWHERE] + [NEAR] * len(parts),
            jax.ShapeDtypeStruct((len(parts) * rows, columns), part.dtype),
        )
    held = [(part, (fsdp_count // 2,) * CORES, members)]
    for block, flips in wholes:
        held.append((lax.optimization_barrier((block, part))[0], flips, [None]))
    moved = []
    for block, flips, members in held:
        places = [m if m is None else m ^ 1 for m in members]
        moved.append((flip(block, "dp", dp_count, 1), flips[::-1], places))
    return held, moved


def shards(events, query_weight, keys, values, gates, cotangent, lengths):
    slots, span, model_width = events.shape
    width = query_weight.shape[1]
    half_width = width // CORES
    rows = slots * span
    dp_count, fsdp_count = lax.axis_size("dp"), lax.axis_size("fsdp")
    chips = dp_count // CORES
    shard_rows = model_width // fsdp_count
    total_seqs = slots * dp_count * fsdp_count
    bf16, f32 = jnp.bfloat16, jnp.float32

    def shape(*dims, dtype=bf16):
        return jax.ShapeDtypeStruct(dims, dtype)

    flat_events = events.reshape(rows, model_width)
    keys, values, gates, cotangent = (
        a.reshape(rows, width) for a in (keys, values, gates, cotangent)
    )
    sibling_events = flip(flat_events, "dp", dp_count, 1)
    group, part, wholes = across_z(query_weight, dp_count, fsdp_count)
    prepared = call(
        functools.partial(prepare_kernel, slots),
        "prepared_operands",
        [part, lengths, sibling_events]
        + [flat_events, keys, values, cotangent, query_weight, gates],
        [ANYWHERE, FAR, NEAR] + [FAR] * 6,
        (
            shape(rows, model_width),
            shape(rows, width),
            shape(rows, width),
            shape(rows, width),
            shape(shard_rows, width),
            shape(model_width, CORES * rows),
            shape(width, rows),
            shape(width, rows),
            shape(slots, span, span, dtype=f32),
            shape(rows, width, dtype=f32),
            shape(rows, span, dtype=f32),
        ),
        [
            pltpu.VMEM((rows, width), bf16),
            pltpu.SMEM(lengths.shape, jnp.int32),
            pltpu.SemaphoreType.DMA((7,)),
        ],
        flops=5 * 10**9,
    )
    near_events, near_keys, near_values, near_cotangent, near_weight = prepared[:5]
    events_t, keys_t, values_t, weight, gated, first = prepared[5:]
    held, moved = share(group, part, wholes, first, dp_count, fsdp_count)
    held = [(near_weight, (0, 0), [None])] + held
    if not aligned(shard_rows):
        held, moved = [], held + moved

    def split(found):
        return [f[0] for f in found], [f[1:] for f in found]

    terms = []
    if held:
        pieces, origins = split(held)
        terms = [
            call(
                functools.partial(held_projection_kernel, group, shard_rows, origins),
                "projection_by_held_rows",
                pieces + [near_events],
                [NEAR] * (len(pieces) + 1),
                shape(rows, width, dtype=f32),
                projection_scratch(shard_rows, model_width, width, origins),
                flops=2 * rows * width * shard_rows * len(pieces),
                moved=4 * rows * width,
            )
        ]
    pieces, origins = split(moved)
    blocks = shape(slots * HEADS, span, span)
    grad_query, query, normed, grad_mixed, attention, grad_scores = call(
        functools.partial(attention_kernel, slots, group, shard_rows, origins),
        "attention_to_grad_query",
        pieces
        + terms
        + [near_events, near_keys, near_values, keys_t, values_t, weight, gated, first],
        [NEAR] * (len(pieces) + len(terms) + 8),
        (
            shape(rows, width),
            shape(rows, width),
            shape(rows, width, dtype=f32),
            shape(rows, width),
            blocks,
            blocks,
        ),
        projection_scratch(shard_rows, model_width, width, origins),
        flops=2 * rows * width * (model_width + 4 * span),
        moved=24 * rows * width,
    )
    part_rows = shard_rows // chips
    staged = part_rows % 16 == 0 and fsdp_count % 4 == 0
    terms = [grad_query]
    if staged:
        alike = (0,) * CORES

        def to_chip(block, k):
            return cross(block, dp_count, fsdp_count, k, alike)

        order = (0,) + tuple(range(chips - 1, 0, -1))

        def summed_over_chips(terms, name, which, after):
            flips = sets[which]
            terms = [terms[0]] + [to_chip(a, k) for a, k in zip(terms[1:], order[1:])]
            return call(
                functools.partial(chip_sum_kernel, chips),
                name,
                [after] + terms,
                [ANYWHERE] + [NEAR] * chips,
                tuple(shape(part_rows, half_width, dtype=bf16 if z else f32) for z in flips),
            )

        sets = (tuple(range(2, fsdp_count)), (0, 1))
        picked_rows = [len(flips) * shard_rows for flips in sets]
        got = flip(grad_query, "dp", dp_count, 1)
        own_terms = call(
            functools.partial(own_gradient_kernel, chips, sets),
            "weight_gradient_of_own_events",
            [events_t, grad_query],
            [NEAR] * 2,
            tuple(
                a
                for n in picked_rows
                for a in (shape(n, half_width, dtype=f32), shape(n, rows))
            ),
            [pltpu.VMEM((max(picked_rows), rows), bf16)],
            flops=2 * rows * model_width * half_width,
            moved=8 * model_width * rows,
        )

        def gradient(which, name, after):
            columns = len(sets[which]) * half_width
            return call(
                functools.partial(gradient_kernel, order, sets[which]),
                name,
                [after, *own_terms[2 * which : 2 * which + 2], got],
                [ANYWHERE] + [NEAR] * 3,
                tuple(shape(part_rows, columns, dtype=bf16 if k else f32) for k in order),
                flops=2 * rows * picked_rows[which] * half_width,
                moved=2 * picked_rows[which] * (rows + 2 * half_width),
            )

        far_terms = gradient(0, "weight_gradient_of_far_shards", got)
        terms = gradient(1, "weight_gradient_of_near_shards", far_terms[0])

        def to_shard(block, z):
            return cross(block, dp_count, fsdp_count, 0, (z,) * CORES)

        far_sums = summed_over_chips(far_terms, "far_shards_over_chips", 0, got)
        own_sum, next_sum = summed_over_chips(
            terms, "near_shards_over_chips", 1, far_sums[0]
        )
        far_sums = [to_shard(a, z) for a, z in reversed(list(zip(far_sums, sets[0])))]
        terms = [next_sum]
        next_sum = to_shard(next_sum, 1)
    grad_keys, grad_values, grad_gates = call(
        functools.partial(outputs_kernel, slots),
        "key_value_gate_gradients",
        [terms[0], query, normed, grad_mixed, attention, grad_scores, near_cotangent],
        [ANYWHERE] + [NEAR] * 6,
        (shape(rows, width),) * 3,
        flops=4 * rows * width * span,
        moved=12 * rows * width,
    )
    if staged:
        mean = call(
            functools.partial(mean_kernel, total_seqs),
            "mean_over_shards",
            [grad_keys, own_sum, next_sum] + far_sums,
            [FAR] + [NEAR] * fsdp_count,
            shape(part_rows, half_width),
        )
        blocks = call(
            stack_kernel,
            "blocks_of_chips",
            [mean, mean] + far_first(chips, lambda k: to_chip(mean, k)),
            [ANYWHERE] + [NEAR] * chips,
            shape(shard_rows, half_width),
        )
        grad_weight = ()
        for side in range(CORES):
            grad_weight = call(
                functools.partial(place_kernel, side, chips),
                f"blocks_of_{'sibling' if side else 'own'}_core_in_place",
                [flip(blocks, "dp", dp_count, 1) if side else blocks, *grad_weight],
                [NEAR] + [FAR] * side,
                shape(shard_rows, width, dtype=f32),
                [
                    pltpu.VMEM((shard_rows, half_width), f32),
                    pltpu.SemaphoreType.DMA((chips,)),
                ],
                out_specs=FAR,
                aliases={1: 0} if side else {},
            )
            grad_weight = grad_weight if side else (grad_weight,)
    else:
        whole = lax.dot_general(flat_events, grad_query, FIRST, preferred_element_type=f32)
        mine = lax.psum_scatter(whole, "fsdp", scatter_dimension=0, tiled=True)
        grad_weight = lax.psum(mine, "dp") / total_seqs

    full = (slots, span, width)
    return (
        grad_keys.reshape(full),
        grad_values.reshape(full),
        grad_gates.reshape(full),
        grad_weight,
    )


def solution(mesh):
    split = P(BOTH, None, None)
    return jax.shard_map(
        shards,
        mesh=mesh,
        in_specs=(split, P("fsdp", None), split, split, split, split, P()),
        out_specs=(split, split, split, P("fsdp", None)),
        check_vma=False,
    )
```

```python
import functools
import math

import jax
import jax.numpy as jnp
from jax import lax
from jax.experimental import pallas as pl
from jax.experimental.pallas import tpu as pltpu
from jax.sharding import PartitionSpec as P

HEADS = 4
EPSILON = 1e-06
CORES = 2
BOTH = ("dp", "fsdp")
VMEM_LIMIT = 24 * 1024 * 1024

LAST = (((1,), (1,)), ((), ()))
FIRST = (((0,), (0,)), ((), ()))


def dot(lhs, rhs, dims=(((1,), (0,)), ((), ()))):
    return lax.dot_general(lhs, rhs, dims, preferred_element_type=jnp.float32)


def call(kernel, name, operands, in_specs, out_shape, scratch=(), flops=0, moved=0,
         out_specs=None, aliases=None):
    vmem = pl.BlockSpec(memory_space=pltpu.VMEM)
    many = isinstance(out_shape, tuple)
    operands = [
        pltpu.with_memory_space_constraint(a, pltpu.HBM) if spec is FAR else a
        for a, spec in zip(operands, in_specs)
    ]
    return pl.pallas_call(
        kernel,
        out_shape=out_shape,
        in_specs=in_specs,
        out_specs=out_specs or ((vmem,) * len(out_shape) if many else vmem),
        scratch_shapes=list(scratch),
        input_output_aliases=aliases or {},
        compiler_params=pltpu.CompilerParams(vmem_limit_bytes=VMEM_LIMIT),
        cost_estimate=pl.CostEstimate(flops=flops, bytes_accessed=moved, transcendentals=0),
        name=name,
    )(*operands)


NEAR = pl.BlockSpec(memory_space=pltpu.VMEM)
ANYWHERE = pl.BlockSpec(memory_space=pl.ANY)
FAR = pl.BlockSpec(memory_space=pltpu.HBM)


def head_columns(width):
    depth = width // HEADS
    return [slice(h * depth, (h + 1) * depth) for h in range(HEADS)]


def slot_rows(rows, slots):
    span = rows // slots
    return [slice(s * span, (s + 1) * span) for s in range(slots)]


def row_mean(blocks, width):
    return jnp.sum(sum(blocks[1:], blocks[0]), axis=1, keepdims=True) / width


def slice_kernel(group, block_ref, out_ref, sem):
    rows = out_ref.shape[0]
    start = pl.multiple_of(lax.rem(lax.axis_index("dp"), group) * rows, rows)
    copy = pltpu.make_async_copy(block_ref.at[pl.ds(start, rows)], out_ref, sem)
    copy.start()
    copy.wait()


def prepare_kernel(slots, _, lengths_ref, sibling_ref, *refs):
    inputs, held = refs[:6], refs[6:11]
    (events_t_ref, key_t_ref, value_t_ref, weight_ref, gated_ref, first_ref,
     gate_ref, own_lengths_ref, sems) = refs[11:]
    events_ref, key_ref, value_ref, upstream_ref, _ = held
    copies = [
        pltpu.make_async_copy(source, target, sems.at[i])
        for i, (source, target) in enumerate(zip(inputs, held + (gate_ref,)))
    ]
    copies.append(pltpu.make_async_copy(lengths_ref, own_lengths_ref, sems.at[len(copies)]))
    for copy in copies:
        copy.start()
    rows, width = key_ref.shape
    events_t_ref[:, rows:] = sibling_ref[...].T
    for copy in copies:
        copy.wait()
    events_t_ref[:, :rows] = events_ref[...].T
    key_t_ref[...] = key_ref[...].T
    value_t_ref[...] = value_ref[...].T
    span = rows // slots
    row = lax.broadcasted_iota(jnp.int32, (span, span), 0)
    column = lax.broadcasted_iota(jnp.int32, (span, span), 1)
    first_slot = (lax.axis_index("dp") * lax.axis_size("fsdp") + lax.axis_index("fsdp")) * slots
    for s, place in enumerate(slot_rows(rows, slots)):
        length = own_lengths_ref[first_slot + s]
        inverse = 1.0 / jnp.full((span, span), length, jnp.int32).astype(jnp.float32)
        weight_ref[s] = jnp.where((column <= row) & (row < length), inverse, 0.0)
        live = lax.broadcasted_iota(jnp.int32, (span, width), 0) < length
        gated = upstream_ref[place].astype(jnp.float32) * gate_ref[place].astype(jnp.float32)
        gated = jnp.where(live, gated, 0.0)
        gated_ref[place] = gated
        first = row_mean([gated[:, c] for c in head_columns(width)], width)
        first_ref[place] = jnp.broadcast_to(first, (span, first_ref.shape[1]))


def piece_start(shard_rows, group, part_rows, flips, member_flip):
    device = lax.axis_index("dp")
    start = (
        lax.axis_index("fsdp") ^ jnp.where(lax.rem(device, CORES) == 0, flips[0], flips[1])
    ) * shard_rows
    if member_flip is not None:
        start = start + (lax.rem(device, group) ^ member_flip) * part_rows
    return pl.multiple_of(start, 16)


def aligned(shard_rows):
    return shard_rows % 128 == 0


def project(events_ref, pieces, origins, group, shard_rows, spare_ref, sems):
    copies, total = [], None
    for piece, (flips, members) in zip(pieces, origins):
        rows = piece.shape[0] // len(members)
        starts = [piece_start(shard_rows, group, rows, flips, m) for m in members]
        if not aligned(shard_rows):
            for i, start in enumerate(starts):
                copy = pltpu.make_async_copy(
                    piece.at[pl.ds(i * rows, rows)],
                    spare_ref.at[pl.ds(start, rows)],
                    sems.at[len(copies)],
                )
                copy.start()
                copies.append(copy)
            continue
        first = piece_start(shard_rows, group, rows, flips, None)
        if len(members) > 1:
            spare_ref[...] = jnp.zeros_like(spare_ref)
            for i, start in enumerate(starts):
                place = pl.ds(pl.multiple_of(start - first, 16), rows)
                spare_ref[place] = piece[i * rows : (i + 1) * rows]
            piece = spare_ref
        columns = pl.ds(pl.multiple_of(first, 128), shard_rows)
        term = dot(events_ref[:, columns], piece[...])
        total = term if total is None else total + term
    if copies:
        for copy in copies:
            copy.wait()
        total = dot(events_ref[...], spare_ref[...])
    return total


def projection_scratch(shard_rows, model_width, width, origins):
    count = sum(len(members) for _, members in origins)
    spare_rows = shard_rows if aligned(shard_rows) else model_width
    return [pltpu.VMEM((spare_rows, width), jnp.bfloat16), pltpu.SemaphoreType.DMA((count,))]


def held_projection_kernel(group, shard_rows, origins, *refs):
    pieces, (events_ref, out_ref, spare_ref, sems) = refs[: len(origins)], refs[len(origins) :]
    out_ref[...] = project(events_ref, pieces, origins, group, shard_rows, spare_ref, sems)


def attention_kernel(slots, group, shard_rows, origins, *refs):
    pieces = refs[: len(origins)]
    terms, refs = refs[len(origins) : -16], refs[-16:]
    (events_ref, key_ref, value_ref, key_t_ref, value_t_ref, weight_ref, gated_ref, first_ref,
     grad_query_ref, query_ref, normed_ref, mixed_grad_ref, attention_ref, scores_grad_ref,
     spare_ref, sems) = refs
    query = project(events_ref, pieces, origins, group, shard_rows, spare_ref, sems)
    for term in terms:
        query = query + term[...]
    query_ref[...] = query.astype(jnp.bfloat16)

    rows, width = key_ref.shape
    scale = 1.0 / math.sqrt(width // HEADS)
    columns = head_columns(width)
    places = slot_rows(rows, slots)
    each = [(s, h, s * HEADS + h) for s in range(slots) for h in range(HEADS)]
    slopes, mixed, grad_mixed = [], [], []
    for s, h, i in each:
        scores = dot(query_ref[places[s], columns[h]], key_t_ref[columns[h], places[s]]) * scale
        sigmoid = 1.0 / (1.0 + jnp.exp(-scores))
        silu = scores * sigmoid
        attention_ref[i] = (silu * weight_ref[s]).astype(jnp.bfloat16)
        slopes.append((sigmoid + silu * (1.0 - sigmoid)) * weight_ref[s])
    for s, h, i in each:
        mixed.append(dot(attention_ref[i], value_ref[places[s], columns[h]]))
    for s in range(slots):
        own = mixed[s * HEADS : (s + 1) * HEADS]
        mean = row_mean(own, width)
        centred = [m - mean for m in own]
        inv_std = lax.rsqrt(row_mean([c * c for c in centred], width) + EPSILON)
        normed = [c * inv_std for c in centred]
        gated = [gated_ref[places[s], c] for c in columns]
        second = row_mean([g * n for g, n in zip(gated, normed)], width)
        first = first_ref[places[s]]
        for h in range(HEADS):
            normed_ref[places[s], columns[h]] = normed[h]
            grad = inv_std * (gated[h] - first - normed[h] * second)
            mixed_grad_ref[places[s], columns[h]] = grad.astype(jnp.bfloat16)
    for s, h, i in each:
        grad_attention = dot(
            mixed_grad_ref[places[s], columns[h]], value_t_ref[columns[h], places[s]]
        )
        scores_grad_ref[i] = (grad_attention * slopes[i]).astype(jnp.bfloat16)
    for s, h, i in each:
        grad_query = dot(scores_grad_ref[i], key_ref[places[s], columns[h]]) * scale
        grad_query_ref[places[s], columns[h]] = grad_query.astype(jnp.bfloat16)


def outputs_kernel(slots, _, query_ref, normed_ref, mixed_grad_ref, attention_ref, scores_grad_ref,
                   upstream_ref, grad_key_ref, grad_value_ref, grad_gate_ref):
    rows, width = query_ref.shape
    scale = 1.0 / math.sqrt(width // HEADS)
    columns = head_columns(width)
    places = slot_rows(rows, slots)
    grad_gate_ref[...] = (upstream_ref[...].astype(jnp.float32) * normed_ref[...]).astype(
        jnp.bfloat16
    )
    for s in range(slots):
        for h in range(HEADS):
            i = s * HEADS + h
            grad_value = dot(attention_ref[i], mixed_grad_ref[places[s], columns[h]], FIRST)
            grad_value_ref[places[s], columns[h]] = grad_value.astype(jnp.bfloat16)
            grad_key = dot(scores_grad_ref[i], query_ref[places[s], columns[h]], FIRST) * scale
            grad_key_ref[places[s], columns[h]] = grad_key.astype(jnp.bfloat16)


def summing_half(k, z):
    return lax.rem(lax.axis_index("dp"), CORES) ^ (1 if k else 0) ^ (1 if z else 0)


def gradient_picks(chips, shard_flips):
    every = [(k, i, z) for k in range(chips) for i, z in enumerate(shard_flips)]
    return [[p for p in every if (p[0] != 0) ^ (p[2] != 0) == bool(side)] for side in range(CORES)]


def half_columns(side, half):
    return pl.ds(pl.multiple_of(summing_half(side, 0) * half, half), half)


def own_gradient_kernel(chips, sets, events_ref, grad_query_ref, *refs):
    outs, picked_ref = refs[:-1], refs[-1]
    rows, half = grad_query_ref.shape[0], grad_query_ref.shape[1] // CORES
    shard_rows = events_ref.shape[0] // lax.axis_size("fsdp")
    part_rows = shard_rows // chips
    chip, here = lax.div(lax.axis_index("dp"), CORES), lax.axis_index("fsdp")
    for flips, term_ref, other_ref in zip(sets, outs[::2], outs[1::2]):
        at = 0
        for side, picks in enumerate(gradient_picks(chips, flips)):
            first = at
            for k, _, z in picks:
                start = (here ^ z) * shard_rows + (chip ^ k) * part_rows
                source = pl.ds(pl.multiple_of(start, part_rows), part_rows)
                picked_ref[at : at + part_rows] = events_ref[source, :rows]
                other_ref[at : at + part_rows] = events_ref[source, rows:]
                at += part_rows
            columns = half_columns(side, half)
            term_ref[first:at] = dot(picked_ref[first:at], grad_query_ref[:, columns])


def gradient_kernel(order, flips, _, term_ref, events_ref, grad_query_ref, *outs):
    half = term_ref.shape[1]
    part_rows = outs[0].shape[0]
    out_of = dict(zip(order, outs))
    at = 0
    for side, picks in enumerate(gradient_picks(len(order), flips)):
        rows = slice(at, at + len(picks) * part_rows)
        total = term_ref[rows] + dot(events_ref[rows], grad_query_ref[:, half_columns(side, half)])
        for p, (k, i, _) in enumerate(picks):
            block = total[p * part_rows : (p + 1) * part_rows]
            out_of[k][:, i * half : (i + 1) * half] = block.astype(out_of[k].dtype)
        at = rows.stop


def chip_sum_kernel(term_count, _, *refs):
    terms, outs = refs[:term_count], refs[term_count:]
    at = 0
    for out in outs:
        columns = slice(at, at + out.shape[1])
        total = terms[0][:, columns].astype(jnp.float32)
        for term in terms[1:]:
            total = total + term[:, columns].astype(jnp.float32)
        out[...] = total.astype(out.dtype)
        at += out.shape[1]


def mean_kernel(count, _, *refs):
    total = refs[0][...].astype(jnp.float32)
    for term in refs[1:-1]:
        total = total + term[...].astype(jnp.float32)
    refs[-1][...] = (total / count).astype(refs[-1].dtype)


def place_kernel(side, chips, blocks_ref, *refs):
    out_ref, held_ref, sems = refs[-3:]
    rows, half = blocks_ref.shape[0] // chips, blocks_ref.shape[1]
    core, chip = lax.rem(lax.axis_index("dp"), CORES) ^ side, lax.div(lax.axis_index("dp"), CORES)
    held_ref[...] = blocks_ref[...].astype(held_ref.dtype)
    copies = []
    for k in range(chips):
        place = pl.ds(pl.multiple_of((chip ^ k) * rows, rows), rows)
        columns = pl.ds(pl.multiple_of((core ^ (1 if k else 0)) * half, half), half)
        block = held_ref.at[pl.ds(k * rows, rows)]
        copies.append(pltpu.make_async_copy(block, out_ref.at[place, columns], sems.at[k]))
        copies[k].start()
    for copy in copies:
        copy.wait()


def flip(block, axis, count, bits):
    return lax.ppermute(block, axis, [(i, i ^ bits) for i in range(count)])


def cross(block, dp_count, fsdp_count, chip_bits, shard_bits):
    pairs = [
        (
            d * fsdp_count + z,
            (d ^ (chip_bits * CORES) ^ 1) * fsdp_count + (z ^ shard_bits[d % CORES]),
        )
        for d in range(dp_count)
        for z in range(fsdp_count)
    ]
    return lax.ppermute(block, BOTH, pairs)


def far_first(count, send):
    return [send(k) for k in range(count - 1, 0, -1)][::-1]


def shard_pairs(fsdp_count):
    others = range(1, fsdp_count - 1)
    return list(zip(others[::2], others[1::2]))


def across_z(weight, dp_count, fsdp_count):
    rows = weight.shape[0]
    group = max(g for g in (2, 4, 8) if dp_count % g == 0 and rows % (16 * g) == 0)
    part = call(
        functools.partial(slice_kernel, group),
        "own_part_of_weight",
        [weight],
        [FAR],
        jax.ShapeDtypeStruct((rows // group, weight.shape[1]), weight.dtype),
        [pltpu.SemaphoreType.DMA],
    )
    weight, part = lax.optimization_barrier((weight, part))
    part = cross(part, dp_count, fsdp_count, 0, (fsdp_count - 1,) * CORES)
    wholes = [
        (cross(weight, dp_count, fsdp_count, 0, flips), flips[::-1])
        for flips in shard_pairs(fsdp_count)
    ]
    return group, part, wholes


def stack_kernel(_, *refs):
    out_ref = refs[-1]
    rows = refs[0].shape[0]
    for i, block_ref in enumerate(refs[:-1]):
        out_ref[i * rows : (i + 1) * rows] = block_ref[...]


def share(group, part, wholes, ready, dp_count, fsdp_count):
    alike = (0,) * CORES
    parts, members = [part], [1]
    for chip_bits in range(1, group // CORES):
        parts.append(cross(part, dp_count, fsdp_count, chip_bits, alike))
        members.append(CORES * chip_bits)
    if len(parts) > 1:
        rows, columns = part.shape
        part = call(
            stack_kernel,
            "parts_of_weight",
            [ready] + parts,
            [ANYWHERE] + [NEAR] * len(parts),
            jax.ShapeDtypeStruct((len(parts) * rows, columns), part.dtype),
        )
    held = [(part, (fsdp_count - 1,) * CORES, members)]
    for block, flips in wholes:
        held.append((lax.optimization_barrier((block, part))[0], flips, [None]))
    moved = []
    for block, flips, members in held:
        places = [m if m is None else m ^ 1 for m in members]
        moved.append((flip(block, "dp", dp_count, 1), flips[::-1], places))
    return held, moved


def shards(events, query_weight, keys, values, gates, cotangent, lengths):
    slots, span, model_width = events.shape
    width = query_weight.shape[1]
    half_width = width // CORES
    rows = slots * span
    dp_count, fsdp_count = lax.axis_size("dp"), lax.axis_size("fsdp")
    chips = dp_count // CORES
    shard_rows = model_width // fsdp_count
    total_seqs = slots * dp_count * fsdp_count
    bf16, f32 = jnp.bfloat16, jnp.float32

    def shape(*dims, dtype=bf16):
        return jax.ShapeDtypeStruct(dims, dtype)

    flat_events = events.reshape(rows, model_width)
    keys, values, gates, cotangent = (
        a.reshape(rows, width) for a in (keys, values, gates, cotangent)
    )
    sibling_events = flip(flat_events, "dp", dp_count, 1)
    group, part, wholes = across_z(query_weight, dp_count, fsdp_count)
    prepared = call(
        functools.partial(prepare_kernel, slots),
        "prepared_operands",
        [part, lengths, sibling_events]
        + [flat_events, keys, values, cotangent, query_weight, gates],
        [ANYWHERE, FAR, NEAR] + [FAR] * 6,
        (
            shape(rows, model_width),
            shape(rows, width),
            shape(rows, width),
            shape(rows, width),
            shape(shard_rows, width),
            shape(model_width, CORES * rows),
            shape(width, rows),
            shape(width, rows),
            shape(slots, span, span, dtype=f32),
            shape(rows, width, dtype=f32),
            shape(rows, span, dtype=f32),
        ),
        [
            pltpu.VMEM((rows, width), bf16),
            pltpu.SMEM(lengths.shape, jnp.int32),
            pltpu.SemaphoreType.DMA((7,)),
        ],
        flops=5 * 10**9,
    )
    near_events, near_keys, near_values, near_cotangent, near_weight = prepared[:5]
    events_t, keys_t, values_t, weight, gated, first = prepared[5:]
    held, moved = share(group, part, wholes, first, dp_count, fsdp_count)
    held = [(near_weight, (0, 0), [None])] + held
    if not aligned(shard_rows):
        held, moved = [], held + moved

    def split(found):
        return [f[0] for f in found], [f[1:] for f in found]

    terms = []
    if held:
        pieces, origins = split(held)
        terms = [
            call(
                functools.partial(held_projection_kernel, group, shard_rows, origins),
                "projection_by_held_rows",
                pieces + [near_events],
                [NEAR] * (len(pieces) + 1),
                shape(rows, width, dtype=f32),
                projection_scratch(shard_rows, model_width, width, origins),
                flops=2 * rows * width * shard_rows * len(pieces),
                moved=4 * rows * width,
            )
        ]
    pieces, origins = split(moved)
    blocks = shape(slots * HEADS, span, span)
    grad_query, query, normed, grad_mixed, attention, grad_scores = call(
        functools.partial(attention_kernel, slots, group, shard_rows, origins),
        "attention_to_grad_query",
        pieces
        + terms
        + [near_events, near_keys, near_values, keys_t, values_t, weight, gated, first],
        [NEAR] * (len(pieces) + len(terms) + 8),
        (
            shape(rows, width),
            shape(rows, width),
            shape(rows, width, dtype=f32),
            shape(rows, width),
            blocks,
            blocks,
        ),
        projection_scratch(shard_rows, model_width, width, origins),
        flops=2 * rows * width * (model_width + 4 * span),
        moved=24 * rows * width,
    )
    part_rows = shard_rows // chips
    staged = part_rows % 16 == 0 and fsdp_count % 4 == 0
    terms = [grad_query]
    if staged:
        alike = (0,) * CORES

        def to_chip(block, k):
            return cross(block, dp_count, fsdp_count, k, alike)

        order = (0,) + tuple(range(chips - 1, 0, -1))

        def summed_over_chips(terms, name, which, after):
            flips = sets[which]
            terms = [terms[0]] + [to_chip(a, k) for a, k in zip(terms[1:], order[1:])]
            return call(
                functools.partial(chip_sum_kernel, chips),
                name,
                [after] + terms,
                [ANYWHERE] + [NEAR] * chips,
                tuple(shape(part_rows, half_width, dtype=bf16 if z else f32) for z in flips),
            )

        sets = (tuple(range(2, fsdp_count)), (0, 1))
        picked_rows = [len(flips) * shard_rows for flips in sets]
        got = flip(grad_query, "dp", dp_count, 1)
        own_terms = call(
            functools.partial(own_gradient_kernel, chips, sets),
            "weight_gradient_of_own_events",
            [events_t, grad_query],
            [NEAR] * 2,
            tuple(
                a
                for n in picked_rows
                for a in (shape(n, half_width, dtype=f32), shape(n, rows))
            ),
            [pltpu.VMEM((max(picked_rows), rows), bf16)],
            flops=2 * rows * model_width * half_width,
            moved=8 * model_width * rows,
        )

        def gradient(which, name, after):
            columns = len(sets[which]) * half_width
            return call(
                functools.partial(gradient_kernel, order, sets[which]),
                name,
                [after, *own_terms[2 * which : 2 * which + 2], got],
                [ANYWHERE] + [NEAR] * 3,
                tuple(shape(part_rows, columns, dtype=bf16 if k else f32) for k in order),
                flops=2 * rows * picked_rows[which] * half_width,
                moved=2 * picked_rows[which] * (rows + 2 * half_width),
            )

        far_terms = gradient(0, "weight_gradient_of_far_shards", got)
        terms = gradient(1, "weight_gradient_of_near_shards", far_terms[0])

        def to_shard(block, z):
            return cross(block, dp_count, fsdp_count, 0, (z,) * CORES)

        far_sums = summed_over_chips(far_terms, "far_shards_over_chips", 0, got)
        own_sum, next_sum = summed_over_chips(
            terms, "near_shards_over_chips", 1, far_sums[0]
        )
        far_sums = [to_shard(a, z) for a, z in reversed(list(zip(far_sums, sets[0])))]
        terms = [next_sum]
        next_sum = to_shard(next_sum, 1)
    grad_keys, grad_values, grad_gates = call(
        functools.partial(outputs_kernel, slots),
        "key_value_gate_gradients",
        [terms[0], query, normed, grad_mixed, attention, grad_scores, near_cotangent],
        [ANYWHERE] + [NEAR] * 6,
        (shape(rows, width),) * 3,
        flops=4 * rows * width * span,
        moved=12 * rows * width,
    )
    if staged:
        mean = call(
            functools.partial(mean_kernel, total_seqs),
            "mean_over_shards",
            [grad_keys, own_sum, next_sum] + far_sums,
            [FAR] + [NEAR] * fsdp_count,
            shape(part_rows, half_width),
        )
        blocks = call(
            stack_kernel,
            "blocks_of_chips",
            [mean, mean] + far_first(chips, lambda k: to_chip(mean, k)),
            [ANYWHERE] + [NEAR] * chips,
            shape(shard_rows, half_width),
        )
        grad_weight = ()
        for side in range(CORES):
            grad_weight = call(
                functools.partial(place_kernel, side, chips),
                f"blocks_of_{'sibling' if side else 'own'}_core_in_place",
                [flip(blocks, "dp", dp_count, 1) if side else blocks, *grad_weight],
                [NEAR] + [FAR] * side,
                shape(shard_rows, width, dtype=f32),
                [
                    pltpu.VMEM((shard_rows, half_width), f32),
                    pltpu.SemaphoreType.DMA((chips,)),
                ],
                out_specs=FAR,
                aliases={1: 0} if side else {},
            )
            grad_weight = grad_weight if side else (grad_weight,)
    else:
        whole = lax.dot_general(flat_events, grad_query, FIRST, preferred_element_type=f32)
        mine = lax.psum_scatter(whole, "fsdp", scatter_dimension=0, tiled=True)
        grad_weight = lax.psum(mine, "dp") / total_seqs

    full = (slots, span, width)
    return (
        grad_keys.reshape(full),
        grad_values.reshape(full),
        grad_gates.reshape(full),
        grad_weight,
    )


def solution(mesh):
    split = P(BOTH, None, None)
    return jax.shard_map(
        shards,
        mesh=mesh,
        in_specs=(split, P("fsdp", None), split, split, split, split, P()),
        out_specs=(split, split, split, P("fsdp", None)),
        check_vma=False,
    )
```

```python
import functools
import math

import jax
import jax.numpy as jnp
from jax import lax
from jax.experimental import pallas as pl
from jax.experimental.pallas import tpu as pltpu
from jax.sharding import PartitionSpec as P

HEADS = 4
EPSILON = 1e-06
CORES = 2
BOTH = ("dp", "fsdp")
VMEM_LIMIT = 24 * 1024 * 1024

LAST = (((1,), (1,)), ((), ()))
FIRST = (((0,), (0,)), ((), ()))


def dot(lhs, rhs, dims=(((1,), (0,)), ((), ()))):
    return lax.dot_general(lhs, rhs, dims, preferred_element_type=jnp.float32)


def call(kernel, name, operands, in_specs, out_shape, scratch=(), flops=0, moved=0,
         out_specs=None, aliases=None):
    vmem = pl.BlockSpec(memory_space=pltpu.VMEM)
    many = isinstance(out_shape, tuple)
    operands = [
        pltpu.with_memory_space_constraint(a, pltpu.HBM) if spec is FAR else a
        for a, spec in zip(operands, in_specs)
    ]
    return pl.pallas_call(
        kernel,
        out_shape=out_shape,
        in_specs=in_specs,
        out_specs=out_specs or ((vmem,) * len(out_shape) if many else vmem),
        scratch_shapes=list(scratch),
        input_output_aliases=aliases or {},
        compiler_params=pltpu.CompilerParams(vmem_limit_bytes=VMEM_LIMIT),
        cost_estimate=pl.CostEstimate(flops=flops, bytes_accessed=moved, transcendentals=0),
        name=name,
    )(*operands)


NEAR = pl.BlockSpec(memory_space=pltpu.VMEM)
ANYWHERE = pl.BlockSpec(memory_space=pl.ANY)
FAR = pl.BlockSpec(memory_space=pltpu.HBM)


def head_columns(width):
    depth = width // HEADS
    return [slice(h * depth, (h + 1) * depth) for h in range(HEADS)]


def slot_rows(rows, slots):
    span = rows // slots
    return [slice(s * span, (s + 1) * span) for s in range(slots)]


def row_mean(blocks, width):
    return jnp.sum(sum(blocks[1:], blocks[0]), axis=1, keepdims=True) / width


def slice_kernel(block_ref, *refs):
    outs, sems = refs[:-1], refs[-1]
    copies = []
    for i, out_ref in enumerate(outs):
        rows = out_ref.shape[0]
        member = lax.rem(lax.axis_index("dp"), block_ref.shape[0] // rows)
        start = pl.multiple_of(member * rows, rows)
        copies.append(pltpu.make_async_copy(block_ref.at[pl.ds(start, rows)], out_ref, sems.at[i]))
        copies[i].start()
    for copy in copies:
        copy.wait()


def prepare_kernel(slots, _, lengths_ref, sibling_ref, *refs):
    inputs, held = refs[:6], refs[6:11]
    (events_t_ref, key_t_ref, value_t_ref, weight_ref, gated_ref, first_ref,
     gate_ref, own_lengths_ref, sems) = refs[11:]
    events_ref, key_ref, value_ref, upstream_ref, _ = held
    copies = [
        pltpu.make_async_copy(source, target, sems.at[i])
        for i, (source, target) in enumerate(zip(inputs, held + (gate_ref,)))
    ]
    copies.append(pltpu.make_async_copy(lengths_ref, own_lengths_ref, sems.at[len(copies)]))
    for copy in copies:
        copy.start()
    rows, width = key_ref.shape
    events_t_ref[:, rows:] = sibling_ref[...].T
    for copy in copies:
        copy.wait()
    events_t_ref[:, :rows] = events_ref[...].T
    key_t_ref[...] = key_ref[...].T
    value_t_ref[...] = value_ref[...].T
    span = rows // slots
    row = lax.broadcasted_iota(jnp.int32, (span, span), 0)
    column = lax.broadcasted_iota(jnp.int32, (span, span), 1)
    first_slot = (lax.axis_index("dp") * lax.axis_size("fsdp") + lax.axis_index("fsdp")) * slots
    for s, place in enumerate(slot_rows(rows, slots)):
        length = own_lengths_ref[first_slot + s]
        inverse = 1.0 / jnp.full((span, span), length, jnp.int32).astype(jnp.float32)
        weight_ref[s] = jnp.where((column <= row) & (row < length), inverse, 0.0)
        live = lax.broadcasted_iota(jnp.int32, (span, width), 0) < length
        gated = upstream_ref[place].astype(jnp.float32) * gate_ref[place].astype(jnp.float32)
        gated = jnp.where(live, gated, 0.0)
        gated_ref[place] = gated
        first = row_mean([gated[:, c] for c in head_columns(width)], width)
        first_ref[place] = jnp.broadcast_to(first, (span, first_ref.shape[1]))


def piece_start(shard_rows, part_rows, shard_flip, member_flip):
    start = (lax.axis_index("fsdp") ^ shard_flip) * shard_rows
    if member_flip is not None:
        member = lax.rem(lax.axis_index("dp"), shard_rows // part_rows) ^ member_flip
        start = start + member * part_rows
    return pl.multiple_of(start, 16)


def aligned(shard_rows):
    return shard_rows % (CORES * 128) == 0


def project(events_ref, pieces, origins, shard_rows, spare_ref, sems):
    copies, total = [], None
    for piece, parts in zip(pieces, origins):
        rows = piece.shape[0] // len(parts)
        if not aligned(shard_rows):
            for i, part in enumerate(parts):
                place = pl.ds(piece_start(shard_rows, rows, *part), rows)
                copy = pltpu.make_async_copy(
                    piece.at[pl.ds(i * rows, rows)], spare_ref.at[place], sems.at[len(copies)]
                )
                copy.start()
                copies.append(copy)
            continue
        if rows % 128 == 0:
            terms = [
                (piece_start(shard_rows, rows, *part), piece.at[pl.ds(i * rows, rows)])
                for i, part in enumerate(parts)
            ]
        else:
            first = piece_start(shard_rows, shard_rows, parts[0][0], None)
            spare_ref[...] = jnp.zeros_like(spare_ref)
            for i, part in enumerate(parts):
                start = piece_start(shard_rows, rows, *part) - first
                spare_ref[pl.ds(pl.multiple_of(start, 16), rows)] = piece[i * rows : (i + 1) * rows]
            terms = [(first, spare_ref)]
        for start, rows_ref in terms:
            columns = pl.ds(pl.multiple_of(start, 128), rows_ref.shape[0])
            term = dot(events_ref[:, columns], rows_ref[...])
            total = term if total is None else total + term
    if copies:
        for copy in copies:
            copy.wait()
        total = dot(events_ref[...], spare_ref[...])
    return total


def projection_scratch(shard_rows, model_width, width, origins):
    count = sum(len(parts) for parts in origins)
    spare_rows = shard_rows if aligned(shard_rows) else model_width
    return [pltpu.VMEM((spare_rows, width), jnp.bfloat16), pltpu.SemaphoreType.DMA((count,))]


def held_projection_kernel(shard_rows, origins, *refs):
    pieces, (events_ref, out_ref, spare_ref, sems) = refs[: len(origins)], refs[len(origins) :]
    out_ref[...] = project(events_ref, pieces, origins, shard_rows, spare_ref, sems)


def attention_kernel(slots, shard_rows, origins, *refs):
    pieces = refs[: len(origins)]
    terms, refs = refs[len(origins) : -16], refs[-16:]
    (events_ref, key_ref, value_ref, key_t_ref, value_t_ref, weight_ref, gated_ref, first_ref,
     grad_query_ref, query_ref, normed_ref, mixed_grad_ref, attention_ref, scores_grad_ref,
     spare_ref, sems) = refs
    query = project(events_ref, pieces, origins, shard_rows, spare_ref, sems)
    for term in terms:
        query = query + term[...]
    query_ref[...] = query.astype(jnp.bfloat16)

    rows, width = key_ref.shape
    scale = 1.0 / math.sqrt(width // HEADS)
    columns = head_columns(width)
    places = slot_rows(rows, slots)
    each = [(s, h, s * HEADS + h) for s in range(slots) for h in range(HEADS)]
    slopes, mixed, grad_mixed = [], [], []
    for s, h, i in each:
        scores = dot(query_ref[places[s], columns[h]], key_t_ref[columns[h], places[s]]) * scale
        sigmoid = 1.0 / (1.0 + jnp.exp(-scores))
        silu = scores * sigmoid
        attention_ref[i] = (silu * weight_ref[s]).astype(jnp.bfloat16)
        slopes.append((sigmoid + silu * (1.0 - sigmoid)) * weight_ref[s])
    for s, h, i in each:
        mixed.append(dot(attention_ref[i], value_ref[places[s], columns[h]]))
    for s in range(slots):
        own = mixed[s * HEADS : (s + 1) * HEADS]
        mean = row_mean(own, width)
        centred = [m - mean for m in own]
        inv_std = lax.rsqrt(row_mean([c * c for c in centred], width) + EPSILON)
        normed = [c * inv_std for c in centred]
        gated = [gated_ref[places[s], c] for c in columns]
        second = row_mean([g * n for g, n in zip(gated, normed)], width)
        first = first_ref[places[s]]
        for h in range(HEADS):
            normed_ref[places[s], columns[h]] = normed[h]
            grad = inv_std * (gated[h] - first - normed[h] * second)
            mixed_grad_ref[places[s], columns[h]] = grad.astype(jnp.bfloat16)
    for s, h, i in each:
        grad_attention = dot(
            mixed_grad_ref[places[s], columns[h]], value_t_ref[columns[h], places[s]]
        )
        scores_grad_ref[i] = (grad_attention * slopes[i]).astype(jnp.bfloat16)
    for s, h, i in each:
        grad_query = dot(scores_grad_ref[i], key_ref[places[s], columns[h]]) * scale
        grad_query_ref[places[s], columns[h]] = grad_query.astype(jnp.bfloat16)


def outputs_kernel(slots, _, query_ref, normed_ref, mixed_grad_ref, attention_ref, scores_grad_ref,
                   upstream_ref, grad_key_ref, grad_value_ref, grad_gate_ref):
    rows, width = query_ref.shape
    scale = 1.0 / math.sqrt(width // HEADS)
    columns = head_columns(width)
    places = slot_rows(rows, slots)
    grad_gate_ref[...] = (upstream_ref[...].astype(jnp.float32) * normed_ref[...]).astype(
        jnp.bfloat16
    )
    for s in range(slots):
        for h in range(HEADS):
            i = s * HEADS + h
            grad_value = dot(attention_ref[i], mixed_grad_ref[places[s], columns[h]], FIRST)
            grad_value_ref[places[s], columns[h]] = grad_value.astype(jnp.bfloat16)
            grad_key = dot(scores_grad_ref[i], query_ref[places[s], columns[h]], FIRST) * scale
            grad_key_ref[places[s], columns[h]] = grad_key.astype(jnp.bfloat16)


def summing_half(k, z):
    return lax.rem(lax.axis_index("dp"), CORES) ^ (1 if k else 0) ^ (1 if z else 0)


def gradient_picks(chips, shard_flips):
    every = [(k, i, z) for k in range(chips) for i, z in enumerate(shard_flips)]
    return [[p for p in every if (p[0] != 0) ^ (p[2] != 0) == bool(side)] for side in range(CORES)]


def half_columns(side, half):
    return pl.ds(pl.multiple_of(summing_half(side, 0) * half, half), half)


def own_gradient_kernel(chips, sets, events_ref, grad_query_ref, *refs):
    outs, picked_ref = refs[:-1], refs[-1]
    rows, half = grad_query_ref.shape[0], grad_query_ref.shape[1] // CORES
    shard_rows = events_ref.shape[0] // lax.axis_size("fsdp")
    part_rows = shard_rows // chips
    chip, here = lax.div(lax.axis_index("dp"), CORES), lax.axis_index("fsdp")
    for flips, term_ref, other_ref in zip(sets, outs[::2], outs[1::2]):
        at = 0
        for side, picks in enumerate(gradient_picks(chips, flips)):
            first = at
            for k, _, z in picks:
                start = (here ^ z) * shard_rows + (chip ^ k) * part_rows
                source = pl.ds(pl.multiple_of(start, part_rows), part_rows)
                picked_ref[at : at + part_rows] = events_ref[source, :rows]
                other_ref[at : at + part_rows] = events_ref[source, rows:]
                at += part_rows
            columns = half_columns(side, half)
            term_ref[first:at] = dot(picked_ref[first:at], grad_query_ref[:, columns])


def gradient_kernel(order, flips, _, term_ref, events_ref, grad_query_ref, *outs):
    half = term_ref.shape[1]
    part_rows = outs[0].shape[0]
    out_of = dict(zip(order, outs))
    at = 0
    for side, picks in enumerate(gradient_picks(len(order), flips)):
        rows = slice(at, at + len(picks) * part_rows)
        total = term_ref[rows] + dot(events_ref[rows], grad_query_ref[:, half_columns(side, half)])
        for p, (k, i, _) in enumerate(picks):
            block = total[p * part_rows : (p + 1) * part_rows]
            out_of[k][:, i * half : (i + 1) * half] = block.astype(out_of[k].dtype)
        at = rows.stop


def chip_sum_kernel(term_count, _, *refs):
    terms, outs = refs[:term_count], refs[term_count:]
    at = 0
    for out in outs:
        columns = slice(at, at + out.shape[1])
        total = terms[0][:, columns].astype(jnp.float32)
        for term in terms[1:]:
            total = total + term[:, columns].astype(jnp.float32)
        out[...] = total.astype(out.dtype)
        at += out.shape[1]


def mean_kernel(count, _, *refs):
    total = refs[0][...].astype(jnp.float32)
    for term in refs[1:-1]:
        total = total + term[...].astype(jnp.float32)
    refs[-1][...] = (total / count).astype(refs[-1].dtype)


def place_kernel(side, chips, blocks_ref, *refs):
    out_ref, held_ref, sems = refs[-3:]
    rows, half = blocks_ref.shape[0] // chips, blocks_ref.shape[1]
    core, chip = lax.rem(lax.axis_index("dp"), CORES) ^ side, lax.div(lax.axis_index("dp"), CORES)
    held_ref[...] = blocks_ref[...].astype(held_ref.dtype)
    copies = []
    for k in range(chips):
        place = pl.ds(pl.multiple_of((chip ^ k) * rows, rows), rows)
        columns = pl.ds(pl.multiple_of((core ^ (1 if k else 0)) * half, half), half)
        block = held_ref.at[pl.ds(k * rows, rows)]
        copies.append(pltpu.make_async_copy(block, out_ref.at[place, columns], sems.at[k]))
        copies[k].start()
    for copy in copies:
        copy.wait()


def flip(block, axis, count, bits):
    return lax.ppermute(block, axis, [(i, i ^ bits) for i in range(count)])


def cross(block, dp_count, fsdp_count, chip_bits, shard_bits):
    pairs = [
        (
            d * fsdp_count + z,
            (d ^ (chip_bits * CORES) ^ 1) * fsdp_count + (z ^ shard_bits[d % CORES]),
        )
        for d in range(dp_count)
        for z in range(fsdp_count)
    ]
    return lax.ppermute(block, BOTH, pairs)


def far_first(count, send):
    return [send(k) for k in range(count - 1, 0, -1)][::-1]


def across_z(weight, dp_count, fsdp_count):
    rows = weight.shape[0]
    group = max(g for g in (2, 4, 8) if dp_count % g == 0 and rows % (16 * g) == 0)
    part, half = call(
        slice_kernel,
        "own_parts_of_weight",
        [weight],
        [FAR],
        tuple(
            jax.ShapeDtypeStruct((rows // g, weight.shape[1]), weight.dtype)
            for g in (group, CORES)
        ),
        [pltpu.SemaphoreType.DMA((2,))],
    )
    middle = fsdp_count // 2
    part = cross(part, dp_count, fsdp_count, 0, (middle,) * CORES)
    halves = [
        (cross(half, dp_count, fsdp_count, 0, (z,) * CORES), z)
        for z in range(1, fsdp_count)
        if z != middle
    ]
    return group, part, halves


def stack_kernel(_, *refs):
    out_ref = refs[-1]
    rows = refs[0].shape[0]
    for i, block_ref in enumerate(refs[:-1]):
        out_ref[i * rows : (i + 1) * rows] = block_ref[...]


def share(group, part, halves, ready, dp_count, fsdp_count):
    alike = (0,) * CORES
    middle = fsdp_count // 2
    parts, members = [part], [1]
    for chip_bits in range(1, group // CORES):
        parts.append(cross(part, dp_count, fsdp_count, chip_bits, alike))
        members.append(CORES * chip_bits)

    def stacked(blocks, name, after):
        if len(blocks) == 1:
            return blocks[0]
        rows, columns = blocks[0].shape
        return call(
            stack_kernel,
            name,
            [after] + blocks,
            [ANYWHERE] + [NEAR] * len(blocks),
            jax.ShapeDtypeStruct((len(blocks) * rows, columns), part.dtype),
        )

    part = stacked(parts, "parts_of_weight", ready)
    halves, flips = zip(*halves)
    half = stacked(list(halves), "halves_of_weight", part)
    held = [(part, [(middle, m) for m in members]), (half, [(z, 1) for z in flips])]
    moved = [
        (flip(block, "dp", dp_count, 1), [(z, m ^ 1) for z, m in origin]) for block, origin in held
    ]
    return held, moved


def shards(events, query_weight, keys, values, gates, cotangent, lengths):
    slots, span, model_width = events.shape
    width = query_weight.shape[1]
    half_width = width // CORES
    rows = slots * span
    dp_count, fsdp_count = lax.axis_size("dp"), lax.axis_size("fsdp")
    chips = dp_count // CORES
    shard_rows = model_width // fsdp_count
    total_seqs = slots * dp_count * fsdp_count
    bf16, f32 = jnp.bfloat16, jnp.float32

    def shape(*dims, dtype=bf16):
        return jax.ShapeDtypeStruct(dims, dtype)

    flat_events = events.reshape(rows, model_width)
    keys, values, gates, cotangent = (
        a.reshape(rows, width) for a in (keys, values, gates, cotangent)
    )
    sibling_events = flip(flat_events, "dp", dp_count, 1)
    group, part, halves = across_z(query_weight, dp_count, fsdp_count)
    prepared = call(
        functools.partial(prepare_kernel, slots),
        "prepared_operands",
        [part, lengths, sibling_events]
        + [flat_events, keys, values, cotangent, query_weight, gates],
        [ANYWHERE, FAR, NEAR] + [FAR] * 6,
        (
            shape(rows, model_width),
            shape(rows, width),
            shape(rows, width),
            shape(rows, width),
            shape(shard_rows, width),
            shape(model_width, CORES * rows),
            shape(width, rows),
            shape(width, rows),
            shape(slots, span, span, dtype=f32),
            shape(rows, width, dtype=f32),
            shape(rows, span, dtype=f32),
        ),
        [
            pltpu.VMEM((rows, width), bf16),
            pltpu.SMEM(lengths.shape, jnp.int32),
            pltpu.SemaphoreType.DMA((7,)),
        ],
        flops=5 * 10**9,
    )
    near_events, near_keys, near_values, near_cotangent, near_weight = prepared[:5]
    events_t, keys_t, values_t, weight, gated, first = prepared[5:]
    held, moved = share(group, part, halves, first, dp_count, fsdp_count)
    held = [(near_weight, [(0, None)])] + held
    if not aligned(shard_rows):
        held, moved = [], held + moved

    def split(found):
        return [f[0] for f in found], [f[1] for f in found]

    terms = []
    if held:
        pieces, origins = split(held)
        terms = [
            call(
                functools.partial(held_projection_kernel, shard_rows, origins),
                "projection_by_held_rows",
                pieces + [near_events],
                [NEAR] * (len(pieces) + 1),
                shape(rows, width, dtype=f32),
                projection_scratch(shard_rows, model_width, width, origins),
                flops=2 * rows * width * shard_rows * len(pieces),
                moved=4 * rows * width,
            )
        ]
    pieces, origins = split(moved)
    blocks = shape(slots * HEADS, span, span)
    grad_query, query, normed, grad_mixed, attention, grad_scores = call(
        functools.partial(attention_kernel, slots, shard_rows, origins),
        "attention_to_grad_query",
        pieces
        + terms
        + [near_events, near_keys, near_values, keys_t, values_t, weight, gated, first],
        [NEAR] * (len(pieces) + len(terms) + 8),
        (
            shape(rows, width),
            shape(rows, width),
            shape(rows, width, dtype=f32),
            shape(rows, width),
            blocks,
            blocks,
        ),
        projection_scratch(shard_rows, model_width, width, origins),
        flops=2 * rows * width * (model_width + 4 * span),
        moved=24 * rows * width,
    )
    part_rows = shard_rows // chips
    staged = part_rows % 16 == 0 and fsdp_count % 4 == 0
    terms = [grad_query]
    if staged:
        alike = (0,) * CORES

        def to_chip(block, k):
            return cross(block, dp_count, fsdp_count, k, alike)

        order = (0,) + tuple(range(chips - 1, 0, -1))

        def summed_over_chips(terms, name, which, after):
            flips = sets[which]
            terms = [terms[0]] + [to_chip(a, k) for a, k in zip(terms[1:], order[1:])]
            return call(
                functools.partial(chip_sum_kernel, chips),
                name,
                [after] + terms,
                [ANYWHERE] + [NEAR] * chips,
                tuple(shape(part_rows, half_width, dtype=bf16 if z else f32) for z in flips),
            )

        sets = (tuple(range(2, fsdp_count)), (0, 1))
        picked_rows = [len(flips) * shard_rows for flips in sets]
        got = flip(grad_query, "dp", dp_count, 1)
        own_terms = call(
            functools.partial(own_gradient_kernel, chips, sets),
            "weight_gradient_of_own_events",
            [events_t, grad_query],
            [NEAR] * 2,
            tuple(
                a
                for n in picked_rows
                for a in (shape(n, half_width, dtype=f32), shape(n, rows))
            ),
            [pltpu.VMEM((max(picked_rows), rows), bf16)],
            flops=2 * rows * model_width * half_width,
            moved=8 * model_width * rows,
        )

        def gradient(which, name, after):
            columns = len(sets[which]) * half_width
            return call(
                functools.partial(gradient_kernel, order, sets[which]),
                name,
                [after, *own_terms[2 * which : 2 * which + 2], got],
                [ANYWHERE] + [NEAR] * 3,
                tuple(shape(part_rows, columns, dtype=bf16 if k else f32) for k in order),
                flops=2 * rows * picked_rows[which] * half_width,
                moved=2 * picked_rows[which] * (rows + 2 * half_width),
            )

        far_terms = gradient(0, "weight_gradient_of_far_shards", got)
        terms = gradient(1, "weight_gradient_of_near_shards", far_terms[0])

        def to_shard(block, z):
            return cross(block, dp_count, fsdp_count, 0, (z,) * CORES)

        far_sums = summed_over_chips(far_terms, "far_shards_over_chips", 0, got)
        own_sum, next_sum = summed_over_chips(
            terms, "near_shards_over_chips", 1, far_sums[0]
        )
        far_sums = [to_shard(a, z) for a, z in reversed(list(zip(far_sums, sets[0])))]
        terms = [next_sum]
        next_sum = to_shard(next_sum, 1)
    grad_keys, grad_values, grad_gates = call(
        functools.partial(outputs_kernel, slots),
        "key_value_gate_gradients",
        [terms[0], query, normed, grad_mixed, attention, grad_scores, near_cotangent],
        [ANYWHERE] + [NEAR] * 6,
        (shape(rows, width),) * 3,
        flops=4 * rows * width * span,
        moved=12 * rows * width,
    )
    if staged:
        mean = call(
            functools.partial(mean_kernel, total_seqs),
            "mean_over_shards",
            [grad_keys, own_sum, next_sum] + far_sums,
            [FAR] + [NEAR] * fsdp_count,
            shape(part_rows, half_width),
        )
        blocks = call(
            stack_kernel,
            "blocks_of_chips",
            [mean, mean] + far_first(chips, lambda k: to_chip(mean, k)),
            [ANYWHERE] + [NEAR] * chips,
            shape(shard_rows, half_width),
        )
        grad_weight = ()
        for side in range(CORES):
            grad_weight = call(
                functools.partial(place_kernel, side, chips),
                f"blocks_of_{'sibling' if side else 'own'}_core_in_place",
                [flip(blocks, "dp", dp_count, 1) if side else blocks, *grad_weight],
                [NEAR] + [FAR] * side,
                shape(shard_rows, width, dtype=f32),
                [
                    pltpu.VMEM((shard_rows, half_width), f32),
                    pltpu.SemaphoreType.DMA((chips,)),
                ],
                out_specs=FAR,
                aliases={1: 0} if side else {},
            )
            grad_weight = grad_weight if side else (grad_weight,)
    else:
        whole = lax.dot_general(flat_events, grad_query, FIRST, preferred_element_type=f32)
        mine = lax.psum_scatter(whole, "fsdp", scatter_dimension=0, tiled=True)
        grad_weight = lax.psum(mine, "dp") / total_seqs

    full = (slots, span, width)
    return (
        grad_keys.reshape(full),
        grad_values.reshape(full),
        grad_gates.reshape(full),
        grad_weight,
    )


def solution(mesh):
    split = P(BOTH, None, None)
    return jax.shard_map(
        shards,
        mesh=mesh,
        in_specs=(split, P("fsdp", None), split, split, split, split, P()),
        out_specs=(split, split, split, P("fsdp", None)),
        check_vma=False,
    )
```

```python
import functools
import math

import jax
import jax.numpy as jnp
from jax import lax
from jax.experimental import pallas as pl
from jax.experimental.pallas import tpu as pltpu
from jax.sharding import PartitionSpec as P

HEADS = 4
EPSILON = 1e-06
CORES = 2
BOTH = ("dp", "fsdp")
VMEM_LIMIT = 24 * 1024 * 1024

LAST = (((1,), (1,)), ((), ()))
FIRST = (((0,), (0,)), ((), ()))


def dot(lhs, rhs, dims=(((1,), (0,)), ((), ()))):
    return lax.dot_general(lhs, rhs, dims, preferred_element_type=jnp.float32)


def call(kernel, name, operands, in_specs, out_shape, scratch=(), flops=0, moved=0,
         out_specs=None, aliases=None):
    vmem = pl.BlockSpec(memory_space=pltpu.VMEM)
    many = isinstance(out_shape, tuple)
    operands = [
        pltpu.with_memory_space_constraint(a, pltpu.HBM) if spec is FAR else a
        for a, spec in zip(operands, in_specs)
    ]
    return pl.pallas_call(
        kernel,
        out_shape=out_shape,
        in_specs=in_specs,
        out_specs=out_specs or ((vmem,) * len(out_shape) if many else vmem),
        scratch_shapes=list(scratch),
        input_output_aliases=aliases or {},
        compiler_params=pltpu.CompilerParams(vmem_limit_bytes=VMEM_LIMIT),
        cost_estimate=pl.CostEstimate(flops=flops, bytes_accessed=moved, transcendentals=0),
        name=name,
    )(*operands)


NEAR = pl.BlockSpec(memory_space=pltpu.VMEM)
ANYWHERE = pl.BlockSpec(memory_space=pl.ANY)
FAR = pl.BlockSpec(memory_space=pltpu.HBM)


def head_columns(width):
    depth = width // HEADS
    return [slice(h * depth, (h + 1) * depth) for h in range(HEADS)]


def slot_rows(rows, slots):
    span = rows // slots
    return [slice(s * span, (s + 1) * span) for s in range(slots)]


def row_mean(blocks, width):
    return jnp.sum(sum(blocks[1:], blocks[0]), axis=1, keepdims=True) / width


def slice_kernel(group, block_ref, out_ref, sem):
    rows = out_ref.shape[0]
    start = pl.multiple_of(lax.rem(lax.axis_index("dp"), group) * rows, rows)
    copy = pltpu.make_async_copy(block_ref.at[pl.ds(start, rows)], out_ref, sem)
    copy.start()
    copy.wait()


def prepare_kernel(slots, _, lengths_ref, sibling_ref, *refs):
    inputs, held = refs[:6], refs[6:11]
    (events_t_ref, key_t_ref, value_t_ref, weight_ref, gated_ref, first_ref,
     gate_ref, own_lengths_ref, sems) = refs[11:]
    events_ref, key_ref, value_ref, upstream_ref, _ = held
    copies = [
        pltpu.make_async_copy(source, target, sems.at[i])
        for i, (source, target) in enumerate(zip(inputs, held + (gate_ref,)))
    ]
    copies.append(pltpu.make_async_copy(lengths_ref, own_lengths_ref, sems.at[len(copies)]))
    for copy in copies:
        copy.start()
    rows, width = key_ref.shape
    events_t_ref[:, rows:] = sibling_ref[...].T
    for copy in copies:
        copy.wait()
    events_t_ref[:, :rows] = events_ref[...].T
    key_t_ref[...] = key_ref[...].T
    value_t_ref[...] = value_ref[...].T
    span = rows // slots
    row = lax.broadcasted_iota(jnp.int32, (span, span), 0)
    column = lax.broadcasted_iota(jnp.int32, (span, span), 1)
    first_slot = (lax.axis_index("dp") * lax.axis_size("fsdp") + lax.axis_index("fsdp")) * slots
    for s, place in enumerate(slot_rows(rows, slots)):
        length = own_lengths_ref[first_slot + s]
        inverse = 1.0 / jnp.full((span, span), length, jnp.int32).astype(jnp.float32)
        weight_ref[s] = jnp.where((column <= row) & (row < length), inverse, 0.0)
        live = lax.broadcasted_iota(jnp.int32, (span, width), 0) < length
        gated = upstream_ref[place].astype(jnp.float32) * gate_ref[place].astype(jnp.float32)
        gated = jnp.where(live, gated, 0.0)
        gated_ref[place] = gated
        first = row_mean([gated[:, c] for c in head_columns(width)], width)
        first_ref[place] = jnp.broadcast_to(first, (span, first_ref.shape[1]))


def piece_start(shard_rows, group, part_rows, flips, member_flip):
    device = lax.axis_index("dp")
    start = (
        lax.axis_index("fsdp") ^ jnp.where(lax.rem(device, CORES) == 0, flips[0], flips[1])
    ) * shard_rows
    if member_flip is not None:
        start = start + (lax.rem(device, group) ^ member_flip) * part_rows
    return pl.multiple_of(start, 16)


def aligned(shard_rows):
    return shard_rows % 128 == 0


def project(events_ref, pieces, origins, group, shard_rows, spare_ref, sems):
    copies, total = [], None
    for piece, (flips, members) in zip(pieces, origins):
        rows = piece.shape[0] // len(members)
        starts = [piece_start(shard_rows, group, rows, flips, m) for m in members]
        if not aligned(shard_rows):
            for i, start in enumerate(starts):
                copy = pltpu.make_async_copy(
                    piece.at[pl.ds(i * rows, rows)],
                    spare_ref.at[pl.ds(start, rows)],
                    sems.at[len(copies)],
                )
                copy.start()
                copies.append(copy)
            continue
        first = piece_start(shard_rows, group, rows, flips, None)
        if len(members) > 1:
            spare_ref[...] = jnp.zeros_like(spare_ref)
            for i, start in enumerate(starts):
                place = pl.ds(pl.multiple_of(start - first, 16), rows)
                spare_ref[place] = piece[i * rows : (i + 1) * rows]
            piece = spare_ref
        columns = pl.ds(pl.multiple_of(first, 128), shard_rows)
        term = dot(events_ref[:, columns], piece[...])
        total = term if total is None else total + term
    if copies:
        for copy in copies:
            copy.wait()
        total = dot(events_ref[...], spare_ref[...])
    return total


def projection_scratch(shard_rows, model_width, width, origins):
    count = sum(len(members) for _, members in origins)
    spare_rows = shard_rows if aligned(shard_rows) else model_width
    return [pltpu.VMEM((spare_rows, width), jnp.bfloat16), pltpu.SemaphoreType.DMA((count,))]


def held_projection_kernel(group, shard_rows, origins, *refs):
    pieces, (events_ref, out_ref, spare_ref, sems) = refs[: len(origins)], refs[len(origins) :]
    out_ref[...] = project(events_ref, pieces, origins, group, shard_rows, spare_ref, sems)


def attention_kernel(slots, group, shard_rows, origins, *refs):
    pieces = refs[: len(origins)]
    terms, refs = refs[len(origins) : -16], refs[-16:]
    (events_ref, key_ref, value_ref, key_t_ref, value_t_ref, weight_ref, gated_ref, first_ref,
     grad_query_ref, query_ref, normed_ref, mixed_grad_ref, attention_ref, scores_grad_ref,
     spare_ref, sems) = refs
    query = project(events_ref, pieces, origins, group, shard_rows, spare_ref, sems)
    for term in terms:
        query = query + term[...]
    query_ref[...] = query.astype(jnp.bfloat16)

    rows, width = key_ref.shape
    scale = 1.0 / math.sqrt(width // HEADS)
    columns = head_columns(width)
    places = slot_rows(rows, slots)
    each = [(s, h, s * HEADS + h) for s in range(slots) for h in range(HEADS)]
    slopes, mixed, grad_mixed = [], [], []
    for s, h, i in each:
        scores = dot(query_ref[places[s], columns[h]], key_t_ref[columns[h], places[s]]) * scale
        sigmoid = 1.0 / (1.0 + jnp.exp(-scores))
        silu = scores * sigmoid
        attention_ref[i] = (silu * weight_ref[s]).astype(jnp.bfloat16)
        slopes.append((sigmoid + silu * (1.0 - sigmoid)) * weight_ref[s])
    for s, h, i in each:
        mixed.append(dot(attention_ref[i], value_ref[places[s], columns[h]]))
    for s in range(slots):
        own = mixed[s * HEADS : (s + 1) * HEADS]
        mean = row_mean(own, width)
        centred = [m - mean for m in own]
        inv_std = lax.rsqrt(row_mean([c * c for c in centred], width) + EPSILON)
        normed = [c * inv_std for c in centred]
        gated = [gated_ref[places[s], c] for c in columns]
        second = row_mean([g * n for g, n in zip(gated, normed)], width)
        first = first_ref[places[s]]
        for h in range(HEADS):
            normed_ref[places[s], columns[h]] = normed[h]
            grad = inv_std * (gated[h] - first - normed[h] * second)
            mixed_grad_ref[places[s], columns[h]] = grad.astype(jnp.bfloat16)
    for s, h, i in each:
        grad_attention = dot(
            mixed_grad_ref[places[s], columns[h]], value_t_ref[columns[h], places[s]]
        )
        scores_grad_ref[i] = (grad_attention * slopes[i]).astype(jnp.bfloat16)
    for s, h, i in each:
        grad_query = dot(scores_grad_ref[i], key_ref[places[s], columns[h]]) * scale
        grad_query_ref[places[s], columns[h]] = grad_query.astype(jnp.bfloat16)


def outputs_kernel(slots, _, query_ref, normed_ref, mixed_grad_ref, attention_ref, scores_grad_ref,
                   upstream_ref, grad_key_ref, grad_value_ref, grad_gate_ref):
    rows, width = query_ref.shape
    scale = 1.0 / math.sqrt(width // HEADS)
    columns = head_columns(width)
    places = slot_rows(rows, slots)
    grad_gate_ref[...] = (upstream_ref[...].astype(jnp.float32) * normed_ref[...]).astype(
        jnp.bfloat16
    )
    for s in range(slots):
        for h in range(HEADS):
            i = s * HEADS + h
            grad_value = dot(attention_ref[i], mixed_grad_ref[places[s], columns[h]], FIRST)
            grad_value_ref[places[s], columns[h]] = grad_value.astype(jnp.bfloat16)
            grad_key = dot(scores_grad_ref[i], query_ref[places[s], columns[h]], FIRST) * scale
            grad_key_ref[places[s], columns[h]] = grad_key.astype(jnp.bfloat16)


def summing_half(k, z):
    return lax.rem(lax.axis_index("dp"), CORES) ^ (1 if k else 0) ^ (1 if z else 0)


def gradient_picks(chips, shard_flips):
    every = [(k, i, z) for k in range(chips) for i, z in enumerate(shard_flips)]
    return [[p for p in every if (p[0] != 0) ^ (p[2] != 0) == bool(side)] for side in range(CORES)]


def half_columns(side, half):
    return pl.ds(pl.multiple_of(summing_half(side, 0) * half, half), half)


def own_gradient_kernel(chips, sets, events_ref, grad_query_ref, *refs):
    outs, picked_ref = refs[:-1], refs[-1]
    rows, half = grad_query_ref.shape[0], grad_query_ref.shape[1] // CORES
    shard_rows = events_ref.shape[0] // lax.axis_size("fsdp")
    part_rows = shard_rows // chips
    chip, here = lax.div(lax.axis_index("dp"), CORES), lax.axis_index("fsdp")
    for flips, term_ref, other_ref in zip(sets, outs[::2], outs[1::2]):
        at = 0
        for side, picks in enumerate(gradient_picks(chips, flips)):
            first = at
            for k, _, z in picks:
                start = (here ^ z) * shard_rows + (chip ^ k) * part_rows
                source = pl.ds(pl.multiple_of(start, part_rows), part_rows)
                picked_ref[at : at + part_rows] = events_ref[source, :rows]
                other_ref[at : at + part_rows] = events_ref[source, rows:]
                at += part_rows
            columns = half_columns(side, half)
            term_ref[first:at] = dot(picked_ref[first:at], grad_query_ref[:, columns])


def gradient_kernel(order, sets, grad_query_ref, *refs):
    terms, outs = refs[: 2 * len(sets)], refs[2 * len(sets) :]
    for which, flips in enumerate(sets):
        term_ref, events_ref = terms[2 * which : 2 * which + 2]
        out_of = dict(zip(order, outs[which * len(order) :]))
        half = term_ref.shape[1]
        part_rows = out_of[0].shape[0]
        at = 0
        for side, picks in enumerate(gradient_picks(len(order), flips)):
            rows = slice(at, at + len(picks) * part_rows)
            columns = half_columns(side, half)
            total = term_ref[rows] + dot(events_ref[rows], grad_query_ref[:, columns])
            for p, (k, i, _) in enumerate(picks):
                block = total[p * part_rows : (p + 1) * part_rows]
                out_of[k][:, i * half : (i + 1) * half] = block.astype(out_of[k].dtype)
            at = rows.stop


def chip_sum_kernel(term_count, _, *refs):
    terms, outs = refs[:term_count], refs[term_count:]
    at = 0
    for out in outs:
        columns = slice(at, at + out.shape[1])
        total = terms[0][:, columns].astype(jnp.float32)
        for term in terms[1:]:
            total = total + term[:, columns].astype(jnp.float32)
        out[...] = total.astype(out.dtype)
        at += out.shape[1]


def mean_kernel(count, _, *refs):
    total = refs[0][...].astype(jnp.float32)
    for term in refs[1:-1]:
        total = total + term[...].astype(jnp.float32)
    refs[-1][...] = (total / count).astype(refs[-1].dtype)


def place_kernel(side, chips, blocks_ref, *refs):
    out_ref, held_ref, sems = refs[-3:]
    rows, half = blocks_ref.shape[0] // chips, blocks_ref.shape[1]
    core, chip = lax.rem(lax.axis_index("dp"), CORES) ^ side, lax.div(lax.axis_index("dp"), CORES)
    held_ref[...] = blocks_ref[...].astype(held_ref.dtype)
    copies = []
    for k in range(chips):
        place = pl.ds(pl.multiple_of((chip ^ k) * rows, rows), rows)
        columns = pl.ds(pl.multiple_of((core ^ (1 if k else 0)) * half, half), half)
        block = held_ref.at[pl.ds(k * rows, rows)]
        copies.append(pltpu.make_async_copy(block, out_ref.at[place, columns], sems.at[k]))
        copies[k].start()
    for copy in copies:
        copy.wait()


def flip(block, axis, count, bits):
    return lax.ppermute(block, axis, [(i, i ^ bits) for i in range(count)])


def cross(block, dp_count, fsdp_count, chip_bits, shard_bits):
    pairs = [
        (
            d * fsdp_count + z,
            (d ^ (chip_bits * CORES) ^ 1) * fsdp_count + (z ^ shard_bits[d % CORES]),
        )
        for d in range(dp_count)
        for z in range(fsdp_count)
    ]
    return lax.ppermute(block, BOTH, pairs)


def far_first(count, send):
    return [send(k) for k in range(count - 1, 0, -1)][::-1]


def shard_pairs(fsdp_count):
    others = [d for d in range(1, fsdp_count) if d != fsdp_count // 2]
    return list(zip(others[::2], others[1::2]))


def across_z(weight, dp_count, fsdp_count):
    rows = weight.shape[0]
    group = max(g for g in (2, 4, 8) if dp_count % g == 0 and rows % (16 * g) == 0)
    part = call(
        functools.partial(slice_kernel, group),
        "own_part_of_weight",
        [weight],
        [FAR],
        jax.ShapeDtypeStruct((rows // group, weight.shape[1]), weight.dtype),
        [pltpu.SemaphoreType.DMA],
    )
    weight, part = lax.optimization_barrier((weight, part))
    middle = (fsdp_count // 2,) * CORES
    part = cross(part, dp_count, fsdp_count, 0, middle)
    wholes = [
        (cross(weight, dp_count, fsdp_count, 0, flips), flips[::-1])
        for flips in shard_pairs(fsdp_count)
    ]
    return group, part, wholes


def stack_kernel(_, *refs):
    out_ref = refs[-1]
    rows = refs[0].shape[0]
    for i, block_ref in enumerate(refs[:-1]):
        out_ref[i * rows : (i + 1) * rows] = block_ref[...]


def share(group, part, wholes, ready, dp_count, fsdp_count):
    alike = (0,) * CORES
    parts, members = [part], [1]
    for chip_bits in range(1, group // CORES):
        parts.append(cross(part, dp_count, fsdp_count, chip_bits, alike))
        members.append(CORES * chip_bits)
    if len(parts) > 1:
        rows, columns = part.shape
        part = call(
            stack_kernel,
            "parts_of_weight",
            [ready] + parts,
            [ANYWHERE] + [NEAR] * len(parts),
            jax.ShapeDtypeStruct((len(parts) * rows, columns), part.dtype),
        )
    held = [(part, (fsdp_count // 2,) * CORES, members)]
    for block, flips in wholes:
        held.append((lax.optimization_barrier((block, part))[0], flips, [None]))
    moved = []
    for block, flips, members in held:
        places = [m if m is None else m ^ 1 for m in members]
        moved.append((flip(block, "dp", dp_count, 1), flips[::-1], places))
    return held, moved


def shards(events, query_weight, keys, values, gates, cotangent, lengths):
    slots, span, model_width = events.shape
    width = query_weight.shape[1]
    half_width = width // CORES
    rows = slots * span
    dp_count, fsdp_count = lax.axis_size("dp"), lax.axis_size("fsdp")
    chips = dp_count // CORES
    shard_rows = model_width // fsdp_count
    total_seqs = slots * dp_count * fsdp_count
    bf16, f32 = jnp.bfloat16, jnp.float32

    def shape(*dims, dtype=bf16):
        return jax.ShapeDtypeStruct(dims, dtype)

    flat_events = events.reshape(rows, model_width)
    keys, values, gates, cotangent = (
        a.reshape(rows, width) for a in (keys, values, gates, cotangent)
    )
    sibling_events = flip(flat_events, "dp", dp_count, 1)
    group, part, wholes = across_z(query_weight, dp_count, fsdp_count)
    prepared = call(
        functools.partial(prepare_kernel, slots),
        "prepared_operands",
        [part, lengths, sibling_events]
        + [flat_events, keys, values, cotangent, query_weight, gates],
        [ANYWHERE, FAR, NEAR] + [FAR] * 6,
        (
            shape(rows, model_width),
            shape(rows, width),
            shape(rows, width),
            shape(rows, width),
            shape(shard_rows, width),
            shape(model_width, CORES * rows),
            shape(width, rows),
            shape(width, rows),
            shape(slots, span, span, dtype=f32),
            shape(rows, width, dtype=f32),
            shape(rows, span, dtype=f32),
        ),
        [
            pltpu.VMEM((rows, width), bf16),
            pltpu.SMEM(lengths.shape, jnp.int32),
            pltpu.SemaphoreType.DMA((7,)),
        ],
        flops=5 * 10**9,
    )
    near_events, near_keys, near_values, near_cotangent, near_weight = prepared[:5]
    events_t, keys_t, values_t, weight, gated, first = prepared[5:]
    held, moved = share(group, part, wholes, first, dp_count, fsdp_count)
    held = [(near_weight, (0, 0), [None])] + held
    if not aligned(shard_rows):
        held, moved = [], held + moved

    def split(found):
        return [f[0] for f in found], [f[1:] for f in found]

    terms = []
    if held:
        pieces, origins = split(held)
        terms = [
            call(
                functools.partial(held_projection_kernel, group, shard_rows, origins),
                "projection_by_held_rows",
                pieces + [near_events],
                [NEAR] * (len(pieces) + 1),
                shape(rows, width, dtype=f32),
                projection_scratch(shard_rows, model_width, width, origins),
                flops=2 * rows * width * shard_rows * len(pieces),
                moved=4 * rows * width,
            )
        ]
    pieces, origins = split(moved)
    blocks = shape(slots * HEADS, span, span)
    grad_query, query, normed, grad_mixed, attention, grad_scores = call(
        functools.partial(attention_kernel, slots, group, shard_rows, origins),
        "attention_to_grad_query",
        pieces
        + terms
        + [near_events, near_keys, near_values, keys_t, values_t, weight, gated, first],
        [NEAR] * (len(pieces) + len(terms) + 8),
        (
            shape(rows, width),
            shape(rows, width),
            shape(rows, width, dtype=f32),
            shape(rows, width),
            blocks,
            blocks,
        ),
        projection_scratch(shard_rows, model_width, width, origins),
        flops=2 * rows * width * (model_width + 4 * span),
        moved=24 * rows * width,
    )
    part_rows = shard_rows // chips
    staged = part_rows % 16 == 0 and fsdp_count % 4 == 0
    terms = [grad_query]
    if staged:
        alike = (0,) * CORES

        def to_chip(block, k):
            return cross(block, dp_count, fsdp_count, k, alike)

        order = (0,) + tuple(range(chips - 1, 0, -1))

        def summed_over_chips(terms, name, which, after):
            flips = sets[which]
            terms = [terms[0]] + [to_chip(a, k) for a, k in zip(terms[1:], order[1:])]
            return call(
                functools.partial(chip_sum_kernel, chips),
                name,
                [after] + terms,
                [ANYWHERE] + [NEAR] * chips,
                tuple(shape(part_rows, half_width, dtype=bf16 if z else f32) for z in flips),
            )

        sets = (tuple(range(2, fsdp_count)), (0, 1))
        picked_rows = [len(flips) * shard_rows for flips in sets]
        got = flip(grad_query, "dp", dp_count, 1)
        own_terms = call(
            functools.partial(own_gradient_kernel, chips, sets),
            "weight_gradient_of_own_events",
            [events_t, grad_query],
            [NEAR] * 2,
            tuple(
                a
                for n in picked_rows
                for a in (shape(n, half_width, dtype=f32), shape(n, rows))
            ),
            [pltpu.VMEM((max(picked_rows), rows), bf16)],
            flops=2 * rows * model_width * half_width,
            moved=8 * model_width * rows,
        )

        finished = call(
            functools.partial(gradient_kernel, order, sets),
            "weight_gradient_of_both_cores",
            [got, *own_terms],
            [NEAR] * (1 + len(own_terms)),
            tuple(
                shape(part_rows, len(flips) * half_width, dtype=bf16 if k else f32)
                for flips in sets
                for k in order
            ),
            flops=2 * rows * model_width * half_width,
            moved=2 * model_width * (rows + 2 * half_width),
        )
        far_terms, terms = finished[:chips], finished[chips:]

        def to_shard(block, z):
            return cross(block, dp_count, fsdp_count, 0, (z,) * CORES)

        far_sums = summed_over_chips(far_terms, "far_shards_over_chips", 0, got)
        own_sum, next_sum = summed_over_chips(
            terms, "near_shards_over_chips", 1, far_sums[0]
        )
        far_sums = [to_shard(a, z) for a, z in reversed(list(zip(far_sums, sets[0])))]
        terms = [next_sum]
        next_sum = to_shard(next_sum, 1)
    grad_keys, grad_values, grad_gates = call(
        functools.partial(outputs_kernel, slots),
        "key_value_gate_gradients",
        [terms[0], query, normed, grad_mixed, attention, grad_scores, near_cotangent],
        [ANYWHERE] + [NEAR] * 6,
        (shape(rows, width),) * 3,
        flops=4 * rows * width * span,
        moved=12 * rows * width,
    )
    if staged:
        mean = call(
            functools.partial(mean_kernel, total_seqs),
            "mean_over_shards",
            [grad_keys, own_sum, next_sum] + far_sums,
            [FAR] + [NEAR] * fsdp_count,
            shape(part_rows, half_width),
        )
        blocks = call(
            stack_kernel,
            "blocks_of_chips",
            [mean, mean] + far_first(chips, lambda k: to_chip(mean, k)),
            [ANYWHERE] + [NEAR] * chips,
            shape(shard_rows, half_width),
        )
        grad_weight = ()
        for side in range(CORES):
            grad_weight = call(
                functools.partial(place_kernel, side, chips),
                f"blocks_of_{'sibling' if side else 'own'}_core_in_place",
                [flip(blocks, "dp", dp_count, 1) if side else blocks, *grad_weight],
                [NEAR] + [FAR] * side,
                shape(shard_rows, width, dtype=f32),
                [
                    pltpu.VMEM((shard_rows, half_width), f32),
                    pltpu.SemaphoreType.DMA((chips,)),
                ],
                out_specs=FAR,
                aliases={1: 0} if side else {},
            )
            grad_weight = grad_weight if side else (grad_weight,)
    else:
        whole = lax.dot_general(flat_events, grad_query, FIRST, preferred_element_type=f32)
        mine = lax.psum_scatter(whole, "fsdp", scatter_dimension=0, tiled=True)
        grad_weight = lax.psum(mine, "dp") / total_seqs

    full = (slots, span, width)
    return (
        grad_keys.reshape(full),
        grad_values.reshape(full),
        grad_gates.reshape(full),
        grad_weight,
    )


def solution(mesh):
    split = P(BOTH, None, None)
    return jax.shard_map(
        shards,
        mesh=mesh,
        in_specs=(split, P("fsdp", None), split, split, split, split, P()),
        out_specs=(split, split, split, P("fsdp", None)),
        check_vma=False,
    )
```

```python
import functools
import math

import jax
import jax.numpy as jnp
from jax import lax
from jax.experimental import pallas as pl
from jax.experimental.pallas import tpu as pltpu
from jax.sharding import PartitionSpec as P

HEADS = 4
EPSILON = 1e-06
CORES = 2
BOTH = ("dp", "fsdp")
VMEM_LIMIT = 24 * 1024 * 1024

LAST = (((1,), (1,)), ((), ()))
FIRST = (((0,), (0,)), ((), ()))


def dot(lhs, rhs, dims=(((1,), (0,)), ((), ()))):
    return lax.dot_general(lhs, rhs, dims, preferred_element_type=jnp.float32)


def call(kernel, name, operands, in_specs, out_shape, scratch=(), flops=0, moved=0,
         out_specs=None, aliases=None):
    vmem = pl.BlockSpec(memory_space=pltpu.VMEM)
    many = isinstance(out_shape, tuple)
    operands = [
        pltpu.with_memory_space_constraint(a, pltpu.HBM) if spec is FAR else a
        for a, spec in zip(operands, in_specs)
    ]
    return pl.pallas_call(
        kernel,
        out_shape=out_shape,
        in_specs=in_specs,
        out_specs=out_specs or ((vmem,) * len(out_shape) if many else vmem),
        scratch_shapes=list(scratch),
        input_output_aliases=aliases or {},
        compiler_params=pltpu.CompilerParams(vmem_limit_bytes=VMEM_LIMIT),
        cost_estimate=pl.CostEstimate(flops=flops, bytes_accessed=moved, transcendentals=0),
        name=name,
    )(*operands)


NEAR = pl.BlockSpec(memory_space=pltpu.VMEM)
ANYWHERE = pl.BlockSpec(memory_space=pl.ANY)
FAR = pl.BlockSpec(memory_space=pltpu.HBM)


def head_columns(width):
    depth = width // HEADS
    return [slice(h * depth, (h + 1) * depth) for h in range(HEADS)]


def slot_rows(rows, slots):
    span = rows // slots
    return [slice(s * span, (s + 1) * span) for s in range(slots)]


def row_mean(blocks, width):
    return jnp.sum(sum(blocks[1:], blocks[0]), axis=1, keepdims=True) / width


def slice_kernel(group, block_ref, out_ref, sem):
    rows = out_ref.shape[0]
    start = pl.multiple_of(lax.rem(lax.axis_index("dp"), group) * rows, rows)
    copy = pltpu.make_async_copy(block_ref.at[pl.ds(start, rows)], out_ref, sem)
    copy.start()
    copy.wait()


def prepare_kernel(slots, _, lengths_ref, sibling_ref, *refs):
    inputs, held = refs[:6], refs[6:11]
    (events_t_ref, key_t_ref, value_t_ref, weight_ref, gated_ref, first_ref,
     gate_ref, own_lengths_ref, sems) = refs[11:]
    events_ref, key_ref, value_ref, upstream_ref, _ = held
    copies = [
        pltpu.make_async_copy(source, target, sems.at[i])
        for i, (source, target) in enumerate(zip(inputs, held + (gate_ref,)))
    ]
    copies.append(pltpu.make_async_copy(lengths_ref, own_lengths_ref, sems.at[len(copies)]))
    for copy in copies:
        copy.start()
    rows, width = key_ref.shape
    events_t_ref[:, rows:] = sibling_ref[...].T
    for copy in copies:
        copy.wait()
    events_t_ref[:, :rows] = events_ref[...].T
    key_t_ref[...] = key_ref[...].T
    value_t_ref[...] = value_ref[...].T
    span = rows // slots
    row = lax.broadcasted_iota(jnp.int32, (span, span), 0)
    column = lax.broadcasted_iota(jnp.int32, (span, span), 1)
    first_slot = (lax.axis_index("dp") * lax.axis_size("fsdp") + lax.axis_index("fsdp")) * slots
    for s, place in enumerate(slot_rows(rows, slots)):
        length = own_lengths_ref[first_slot + s]
        inverse = 1.0 / jnp.full((span, span), length, jnp.int32).astype(jnp.float32)
        weight_ref[s] = jnp.where((column <= row) & (row < length), inverse, 0.0)
        live = lax.broadcasted_iota(jnp.int32, (span, width), 0) < length
        gated = upstream_ref[place].astype(jnp.float32) * gate_ref[place].astype(jnp.float32)
        gated = jnp.where(live, gated, 0.0)
        gated_ref[place] = gated
        first = row_mean([gated[:, c] for c in head_columns(width)], width)
        first_ref[place] = jnp.broadcast_to(first, (span, first_ref.shape[1]))


def piece_start(shard_rows, group, part_rows, flips, member_flip):
    device = lax.axis_index("dp")
    start = (
        lax.axis_index("fsdp") ^ jnp.where(lax.rem(device, CORES) == 0, flips[0], flips[1])
    ) * shard_rows
    if member_flip is not None:
        start = start + (lax.rem(device, group) ^ member_flip) * part_rows
    return pl.multiple_of(start, 16)


def aligned(shard_rows):
    return shard_rows % 128 == 0


def project(events_ref, pieces, origins, group, shard_rows, spare_ref, sems):
    copies, total = [], None
    for piece, (flips, members) in zip(pieces, origins):
        rows = piece.shape[0] // len(members)
        starts = [piece_start(shard_rows, group, rows, flips, m) for m in members]
        if not aligned(shard_rows):
            for i, start in enumerate(starts):
                copy = pltpu.make_async_copy(
                    piece.at[pl.ds(i * rows, rows)],
                    spare_ref.at[pl.ds(start, rows)],
                    sems.at[len(copies)],
                )
                copy.start()
                copies.append(copy)
            continue
        first = piece_start(shard_rows, group, rows, flips, None)
        if len(members) > 1:
            spare_ref[...] = jnp.zeros_like(spare_ref)
            for i, start in enumerate(starts):
                place = pl.ds(pl.multiple_of(start - first, 16), rows)
                spare_ref[place] = piece[i * rows : (i + 1) * rows]
            piece = spare_ref
        columns = pl.ds(pl.multiple_of(first, 128), shard_rows)
        term = dot(events_ref[:, columns], piece[...])
        total = term if total is None else total + term
    if copies:
        for copy in copies:
            copy.wait()
        total = dot(events_ref[...], spare_ref[...])
    return total


def projection_scratch(shard_rows, model_width, width, origins):
    count = sum(len(members) for _, members in origins)
    spare_rows = shard_rows if aligned(shard_rows) else model_width
    return [pltpu.VMEM((spare_rows, width), jnp.bfloat16), pltpu.SemaphoreType.DMA((count,))]


def projection_kernel(group, shard_rows, origins, *refs):
    pieces, (events_ref, *terms) = refs[: len(origins)], refs[len(origins) : -3]
    out_ref, spare_ref, sems = refs[-3:]
    total = project(events_ref, pieces, origins, group, shard_rows, spare_ref, sems)
    for term in terms:
        total = total + term[...]
    out_ref[...] = total


def attention_kernel(slots, group, shard_rows, origins, *refs):
    pieces = refs[: len(origins)]
    terms, refs = refs[len(origins) : -16], refs[-16:]
    (events_ref, key_ref, value_ref, key_t_ref, value_t_ref, weight_ref, gated_ref, first_ref,
     grad_query_ref, query_ref, normed_ref, mixed_grad_ref, attention_ref, scores_grad_ref,
     spare_ref, sems) = refs
    query = project(events_ref, pieces, origins, group, shard_rows, spare_ref, sems)
    for term in terms:
        query = query + term[...]
    query_ref[...] = query.astype(jnp.bfloat16)

    rows, width = key_ref.shape
    scale = 1.0 / math.sqrt(width // HEADS)
    columns = head_columns(width)
    places = slot_rows(rows, slots)
    each = [(s, h, s * HEADS + h) for s in range(slots) for h in range(HEADS)]
    slopes, mixed, grad_mixed = [], [], []
    for s, h, i in each:
        scores = dot(query_ref[places[s], columns[h]], key_t_ref[columns[h], places[s]]) * scale
        sigmoid = 1.0 / (1.0 + jnp.exp(-scores))
        silu = scores * sigmoid
        attention_ref[i] = (silu * weight_ref[s]).astype(jnp.bfloat16)
        slopes.append((sigmoid + silu * (1.0 - sigmoid)) * weight_ref[s])
    for s, h, i in each:
        mixed.append(dot(attention_ref[i], value_ref[places[s], columns[h]]))
    for s in range(slots):
        own = mixed[s * HEADS : (s + 1) * HEADS]
        mean = row_mean(own, width)
        centred = [m - mean for m in own]
        inv_std = lax.rsqrt(row_mean([c * c for c in centred], width) + EPSILON)
        normed = [c * inv_std for c in centred]
        gated = [gated_ref[places[s], c] for c in columns]
        second = row_mean([g * n for g, n in zip(gated, normed)], width)
        first = first_ref[places[s]]
        for h in range(HEADS):
            normed_ref[places[s], columns[h]] = normed[h]
            grad = inv_std * (gated[h] - first - normed[h] * second)
            mixed_grad_ref[places[s], columns[h]] = grad.astype(jnp.bfloat16)
    for s, h, i in each:
        grad_attention = dot(
            mixed_grad_ref[places[s], columns[h]], value_t_ref[columns[h], places[s]]
        )
        scores_grad_ref[i] = (grad_attention * slopes[i]).astype(jnp.bfloat16)
    for s, h, i in each:
        grad_query = dot(scores_grad_ref[i], key_ref[places[s], columns[h]]) * scale
        grad_query_ref[places[s], columns[h]] = grad_query.astype(jnp.bfloat16)


def outputs_kernel(slots, _, query_ref, normed_ref, mixed_grad_ref, attention_ref, scores_grad_ref,
                   upstream_ref, grad_key_ref, grad_value_ref, grad_gate_ref):
    rows, width = query_ref.shape
    scale = 1.0 / math.sqrt(width // HEADS)
    columns = head_columns(width)
    places = slot_rows(rows, slots)
    grad_gate_ref[...] = (upstream_ref[...].astype(jnp.float32) * normed_ref[...]).astype(
        jnp.bfloat16
    )
    for s in range(slots):
        for h in range(HEADS):
            i = s * HEADS + h
            grad_value = dot(attention_ref[i], mixed_grad_ref[places[s], columns[h]], FIRST)
            grad_value_ref[places[s], columns[h]] = grad_value.astype(jnp.bfloat16)
            grad_key = dot(scores_grad_ref[i], query_ref[places[s], columns[h]], FIRST) * scale
            grad_key_ref[places[s], columns[h]] = grad_key.astype(jnp.bfloat16)


def summing_half(k, z):
    return lax.rem(lax.axis_index("dp"), CORES) ^ (1 if k else 0) ^ (1 if z else 0)


def gradient_picks(chips, shard_flips):
    every = [(k, i, z) for k in range(chips) for i, z in enumerate(shard_flips)]
    return [[p for p in every if (p[0] != 0) ^ (p[2] != 0) == bool(side)] for side in range(CORES)]


def half_columns(side, half):
    return pl.ds(pl.multiple_of(summing_half(side, 0) * half, half), half)


def own_gradient_kernel(chips, sets, events_ref, grad_query_ref, *refs):
    outs, picked_ref = refs[:-1], refs[-1]
    rows, half = grad_query_ref.shape[0], grad_query_ref.shape[1] // CORES
    shard_rows = events_ref.shape[0] // lax.axis_size("fsdp")
    part_rows = shard_rows // chips
    chip, here = lax.div(lax.axis_index("dp"), CORES), lax.axis_index("fsdp")
    for flips, term_ref, other_ref in zip(sets, outs[::2], outs[1::2]):
        at = 0
        for side, picks in enumerate(gradient_picks(chips, flips)):
            first = at
            for k, _, z in picks:
                start = (here ^ z) * shard_rows + (chip ^ k) * part_rows
                source = pl.ds(pl.multiple_of(start, part_rows), part_rows)
                picked_ref[at : at + part_rows] = events_ref[source, :rows]
                other_ref[at : at + part_rows] = events_ref[source, rows:]
                at += part_rows
            columns = half_columns(side, half)
            term_ref[first:at] = dot(picked_ref[first:at], grad_query_ref[:, columns])


def gradient_kernel(order, sets, grad_query_ref, *refs):
    terms, outs = refs[: 2 * len(sets)], refs[2 * len(sets) :]
    for which, flips in enumerate(sets):
        term_ref, events_ref = terms[2 * which : 2 * which + 2]
        out_of = dict(zip(order, outs[which * len(order) :]))
        half = term_ref.shape[1]
        part_rows = out_of[0].shape[0]
        at = 0
        for side, picks in enumerate(gradient_picks(len(order), flips)):
            rows = slice(at, at + len(picks) * part_rows)
            columns = half_columns(side, half)
            total = term_ref[rows] + dot(events_ref[rows], grad_query_ref[:, columns])
            for p, (k, i, _) in enumerate(picks):
                block = total[p * part_rows : (p + 1) * part_rows]
                out_of[k][:, i * half : (i + 1) * half] = block.astype(out_of[k].dtype)
            at = rows.stop


def chip_sum_kernel(term_count, _, *refs):
    terms, outs = refs[:term_count], refs[term_count:]
    at = 0
    for out in outs:
        columns = slice(at, at + out.shape[1])
        total = terms[0][:, columns].astype(jnp.float32)
        for term in terms[1:]:
            total = total + term[:, columns].astype(jnp.float32)
        out[...] = total.astype(out.dtype)
        at += out.shape[1]


def mean_kernel(count, _, *refs):
    total = refs[0][...].astype(jnp.float32)
    for term in refs[1:-1]:
        total = total + term[...].astype(jnp.float32)
    refs[-1][...] = (total / count).astype(refs[-1].dtype)


def place_kernel(side, chips, blocks_ref, *refs):
    out_ref, held_ref, sems = refs[-3:]
    rows, half = blocks_ref.shape[0] // chips, blocks_ref.shape[1]
    core, chip = lax.rem(lax.axis_index("dp"), CORES) ^ side, lax.div(lax.axis_index("dp"), CORES)
    held_ref[...] = blocks_ref[...].astype(held_ref.dtype)
    copies = []
    for k in range(chips):
        place = pl.ds(pl.multiple_of((chip ^ k) * rows, rows), rows)
        columns = pl.ds(pl.multiple_of((core ^ (1 if k else 0)) * half, half), half)
        block = held_ref.at[pl.ds(k * rows, rows)]
        copies.append(pltpu.make_async_copy(block, out_ref.at[place, columns], sems.at[k]))
        copies[k].start()
    for copy in copies:
        copy.wait()


def flip(block, axis, count, bits):
    return lax.ppermute(block, axis, [(i, i ^ bits) for i in range(count)])


def cross(block, dp_count, fsdp_count, chip_bits, shard_bits):
    pairs = [
        (
            d * fsdp_count + z,
            (d ^ (chip_bits * CORES) ^ 1) * fsdp_count + (z ^ shard_bits[d % CORES]),
        )
        for d in range(dp_count)
        for z in range(fsdp_count)
    ]
    return lax.ppermute(block, BOTH, pairs)


def far_first(count, send):
    return [send(k) for k in range(count - 1, 0, -1)][::-1]


def shard_pairs(fsdp_count):
    others = [d for d in range(1, fsdp_count) if d != fsdp_count // 2]
    return list(zip(others[::2], others[1::2]))


def across_z(weight, dp_count, fsdp_count):
    rows = weight.shape[0]
    group = max(g for g in (2, 4, 8) if dp_count % g == 0 and rows % (16 * g) == 0)
    part = call(
        functools.partial(slice_kernel, group),
        "own_part_of_weight",
        [weight],
        [FAR],
        jax.ShapeDtypeStruct((rows // group, weight.shape[1]), weight.dtype),
        [pltpu.SemaphoreType.DMA],
    )
    weight, part = lax.optimization_barrier((weight, part))
    middle = (fsdp_count // 2,) * CORES
    part = cross(part, dp_count, fsdp_count, 0, middle)
    wholes = [
        (cross(weight, dp_count, fsdp_count, 0, flips), flips[::-1])
        for flips in shard_pairs(fsdp_count)
    ]
    return group, part, wholes


def stack_kernel(_, *refs):
    out_ref = refs[-1]
    rows = refs[0].shape[0]
    for i, block_ref in enumerate(refs[:-1]):
        out_ref[i * rows : (i + 1) * rows] = block_ref[...]


def share(group, part, wholes, ready, dp_count, fsdp_count):
    alike = (0,) * CORES
    parts, members = [part], [1]
    for chip_bits in range(1, group // CORES):
        parts.append(cross(part, dp_count, fsdp_count, chip_bits, alike))
        members.append(CORES * chip_bits)
    if len(parts) > 1:
        rows, columns = part.shape
        part = call(
            stack_kernel,
            "parts_of_weight",
            [ready] + parts,
            [ANYWHERE] + [NEAR] * len(parts),
            jax.ShapeDtypeStruct((len(parts) * rows, columns), part.dtype),
        )
    held = [(part, (fsdp_count // 2,) * CORES, members)]
    for block, flips in wholes:
        held.append((lax.optimization_barrier((block, part))[0], flips, [None]))
    moved = []
    for block, flips, members in held:
        places = [m if m is None else m ^ 1 for m in members]
        moved.append((flip(block, "dp", dp_count, 1), flips[::-1], places))
    return held, moved


def shards(events, query_weight, keys, values, gates, cotangent, lengths):
    slots, span, model_width = events.shape
    width = query_weight.shape[1]
    half_width = width // CORES
    rows = slots * span
    dp_count, fsdp_count = lax.axis_size("dp"), lax.axis_size("fsdp")
    chips = dp_count // CORES
    shard_rows = model_width // fsdp_count
    total_seqs = slots * dp_count * fsdp_count
    bf16, f32 = jnp.bfloat16, jnp.float32

    def shape(*dims, dtype=bf16):
        return jax.ShapeDtypeStruct(dims, dtype)

    flat_events = events.reshape(rows, model_width)
    keys, values, gates, cotangent = (
        a.reshape(rows, width) for a in (keys, values, gates, cotangent)
    )
    sibling_events = flip(flat_events, "dp", dp_count, 1)
    group, part, wholes = across_z(query_weight, dp_count, fsdp_count)
    prepared = call(
        functools.partial(prepare_kernel, slots),
        "prepared_operands",
        [part, lengths, sibling_events]
        + [flat_events, keys, values, cotangent, query_weight, gates],
        [ANYWHERE, FAR, NEAR] + [FAR] * 6,
        (
            shape(rows, model_width),
            shape(rows, width),
            shape(rows, width),
            shape(rows, width),
            shape(shard_rows, width),
            shape(model_width, CORES * rows),
            shape(width, rows),
            shape(width, rows),
            shape(slots, span, span, dtype=f32),
            shape(rows, width, dtype=f32),
            shape(rows, span, dtype=f32),
        ),
        [
            pltpu.VMEM((rows, width), bf16),
            pltpu.SMEM(lengths.shape, jnp.int32),
            pltpu.SemaphoreType.DMA((7,)),
        ],
        flops=5 * 10**9,
    )
    near_events, near_keys, near_values, near_cotangent, near_weight = prepared[:5]
    events_t, keys_t, values_t, weight, gated, first = prepared[5:]
    held, moved = share(group, part, wholes, first, dp_count, fsdp_count)
    held = [(near_weight, (0, 0), [None])] + held
    if not aligned(shard_rows):
        held, moved = [], held + moved

    def split(found):
        return [f[0] for f in found], [f[1:] for f in found]

    terms = []
    for name, found in (("held", held), ("passed", moved[:1])):
        if not held:
            break
        pieces, origins = split(found)
        operands = pieces + [near_events] + terms
        terms = [
            call(
                functools.partial(projection_kernel, group, shard_rows, origins),
                f"projection_by_{name}_rows",
                operands,
                [NEAR] * len(operands),
                shape(rows, width, dtype=f32),
                projection_scratch(shard_rows, model_width, width, origins),
                flops=2 * rows * width * shard_rows * len(pieces),
                moved=4 * rows * width,
            )
        ]
    if held:
        moved = moved[1:]
    pieces, origins = split(moved)
    blocks = shape(slots * HEADS, span, span)
    grad_query, query, normed, grad_mixed, attention, grad_scores = call(
        functools.partial(attention_kernel, slots, group, shard_rows, origins),
        "attention_to_grad_query",
        pieces
        + terms
        + [near_events, near_keys, near_values, keys_t, values_t, weight, gated, first],
        [NEAR] * (len(pieces) + len(terms) + 8),
        (
            shape(rows, width),
            shape(rows, width),
            shape(rows, width, dtype=f32),
            shape(rows, width),
            blocks,
            blocks,
        ),
        projection_scratch(shard_rows, model_width, width, origins),
        flops=2 * rows * width * (model_width + 4 * span),
        moved=24 * rows * width,
    )
    part_rows = shard_rows // chips
    staged = part_rows % 16 == 0 and fsdp_count % 4 == 0
    terms = [grad_query]
    if staged:
        alike = (0,) * CORES

        def to_chip(block, k):
            return cross(block, dp_count, fsdp_count, k, alike)

        order = (0,) + tuple(range(chips - 1, 0, -1))

        def summed_over_chips(terms, name, which, after):
            flips = sets[which]
            terms = [terms[0]] + [to_chip(a, k) for a, k in zip(terms[1:], order[1:])]
            return call(
                functools.partial(chip_sum_kernel, chips),
                name,
                [after] + terms,
                [ANYWHERE] + [NEAR] * chips,
                tuple(shape(part_rows, half_width, dtype=bf16 if z else f32) for z in flips),
            )

        sets = (tuple(range(2, fsdp_count)), (0, 1))
        picked_rows = [len(flips) * shard_rows for flips in sets]
        got = flip(grad_query, "dp", dp_count, 1)
        own_terms = call(
            functools.partial(own_gradient_kernel, chips, sets),
            "weight_gradient_of_own_events",
            [events_t, grad_query],
            [NEAR] * 2,
            tuple(
                a
                for n in picked_rows
                for a in (shape(n, half_width, dtype=f32), shape(n, rows))
            ),
            [pltpu.VMEM((max(picked_rows), rows), bf16)],
            flops=2 * rows * model_width * half_width,
            moved=8 * model_width * rows,
        )

        finished = call(
            functools.partial(gradient_kernel, order, sets),
            "weight_gradient_of_both_cores",
            [got, *own_terms],
            [NEAR] * (1 + len(own_terms)),
            tuple(
                shape(part_rows, len(flips) * half_width, dtype=bf16 if k else f32)
                for flips in sets
                for k in order
            ),
            flops=2 * rows * model_width * half_width,
            moved=2 * model_width * (rows + 2 * half_width),
        )
        far_terms, terms = finished[:chips], finished[chips:]

        def to_shard(block, z):
            return cross(block, dp_count, fsdp_count, 0, (z,) * CORES)

        far_sums = summed_over_chips(far_terms, "far_shards_over_chips", 0, got)
        own_sum, next_sum = summed_over_chips(
            terms, "near_shards_over_chips", 1, far_sums[0]
        )
        far_sums = [to_shard(a, z) for a, z in reversed(list(zip(far_sums, sets[0])))]
        terms = [next_sum]
        next_sum = to_shard(next_sum, 1)
    grad_keys, grad_values, grad_gates = call(
        functools.partial(outputs_kernel, slots),
        "key_value_gate_gradients",
        [terms[0], query, normed, grad_mixed, attention, grad_scores, near_cotangent],
        [ANYWHERE] + [NEAR] * 6,
        (shape(rows, width),) * 3,
        flops=4 * rows * width * span,
        moved=12 * rows * width,
    )
    if staged:
        mean = call(
            functools.partial(mean_kernel, total_seqs),
            "mean_over_shards",
            [grad_keys, own_sum, next_sum] + far_sums,
            [FAR] + [NEAR] * fsdp_count,
            shape(part_rows, half_width),
        )
        blocks = call(
            stack_kernel,
            "blocks_of_chips",
            [mean, mean] + far_first(chips, lambda k: to_chip(mean, k)),
            [ANYWHERE] + [NEAR] * chips,
            shape(shard_rows, half_width),
        )
        grad_weight = ()
        for side in range(CORES):
            grad_weight = call(
                functools.partial(place_kernel, side, chips),
                f"blocks_of_{'sibling' if side else 'own'}_core_in_place",
                [flip(blocks, "dp", dp_count, 1) if side else blocks, *grad_weight],
                [NEAR] + [FAR] * side,
                shape(shard_rows, width, dtype=f32),
                [
                    pltpu.VMEM((shard_rows, half_width), f32),
                    pltpu.SemaphoreType.DMA((chips,)),
                ],
                out_specs=FAR,
                aliases={1: 0} if side else {},
            )
            grad_weight = grad_weight if side else (grad_weight,)
    else:
        whole = lax.dot_general(flat_events, grad_query, FIRST, preferred_element_type=f32)
        mine = lax.psum_scatter(whole, "fsdp", scatter_dimension=0, tiled=True)
        grad_weight = lax.psum(mine, "dp") / total_seqs

    full = (slots, span, width)
    return (
        grad_keys.reshape(full),
        grad_values.reshape(full),
        grad_gates.reshape(full),
        grad_weight,
    )


def solution(mesh):
    split = P(BOTH, None, None)
    return jax.shard_map(
        shards,
        mesh=mesh,
        in_specs=(split, P("fsdp", None), split, split, split, split, P()),
        out_specs=(split, split, split, P("fsdp", None)),
        check_vma=False,
    )
```

```python
import functools
import math

import jax
import jax.numpy as jnp
from jax import lax
from jax.experimental import pallas as pl
from jax.experimental.pallas import tpu as pltpu
from jax.sharding import PartitionSpec as P

HEADS = 4
EPSILON = 1e-06
CORES = 2
BOTH = ("dp", "fsdp")
VMEM_LIMIT = 24 * 1024 * 1024

LAST = (((1,), (1,)), ((), ()))
FIRST = (((0,), (0,)), ((), ()))


def dot(lhs, rhs, dims=(((1,), (0,)), ((), ()))):
    return lax.dot_general(lhs, rhs, dims, preferred_element_type=jnp.float32)


def call(kernel, name, operands, in_specs, out_shape, scratch=(), flops=0, moved=0,
         out_specs=None, aliases=None):
    vmem = pl.BlockSpec(memory_space=pltpu.VMEM)
    many = isinstance(out_shape, tuple)
    operands = [
        pltpu.with_memory_space_constraint(a, pltpu.HBM) if spec is FAR else a
        for a, spec in zip(operands, in_specs)
    ]
    return pl.pallas_call(
        kernel,
        out_shape=out_shape,
        in_specs=in_specs,
        out_specs=out_specs or ((vmem,) * len(out_shape) if many else vmem),
        scratch_shapes=list(scratch),
        input_output_aliases=aliases or {},
        compiler_params=pltpu.CompilerParams(vmem_limit_bytes=VMEM_LIMIT),
        cost_estimate=pl.CostEstimate(flops=flops, bytes_accessed=moved, transcendentals=0),
        name=name,
    )(*operands)


NEAR = pl.BlockSpec(memory_space=pltpu.VMEM)
ANYWHERE = pl.BlockSpec(memory_space=pl.ANY)
FAR = pl.BlockSpec(memory_space=pltpu.HBM)


def head_columns(width):
    depth = width // HEADS
    return [slice(h * depth, (h + 1) * depth) for h in range(HEADS)]


def slot_rows(rows, slots):
    span = rows // slots
    return [slice(s * span, (s + 1) * span) for s in range(slots)]


def row_mean(blocks, width):
    return jnp.sum(sum(blocks[1:], blocks[0]), axis=1, keepdims=True) / width


def slice_kernel(group, block_ref, out_ref, sem):
    rows = out_ref.shape[0]
    start = pl.multiple_of(lax.rem(lax.axis_index("dp"), group) * rows, rows)
    copy = pltpu.make_async_copy(block_ref.at[pl.ds(start, rows)], out_ref, sem)
    copy.start()
    copy.wait()


def prepare_kernel(slots, _, lengths_ref, sibling_ref, *refs):
    inputs, held = refs[:6], refs[6:11]
    (events_t_ref, key_t_ref, value_t_ref, weight_ref, gated_ref, first_ref,
     gate_ref, own_lengths_ref, sems) = refs[11:]
    events_ref, key_ref, value_ref, upstream_ref, _ = held
    copies = [
        pltpu.make_async_copy(source, target, sems.at[i])
        for i, (source, target) in enumerate(zip(inputs, held + (gate_ref,)))
    ]
    copies.append(pltpu.make_async_copy(lengths_ref, own_lengths_ref, sems.at[len(copies)]))
    for copy in copies:
        copy.start()
    rows, width = key_ref.shape
    events_t_ref[:, rows:] = sibling_ref[...].T
    for copy in copies:
        copy.wait()
    events_t_ref[:, :rows] = events_ref[...].T
    key_t_ref[...] = key_ref[...].T
    value_t_ref[...] = value_ref[...].T
    span = rows // slots
    row = lax.broadcasted_iota(jnp.int32, (span, span), 0)
    column = lax.broadcasted_iota(jnp.int32, (span, span), 1)
    first_slot = (lax.axis_index("dp") * lax.axis_size("fsdp") + lax.axis_index("fsdp")) * slots
    for s, place in enumerate(slot_rows(rows, slots)):
        length = own_lengths_ref[first_slot + s]
        inverse = 1.0 / jnp.full((span, span), length, jnp.int32).astype(jnp.float32)
        weight_ref[s] = jnp.where((column <= row) & (row < length), inverse, 0.0)
        live = lax.broadcasted_iota(jnp.int32, (span, width), 0) < length
        gated = upstream_ref[place].astype(jnp.float32) * gate_ref[place].astype(jnp.float32)
        gated = jnp.where(live, gated, 0.0)
        gated_ref[place] = gated
        first = row_mean([gated[:, c] for c in head_columns(width)], width)
        first_ref[place] = jnp.broadcast_to(first, (span, first_ref.shape[1]))


def piece_start(shard_rows, group, part_rows, flips, member_flip):
    device = lax.axis_index("dp")
    start = (
        lax.axis_index("fsdp") ^ jnp.where(lax.rem(device, CORES) == 0, flips[0], flips[1])
    ) * shard_rows
    if member_flip is not None:
        start = start + (lax.rem(device, group) ^ member_flip) * part_rows
    return pl.multiple_of(start, 16)


def aligned(shard_rows):
    return shard_rows % 128 == 0


def project(events_ref, pieces, origins, group, shard_rows, spare_ref, sems):
    copies, total = [], None
    for piece, (flips, members) in zip(pieces, origins):
        rows = piece.shape[0] // len(members)
        starts = [piece_start(shard_rows, group, rows, flips, m) for m in members]
        if not aligned(shard_rows):
            for i, start in enumerate(starts):
                copy = pltpu.make_async_copy(
                    piece.at[pl.ds(i * rows, rows)],
                    spare_ref.at[pl.ds(start, rows)],
                    sems.at[len(copies)],
                )
                copy.start()
                copies.append(copy)
            continue
        first = piece_start(shard_rows, group, rows, flips, None)
        if len(members) > 1:
            spare_ref[...] = jnp.zeros_like(spare_ref)
            for i, start in enumerate(starts):
                place = pl.ds(pl.multiple_of(start - first, 16), rows)
                spare_ref[place] = piece[i * rows : (i + 1) * rows]
            piece = spare_ref
        columns = pl.ds(pl.multiple_of(first, 128), shard_rows)
        term = dot(events_ref[:, columns], piece[...])
        total = term if total is None else total + term
    if copies:
        for copy in copies:
            copy.wait()
        total = dot(events_ref[...], spare_ref[...])
    return total


def projection_scratch(shard_rows, model_width, width, origins):
    count = sum(len(members) for _, members in origins)
    spare_rows = shard_rows if aligned(shard_rows) else model_width
    return [pltpu.VMEM((spare_rows, width), jnp.bfloat16), pltpu.SemaphoreType.DMA((count,))]


def projection_kernel(group, shard_rows, origins, *refs):
    pieces, (events_ref, *terms) = refs[: len(origins)], refs[len(origins) : -3]
    out_ref, spare_ref, sems = refs[-3:]
    total = project(events_ref, pieces, origins, group, shard_rows, spare_ref, sems)
    for term in terms:
        total = total + term[...]
    out_ref[...] = total


def attention_kernel(slots, group, shard_rows, origins, *refs):
    pieces = refs[: len(origins)]
    terms, refs = refs[len(origins) : -16], refs[-16:]
    (events_ref, key_ref, value_ref, key_t_ref, value_t_ref, weight_ref, gated_ref, first_ref,
     grad_query_ref, query_ref, normed_ref, mixed_grad_ref, attention_ref, scores_grad_ref,
     spare_ref, sems) = refs
    query = project(events_ref, pieces, origins, group, shard_rows, spare_ref, sems)
    for term in terms:
        query = query + term[...]
    query_ref[...] = query.astype(jnp.bfloat16)

    rows, width = key_ref.shape
    scale = 1.0 / math.sqrt(width // HEADS)
    columns = head_columns(width)
    places = slot_rows(rows, slots)
    each = [(s, h, s * HEADS + h) for s in range(slots) for h in range(HEADS)]
    slopes, mixed, grad_mixed = [], [], []
    for s, h, i in each:
        scores = dot(query_ref[places[s], columns[h]], key_t_ref[columns[h], places[s]]) * scale
        sigmoid = 1.0 / (1.0 + jnp.exp(-scores))
        silu = scores * sigmoid
        attention_ref[i] = (silu * weight_ref[s]).astype(jnp.bfloat16)
        slopes.append((sigmoid + silu * (1.0 - sigmoid)) * weight_ref[s])
    for s, h, i in each:
        mixed.append(dot(attention_ref[i], value_ref[places[s], columns[h]]))
    for s in range(slots):
        own = mixed[s * HEADS : (s + 1) * HEADS]
        mean = row_mean(own, width)
        centred = [m - mean for m in own]
        inv_std = lax.rsqrt(row_mean([c * c for c in centred], width) + EPSILON)
        normed = [c * inv_std for c in centred]
        gated = [gated_ref[places[s], c] for c in columns]
        second = row_mean([g * n for g, n in zip(gated, normed)], width)
        first = first_ref[places[s]]
        for h in range(HEADS):
            normed_ref[places[s], columns[h]] = normed[h]
            grad = inv_std * (gated[h] - first - normed[h] * second)
            mixed_grad_ref[places[s], columns[h]] = grad.astype(jnp.bfloat16)
    for s, h, i in each:
        grad_attention = dot(
            mixed_grad_ref[places[s], columns[h]], value_t_ref[columns[h], places[s]]
        )
        scores_grad_ref[i] = (grad_attention * slopes[i]).astype(jnp.bfloat16)
    for s, h, i in each:
        grad_query = dot(scores_grad_ref[i], key_ref[places[s], columns[h]]) * scale
        grad_query_ref[places[s], columns[h]] = grad_query.astype(jnp.bfloat16)


def outputs_kernel(slots, _, query_ref, normed_ref, mixed_grad_ref, attention_ref, scores_grad_ref,
                   upstream_ref, grad_key_ref, grad_value_ref, grad_gate_ref):
    rows, width = query_ref.shape
    scale = 1.0 / math.sqrt(width // HEADS)
    columns = head_columns(width)
    places = slot_rows(rows, slots)
    grad_gate_ref[...] = (upstream_ref[...].astype(jnp.float32) * normed_ref[...]).astype(
        jnp.bfloat16
    )
    for s in range(slots):
        for h in range(HEADS):
            i = s * HEADS + h
            grad_value = dot(attention_ref[i], mixed_grad_ref[places[s], columns[h]], FIRST)
            grad_value_ref[places[s], columns[h]] = grad_value.astype(jnp.bfloat16)
            grad_key = dot(scores_grad_ref[i], query_ref[places[s], columns[h]], FIRST) * scale
            grad_key_ref[places[s], columns[h]] = grad_key.astype(jnp.bfloat16)


def summing_half(k, z):
    return lax.rem(lax.axis_index("dp"), CORES) ^ (1 if k else 0) ^ (1 if z else 0)


def gradient_picks(chips, shard_flips):
    every = [(k, i, z) for k in range(chips) for i, z in enumerate(shard_flips)]
    return [[p for p in every if (p[0] != 0) ^ (p[2] != 0) == bool(side)] for side in range(CORES)]


def half_columns(side, half):
    return pl.ds(pl.multiple_of(summing_half(side, 0) * half, half), half)


def own_gradient_kernel(chips, sets, events_ref, grad_query_ref, *refs):
    outs, picked_ref = refs[:-1], refs[-1]
    rows, half = grad_query_ref.shape[0], grad_query_ref.shape[1] // CORES
    shard_rows = events_ref.shape[0] // lax.axis_size("fsdp")
    part_rows = shard_rows // chips
    chip, here = lax.div(lax.axis_index("dp"), CORES), lax.axis_index("fsdp")
    for flips, term_ref, other_ref in zip(sets, outs[::2], outs[1::2]):
        at = 0
        for side, picks in enumerate(gradient_picks(chips, flips)):
            first = at
            for k, _, z in picks:
                start = (here ^ z) * shard_rows + (chip ^ k) * part_rows
                source = pl.ds(pl.multiple_of(start, part_rows), part_rows)
                picked_ref[at : at + part_rows] = events_ref[source, :rows]
                other_ref[at : at + part_rows] = events_ref[source, rows:]
                at += part_rows
            columns = half_columns(side, half)
            term_ref[first:at] = dot(picked_ref[first:at], grad_query_ref[:, columns])


def gradient_kernel(order, sets, grad_query_ref, *refs):
    terms, outs = refs[: 2 * len(sets)], refs[2 * len(sets) :]
    for which, flips in enumerate(sets):
        term_ref, events_ref = terms[2 * which : 2 * which + 2]
        out_of = dict(zip(order, outs[which * len(order) :]))
        half = term_ref.shape[1]
        part_rows = out_of[0].shape[0]
        at = 0
        for side, picks in enumerate(gradient_picks(len(order), flips)):
            rows = slice(at, at + len(picks) * part_rows)
            columns = half_columns(side, half)
            total = term_ref[rows] + dot(events_ref[rows], grad_query_ref[:, columns])
            for p, (k, i, _) in enumerate(picks):
                block = total[p * part_rows : (p + 1) * part_rows]
                out_of[k][:, i * half : (i + 1) * half] = block.astype(out_of[k].dtype)
            at = rows.stop


def chip_sum_kernel(term_count, _, *refs):
    terms, outs = refs[:term_count], refs[term_count:]
    at = 0
    for out in outs:
        columns = slice(at, at + out.shape[1])
        total = terms[0][:, columns].astype(jnp.float32)
        for term in terms[1:]:
            total = total + term[:, columns].astype(jnp.float32)
        out[...] = total.astype(out.dtype)
        at += out.shape[1]


def mean_kernel(count, _, *refs):
    total = refs[0][...].astype(jnp.float32)
    for term in refs[1:-1]:
        total = total + term[...].astype(jnp.float32)
    refs[-1][...] = (total / count).astype(refs[-1].dtype)


def place_kernel(side, chips, blocks_ref, *refs):
    out_ref, held_ref, sems = refs[-3:]
    rows, half = blocks_ref.shape[0] // chips, blocks_ref.shape[1]
    core, chip = lax.rem(lax.axis_index("dp"), CORES) ^ side, lax.div(lax.axis_index("dp"), CORES)
    held_ref[...] = blocks_ref[...].astype(held_ref.dtype)
    copies = []
    for k in range(chips):
        place = pl.ds(pl.multiple_of((chip ^ k) * rows, rows), rows)
        columns = pl.ds(pl.multiple_of((core ^ (1 if k else 0)) * half, half), half)
        block = held_ref.at[pl.ds(k * rows, rows)]
        copies.append(pltpu.make_async_copy(block, out_ref.at[place, columns], sems.at[k]))
        copies[k].start()
    for copy in copies:
        copy.wait()


def flip(block, axis, count, bits):
    return lax.ppermute(block, axis, [(i, i ^ bits) for i in range(count)])


def cross(block, dp_count, fsdp_count, chip_bits, shard_bits):
    pairs = [
        (
            d * fsdp_count + z,
            (d ^ (chip_bits * CORES) ^ 1) * fsdp_count + (z ^ shard_bits[d % CORES]),
        )
        for d in range(dp_count)
        for z in range(fsdp_count)
    ]
    return lax.ppermute(block, BOTH, pairs)


def far_first(count, send):
    return [send(k) for k in range(count - 1, 0, -1)][::-1]


def shard_pairs(fsdp_count):
    others = [d for d in range(1, fsdp_count) if d != fsdp_count // 2]
    return list(zip(others[::2], others[1::2]))


def across_z(weight, dp_count, fsdp_count):
    rows = weight.shape[0]
    group = max(g for g in (2, 4, 8) if dp_count % g == 0 and rows % (16 * g) == 0)
    part = call(
        functools.partial(slice_kernel, group),
        "own_part_of_weight",
        [weight],
        [FAR],
        jax.ShapeDtypeStruct((rows // group, weight.shape[1]), weight.dtype),
        [pltpu.SemaphoreType.DMA],
    )
    weight, part = lax.optimization_barrier((weight, part))
    middle = (fsdp_count // 2,) * CORES
    part = cross(part, dp_count, fsdp_count, 0, middle)
    wholes = [
        (cross(weight, dp_count, fsdp_count, 0, flips), flips[::-1])
        for flips in shard_pairs(fsdp_count)
    ]
    return group, part, wholes


def stack_kernel(_, *refs):
    out_ref = refs[-1]
    rows = refs[0].shape[0]
    for i, block_ref in enumerate(refs[:-1]):
        out_ref[i * rows : (i + 1) * rows] = block_ref[...]


def share(group, part, wholes, ready, dp_count, fsdp_count):
    alike = (0,) * CORES
    parts, members = [part], [1]
    for chip_bits in range(1, group // CORES):
        parts.append(cross(part, dp_count, fsdp_count, chip_bits, alike))
        members.append(CORES * chip_bits)
    if len(parts) > 1:
        rows, columns = part.shape
        part = call(
            stack_kernel,
            "parts_of_weight",
            [ready] + parts,
            [ANYWHERE] + [NEAR] * len(parts),
            jax.ShapeDtypeStruct((len(parts) * rows, columns), part.dtype),
        )
    held = [(part, (fsdp_count // 2,) * CORES, members)]
    for block, flips in wholes:
        held.append((lax.optimization_barrier((block, part))[0], flips, [None]))
    moved = []
    for block, flips, members in held:
        places = [m if m is None else m ^ 1 for m in members]
        moved.append((flip(block, "dp", dp_count, 1), flips[::-1], places))
    return held, moved


def shards(events, query_weight, keys, values, gates, cotangent, lengths):
    slots, span, model_width = events.shape
    width = query_weight.shape[1]
    half_width = width // CORES
    rows = slots * span
    dp_count, fsdp_count = lax.axis_size("dp"), lax.axis_size("fsdp")
    chips = dp_count // CORES
    shard_rows = model_width // fsdp_count
    total_seqs = slots * dp_count * fsdp_count
    bf16, f32 = jnp.bfloat16, jnp.float32

    def shape(*dims, dtype=bf16):
        return jax.ShapeDtypeStruct(dims, dtype)

    flat_events = events.reshape(rows, model_width)
    keys, values, gates, cotangent = (
        a.reshape(rows, width) for a in (keys, values, gates, cotangent)
    )
    sibling_events = flip(flat_events, "dp", dp_count, 1)
    group, part, wholes = across_z(query_weight, dp_count, fsdp_count)
    prepared = call(
        functools.partial(prepare_kernel, slots),
        "prepared_operands",
        [part, lengths, sibling_events]
        + [flat_events, keys, values, cotangent, query_weight, gates],
        [ANYWHERE, FAR, NEAR] + [FAR] * 6,
        (
            shape(rows, model_width),
            shape(rows, width),
            shape(rows, width),
            shape(rows, width),
            shape(shard_rows, width),
            shape(model_width, CORES * rows),
            shape(width, rows),
            shape(width, rows),
            shape(slots, span, span, dtype=f32),
            shape(rows, width, dtype=f32),
            shape(rows, span, dtype=f32),
        ),
        [
            pltpu.VMEM((rows, width), bf16),
            pltpu.SMEM(lengths.shape, jnp.int32),
            pltpu.SemaphoreType.DMA((7,)),
        ],
        flops=5 * 10**9,
    )
    near_events, near_keys, near_values, near_cotangent, near_weight = prepared[:5]
    events_t, keys_t, values_t, weight, gated, first = prepared[5:]
    held, moved = share(group, part, wholes, first, dp_count, fsdp_count)
    held = [(near_weight, (0, 0), [None])] + held
    if not aligned(shard_rows):
        held, moved = [], held + moved

    def split(found):
        return [f[0] for f in found], [f[1:] for f in found]

    terms = []
    for name, found in (("held", held), ("passed", moved[:1])):
        if not held:
            break
        pieces, origins = split(found)
        operands = pieces + [near_events] + terms
        terms = [
            call(
                functools.partial(projection_kernel, group, shard_rows, origins),
                f"projection_by_{name}_rows",
                operands,
                [NEAR] * len(operands),
                shape(rows, width, dtype=f32),
                projection_scratch(shard_rows, model_width, width, origins),
                flops=3 * 10**9 if terms else 2 * rows * width * shard_rows * len(pieces),
                moved=4 * rows * width,
            )
        ]
    if held:
        moved = moved[1:]
    pieces, origins = split(moved)
    blocks = shape(slots * HEADS, span, span)
    grad_query, query, normed, grad_mixed, attention, grad_scores = call(
        functools.partial(attention_kernel, slots, group, shard_rows, origins),
        "attention_to_grad_query",
        pieces
        + terms
        + [near_events, near_keys, near_values, keys_t, values_t, weight, gated, first],
        [NEAR] * (len(pieces) + len(terms) + 8),
        (
            shape(rows, width),
            shape(rows, width),
            shape(rows, width, dtype=f32),
            shape(rows, width),
            blocks,
            blocks,
        ),
        projection_scratch(shard_rows, model_width, width, origins),
        flops=2 * rows * width * (model_width + 4 * span),
        moved=24 * rows * width,
    )
    part_rows = shard_rows // chips
    staged = part_rows % 16 == 0 and fsdp_count % 4 == 0
    terms = [grad_query]
    if staged:
        alike = (0,) * CORES

        def to_chip(block, k):
            return cross(block, dp_count, fsdp_count, k, alike)

        order = (0,) + tuple(range(chips - 1, 0, -1))

        def summed_over_chips(terms, name, which, after):
            flips = sets[which]
            terms = [terms[0]] + [to_chip(a, k) for a, k in zip(terms[1:], order[1:])]
            return call(
                functools.partial(chip_sum_kernel, chips),
                name,
                [after] + terms,
                [ANYWHERE] + [NEAR] * chips,
                tuple(shape(part_rows, half_width, dtype=bf16 if z else f32) for z in flips),
            )

        sets = (tuple(range(2, fsdp_count)), (0, 1))
        picked_rows = [len(flips) * shard_rows for flips in sets]
        got = flip(grad_query, "dp", dp_count, 1)
        own_terms = call(
            functools.partial(own_gradient_kernel, chips, sets),
            "weight_gradient_of_own_events",
            [events_t, grad_query],
            [NEAR] * 2,
            tuple(
                a
                for n in picked_rows
                for a in (shape(n, half_width, dtype=f32), shape(n, rows))
            ),
            [pltpu.VMEM((max(picked_rows), rows), bf16)],
            flops=2 * rows * model_width * half_width,
            moved=8 * model_width * rows,
        )

        finished = call(
            functools.partial(gradient_kernel, order, sets),
            "weight_gradient_of_both_cores",
            [got, *own_terms],
            [NEAR] * (1 + len(own_terms)),
            tuple(
                shape(part_rows, len(flips) * half_width, dtype=bf16 if k else f32)
                for flips in sets
                for k in order
            ),
            flops=2 * rows * model_width * half_width,
            moved=2 * model_width * (rows + 2 * half_width),
        )
        far_terms, terms = finished[:chips], finished[chips:]

        def to_shard(block, z):
            return cross(block, dp_count, fsdp_count, 0, (z,) * CORES)

        far_sums = summed_over_chips(far_terms, "far_shards_over_chips", 0, got)
        own_sum, next_sum = summed_over_chips(
            terms, "near_shards_over_chips", 1, far_sums[0]
        )
        far_sums = [to_shard(a, z) for a, z in reversed(list(zip(far_sums, sets[0])))]
        terms = [next_sum]
        next_sum = to_shard(next_sum, 1)
    grad_keys, grad_values, grad_gates = call(
        functools.partial(outputs_kernel, slots),
        "key_value_gate_gradients",
        [terms[0], query, normed, grad_mixed, attention, grad_scores, near_cotangent],
        [ANYWHERE] + [NEAR] * 6,
        (shape(rows, width),) * 3,
        flops=4 * rows * width * span,
        moved=12 * rows * width,
    )
    if staged:
        mean = call(
            functools.partial(mean_kernel, total_seqs),
            "mean_over_shards",
            [grad_keys, own_sum, next_sum] + far_sums,
            [FAR] + [NEAR] * fsdp_count,
            shape(part_rows, half_width),
        )
        blocks = call(
            stack_kernel,
            "blocks_of_chips",
            [mean, mean] + far_first(chips, lambda k: to_chip(mean, k)),
            [ANYWHERE] + [NEAR] * chips,
            shape(shard_rows, half_width),
        )
        grad_weight = ()
        for side in range(CORES):
            grad_weight = call(
                functools.partial(place_kernel, side, chips),
                f"blocks_of_{'sibling' if side else 'own'}_core_in_place",
                [flip(blocks, "dp", dp_count, 1) if side else blocks, *grad_weight],
                [NEAR] + [FAR] * side,
                shape(shard_rows, width, dtype=f32),
                [
                    pltpu.VMEM((shard_rows, half_width), f32),
                    pltpu.SemaphoreType.DMA((chips,)),
                ],
                out_specs=FAR,
                aliases={1: 0} if side else {},
            )
            grad_weight = grad_weight if side else (grad_weight,)
    else:
        whole = lax.dot_general(flat_events, grad_query, FIRST, preferred_element_type=f32)
        mine = lax.psum_scatter(whole, "fsdp", scatter_dimension=0, tiled=True)
        grad_weight = lax.psum(mine, "dp") / total_seqs

    full = (slots, span, width)
    return (
        grad_keys.reshape(full),
        grad_values.reshape(full),
        grad_gates.reshape(full),
        grad_weight,
    )


def solution(mesh):
    split = P(BOTH, None, None)
    return jax.shard_map(
        shards,
        mesh=mesh,
        in_specs=(split, P("fsdp", None), split, split, split, split, P()),
        out_specs=(split, split, split, P("fsdp", None)),
        check_vma=False,
    )
```

```python
import functools
import math

import jax
import jax.numpy as jnp
from jax import lax
from jax.experimental import pallas as pl
from jax.experimental.pallas import tpu as pltpu
from jax.sharding import PartitionSpec as P

HEADS = 4
EPSILON = 1e-06
CORES = 2
BOTH = ("dp", "fsdp")
VMEM_LIMIT = 24 * 1024 * 1024

LAST = (((1,), (1,)), ((), ()))
FIRST = (((0,), (0,)), ((), ()))


def dot(lhs, rhs, dims=(((1,), (0,)), ((), ()))):
    return lax.dot_general(lhs, rhs, dims, preferred_element_type=jnp.float32)


def call(kernel, name, operands, in_specs, out_shape, scratch=(), flops=0, moved=0,
         out_specs=None, aliases=None):
    vmem = pl.BlockSpec(memory_space=pltpu.VMEM)
    many = isinstance(out_shape, tuple)
    operands = [
        pltpu.with_memory_space_constraint(a, pltpu.HBM) if spec is FAR else a
        for a, spec in zip(operands, in_specs)
    ]
    return pl.pallas_call(
        kernel,
        out_shape=out_shape,
        in_specs=in_specs,
        out_specs=out_specs or ((vmem,) * len(out_shape) if many else vmem),
        scratch_shapes=list(scratch),
        input_output_aliases=aliases or {},
        compiler_params=pltpu.CompilerParams(vmem_limit_bytes=VMEM_LIMIT),
        cost_estimate=pl.CostEstimate(flops=flops, bytes_accessed=moved, transcendentals=0),
        name=name,
    )(*operands)


NEAR = pl.BlockSpec(memory_space=pltpu.VMEM)
ANYWHERE = pl.BlockSpec(memory_space=pl.ANY)
FAR = pl.BlockSpec(memory_space=pltpu.HBM)


def head_columns(width):
    depth = width // HEADS
    return [slice(h * depth, (h + 1) * depth) for h in range(HEADS)]


def slot_rows(rows, slots):
    span = rows // slots
    return [slice(s * span, (s + 1) * span) for s in range(slots)]


def row_mean(blocks, width):
    return jnp.sum(sum(blocks[1:], blocks[0]), axis=1, keepdims=True) / width


def slice_kernel(group, block_ref, out_ref, sem):
    rows = out_ref.shape[0]
    start = pl.multiple_of(lax.rem(lax.axis_index("dp"), group) * rows, rows)
    copy = pltpu.make_async_copy(block_ref.at[pl.ds(start, rows)], out_ref, sem)
    copy.start()
    copy.wait()


def prepare_kernel(slots, _, lengths_ref, sibling_ref, *refs):
    inputs, held = refs[:6], refs[6:11]
    (events_t_ref, key_t_ref, value_t_ref, weight_ref, gated_ref, first_ref,
     gate_ref, own_lengths_ref, sems) = refs[11:]
    events_ref, key_ref, value_ref, upstream_ref, _ = held
    copies = [
        pltpu.make_async_copy(source, target, sems.at[i])
        for i, (source, target) in enumerate(zip(inputs, held + (gate_ref,)))
    ]
    copies.append(pltpu.make_async_copy(lengths_ref, own_lengths_ref, sems.at[len(copies)]))
    for copy in copies:
        copy.start()
    rows, width = key_ref.shape
    events_t_ref[:, rows:] = sibling_ref[...].T
    for copy in copies:
        copy.wait()
    events_t_ref[:, :rows] = events_ref[...].T
    key_t_ref[...] = key_ref[...].T
    value_t_ref[...] = value_ref[...].T
    span = rows // slots
    row = lax.broadcasted_iota(jnp.int32, (span, span), 0)
    column = lax.broadcasted_iota(jnp.int32, (span, span), 1)
    first_slot = (lax.axis_index("dp") * lax.axis_size("fsdp") + lax.axis_index("fsdp")) * slots
    for s, place in enumerate(slot_rows(rows, slots)):
        length = own_lengths_ref[first_slot + s]
        inverse = 1.0 / jnp.full((span, span), length, jnp.int32).astype(jnp.float32)
        weight_ref[s] = jnp.where((column <= row) & (row < length), inverse, 0.0)
        live = lax.broadcasted_iota(jnp.int32, (span, width), 0) < length
        gated = upstream_ref[place].astype(jnp.float32) * gate_ref[place].astype(jnp.float32)
        gated = jnp.where(live, gated, 0.0)
        gated_ref[place] = gated
        first = row_mean([gated[:, c] for c in head_columns(width)], width)
        first_ref[place] = jnp.broadcast_to(first, (span, first_ref.shape[1]))


def piece_start(shard_rows, group, part_rows, flips, member_flip):
    device = lax.axis_index("dp")
    start = (
        lax.axis_index("fsdp") ^ jnp.where(lax.rem(device, CORES) == 0, flips[0], flips[1])
    ) * shard_rows
    if member_flip is not None:
        start = start + (lax.rem(device, group) ^ member_flip) * part_rows
    return pl.multiple_of(start, 16)


def aligned(shard_rows):
    return shard_rows % 128 == 0


def project(events_ref, pieces, origins, group, shard_rows, spare_ref, sems):
    copies, total = [], None
    for piece, (flips, members) in zip(pieces, origins):
        rows = piece.shape[0] // len(members)
        starts = [piece_start(shard_rows, group, rows, flips, m) for m in members]
        if not aligned(shard_rows):
            for i, start in enumerate(starts):
                copy = pltpu.make_async_copy(
                    piece.at[pl.ds(i * rows, rows)],
                    spare_ref.at[pl.ds(start, rows)],
                    sems.at[len(copies)],
                )
                copy.start()
                copies.append(copy)
            continue
        first = piece_start(shard_rows, group, rows, flips, None)
        if len(members) > 1:
            spare_ref[...] = jnp.zeros_like(spare_ref)
            for i, start in enumerate(starts):
                place = pl.ds(pl.multiple_of(start - first, 16), rows)
                spare_ref[place] = piece[i * rows : (i + 1) * rows]
            piece = spare_ref
        columns = pl.ds(pl.multiple_of(first, 128), shard_rows)
        term = dot(events_ref[:, columns], piece[...])
        total = term if total is None else total + term
    if copies:
        for copy in copies:
            copy.wait()
        total = dot(events_ref[...], spare_ref[...])
    return total


def projection_scratch(shard_rows, model_width, width, origins):
    count = sum(len(members) for _, members in origins)
    spare_rows = shard_rows if aligned(shard_rows) else model_width
    return [pltpu.VMEM((spare_rows, width), jnp.bfloat16), pltpu.SemaphoreType.DMA((count,))]


def projection_kernel(group, shard_rows, origins, *refs):
    pieces, (events_ref, *terms) = refs[: len(origins)], refs[len(origins) : -3]
    out_ref, spare_ref, sems = refs[-3:]
    total = project(events_ref, pieces, origins, group, shard_rows, spare_ref, sems)
    for term in terms:
        total = total + term[...]
    out_ref[...] = total


def attention_kernel(slots, group, shard_rows, origins, *refs):
    pieces = refs[: len(origins)]
    terms, refs = refs[len(origins) : -16], refs[-16:]
    (events_ref, key_ref, value_ref, key_t_ref, value_t_ref, weight_ref, gated_ref, first_ref,
     grad_query_ref, query_ref, normed_ref, mixed_grad_ref, attention_ref, scores_grad_ref,
     spare_ref, sems) = refs
    query = project(events_ref, pieces, origins, group, shard_rows, spare_ref, sems)
    for term in terms:
        query = query + term[...]
    query_ref[...] = query.astype(jnp.bfloat16)

    rows, width = key_ref.shape
    scale = 1.0 / math.sqrt(width // HEADS)
    columns = head_columns(width)
    places = slot_rows(rows, slots)
    each = [(s, h, s * HEADS + h) for s in range(slots) for h in range(HEADS)]
    slopes, mixed, grad_mixed = [], [], []
    for s, h, i in each:
        scores = dot(query_ref[places[s], columns[h]], key_t_ref[columns[h], places[s]]) * scale
        sigmoid = 1.0 / (1.0 + jnp.exp(-scores))
        silu = scores * sigmoid
        attention_ref[i] = (silu * weight_ref[s]).astype(jnp.bfloat16)
        slopes.append((sigmoid + silu * (1.0 - sigmoid)) * weight_ref[s])
    for s, h, i in each:
        mixed.append(dot(attention_ref[i], value_ref[places[s], columns[h]]))
    for s in range(slots):
        own = mixed[s * HEADS : (s + 1) * HEADS]
        mean = row_mean(own, width)
        centred = [m - mean for m in own]
        inv_std = lax.rsqrt(row_mean([c * c for c in centred], width) + EPSILON)
        normed = [c * inv_std for c in centred]
        gated = [gated_ref[places[s], c] for c in columns]
        second = row_mean([g * n for g, n in zip(gated, normed)], width)
        first = first_ref[places[s]]
        for h in range(HEADS):
            normed_ref[places[s], columns[h]] = normed[h]
            grad = inv_std * (gated[h] - first - normed[h] * second)
            mixed_grad_ref[places[s], columns[h]] = grad.astype(jnp.bfloat16)
    for s, h, i in each:
        grad_attention = dot(
            mixed_grad_ref[places[s], columns[h]], value_t_ref[columns[h], places[s]]
        )
        scores_grad_ref[i] = (grad_attention * slopes[i]).astype(jnp.bfloat16)
    for s, h, i in each:
        grad_query = dot(scores_grad_ref[i], key_ref[places[s], columns[h]]) * scale
        grad_query_ref[places[s], columns[h]] = grad_query.astype(jnp.bfloat16)


def outputs_kernel(slots, _, query_ref, normed_ref, mixed_grad_ref, attention_ref, scores_grad_ref,
                   upstream_ref, grad_key_ref, grad_value_ref, grad_gate_ref):
    rows, width = query_ref.shape
    scale = 1.0 / math.sqrt(width // HEADS)
    columns = head_columns(width)
    places = slot_rows(rows, slots)
    grad_gate_ref[...] = (upstream_ref[...].astype(jnp.float32) * normed_ref[...]).astype(
        jnp.bfloat16
    )
    for s in range(slots):
        for h in range(HEADS):
            i = s * HEADS + h
            grad_value = dot(attention_ref[i], mixed_grad_ref[places[s], columns[h]], FIRST)
            grad_value_ref[places[s], columns[h]] = grad_value.astype(jnp.bfloat16)
            grad_key = dot(scores_grad_ref[i], query_ref[places[s], columns[h]], FIRST) * scale
            grad_key_ref[places[s], columns[h]] = grad_key.astype(jnp.bfloat16)


def summing_half(k, z):
    return lax.rem(lax.axis_index("dp"), CORES) ^ (1 if k else 0) ^ (1 if z else 0)


def gradient_picks(chips, shard_flips):
    every = [(k, i, z) for k in range(chips) for i, z in enumerate(shard_flips)]
    return [[p for p in every if (p[0] != 0) ^ (p[2] != 0) == bool(side)] for side in range(CORES)]


def half_columns(side, half):
    return pl.ds(pl.multiple_of(summing_half(side, 0) * half, half), half)


def own_gradient_kernel(chips, sets, events_ref, grad_query_ref, *refs):
    outs, picked_ref = refs[:-1], refs[-1]
    rows, half = grad_query_ref.shape[0], grad_query_ref.shape[1] // CORES
    shard_rows = events_ref.shape[0] // lax.axis_size("fsdp")
    part_rows = shard_rows // chips
    chip, here = lax.div(lax.axis_index("dp"), CORES), lax.axis_index("fsdp")
    for flips, term_ref, other_ref in zip(sets, outs[::2], outs[1::2]):
        at = 0
        for side, picks in enumerate(gradient_picks(chips, flips)):
            first = at
            for k, _, z in picks:
                start = (here ^ z) * shard_rows + (chip ^ k) * part_rows
                source = pl.ds(pl.multiple_of(start, part_rows), part_rows)
                picked_ref[at : at + part_rows] = events_ref[source, :rows]
                other_ref[at : at + part_rows] = events_ref[source, rows:]
                at += part_rows
            columns = half_columns(side, half)
            term_ref[first:at] = dot(picked_ref[first:at], grad_query_ref[:, columns])


def gradient_kernel(order, sets, grad_query_ref, *refs):
    terms, outs = refs[: 2 * len(sets)], refs[2 * len(sets) :]
    for which, flips in enumerate(sets):
        term_ref, events_ref = terms[2 * which : 2 * which + 2]
        out_of = dict(zip(order, outs[which * len(order) :]))
        half = term_ref.shape[1]
        part_rows = out_of[0].shape[0]
        at = 0
        for side, picks in enumerate(gradient_picks(len(order), flips)):
            rows = slice(at, at + len(picks) * part_rows)
            columns = half_columns(side, half)
            total = term_ref[rows] + dot(events_ref[rows], grad_query_ref[:, columns])
            for p, (k, i, _) in enumerate(picks):
                block = total[p * part_rows : (p + 1) * part_rows]
                out_of[k][:, i * half : (i + 1) * half] = block.astype(out_of[k].dtype)
            at = rows.stop


def chip_sum_kernel(term_count, _, *refs):
    terms, outs = refs[:term_count], refs[term_count:]
    at = 0
    for out in outs:
        columns = slice(at, at + out.shape[1])
        total = terms[0][:, columns].astype(jnp.float32)
        for term in terms[1:]:
            total = total + term[:, columns].astype(jnp.float32)
        out[...] = total.astype(out.dtype)
        at += out.shape[1]


def mean_kernel(count, _, *refs):
    total = refs[0][...].astype(jnp.float32)
    for term in refs[1:-1]:
        total = total + term[...].astype(jnp.float32)
    refs[-1][...] = (total / count).astype(refs[-1].dtype)


def place_kernel(side, chips, blocks_ref, *refs):
    out_ref, held_ref, sems = refs[-3:]
    rows, half = blocks_ref.shape[0] // chips, blocks_ref.shape[1]
    core, chip = lax.rem(lax.axis_index("dp"), CORES) ^ side, lax.div(lax.axis_index("dp"), CORES)
    held_ref[...] = blocks_ref[...].astype(held_ref.dtype)
    copies = []
    for k in range(chips):
        place = pl.ds(pl.multiple_of((chip ^ k) * rows, rows), rows)
        columns = pl.ds(pl.multiple_of((core ^ (1 if k else 0)) * half, half), half)
        block = held_ref.at[pl.ds(k * rows, rows)]
        copies.append(pltpu.make_async_copy(block, out_ref.at[place, columns], sems.at[k]))
        copies[k].start()
    for copy in copies:
        copy.wait()


def flip(block, axis, count, bits):
    return lax.ppermute(block, axis, [(i, i ^ bits) for i in range(count)])


def cross(block, dp_count, fsdp_count, chip_bits, shard_bits):
    pairs = [
        (
            d * fsdp_count + z,
            (d ^ (chip_bits * CORES) ^ 1) * fsdp_count + (z ^ shard_bits[d % CORES]),
        )
        for d in range(dp_count)
        for z in range(fsdp_count)
    ]
    return lax.ppermute(block, BOTH, pairs)


def far_first(count, send):
    return [send(k) for k in range(count - 1, 0, -1)][::-1]


def shard_pairs(fsdp_count):
    others = [d for d in range(1, fsdp_count) if d != fsdp_count // 2]
    return list(zip(others[::2], others[1::2]))


def across_z(weight, dp_count, fsdp_count):
    rows = weight.shape[0]
    group = max(g for g in (2, 4, 8) if dp_count % g == 0 and rows % (16 * g) == 0)
    part = call(
        functools.partial(slice_kernel, group),
        "own_part_of_weight",
        [weight],
        [FAR],
        jax.ShapeDtypeStruct((rows // group, weight.shape[1]), weight.dtype),
        [pltpu.SemaphoreType.DMA],
    )
    weight, part = lax.optimization_barrier((weight, part))
    middle = (fsdp_count // 2,) * CORES
    part = cross(part, dp_count, fsdp_count, 0, middle)
    wholes = [
        (cross(weight, dp_count, fsdp_count, 0, flips), flips[::-1])
        for flips in shard_pairs(fsdp_count)
    ]
    return group, part, wholes


def stack_kernel(_, *refs):
    out_ref = refs[-1]
    rows = refs[0].shape[0]
    for i, block_ref in enumerate(refs[:-1]):
        out_ref[i * rows : (i + 1) * rows] = block_ref[...]


def share(group, part, wholes, ready, dp_count, fsdp_count):
    alike = (0,) * CORES
    parts, members = [part], [1]
    for chip_bits in range(1, group // CORES):
        parts.append(cross(part, dp_count, fsdp_count, chip_bits, alike))
        members.append(CORES * chip_bits)
    if len(parts) > 1:
        rows, columns = part.shape
        part = call(
            stack_kernel,
            "parts_of_weight",
            [ready] + parts,
            [ANYWHERE] + [NEAR] * len(parts),
            jax.ShapeDtypeStruct((len(parts) * rows, columns), part.dtype),
        )
    held = [(part, (fsdp_count // 2,) * CORES, members)]
    for block, flips in wholes:
        held.append((lax.optimization_barrier((block, part))[0], flips, [None]))
    moved = []
    for block, flips, members in held:
        places = [m if m is None else m ^ 1 for m in members]
        moved.append((flip(block, "dp", dp_count, 1), flips[::-1], places))
    return held, moved


def shards(events, query_weight, keys, values, gates, cotangent, lengths):
    slots, span, model_width = events.shape
    width = query_weight.shape[1]
    half_width = width // CORES
    rows = slots * span
    dp_count, fsdp_count = lax.axis_size("dp"), lax.axis_size("fsdp")
    chips = dp_count // CORES
    shard_rows = model_width // fsdp_count
    total_seqs = slots * dp_count * fsdp_count
    bf16, f32 = jnp.bfloat16, jnp.float32

    def shape(*dims, dtype=bf16):
        return jax.ShapeDtypeStruct(dims, dtype)

    flat_events = events.reshape(rows, model_width)
    keys, values, gates, cotangent = (
        a.reshape(rows, width) for a in (keys, values, gates, cotangent)
    )
    sibling_events = flip(flat_events, "dp", dp_count, 1)
    group, part, wholes = across_z(query_weight, dp_count, fsdp_count)
    prepared = call(
        functools.partial(prepare_kernel, slots),
        "prepared_operands",
        [part, lengths, sibling_events]
        + [flat_events, keys, values, cotangent, query_weight, gates],
        [ANYWHERE, FAR, NEAR] + [FAR] * 6,
        (
            shape(rows, model_width),
            shape(rows, width),
            shape(rows, width),
            shape(rows, width),
            shape(shard_rows, width),
            shape(model_width, CORES * rows),
            shape(width, rows),
            shape(width, rows),
            shape(slots, span, span, dtype=f32),
            shape(rows, width, dtype=f32),
            shape(rows, span, dtype=f32),
        ),
        [
            pltpu.VMEM((rows, width), bf16),
            pltpu.SMEM(lengths.shape, jnp.int32),
            pltpu.SemaphoreType.DMA((7,)),
        ],
        flops=5 * 10**9,
    )
    near_events, near_keys, near_values, near_cotangent, near_weight = prepared[:5]
    events_t, keys_t, values_t, weight, gated, first = prepared[5:]
    held, moved = share(group, part, wholes, first, dp_count, fsdp_count)
    held = [(near_weight, (0, 0), [None])] + held
    if not aligned(shard_rows):
        held, moved = [], held + moved

    def split(found):
        return [f[0] for f in found], [f[1:] for f in found]

    terms = []
    for name, found in (("held", held), ("passed", moved[:1])):
        if not held:
            break
        pieces, origins = split(found)
        operands = pieces + [near_events] + terms
        terms = [
            call(
                functools.partial(projection_kernel, group, shard_rows, origins),
                f"projection_by_{name}_rows",
                operands,
                [NEAR] * len(operands),
                shape(rows, width, dtype=f32),
                projection_scratch(shard_rows, model_width, width, origins),
                flops=3 * 10**9 if terms else 2 * rows * width * shard_rows * len(pieces),
                moved=4 * rows * width,
            )
        ]
    if held:
        moved = moved[1:]
    pieces, origins = split(moved)
    blocks = shape(slots * HEADS, span, span)
    grad_query, query, normed, grad_mixed, attention, grad_scores = call(
        functools.partial(attention_kernel, slots, group, shard_rows, origins),
        "attention_to_grad_query",
        pieces
        + terms
        + [near_events, near_keys, near_values, keys_t, values_t, weight, gated, first],
        [NEAR] * (len(pieces) + len(terms) + 8),
        (
            shape(rows, width),
            shape(rows, width),
            shape(rows, width, dtype=f32),
            shape(rows, width),
            blocks,
            blocks,
        ),
        projection_scratch(shard_rows, model_width, width, origins),
        flops=2 * rows * width * (model_width + 4 * span),
        moved=24 * rows * width,
    )
    part_rows = shard_rows // chips
    staged = part_rows % 16 == 0 and fsdp_count % 4 == 0
    terms = [grad_query]
    if staged:
        alike = (0,) * CORES

        def to_chip(block, k):
            return cross(block, dp_count, fsdp_count, k, alike)

        order = (0,) + tuple(range(chips - 1, 0, -1))

        def summed_over_chips(terms, name, which, after):
            flips = sets[which]
            terms = [terms[0]] + [to_chip(a, k) for a, k in zip(terms[1:], order[1:])]
            return call(
                functools.partial(chip_sum_kernel, chips),
                name,
                [after] + terms,
                [ANYWHERE] + [NEAR] * chips,
                tuple(shape(part_rows, half_width, dtype=bf16 if z else f32) for z in flips),
            )

        sets = (tuple(range(fsdp_count - 1, 1, -1)), (0, 1))
        picked_rows = [len(flips) * shard_rows for flips in sets]
        got = flip(grad_query, "dp", dp_count, 1)
        own_terms = call(
            functools.partial(own_gradient_kernel, chips, sets),
            "weight_gradient_of_own_events",
            [events_t, grad_query],
            [NEAR] * 2,
            tuple(
                a
                for n in picked_rows
                for a in (shape(n, half_width, dtype=f32), shape(n, rows))
            ),
            [pltpu.VMEM((max(picked_rows), rows), bf16)],
            flops=2 * rows * model_width * half_width,
            moved=8 * model_width * rows,
        )

        finished = call(
            functools.partial(gradient_kernel, order, sets),
            "weight_gradient_of_both_cores",
            [got, *own_terms],
            [NEAR] * (1 + len(own_terms)),
            tuple(
                shape(part_rows, len(flips) * half_width, dtype=bf16 if k else f32)
                for flips in sets
                for k in order
            ),
            flops=2 * rows * model_width * half_width,
            moved=2 * model_width * (rows + 2 * half_width),
        )
        far_terms, terms = finished[:chips], finished[chips:]

        def to_shard(block, z):
            return cross(block, dp_count, fsdp_count, 0, (z,) * CORES)

        far_sums = summed_over_chips(far_terms, "far_shards_over_chips", 0, got)
        own_sum, next_sum = summed_over_chips(
            terms, "near_shards_over_chips", 1, far_sums[0]
        )
        far_sums = [to_shard(a, z) for a, z in reversed(list(zip(far_sums, sets[0])))]
        terms = [next_sum]
        next_sum = to_shard(next_sum, 1)
    grad_keys, grad_values, grad_gates = call(
        functools.partial(outputs_kernel, slots),
        "key_value_gate_gradients",
        [terms[0], query, normed, grad_mixed, attention, grad_scores, near_cotangent],
        [ANYWHERE] + [NEAR] * 6,
        (shape(rows, width),) * 3,
        flops=4 * rows * width * span,
        moved=12 * rows * width,
    )
    if staged:
        mean = call(
            functools.partial(mean_kernel, total_seqs),
            "mean_over_shards",
            [grad_keys, own_sum, next_sum] + far_sums,
            [FAR] + [NEAR] * fsdp_count,
            shape(part_rows, half_width),
        )
        blocks = call(
            stack_kernel,
            "blocks_of_chips",
            [mean, mean] + far_first(chips, lambda k: to_chip(mean, k)),
            [ANYWHERE] + [NEAR] * chips,
            shape(shard_rows, half_width),
        )
        grad_weight = ()
        for side in range(CORES):
            grad_weight = call(
                functools.partial(place_kernel, side, chips),
                f"blocks_of_{'sibling' if side else 'own'}_core_in_place",
                [flip(blocks, "dp", dp_count, 1) if side else blocks, *grad_weight],
                [NEAR] + [FAR] * side,
                shape(shard_rows, width, dtype=f32),
                [
                    pltpu.VMEM((shard_rows, half_width), f32),
                    pltpu.SemaphoreType.DMA((chips,)),
                ],
                out_specs=FAR,
                aliases={1: 0} if side else {},
            )
            grad_weight = grad_weight if side else (grad_weight,)
    else:
        whole = lax.dot_general(flat_events, grad_query, FIRST, preferred_element_type=f32)
        mine = lax.psum_scatter(whole, "fsdp", scatter_dimension=0, tiled=True)
        grad_weight = lax.psum(mine, "dp") / total_seqs

    full = (slots, span, width)
    return (
        grad_keys.reshape(full),
        grad_values.reshape(full),
        grad_gates.reshape(full),
        grad_weight,
    )


def solution(mesh):
    split = P(BOTH, None, None)
    return jax.shard_map(
        shards,
        mesh=mesh,
        in_specs=(split, P("fsdp", None), split, split, split, split, P()),
        out_specs=(split, split, split, P("fsdp", None)),
        check_vma=False,
    )
```

```python
import functools
import math

import jax
import jax.numpy as jnp
from jax import lax
from jax.experimental import pallas as pl
from jax.experimental.pallas import tpu as pltpu
from jax.sharding import PartitionSpec as P

HEADS = 4
EPSILON = 1e-06
CORES = 2
BOTH = ("dp", "fsdp")
VMEM_LIMIT = 24 * 1024 * 1024

LAST = (((1,), (1,)), ((), ()))
FIRST = (((0,), (0,)), ((), ()))


def dot(lhs, rhs, dims=(((1,), (0,)), ((), ()))):
    return lax.dot_general(lhs, rhs, dims, preferred_element_type=jnp.float32)


def call(kernel, name, operands, in_specs, out_shape, scratch=(), flops=0, moved=0,
         out_specs=None, aliases=None):
    vmem = pl.BlockSpec(memory_space=pltpu.VMEM)
    many = isinstance(out_shape, tuple)
    operands = [
        pltpu.with_memory_space_constraint(a, pltpu.HBM) if spec is FAR else a
        for a, spec in zip(operands, in_specs)
    ]
    return pl.pallas_call(
        kernel,
        out_shape=out_shape,
        in_specs=in_specs,
        out_specs=out_specs or ((vmem,) * len(out_shape) if many else vmem),
        scratch_shapes=list(scratch),
        input_output_aliases=aliases or {},
        compiler_params=pltpu.CompilerParams(vmem_limit_bytes=VMEM_LIMIT),
        cost_estimate=pl.CostEstimate(flops=flops, bytes_accessed=moved, transcendentals=0),
        name=name,
    )(*operands)


NEAR = pl.BlockSpec(memory_space=pltpu.VMEM)
ANYWHERE = pl.BlockSpec(memory_space=pl.ANY)
FAR = pl.BlockSpec(memory_space=pltpu.HBM)


def head_columns(width):
    depth = width // HEADS
    return [slice(h * depth, (h + 1) * depth) for h in range(HEADS)]


def slot_rows(rows, slots):
    span = rows // slots
    return [slice(s * span, (s + 1) * span) for s in range(slots)]


def row_mean(blocks, width):
    return jnp.sum(sum(blocks[1:], blocks[0]), axis=1, keepdims=True) / width


def slice_kernel(group, block_ref, out_ref, sem):
    rows = out_ref.shape[0]
    start = pl.multiple_of(lax.rem(lax.axis_index("dp"), group) * rows, rows)
    copy = pltpu.make_async_copy(block_ref.at[pl.ds(start, rows)], out_ref, sem)
    copy.start()
    copy.wait()


def prepare_kernel(slots, _, lengths_ref, sibling_ref, *refs):
    inputs, held = refs[:6], refs[6:11]
    (events_t_ref, key_t_ref, value_t_ref, weight_ref, gated_ref, first_ref,
     gate_ref, own_lengths_ref, sems) = refs[11:]
    events_ref, key_ref, value_ref, upstream_ref, _ = held
    copies = [
        pltpu.make_async_copy(source, target, sems.at[i])
        for i, (source, target) in enumerate(zip(inputs, held + (gate_ref,)))
    ]
    copies.append(pltpu.make_async_copy(lengths_ref, own_lengths_ref, sems.at[len(copies)]))
    for copy in copies:
        copy.start()
    rows, width = key_ref.shape
    events_t_ref[:, rows:] = sibling_ref[...].T
    for copy in copies:
        copy.wait()
    events_t_ref[:, :rows] = events_ref[...].T
    key_t_ref[...] = key_ref[...].T
    value_t_ref[...] = value_ref[...].T
    span = rows // slots
    row = lax.broadcasted_iota(jnp.int32, (span, span), 0)
    column = lax.broadcasted_iota(jnp.int32, (span, span), 1)
    first_slot = (lax.axis_index("dp") * lax.axis_size("fsdp") + lax.axis_index("fsdp")) * slots
    for s, place in enumerate(slot_rows(rows, slots)):
        length = own_lengths_ref[first_slot + s]
        inverse = 1.0 / jnp.full((span, span), length, jnp.int32).astype(jnp.float32)
        weight_ref[s] = jnp.where((column <= row) & (row < length), inverse, 0.0)
        live = lax.broadcasted_iota(jnp.int32, (span, width), 0) < length
        gated = upstream_ref[place].astype(jnp.float32) * gate_ref[place].astype(jnp.float32)
        gated = jnp.where(live, gated, 0.0)
        gated_ref[place] = gated
        first = row_mean([gated[:, c] for c in head_columns(width)], width)
        first_ref[place] = jnp.broadcast_to(first, (span, first_ref.shape[1]))


def piece_start(shard_rows, group, part_rows, flips, member_flip):
    device = lax.axis_index("dp")
    start = (
        lax.axis_index("fsdp") ^ jnp.where(lax.rem(device, CORES) == 0, flips[0], flips[1])
    ) * shard_rows
    if member_flip is not None:
        start = start + (lax.rem(device, group) ^ member_flip) * part_rows
    return pl.multiple_of(start, 16)


def aligned(shard_rows):
    return shard_rows % 128 == 0


def project(events_ref, pieces, origins, group, shard_rows, spare_ref, sems):
    copies, total = [], None
    for piece, (flips, members) in zip(pieces, origins):
        rows = piece.shape[0] // len(members)
        starts = [piece_start(shard_rows, group, rows, flips, m) for m in members]
        if not aligned(shard_rows):
            for i, start in enumerate(starts):
                copy = pltpu.make_async_copy(
                    piece.at[pl.ds(i * rows, rows)],
                    spare_ref.at[pl.ds(start, rows)],
                    sems.at[len(copies)],
                )
                copy.start()
                copies.append(copy)
            continue
        first = piece_start(shard_rows, group, rows, flips, None)
        if len(members) > 1:
            spare_ref[...] = jnp.zeros_like(spare_ref)
            for i, start in enumerate(starts):
                place = pl.ds(pl.multiple_of(start - first, 16), rows)
                spare_ref[place] = piece[i * rows : (i + 1) * rows]
            piece = spare_ref
        columns = pl.ds(pl.multiple_of(first, 128), shard_rows)
        term = dot(events_ref[:, columns], piece[...])
        total = term if total is None else total + term
    if copies:
        for copy in copies:
            copy.wait()
        total = dot(events_ref[...], spare_ref[...])
    return total


def projection_scratch(shard_rows, model_width, width, origins):
    count = sum(len(members) for _, members in origins)
    spare_rows = shard_rows if aligned(shard_rows) else model_width
    return [pltpu.VMEM((spare_rows, width), jnp.bfloat16), pltpu.SemaphoreType.DMA((count,))]


def projection_kernel(group, shard_rows, origins, *refs):
    pieces, (events_ref, *terms) = refs[: len(origins)], refs[len(origins) : -3]
    out_ref, spare_ref, sems = refs[-3:]
    total = project(events_ref, pieces, origins, group, shard_rows, spare_ref, sems)
    for term in terms:
        total = total + term[...]
    out_ref[...] = total


def attention_kernel(slots, group, shard_rows, origins, *refs):
    pieces = refs[: len(origins)]
    terms, refs = refs[len(origins) : -16], refs[-16:]
    (events_ref, key_ref, value_ref, key_t_ref, value_t_ref, weight_ref, gated_ref, first_ref,
     grad_query_ref, query_ref, normed_ref, mixed_grad_ref, attention_ref, scores_grad_ref,
     spare_ref, sems) = refs
    query = project(events_ref, pieces, origins, group, shard_rows, spare_ref, sems)
    for term in terms:
        query = query + term[...]
    query_ref[...] = query.astype(jnp.bfloat16)

    rows, width = key_ref.shape
    scale = 1.0 / math.sqrt(width // HEADS)
    columns = head_columns(width)
    places = slot_rows(rows, slots)
    each = [(s, h, s * HEADS + h) for s in range(slots) for h in range(HEADS)]
    slopes, mixed, grad_mixed = [], [], []
    for s, h, i in each:
        scores = dot(query_ref[places[s], columns[h]], key_t_ref[columns[h], places[s]]) * scale
        sigmoid = 1.0 / (1.0 + jnp.exp(-scores))
        silu = scores * sigmoid
        attention_ref[i] = (silu * weight_ref[s]).astype(jnp.bfloat16)
        slopes.append((sigmoid + silu * (1.0 - sigmoid)) * weight_ref[s])
    for s, h, i in each:
        mixed.append(dot(attention_ref[i], value_ref[places[s], columns[h]]))
    for s in range(slots):
        own = mixed[s * HEADS : (s + 1) * HEADS]
        mean = row_mean(own, width)
        centred = [m - mean for m in own]
        inv_std = lax.rsqrt(row_mean([c * c for c in centred], width) + EPSILON)
        normed = [c * inv_std for c in centred]
        gated = [gated_ref[places[s], c] for c in columns]
        second = row_mean([g * n for g, n in zip(gated, normed)], width)
        first = first_ref[places[s]]
        for h in range(HEADS):
            normed_ref[places[s], columns[h]] = normed[h]
            grad = inv_std * (gated[h] - first - normed[h] * second)
            mixed_grad_ref[places[s], columns[h]] = grad.astype(jnp.bfloat16)
    for s, h, i in each:
        grad_attention = dot(
            mixed_grad_ref[places[s], columns[h]], value_t_ref[columns[h], places[s]]
        )
        scores_grad_ref[i] = (grad_attention * slopes[i]).astype(jnp.bfloat16)
    for s, h, i in each:
        grad_query = dot(scores_grad_ref[i], key_ref[places[s], columns[h]]) * scale
        grad_query_ref[places[s], columns[h]] = grad_query.astype(jnp.bfloat16)


def outputs_kernel(slots, _, query_ref, normed_ref, mixed_grad_ref, attention_ref, scores_grad_ref,
                   upstream_ref, grad_key_ref, grad_value_ref, grad_gate_ref):
    rows, width = query_ref.shape
    scale = 1.0 / math.sqrt(width // HEADS)
    columns = head_columns(width)
    places = slot_rows(rows, slots)
    grad_gate_ref[...] = (upstream_ref[...].astype(jnp.float32) * normed_ref[...]).astype(
        jnp.bfloat16
    )
    for s in range(slots):
        for h in range(HEADS):
            i = s * HEADS + h
            grad_value = dot(attention_ref[i], mixed_grad_ref[places[s], columns[h]], FIRST)
            grad_value_ref[places[s], columns[h]] = grad_value.astype(jnp.bfloat16)
            grad_key = dot(scores_grad_ref[i], query_ref[places[s], columns[h]], FIRST) * scale
            grad_key_ref[places[s], columns[h]] = grad_key.astype(jnp.bfloat16)


def summing_half(k, z):
    return lax.rem(lax.axis_index("dp"), CORES) ^ (1 if k else 0) ^ (1 if z else 0)


def gradient_picks(chips, shard_flips):
    every = [(k, i, z) for k in range(chips) for i, z in enumerate(shard_flips)]
    return [[p for p in every if (p[0] != 0) ^ (p[2] != 0) == bool(side)] for side in range(CORES)]


def half_columns(side, half):
    return pl.ds(pl.multiple_of(summing_half(side, 0) * half, half), half)


def own_gradient_kernel(chips, sets, events_ref, grad_query_ref, *refs):
    outs, picked_ref = refs[:-1], refs[-1]
    rows, half = grad_query_ref.shape[0], grad_query_ref.shape[1] // CORES
    shard_rows = events_ref.shape[0] // lax.axis_size("fsdp")
    part_rows = shard_rows // chips
    chip, here = lax.div(lax.axis_index("dp"), CORES), lax.axis_index("fsdp")
    for flips, term_ref, other_ref in zip(sets, outs[::2], outs[1::2]):
        at = 0
        for side, picks in enumerate(gradient_picks(chips, flips)):
            first = at
            for k, _, z in picks:
                start = (here ^ z) * shard_rows + (chip ^ k) * part_rows
                source = pl.ds(pl.multiple_of(start, part_rows), part_rows)
                picked_ref[at : at + part_rows] = events_ref[source, :rows]
                other_ref[at : at + part_rows] = events_ref[source, rows:]
                at += part_rows
            columns = half_columns(side, half)
            term_ref[first:at] = dot(picked_ref[first:at], grad_query_ref[:, columns])


def gradient_kernel(order, sets, grad_query_ref, *refs):
    terms, outs = refs[: 2 * len(sets)], refs[2 * len(sets) :]
    for which, flips in enumerate(sets):
        term_ref, events_ref = terms[2 * which : 2 * which + 2]
        out_of = dict(zip(order, outs[which * len(order) :]))
        half = term_ref.shape[1]
        part_rows = out_of[0].shape[0]
        at = 0
        for side, picks in enumerate(gradient_picks(len(order), flips)):
            rows = slice(at, at + len(picks) * part_rows)
            columns = half_columns(side, half)
            total = term_ref[rows] + dot(events_ref[rows], grad_query_ref[:, columns])
            for p, (k, i, _) in enumerate(picks):
                block = total[p * part_rows : (p + 1) * part_rows]
                out_of[k][:, i * half : (i + 1) * half] = block.astype(out_of[k].dtype)
            at = rows.stop


def chip_sum_kernel(term_count, _, *refs):
    terms, outs = refs[:term_count], refs[term_count:]
    at = 0
    for out in outs:
        columns = slice(at, at + out.shape[1])
        total = terms[0][:, columns].astype(jnp.float32)
        for term in terms[1:]:
            total = total + term[:, columns].astype(jnp.float32)
        out[...] = total.astype(out.dtype)
        at += out.shape[1]


def mean_kernel(count, _, *refs):
    total = refs[0][...].astype(jnp.float32)
    for term in refs[1:-1]:
        total = total + term[...].astype(jnp.float32)
    refs[-1][...] = (total / count).astype(refs[-1].dtype)


def place_kernel(side, chips, blocks_ref, *refs):
    out_ref, held_ref, sems = refs[-3:]
    rows, half = blocks_ref.shape[0] // chips, blocks_ref.shape[1]
    core, chip = lax.rem(lax.axis_index("dp"), CORES) ^ side, lax.div(lax.axis_index("dp"), CORES)
    held_ref[...] = blocks_ref[...].astype(held_ref.dtype)
    copies = []
    for k in range(chips):
        place = pl.ds(pl.multiple_of((chip ^ k) * rows, rows), rows)
        columns = pl.ds(pl.multiple_of((core ^ (1 if k else 0)) * half, half), half)
        block = held_ref.at[pl.ds(k * rows, rows)]
        copies.append(pltpu.make_async_copy(block, out_ref.at[place, columns], sems.at[k]))
        copies[k].start()
    for copy in copies:
        copy.wait()


def flip(block, axis, count, bits):
    return lax.ppermute(block, axis, [(i, i ^ bits) for i in range(count)])


def cross(block, dp_count, fsdp_count, chip_bits, shard_bits):
    pairs = [
        (
            d * fsdp_count + z,
            (d ^ (chip_bits * CORES) ^ 1) * fsdp_count + (z ^ shard_bits[d % CORES]),
        )
        for d in range(dp_count)
        for z in range(fsdp_count)
    ]
    return lax.ppermute(block, BOTH, pairs)


def far_first(count, send):
    return [send(k) for k in range(count - 1, 0, -1)][::-1]


def shard_pairs(fsdp_count):
    others = [d for d in range(1, fsdp_count) if d != fsdp_count // 2]
    return list(zip(others[::2], others[1::2]))


def across_z(weight, dp_count, fsdp_count):
    rows = weight.shape[0]
    group = max(g for g in (2, 4, 8) if dp_count % g == 0 and rows % (16 * g) == 0)
    part = call(
        functools.partial(slice_kernel, group),
        "own_part_of_weight",
        [weight],
        [FAR],
        jax.ShapeDtypeStruct((rows // group, weight.shape[1]), weight.dtype),
        [pltpu.SemaphoreType.DMA],
    )
    weight, part = lax.optimization_barrier((weight, part))
    middle = (fsdp_count // 2,) * CORES
    part = cross(part, dp_count, fsdp_count, 0, middle)
    wholes = [
        (cross(weight, dp_count, fsdp_count, 0, flips), flips[::-1])
        for flips in shard_pairs(fsdp_count)
    ]
    return group, part, wholes


def stack_kernel(_, *refs):
    out_ref = refs[-1]
    rows = refs[0].shape[0]
    for i, block_ref in enumerate(refs[:-1]):
        out_ref[i * rows : (i + 1) * rows] = block_ref[...]


def share(group, part, wholes, ready, dp_count, fsdp_count):
    alike = (0,) * CORES
    parts, members = [part], [1]
    for chip_bits in range(1, group // CORES):
        parts.append(cross(part, dp_count, fsdp_count, chip_bits, alike))
        members.append(CORES * chip_bits)
    if len(parts) > 1:
        rows, columns = part.shape
        part = call(
            stack_kernel,
            "parts_of_weight",
            [ready] + parts,
            [ANYWHERE] + [NEAR] * len(parts),
            jax.ShapeDtypeStruct((len(parts) * rows, columns), part.dtype),
        )
    held = [(part, (fsdp_count // 2,) * CORES, members)]
    for block, flips in wholes:
        held.append((lax.optimization_barrier((block, part))[0], flips, [None]))
    moved = []
    for block, flips, members in held:
        places = [m if m is None else m ^ 1 for m in members]
        moved.append((flip(block, "dp", dp_count, 1), flips[::-1], places))
    return held, moved


def shards(events, query_weight, keys, values, gates, cotangent, lengths):
    slots, span, model_width = events.shape
    width = query_weight.shape[1]
    half_width = width // CORES
    rows = slots * span
    dp_count, fsdp_count = lax.axis_size("dp"), lax.axis_size("fsdp")
    chips = dp_count // CORES
    shard_rows = model_width // fsdp_count
    total_seqs = slots * dp_count * fsdp_count
    bf16, f32 = jnp.bfloat16, jnp.float32

    def shape(*dims, dtype=bf16):
        return jax.ShapeDtypeStruct(dims, dtype)

    flat_events = events.reshape(rows, model_width)
    keys, values, gates, cotangent = (
        a.reshape(rows, width) for a in (keys, values, gates, cotangent)
    )
    sibling_events = flip(flat_events, "dp", dp_count, 1)
    group, part, wholes = across_z(query_weight, dp_count, fsdp_count)
    prepared = call(
        functools.partial(prepare_kernel, slots),
        "prepared_operands",
        [part, lengths, sibling_events]
        + [flat_events, keys, values, cotangent, query_weight, gates],
        [ANYWHERE, FAR, NEAR] + [FAR] * 6,
        (
            shape(rows, model_width),
            shape(rows, width),
            shape(rows, width),
            shape(rows, width),
            shape(shard_rows, width),
            shape(model_width, CORES * rows),
            shape(width, rows),
            shape(width, rows),
            shape(slots, span, span, dtype=f32),
            shape(rows, width, dtype=f32),
            shape(rows, span, dtype=f32),
        ),
        [
            pltpu.VMEM((rows, width), bf16),
            pltpu.SMEM(lengths.shape, jnp.int32),
            pltpu.SemaphoreType.DMA((7,)),
        ],
        flops=5 * 10**9,
    )
    near_events, near_keys, near_values, near_cotangent, near_weight = prepared[:5]
    events_t, keys_t, values_t, weight, gated, first = prepared[5:]
    held, moved = share(group, part, wholes, first, dp_count, fsdp_count)
    held = [(near_weight, (0, 0), [None])] + held
    if not aligned(shard_rows):
        held, moved = [], held + moved

    def split(found):
        return [f[0] for f in found], [f[1:] for f in found]

    terms = []
    for name, found in (("held", held), ("passed", moved[:1])):
        if not held:
            break
        pieces, origins = split(found)
        operands = pieces + [near_events] + terms
        terms = [
            call(
                functools.partial(projection_kernel, group, shard_rows, origins),
                f"projection_by_{name}_rows",
                operands,
                [NEAR] * len(operands),
                shape(rows, width, dtype=f32),
                projection_scratch(shard_rows, model_width, width, origins),
                flops=3 * 10**9 if terms else 2 * rows * width * shard_rows * len(pieces),
                moved=4 * rows * width,
            )
        ]
    if held:
        moved = moved[1:]
    pieces, origins = split(moved)
    blocks = shape(slots * HEADS, span, span)
    grad_query, query, normed, grad_mixed, attention, grad_scores = call(
        functools.partial(attention_kernel, slots, group, shard_rows, origins),
        "attention_to_grad_query",
        pieces
        + terms
        + [near_events, near_keys, near_values, keys_t, values_t, weight, gated, first],
        [NEAR] * (len(pieces) + len(terms) + 8),
        (
            shape(rows, width),
            shape(rows, width),
            shape(rows, width, dtype=f32),
            shape(rows, width),
            blocks,
            blocks,
        ),
        projection_scratch(shard_rows, model_width, width, origins),
        flops=2 * rows * width * (model_width + 4 * span),
        moved=24 * rows * width,
    )
    part_rows = shard_rows // chips
    staged = part_rows % 16 == 0 and fsdp_count % 4 == 0
    terms = [grad_query]
    if staged:
        alike = (0,) * CORES

        def to_chip(block, k):
            return cross(block, dp_count, fsdp_count, k, alike)

        order = (0, 1) + tuple(range(chips - 1, 1, -1))

        def summed_over_chips(terms, name, which, after):
            flips = sets[which]
            terms = [terms[0]] + [to_chip(a, k) for a, k in zip(terms[1:], order[1:])]
            return call(
                functools.partial(chip_sum_kernel, chips),
                name,
                [after] + terms,
                [ANYWHERE] + [NEAR] * chips,
                tuple(shape(part_rows, half_width, dtype=bf16 if z else f32) for z in flips),
            )

        sets = (tuple(range(2, fsdp_count)), (0, 1))
        picked_rows = [len(flips) * shard_rows for flips in sets]
        got = flip(grad_query, "dp", dp_count, 1)
        own_terms = call(
            functools.partial(own_gradient_kernel, chips, sets),
            "weight_gradient_of_own_events",
            [events_t, grad_query],
            [NEAR] * 2,
            tuple(
                a
                for n in picked_rows
                for a in (shape(n, half_width, dtype=f32), shape(n, rows))
            ),
            [pltpu.VMEM((max(picked_rows), rows), bf16)],
            flops=2 * rows * model_width * half_width,
            moved=8 * model_width * rows,
        )

        finished = call(
            functools.partial(gradient_kernel, order, sets),
            "weight_gradient_of_both_cores",
            [got, *own_terms],
            [NEAR] * (1 + len(own_terms)),
            tuple(
                shape(part_rows, len(flips) * half_width, dtype=bf16 if k else f32)
                for flips in sets
                for k in order
            ),
            flops=2 * rows * model_width * half_width,
            moved=2 * model_width * (rows + 2 * half_width),
        )
        far_terms, terms = finished[:chips], finished[chips:]

        def to_shard(block, z):
            return cross(block, dp_count, fsdp_count, 0, (z,) * CORES)

        far_sums = summed_over_chips(far_terms, "far_shards_over_chips", 0, got)
        own_sum, next_sum = summed_over_chips(
            terms, "near_shards_over_chips", 1, far_sums[0]
        )
        far_sums = [to_shard(a, z) for a, z in reversed(list(zip(far_sums, sets[0])))]
        terms = [next_sum]
        next_sum = to_shard(next_sum, 1)
    grad_keys, grad_values, grad_gates = call(
        functools.partial(outputs_kernel, slots),
        "key_value_gate_gradients",
        [terms[0], query, normed, grad_mixed, attention, grad_scores, near_cotangent],
        [ANYWHERE] + [NEAR] * 6,
        (shape(rows, width),) * 3,
        flops=4 * rows * width * span,
        moved=12 * rows * width,
    )
    if staged:
        mean = call(
            functools.partial(mean_kernel, total_seqs),
            "mean_over_shards",
            [grad_keys, own_sum, next_sum] + far_sums,
            [FAR] + [NEAR] * fsdp_count,
            shape(part_rows, half_width),
        )
        blocks = call(
            stack_kernel,
            "blocks_of_chips",
            [mean, mean] + far_first(chips, lambda k: to_chip(mean, k)),
            [ANYWHERE] + [NEAR] * chips,
            shape(shard_rows, half_width),
        )
        grad_weight = ()
        for side in range(CORES):
            grad_weight = call(
                functools.partial(place_kernel, side, chips),
                f"blocks_of_{'sibling' if side else 'own'}_core_in_place",
                [flip(blocks, "dp", dp_count, 1) if side else blocks, *grad_weight],
                [NEAR] + [FAR] * side,
                shape(shard_rows, width, dtype=f32),
                [
                    pltpu.VMEM((shard_rows, half_width), f32),
                    pltpu.SemaphoreType.DMA((chips,)),
                ],
                out_specs=FAR,
                aliases={1: 0} if side else {},
            )
            grad_weight = grad_weight if side else (grad_weight,)
    else:
        whole = lax.dot_general(flat_events, grad_query, FIRST, preferred_element_type=f32)
        mine = lax.psum_scatter(whole, "fsdp", scatter_dimension=0, tiled=True)
        grad_weight = lax.psum(mine, "dp") / total_seqs

    full = (slots, span, width)
    return (
        grad_keys.reshape(full),
        grad_values.reshape(full),
        grad_gates.reshape(full),
        grad_weight,
    )


def solution(mesh):
    split = P(BOTH, None, None)
    return jax.shard_map(
        shards,
        mesh=mesh,
        in_specs=(split, P("fsdp", None), split, split, split, split, P()),
        out_specs=(split, split, split, P("fsdp", None)),
        check_vma=False,
    )
```
